32 devices in a mesh: dp: 8 (over z, y), head: 4 (over x, core).
Axes of the slice: x: 2, y: 2, z: 4, core: 2. Of those that a mesh axis runs over, the one named last changes fastest.
Arguments:
- tokens: float32 [16384, 512], P('dp'), may hold values from -6 to 6
- cotangent: float32 [16384, 512], P('dp'), may hold values from -6 to 6
- timesteps: int32 [64], P('dp'), may hold values from 1 to 1000
- bands: int32 [64], P('dp'), may hold values from 0 to 7
- lengths: int32 [64], P('dp'), may hold values from 1 to 256, as said below
- owners: int32 [16], replicated, may hold values from 0 to 7, as said below
- master_slots: float32 [24, 196608], P('dp', 'head'), as said below
- first_slots: float32 [24, 196608], P('dp', 'head'), as said below
- second_slots: float32 [24, 196608], P('dp', 'head'), as said below
- norm_master: float32 [4, 512], P(None, 'dp'), as said below
- norm_first: float32 [4, 512], P(None, 'dp')
- norm_second: float32 [4, 512], P(None, 'dp'), as said below
Outputs:
- block_output: float32 [16384, 512], P('dp')
- input_grad: float32 [16384, 512], P('dp')
- new_master: float32 [24, 196608], P('dp', 'head')
- new_first: float32 [24, 196608], P('dp', 'head')
- new_second: float32 [24, 196608], P('dp', 'head')
- new_norms: float32 [4, 512], P(None, 'dp')
- new_norm_first: float32 [4, 512], P(None, 'dp')
- new_norm_second: float32 [4, 512], P(None, 'dp')
The draws below stay inside these ranges and needn't reach their ends.
Inputs may be any that keep to these rules, and one draw needn't show every extreme that they name: `lengths`: positions at or past an item's length are padding; the items of higher indices of dp tend to be longer, and some item has all 256 characters. `owners`: every index of dp holds 1 to 3 of the 16 blocks and some holds exactly 3. `master_slots`: row 3 * o + c holds the block that is the c-th, in block order, held by index o; rows past an owner's count are unused. `first_slots`: laid out as master_slots. `second_slots`: laid out as master_slots; positive. `norm_master`: Rows: gain1, shift1, gain2, shift2. `norm_second`: Positive.
All inputs are finite; a program needn't handle non-finite values.
Results may differ from the reference program's by a relative error of at most 0.025.
Values may be sent and summed in bfloat16 or wider, within the bound.
A program may use at most 128 MiB of HBM per device.

```python
import math
import jax
import jax.numpy as jnp
from jax import lax

D = 512
HD = 64
FF = 2048
SEQ = 256
SEQ_DEV = 8
TSTEPS = 1000
NBANDS = 8
CAP = 3
STEP = 5
HEADS_DEV = 2
FF_DEV = 512
ITEMS = 64
TOKENS = 16384
NBLK = 16
SLOTS = 24
BLK = 49152
N_HEAD = 4


def owner_list(key):
    owner_count = NBLK // 2
    owner_order = jax.random.permutation(key, owner_count)
    count_shift = jax.random.randint(jax.random.fold_in(key, 1), (owner_count // 2,), -1, 2)
    count_shift = count_shift.at[0].set(1)
    counts = jnp.zeros((owner_count,), jnp.int32)
    counts = counts.at[owner_order[0::2]].set(2 + count_shift)
    counts = counts.at[owner_order[1::2]].set(2 - count_shift)
    sorted_owners = jnp.repeat(jnp.arange(owner_count, dtype=jnp.int32), counts, total_repeat_length=NBLK)
    mixing = jax.random.permutation(jax.random.fold_in(key, 2), NBLK)
    return sorted_owners[mixing].astype(jnp.int32)


def slot_kinds(owners):
    block_index = jnp.arange(NBLK, dtype=jnp.int32)
    earlier = (owners[None, :] == owners[:, None]) & (block_index[None, :] < block_index[:, None])
    slot_row = owners * CAP + jnp.sum(earlier.astype(jnp.int32), axis=1)
    matches = slot_row[None, :] == jnp.arange(SLOTS, dtype=jnp.int32)[:, None]
    block_of_row = jnp.sum(jnp.where(matches, block_index[None, :], 0), axis=1)
    position = block_of_row[:, None] * BLK + (jnp.arange(N_HEAD * BLK, dtype=jnp.int32) % BLK)[None, :]
    qkv_end = 3 * D * HEADS_DEV * HD
    out_end = qkv_end + HEADS_DEV * HD * D
    up_end = out_end + D * FF_DEV
    kind_index = (position >= qkv_end).astype(jnp.int32) + (position >= out_end).astype(jnp.int32) + (position >= up_end).astype(jnp.int32)
    return kind_index


def choose_by(kind_index, table_values):
    return jnp.where(kind_index == 0, table_values[0], jnp.where(kind_index == 1, table_values[1], jnp.where(kind_index == 2, table_values[2], table_values[3])))


def weight_scales():
    return (D ** (-0.5), 4.0 * D ** (-0.5), D ** (-0.5), FF ** (-0.5))


def grad_scales():
    root_tokens = TOKENS ** 0.5
    return (0.5 * root_tokens, 0.15 * root_tokens, 0.3 * root_tokens, 0.6 * root_tokens)


def draw_owners(key, part):
    return owner_list(key)


def draw_lengths(key, part):
    key = jax.random.fold_in(key, 31)
    item_index = jnp.arange(ITEMS, dtype=jnp.int32)
    device = item_index // SEQ_DEV
    last_device = ITEMS // SEQ_DEV - 1
    low_cap = SEQ // 3
    length_cap = low_cap + (SEQ - low_cap) * device // max(last_device, 1)
    drawn_len = jax.random.randint(key, (ITEMS,), length_cap // 2, length_cap + 1)
    return jnp.where(item_index == ITEMS - SEQ_DEV, SEQ, drawn_len).astype(jnp.int32)


def draw_master_slots(key, part):
    kind_index = slot_kinds(owner_list(key))
    key = jax.random.fold_in(key, 11)
    noise_draw = jnp.clip(jax.random.normal(key, kind_index.shape, jnp.float32), -4.0, 4.0)
    return noise_draw * choose_by(kind_index, weight_scales())


def draw_first_slots(key, part):
    kind_index = slot_kinds(owner_list(key))
    key = jax.random.fold_in(key, 12)
    noise_draw = jnp.clip(jax.random.normal(key, kind_index.shape, jnp.float32), -4.0, 4.0)
    return noise_draw * choose_by(kind_index, grad_scales())


def draw_second_slots(key, part):
    kind_index = slot_kinds(owner_list(key))
    key = jax.random.fold_in(key, 13)
    factor = jnp.exp(jax.random.uniform(key, kind_index.shape, jnp.float32, math.log(0.5), math.log(8.0)))
    scale_row = choose_by(kind_index, grad_scales())
    return factor * scale_row * scale_row


def draw_norm_master(key, part):
    key = jax.random.fold_in(key, 21)
    row_index = jnp.arange(4, dtype=jnp.int32)[:, None]
    gain_draw = jax.random.uniform(key, (4, D), jnp.float32, 0.6, 1.4)
    shifts = 0.3 * jnp.clip(jax.random.normal(jax.random.fold_in(key, 1), (4, D), jnp.float32), -4.0, 4.0)
    return jnp.where(row_index % 2 == 0, gain_draw, shifts)


def draw_norm_first(key, part):
    key = jax.random.fold_in(key, 22)
    noise_draw = jnp.clip(jax.random.normal(key, (4, D), jnp.float32), -4.0, 4.0)
    return noise_draw * 0.8 * TOKENS ** 0.5


def draw_norm_second(key, part):
    key = jax.random.fold_in(key, 23)
    factor = jnp.exp(jax.random.uniform(key, (4, D), jnp.float32, math.log(0.5), math.log(8.0)))
    return factor * 0.64 * TOKENS


def plant(values, key, least, largest):
    longest = values.shape.index(max(values.shape))
    spots = []
    for shift in (0, 1):
        where = [jax.random.randint(jax.random.fold_in(key, axis), (), 0, length) for axis, length in enumerate(values.shape)]
        where[longest] = (where[longest] + shift) % values.shape[longest]
        spots.append(tuple(where))
    return values.at[spots[0]].set(least).at[spots[1]].set(largest)


def block_scale(rng, extent, shards, smallest, top_value):
    def one(dim, blocks):
        steps = jax.random.uniform(jax.random.fold_in(jax.random.fold_in(rng, 6), dim), (blocks,), jnp.float32, smallest / len(shards), top_value / len(shards))
        return jnp.repeat(jnp.exp(steps), extent[dim] // blocks).reshape((-1,) + (1,) * (len(extent) - dim - 1))

    loudness = one(*shards[0])
    for cut in shards[1:]:
        loudness = loudness * one(*cut)
    return loudness


def scatter_about(key, dims, spread, bound, cuts=(), kind=jnp.bfloat16):
    level = block_scale(key, dims, cuts, -0.22, 0.18) if cuts else 1.0
    result = jax.random.normal(key, dims, jnp.float32) * spread * level
    return jnp.minimum(jnp.maximum(result, -bound), bound).astype(kind)


def setup_inputs(seed: int = 0) -> dict:
    key_of = jax.random.split(jax.random.key(seed), 13)
    tokens = scatter_about(key_of[0], (TOKENS, D), 1.0, 6.0, ((0, 8),), jnp.float32)
    cotangent = scatter_about(key_of[1], (TOKENS, D), 1.0, 6.0, ((0, 8),), jnp.float32)
    timesteps = plant(jax.random.randint(key_of[2], (ITEMS,), 1, TSTEPS + 1), jax.random.fold_in(key_of[2], 1), 1, TSTEPS).astype(jnp.int32)
    bands = plant(jax.random.randint(key_of[3], (ITEMS,), 0, NBANDS), jax.random.fold_in(key_of[3], 1), 0, NBANDS - 1).astype(jnp.int32)
    lengths = draw_lengths(jax.random.fold_in(key_of[12], 71), 0)
    owners = draw_owners(jax.random.fold_in(key_of[12], 71), 0)
    master_slots = draw_master_slots(jax.random.fold_in(key_of[12], 71), 0)
    first_slots = draw_first_slots(jax.random.fold_in(key_of[12], 71), 0)
    second_slots = draw_second_slots(jax.random.fold_in(key_of[12], 71), 0)
    norm_master = draw_norm_master(jax.random.fold_in(key_of[12], 71), 0)
    norm_first = draw_norm_first(jax.random.fold_in(key_of[12], 71), 0)
    norm_second = draw_norm_second(jax.random.fold_in(key_of[12], 71), 0)
    return dict(tokens=tokens, cotangent=cotangent, timesteps=timesteps, bands=bands, lengths=lengths, owners=owners, master_slots=master_slots, first_slots=first_slots, second_slots=second_slots, norm_master=norm_master, norm_first=norm_first, norm_second=norm_second)


highest = lax.Precision.HIGHEST
beta_one = 0.5
beta_two = 0.5
learn_rate = 0.04
norm_rate = 0.4
weight_decay = 0.1
adam_eps = 1e-08
norm_eps = 1e-05

@jax.custom_vjp
def low(v):
    return lax.optimization_barrier(v.astype(jnp.bfloat16)).astype(jnp.float32)

@jax.custom_vjp
def low_back(v):
    return v

def low_keep(v):
    return (low(v), None)

def low_pass(kept, grad):
    return (grad,)

def back_keep(v):
    return (v, None)

def back_low(kept, grad):
    return (low(grad),)
low.defvjp(low_keep, low_pass)
low_back.defvjp(back_keep, back_low)

def layer_norm(values, gain_row, shift_row):
    average = lax.optimization_barrier(jnp.mean(values, axis=-1, keepdims=True))
    centred = values - average
    spread_sq = lax.optimization_barrier(jnp.mean(centred * centred, axis=-1, keepdims=True))
    return centred * lax.rsqrt(spread_sq + norm_eps) * gain_row + shift_row

def slot_rows(owners):
    block_index = jnp.arange(owners.shape[0], dtype=jnp.int32)
    earlier = (owners[None, :] == owners[:, None]) & (block_index[None, :] < block_index[:, None])
    return (owners * CAP + lax.optimization_barrier(jnp.sum(earlier.astype(jnp.int32), axis=1))).astype(jnp.int32)

def split_flat(flat_params):
    width_here = HEADS_DEV * HD
    qkv_end = 3 * D * width_here
    out_end = qkv_end + width_here * D
    up_end = out_end + D * FF_DEV
    return (flat_params[:, :qkv_end].reshape(N_HEAD, D, 3, width_here), flat_params[:, qkv_end:out_end].reshape(N_HEAD, width_here, D), flat_params[:, out_end:up_end].reshape(N_HEAD, D, FF_DEV), flat_params[:, up_end:].reshape(N_HEAD, FF_DEV, D))

def forward(tokens_in, qkv_w, out_w, up_w, down_w, norm_w, key_valid):
    group_items = key_valid.shape[0]
    normed_one = low(layer_norm(tokens_in, norm_w[0], norm_w[1]))
    per_group = low_back(jnp.broadcast_to(normed_one, (N_HEAD,) + normed_one.shape))
    projected = jnp.einsum('htd,hdcf->chtf', per_group, qkv_w, precision=highest)
    projected = low_back(low(projected))
    shaped = projected.reshape(3, N_HEAD, group_items, SEQ, HEADS_DEV, HD)
    queries = shaped[0]
    key_vectors = shaped[1]
    values = shaped[2]
    scores = jnp.einsum('hgqad,hgkad->hgaqk', queries, key_vectors, precision=highest) / math.sqrt(HD)
    scores = low_back(scores)
    scores = jnp.where(key_valid[None, :, None, None, :], scores, -1e+30)
    row_max = lax.optimization_barrier(jnp.max(scores, axis=-1, keepdims=True))
    exp_scores = jnp.exp(scores - row_max)
    probabilities = low(exp_scores / lax.optimization_barrier(jnp.sum(exp_scores, axis=-1, keepdims=True)))
    attended = jnp.einsum('hgaqk,hgkad->hgqad', probabilities, values, precision=highest)
    attended = low_back(low(attended)).reshape(N_HEAD, group_items * SEQ, HEADS_DEV * HD)
    partial_one = low(jnp.einsum('htf,hfd->htd', attended, out_w, precision=highest))
    mixed_state = tokens_in + low_back(lax.optimization_barrier(jnp.sum(partial_one, axis=0)))
    normed_two = low(layer_norm(mixed_state, norm_w[2], norm_w[3]))
    per_group_two = low_back(jnp.broadcast_to(normed_two, (N_HEAD,) + normed_two.shape))
    hidden = low_back(jnp.einsum('htd,hdf->htf', per_group_two, up_w, precision=highest))
    activated = low(jax.nn.gelu(hidden, approximate=True))
    partial_two = low(jnp.einsum('htf,hfd->htd', activated, down_w, precision=highest))
    return mixed_state + low_back(lax.optimization_barrier(jnp.sum(partial_two, axis=0)))

def adamw_update(weight, first_moment, second, gradient, decay_rate, step_rate):
    new_first = beta_one * first_moment + (1.0 - beta_one) * gradient
    new_second = beta_two * second + (1.0 - beta_two) * gradient * gradient
    first_hat = new_first / (1.0 - beta_one ** STEP)
    second_hat = new_second / (1.0 - beta_two ** STEP)
    new_weight = weight - step_rate * (first_hat / (jnp.sqrt(second_hat) + adam_eps) + decay_rate * weight)
    return (new_weight, new_first, new_second)

def reference(tokens, cotangent, timesteps, bands, lengths, owners, master_slots, first_slots, second_slots, norm_master, norm_first, norm_second):
    slot_row = slot_rows(owners)

    def to_flat(slots):
        picked = slots[slot_row].reshape(NBLK, N_HEAD, BLK)
        return jnp.transpose(picked, (1, 0, 2)).reshape(N_HEAD, NBLK * BLK)

    def to_slots(flat_params):
        blocks = jnp.transpose(flat_params.reshape(N_HEAD, NBLK, BLK), (1, 0, 2)).reshape(NBLK, N_HEAD * BLK)
        return jnp.zeros((SLOTS, N_HEAD * BLK), flat_params.dtype).at[slot_row].set(blocks)
    master_flat = to_flat(master_slots)
    rounded_flat = lax.optimization_barrier(master_flat.astype(jnp.bfloat16)).astype(jnp.float32)
    rounded_norm = lax.optimization_barrier(norm_master.astype(jnp.bfloat16)).astype(jnp.float32)
    params = split_flat(rounded_flat) + (rounded_norm,)
    item_weight = jnp.exp(-2.0 * timesteps.astype(jnp.float32) / TSTEPS)
    item_length = lengths.astype(jnp.float32)
    band_table = (bands[:, None] == jnp.arange(NBANDS, dtype=jnp.int32)[None, :]).astype(jnp.float32)
    weight_sums = lax.optimization_barrier(jnp.sum(band_table * (item_weight * item_length)[:, None], axis=0))
    count_sums = lax.optimization_barrier(jnp.sum(band_table * item_length[:, None], axis=0))
    item_scale = item_weight * lax.optimization_barrier(jnp.sum(band_table * count_sums[None, :], axis=1)) / lax.optimization_barrier(jnp.sum(band_table * weight_sums[None, :], axis=1))
    key_valid = jnp.arange(SEQ, dtype=jnp.int32)[None, :] < lengths[:, None]
    token_scale = jnp.where(key_valid, item_scale[:, None], 0.0).reshape(TOKENS)
    group_items = math.gcd(ITEMS, 16)
    group_count = ITEMS // group_items
    scan_inputs = (tokens.reshape(group_count, group_items * SEQ, D), (cotangent * token_scale[:, None]).reshape(group_count, group_items * SEQ, D), key_valid.reshape(group_count, group_items, SEQ))

    def one_group(totals, pieces):
        block_tokens, block_cot, block_valid = pieces

        def run_block(inputs_here, qkv_w, out_w, up_w, down_w, norm_w):
            return forward(inputs_here, qkv_w, out_w, up_w, down_w, norm_w, block_valid)
        outputs, pull_back = jax.vjp(run_block, block_tokens, *params)
        gradients = pull_back(block_cot)
        new_totals = tuple((total_item + grad_item for total_item, grad_item in zip(totals, gradients[1:])))
        return (new_totals, (outputs, gradients[0]))
    zero_totals = tuple((jnp.zeros_like(param_item) for param_item in params))
    totals, (outputs, input_grad) = lax.scan(one_group, zero_totals, scan_inputs)
    grad_flat = jnp.concatenate([totals[piece_index].reshape(N_HEAD, -1) for piece_index in range(4)], axis=1)
    new_flat = adamw_update(master_flat, to_flat(first_slots), to_flat(second_slots), grad_flat, weight_decay, learn_rate)
    new_norm = adamw_update(norm_master, norm_first, norm_second, totals[4], 0.0, norm_rate)
    return (outputs.reshape(TOKENS, D), input_grad.reshape(TOKENS, D), to_slots(new_flat[0]), to_slots(new_flat[1]), to_slots(new_flat[2]), new_norm[0], new_norm[1], new_norm[2])
```

```python
import math

import jax
import jax.numpy as jnp
from jax import lax
from jax.experimental import pallas as pl
from jax.experimental.pallas import tpu as pltpu
from jax.sharding import PartitionSpec as P

D = 512
H = 8
HD = 64
FF = 2048
SEQ = 256
TSTEPS = 1000
NBANDS = 8
CAP = 3
STEP = 5


beta_one = 0.5
beta_two = 0.5
learn_rate = 0.04
norm_rate = 0.4
weight_decay = 0.1
adam_eps = 1e-08
norm_eps = 1e-05


def contract_rows(left_side, right_side):
    return lax.dot_general(
        left_side, right_side, (((0,), (0,)), ((), ())), preferred_element_type=jnp.float32
    )


def contract_cols(left_side, right_side):
    return lax.dot_general(
        left_side, right_side, (((1,), (1,)), ((), ())), preferred_element_type=jnp.float32
    )


def gelu_tanh(values):
    return jax.nn.gelu(values, approximate=True)


def norm_forward(values, gain_row, shift_row):
    average = jnp.mean(values, axis=-1, keepdims=True)
    centred = values - average
    inverse = lax.rsqrt(jnp.mean(centred * centred, axis=-1, keepdims=True) + norm_eps)
    scaled = centred * inverse
    return (scaled * gain_row + shift_row, scaled, inverse)


def norm_backward(grad_normed, scaled, inverse, gain_row):
    grad_scaled = grad_normed * gain_row
    centre_term = jnp.mean(grad_scaled, axis=-1, keepdims=True)
    slope_term = jnp.mean(grad_scaled * scaled, axis=-1, keepdims=True)
    return inverse * (grad_scaled - centre_term - scaled * slope_term)


def slot_rows(owners, capacity):
    block_index = jnp.arange(owners.shape[0], dtype=jnp.int32)
    earlier = (owners[None, :] == owners[:, None]) & (block_index[None, :] < block_index[:, None])
    return owners * capacity + jnp.sum(earlier.astype(jnp.int32), axis=1)


def attention_scores(query_heads, key_heads, key_valid):
    scores = jnp.einsum(
        "gqad,gkad->gaqk", query_heads, key_heads, preferred_element_type=jnp.float32
    ) / math.sqrt(HD)
    return jnp.where(key_valid[:, None, None, :], scores, -1e30)


def adamw_update(weight, first_moment, second, gradient, decay_rate, step_rate):
    new_first = beta_one * first_moment + (1.0 - beta_one) * gradient
    new_second = beta_two * second + (1.0 - beta_two) * gradient * gradient
    first_hat = new_first / (1.0 - beta_one**STEP)
    second_hat = new_second / (1.0 - beta_two**STEP)
    new_weight = weight - step_rate * (
        first_hat / (jnp.sqrt(second_hat) + adam_eps) + decay_rate * weight
    )
    return (new_weight, new_first, new_second)


def shards(
    tokens,
    cotangent,
    timesteps,
    bands,
    lengths,
    owners,
    master_slots,
    first_slots,
    second_slots,
    norm_master,
    norm_first,
    norm_second,
):
    head_count = lax.axis_size("head")
    owner_index = lax.axis_index("dp")
    heads_here = H // head_count
    width_here = heads_here * HD
    units_here = FF // head_count
    block_len = master_slots.shape[1]
    norm_cols = norm_master.shape[1]
    row_count = tokens.shape[0]
    item_count = lengths.shape[0]
    block_count = owners.shape[0]
    slot_row = slot_rows(owners, CAP)
    gathered, norm_whole = (
        lax.all_gather(master_slots.astype(jnp.bfloat16), "dp", axis=0, tiled=True),
        lax.all_gather(norm_master.astype(jnp.bfloat16), "dp", axis=1, tiled=True),
    )
    flat_params = gathered[slot_row].reshape(-1)
    qkv_end = 3 * D * width_here
    out_end = qkv_end + width_here * D
    up_end = out_end + D * units_here
    qkv_weight = flat_params[:qkv_end].reshape(D, 3 * width_here)
    out_weight = flat_params[qkv_end:out_end].reshape(width_here, D)
    up_weight = flat_params[out_end:up_end].reshape(D, units_here)
    down_weight = flat_params[up_end:].reshape(units_here, D)
    norm_params = norm_whole.astype(jnp.float32)
    item_weight = jnp.exp(-2.0 * timesteps.astype(jnp.float32) / TSTEPS)
    item_length = lengths.astype(jnp.float32)
    band_table = (bands[:, None] == jnp.arange(NBANDS, dtype=jnp.int32)[None, :]).astype(
        jnp.float32
    )
    weight_sums, count_sums = lax.psum(
        (
            jnp.sum(band_table * (item_weight * item_length)[:, None], axis=0),
            jnp.sum(band_table * item_length[:, None], axis=0),
        ),
        "dp",
    )
    item_scale = (
        item_weight
        * jnp.sum(band_table * count_sums[None, :], axis=1)
        / jnp.sum(band_table * weight_sums[None, :], axis=1)
    )
    key_valid = jnp.arange(SEQ, dtype=jnp.int32)[None, :] < lengths[:, None]
    token_scale = jnp.where(key_valid, item_scale[:, None], 0.0).reshape(row_count)
    normed_one, scaled_one, inverse_one = norm_forward(tokens, norm_params[0], norm_params[1])
    normed_one_low = normed_one.astype(jnp.bfloat16)
    projected_low = jnp.dot(normed_one_low, qkv_weight, preferred_element_type=jnp.float32).astype(
        jnp.bfloat16
    )
    head_shape = (item_count, SEQ, heads_here, HD)
    query_heads = projected_low[:, :width_here].reshape(head_shape)
    key_heads = projected_low[:, width_here : 2 * width_here].reshape(head_shape)
    value_heads = projected_low[:, 2 * width_here :].reshape(head_shape)
    scores = attention_scores(query_heads, key_heads, key_valid)
    row_max = jnp.max(scores, axis=-1, keepdims=True)
    exp_scores = jnp.exp(scores - row_max)
    row_total = jnp.sum(exp_scores, axis=-1, keepdims=True)
    log_total = row_max + jnp.log(row_total)
    prob_low = (exp_scores / row_total).astype(jnp.bfloat16)
    attended_low = (
        jnp.einsum("gaqk,gkad->gqad", prob_low, value_heads, preferred_element_type=jnp.float32)
        .astype(jnp.bfloat16)
        .reshape(row_count, width_here)
    )
    attn_sum = lax.psum(
        jnp.dot(attended_low, out_weight, preferred_element_type=jnp.float32).astype(jnp.bfloat16),
        "head",
    ).astype(jnp.float32)
    mixed_state = tokens + attn_sum
    normed_two, scaled_two, inverse_two = norm_forward(mixed_state, norm_params[2], norm_params[3])
    normed_two_low = normed_two.astype(jnp.bfloat16)
    hidden = jnp.dot(normed_two_low, up_weight, preferred_element_type=jnp.float32)
    activated, gelu_pull = jax.vjp(gelu_tanh, hidden)
    activated_low = activated.astype(jnp.bfloat16)
    ffn_sum = lax.psum(
        jnp.dot(activated_low, down_weight, preferred_element_type=jnp.float32).astype(
            jnp.bfloat16
        ),
        "head",
    ).astype(jnp.float32)
    block_output = mixed_state + ffn_sum
    grad_state = cotangent * token_scale[:, None]
    grad_low_two = grad_state.astype(jnp.bfloat16)
    grad_down = contract_rows(activated_low, grad_low_two)
    grad_activated = contract_cols(grad_low_two, down_weight)
    grad_hidden_low = gelu_pull(grad_activated)[0].astype(jnp.bfloat16)
    grad_up = contract_rows(normed_two_low, grad_hidden_low)
    grad_normed_two = lax.psum(
        contract_cols(grad_hidden_low, up_weight).astype(jnp.bfloat16), "head"
    ).astype(jnp.float32)
    grad_mixed = grad_state + norm_backward(
        grad_normed_two, scaled_two, inverse_two, norm_params[2]
    )
    grad_low_one = grad_mixed.astype(jnp.bfloat16)
    grad_out_proj = contract_rows(attended_low, grad_low_one)
    grad_attended_low = (
        contract_cols(grad_low_one, out_weight).astype(jnp.bfloat16).reshape(head_shape)
    )
    scores_again = attention_scores(query_heads, key_heads, key_valid)
    probabilities = jnp.exp(scores_again - log_total)
    prob_again_low = probabilities.astype(jnp.bfloat16)
    grad_values = jnp.einsum(
        "gaqk,gqad->gkad", prob_again_low, grad_attended_low, preferred_element_type=jnp.float32
    )
    grad_probs = jnp.einsum(
        "gqad,gkad->gaqk", grad_attended_low, value_heads, preferred_element_type=jnp.float32
    )
    grad_scores_low = (
        probabilities * (grad_probs - jnp.sum(grad_probs * probabilities, axis=-1, keepdims=True))
    ).astype(jnp.bfloat16)
    grad_queries = jnp.einsum(
        "gaqk,gkad->gqad", grad_scores_low, key_heads, preferred_element_type=jnp.float32
    ) / math.sqrt(HD)
    grad_keys = jnp.einsum(
        "gaqk,gqad->gkad", grad_scores_low, query_heads, preferred_element_type=jnp.float32
    ) / math.sqrt(HD)
    grad_projected_low = jnp.concatenate(
        [
            grad_queries.reshape(row_count, width_here),
            grad_keys.reshape(row_count, width_here),
            grad_values.reshape(row_count, width_here),
        ],
        axis=1,
    ).astype(jnp.bfloat16)
    grad_qkv = contract_rows(normed_one_low, grad_projected_low)
    grad_normed_one = lax.psum(
        contract_cols(grad_projected_low, qkv_weight).astype(jnp.bfloat16), "head"
    ).astype(jnp.float32)
    input_grad = grad_mixed + norm_backward(
        grad_normed_one, scaled_one, inverse_one, norm_params[0]
    )
    norm_grads = jnp.stack(
        [
            jnp.sum(grad_normed_one * scaled_one, axis=0),
            jnp.sum(grad_normed_one, axis=0),
            jnp.sum(grad_normed_two * scaled_two, axis=0),
            jnp.sum(grad_normed_two, axis=0),
        ]
    )
    grad_blocks = jnp.concatenate(
        [
            grad_qkv.reshape(-1),
            grad_out_proj.reshape(-1),
            grad_up.reshape(-1),
            grad_down.reshape(-1),
        ]
    ).reshape(block_count, block_len)
    summed, norm_summed = (
        lax.psum(grad_blocks.astype(jnp.bfloat16), "dp").astype(jnp.float32),
        lax.psum(norm_grads.astype(jnp.bfloat16), "dp").astype(jnp.float32),
    )
    landing = jnp.where(owners == owner_index, slot_row - owner_index * CAP, CAP)
    owned_grad = jnp.zeros((CAP, block_len), jnp.float32).at[landing].set(summed, mode="drop")
    norm_owned = lax.dynamic_slice_in_dim(norm_summed, owner_index * norm_cols, norm_cols, 1)
    held_count = jnp.sum((owners == owner_index).astype(jnp.int32))
    used_slot = (jnp.arange(CAP, dtype=jnp.int32) < held_count)[:, None]
    new_master, new_first, new_second = adamw_update(
        master_slots, first_slots, second_slots, owned_grad, weight_decay, learn_rate
    )
    new_master = jnp.where(used_slot, new_master, 0.0)
    new_first = jnp.where(used_slot, new_first, 0.0)
    new_second = jnp.where(used_slot, new_second, 0.0)
    new_norms, new_norm_first, new_norm_second = adamw_update(
        norm_master, norm_first, norm_second, norm_owned, 0.0, norm_rate
    )
    return (
        block_output,
        input_grad,
        new_master,
        new_first,
        new_second,
        new_norms,
        new_norm_first,
        new_norm_second,
    )


W = 128
R = 384
QB = 4
CB = 12
MESH = pl.DeviceIdType.MESH
bf16 = jnp.bfloat16
f32 = jnp.float32


def place(sizes):
    dp = lax.axis_index("dp")
    head = lax.axis_index("head")
    return dp // sizes.y, lax.rem(dp, sizes.y), head // sizes.c, lax.rem(head, sizes.c)


class Sizes:
    z, y, x, c = 4, 2, 2, 2


def device(z, y, x, c):
    return (z * Sizes.y + y, x * Sizes.c + c)


def greet(partners):
    barrier = pltpu.get_barrier_semaphore()
    for partner in partners:
        pl.semaphore_signal(barrier, inc=1, device_id=partner, device_id_type=MESH)
    pl.semaphore_wait(barrier, len(partners))


def block_rows(owners):
    ids = [owners[j] for j in range(owners.shape[0])]
    rows = []
    for j, mine in enumerate(ids):
        row = mine * CAP
        for other in ids[:j]:
            row = row + jnp.where(other == mine, 1, 0)
        rows.append(row)
    return rows


def slot_is_wide(rows, slot_row):
    flag = rows[0] == slot_row
    for row in rows[1:QB]:
        flag = jnp.logical_or(flag, row == slot_row)
    return flag


def gather_kernel(
    master, norms, steps, bands, lens, owners, out, meta_out,
    flat, own, mine, core_s, core_r, z_s, z_r, ya_s, ya_r, xa_s, xa_r, xb_s, xb_r, yb_s, yb_r, m_s, m_r, loc,
):
    z, y, x, c = place(Sizes)
    nz = Sizes.z
    partners = [device(lax.rem(z + k, nz), (y + j) % 2, x, c) for k in range(nz) for j in range(2) if k or j]
    x_peer, y_peer, core_peer = device(z, y, 1 - x, c), device(z, 1 - y, x, c), device(z, y, x, 1 - c)
    greet(partners + [x_peer, core_peer])

    def remote(src, dst, send, recv, peer):
        return pltpu.make_async_remote_copy(
            src_ref=src, dst_ref=dst, send_sem=send, recv_sem=recv, device_id=peer, device_id_type=MESH
        )

    sent = []

    def push(*args):
        copy = remote(*args)
        copy.start()
        sent.append(copy)

    rows = block_rows(owners)
    dp = z * Sizes.y + y
    for r in range(CAP):
        flat[...] = master[:, r, :]
        wide = jnp.concatenate([flat[pl.ds(p, W, stride=3), :] for p in range(3)], axis=0)
        narrow = jnp.concatenate([flat[pl.ds(p, R // 4, stride=4), :] for p in range(4)], axis=0)
        own[r] = jnp.where(slot_is_wide(rows, dp * CAP + r), wide, narrow).astype(bf16)
    shard = x * 2 + c
    far = (1 - x) * 2 + c

    def at(sh, zz, yy):
        return out.at[sh, zz, yy]

    local = pltpu.make_async_copy(own, at(shard, z, y), loc)
    local.start()
    for k in range(1, nz):
        push(own, at(shard, z, y), z_s.at[k], z_r.at[k], device(lax.rem(z + k, nz), y, x, c))

    item_weight = jnp.exp(-2.0 * steps[...].astype(f32) / TSTEPS)
    item_length = lens[...].astype(f32)
    items = steps.shape[1]
    table = (bands[...] == lax.broadcasted_iota(jnp.int32, (NBANDS, items), 0)).astype(f32)
    mine[...] = jnp.zeros_like(mine)
    mine[0:4, 0 : norms.shape[1]] = norms[...]
    mine[:, 64:65] = jnp.sum(table * (item_weight * item_length), axis=1, keepdims=True)
    mine[:, 65:66] = jnp.sum(table * item_length, axis=1, keepdims=True)
    meta_out[dp] = mine[...]
    for k, partner in enumerate(partners):
        push(mine, meta_out.at[dp], m_s.at[k], m_r.at[k], partner)

    ra = RA

    def pa(sh, zz, yy):
        return out.at[sh, zz, yy, :, pl.ds(0, ra), :]

    def pb(sh, zz, yy):
        return out.at[sh, zz, yy, :, pl.ds(ra, R - ra), :]

    def zs(k):
        return lax.rem(z + nz - k, nz)

    def wait_recv(dst, send, recv, peer):
        remote(dst, dst, send, recv, peer).wait_recv()

    def stage0(k):
        zz = zs(k)
        if k:
            wait_recv(at(shard, zz, y), z_s.at[k], z_r.at[k], x_peer)
        whole = at(shard, zz, y) if k else own
        first, second = whole.at[:, pl.ds(0, ra), :], whole.at[:, pl.ds(ra, R - ra), :]
        push(first, pa(shard, zz, y), ya_s.at[k], ya_r.at[k], y_peer)
        push(second, pb(shard, zz, y), xb_s.at[k], xb_r.at[k], x_peer)
        push(first, pa(shard, zz, y), xa_s.at[k, 0], xa_r.at[k, 0], x_peer)
        push(second, pb(shard, zz, y), yb_s.at[k, 0], yb_r.at[k, 0], y_peer)
        push(whole, at(shard, zz, y), core_s.at[k, 0], core_r.at[k, 0], core_peer)

    def stage1(k):
        zz = zs(k)
        wait_recv(pb(far, zz, y), xb_s.at[k], xb_r.at[k], x_peer)
        push(pb(far, zz, y), pb(far, zz, y), yb_s.at[k, 1], yb_r.at[k, 1], y_peer)
        wait_recv(pa(shard, zz, 1 - y), ya_s.at[k], ya_r.at[k], y_peer)
        push(pa(shard, zz, 1 - y), pa(shard, zz, 1 - y), xa_s.at[k, 1], xa_r.at[k, 1], x_peer)

    def stage2(k):
        zz = zs(k)
        wait_recv(pa(far, zz, y), xa_s.at[k, 0], xa_r.at[k, 0], x_peer)
        push(at(far, zz, y), at(far, zz, y), core_s.at[k, 1], core_r.at[k, 1], core_peer)
        wait_recv(pb(shard, zz, 1 - y), yb_s.at[k, 0], yb_r.at[k, 0], y_peer)
        push(at(shard, zz, 1 - y), at(shard, zz, 1 - y), core_s.at[k, 2], core_r.at[k, 2], core_peer)
        wait_recv(pa(far, zz, 1 - y), xa_s.at[k, 1], xa_r.at[k, 1], x_peer)
        wait_recv(pb(far, zz, 1 - y), yb_s.at[k, 1], yb_r.at[k, 1], y_peer)
        push(at(far, zz, 1 - y), at(far, zz, 1 - y), core_s.at[k, 3], core_r.at[k, 3], core_peer)

    for step in range(nz + 2):
        if step < nz:
            stage0(step)
        if 0 <= step - 1 < nz:
            stage1(step - 1)
        if 0 <= step - 2 < nz:
            stage2(step - 2)
    other, other_far = x * 2 + 1 - c, (1 - x) * 2 + 1 - c
    for k in range(nz):
        zz = zs(k)
        for i, (sh, yy) in enumerate(((other, y), (other_far, y), (other, 1 - y), (other_far, 1 - y))):
            wait_recv(at(sh, zz, yy), core_s.at[k, i], core_r.at[k, i], core_peer)
    for k in range(len(partners)):
        wait_recv(meta_out.at[dp], m_s.at[k], m_r.at[k], x_peer)
    for copy in sent:
        copy.wait_send()
    local.wait()


RA = 192


def gather_weights(master, norms, steps, bands, lens, owners):
    nz = Sizes.z
    vm = pl.BlockSpec(memory_space=pltpu.VMEM)
    sm = pl.BlockSpec(memory_space=pltpu.SMEM)
    dma = pltpu.SemaphoreType.DMA
    return pl.pallas_call(
        gather_kernel,
        name="gather_weights",
        out_shape=(
            jax.ShapeDtypeStruct((4, nz, 2, CAP, R, W), bf16),
            jax.ShapeDtypeStruct((nz * 2, 8, W), f32),
        ),
        in_specs=[vm, vm, vm, vm, vm, sm],
        out_specs=(pl.BlockSpec(memory_space=pl.ANY), vm),
        scratch_shapes=[
            pltpu.VMEM((R, W), f32), pltpu.VMEM((CAP, R, W), bf16), pltpu.VMEM((8, W), f32),
            dma((nz, 4)), dma((nz, 4)), dma((nz,)), dma((nz,)), dma((nz,)), dma((nz,)), dma((nz, 2)), dma((nz, 2)),
            dma((nz,)), dma((nz,)), dma((nz, 2)), dma((nz, 2)), dma((8,)), dma((8,)), dma,
        ],
        compiler_params=pltpu.CompilerParams(collective_id=0, has_side_effects=True, vmem_limit_bytes=16 << 20),
    )(master, norms, steps, bands, lens, owners)


def dot(left, right):
    return jnp.dot(left, right, preferred_element_type=f32)


def dot_cols(left, right):
    return lax.dot_general(left, right, (((1,), (1,)), ((), ())), preferred_element_type=f32)


def dot_rows(left, right):
    return lax.dot_general(left, right, (((0,), (0,)), ((), ())), preferred_element_type=f32)


def normalise(values):
    centred = values - jnp.mean(values, axis=-1, keepdims=True)
    inverse = lax.rsqrt(jnp.mean(centred * centred, axis=-1, keepdims=True) + norm_eps)
    return centred * inverse, inverse


def panels(ref, h, first, size):
    return jnp.concatenate([ref[h, p, first : first + size, :] for p in range(ref.shape[1])], axis=1)


def cat_pieces(first, size):
    pieces = []
    row = first
    while row < first + size:
        block, inside = divmod(row, R // 4)
        count = min(R // 4 - inside, first + size - row)
        pieces.append((QB + block, inside, row - first, count))
        row += count
    return pieces


def compute_kernel(
    tok_hbm, cot_hbm, wide_hbm, narrow_hbm, meta, steps, bands, lens, owners,
    grads, out_delta, in_delta, norm_grads,
    wq, wc, tok, cot, low1, xhat1, inv1, qkv, probs, att, acc, x1, low2, xhat2, inv2, e2, da2, dx1, e1, da1, gb,
    w_sem, t_sem, g_sem,
):
    head = lax.axis_index("head")
    tokens_here = tok.shape[0]
    items_here = tokens_here // SEQ
    shards_all = wq.shape[0]
    rows = block_rows(owners)

    def weight_copies(h, blocks):
        copies = []
        for j in blocks:
            if j < QB:
                src, dst = wide_hbm.at[h, rows[j]], wq.at[h, :, pl.ds(j * W, W), :]
            else:
                src, dst = narrow_hbm.at[h, rows[j]], wc.at[h, :, pl.ds((j - QB) * (R // 4), R // 4), :]
            copies.append(pltpu.make_async_copy(src, dst, w_sem.at[h, j]))
        return copies

    def grad_copies(h, blocks):
        return [pltpu.make_async_copy(gb.at[h, j], grads.at[h, rows[j]], g_sem.at[h, j]) for j in blocks]

    first_token = pl.multiple_of(head * tokens_here, tokens_here)
    tok_copy = pltpu.make_async_copy(tok_hbm.at[pl.ds(first_token, tokens_here), :], tok, t_sem.at[0])
    cot_copy = pltpu.make_async_copy(cot_hbm.at[pl.ds(first_token, tokens_here), :], cot, t_sem.at[1])
    tok_copy.start()
    for h in range(shards_all):
        for copy in weight_copies(h, range(QB + 2)):
            copy.start()
    cot_copy.start()
    for h in range(shards_all):
        for copy in weight_copies(h, range(QB + 2, QB + CB)):
            copy.start()

    lane = lax.broadcasted_iota(jnp.int32, (8, W), 1)
    chunks = []
    for pair in range(meta.shape[0] // 2):
        chunks.append(jnp.where(lane < W // 2, meta[2 * pair], pltpu.roll(meta[2 * pair + 1], W // 2, 1)))
    norms = jnp.concatenate(chunks, axis=1).astype(bf16).astype(f32)
    gain1, shift1, gain2, shift2 = (norms[i : i + 1, :] for i in range(4))
    sums = meta[0]
    for d in range(1, meta.shape[0]):
        sums = sums + meta[d]
    items = steps.shape[1]
    table = bands[...] == lax.broadcasted_iota(jnp.int32, (NBANDS, items), 0)
    weight_of = jnp.sum(jnp.where(table, sums[:, 64:65], 0.0), axis=0, keepdims=True)
    count_of = jnp.sum(jnp.where(table, sums[:, 65:66], 0.0), axis=0, keepdims=True)
    scales = jnp.exp(-2.0 * steps[...].astype(f32) / TSTEPS) * count_of / weight_of
    item_lane = lax.broadcasted_iota(jnp.int32, (1, items), 1)
    position = lax.broadcasted_iota(jnp.int32, (SEQ, 1), 0)
    columns = []
    for i in range(items_here):
        here = item_lane == head * items_here + i
        scale = jnp.sum(jnp.where(here, scales, 0.0), axis=1, keepdims=True)
        columns.append(jnp.where(position < lens[head * items_here + i], scale, 0.0))
    token_scale = jnp.concatenate(columns, axis=0)

    tok_copy.wait()
    scaled, inverse = normalise(tok[...])
    xhat1[...] = scaled
    inv1[...] = inverse
    low1[...] = (scaled * gain1 + shift1).astype(bf16)
    acc[...] = jnp.zeros_like(acc)

    head_lane = lax.broadcasted_iota(jnp.int32, (1, W), 1)
    head_masks = [head_lane < HD, head_lane >= HD]
    key_pos = lax.broadcasted_iota(jnp.int32, (1, SEQ), 1)

    def only(values, a):
        return jnp.where(head_masks[a], values, jnp.zeros_like(values))

    def attention(h, _):
        for copy in weight_copies(h, range(QB + 2)):
            copy.wait()
        weight = panels(wq, h, 0, D)
        projected = dot(low1[...], weight)
        qkv[h, 0] = (projected[:, :W].astype(bf16).astype(f32) * (1.0 / math.sqrt(HD))).astype(bf16)
        qkv[h, 1] = projected[:, W : 2 * W].astype(bf16)
        qkv[h, 2] = projected[:, 2 * W :].astype(bf16)
        for i in range(items_here):
            here = slice(i * SEQ, (i + 1) * SEQ)
            query, key, value = qkv[h, 0, here, :], qkv[h, 1, here, :], qkv[h, 2, here, :]
            valid = key_pos < lens[head * items_here + i]
            both = []
            for a in range(2):
                scores = jnp.where(valid, dot_cols(only(query, a), key), -1e30)
                exps = jnp.exp(scores - jnp.max(scores, axis=-1, keepdims=True))
                prob = (exps * (1.0 / jnp.sum(exps, axis=-1, keepdims=True))).astype(bf16)
                probs[h, i, a] = prob
                both.append(prob)
            stacked = jnp.concatenate([only(value, 0), only(value, 1)], axis=0)
            att[h, here, :] = dot(jnp.concatenate(both, axis=1), stacked).astype(bf16)
        acc[...] += dot(att[h], panels(wc, h, 0, W))
        return 0

    lax.fori_loop(0, shards_all, attention, 0)

    cot_copy.wait()
    x1[...] = tok[...] + acc[...]
    scaled, inverse = normalise(x1[...])
    xhat2[...] = scaled
    inv2[...] = inverse
    low2[...] = (scaled * gain2 + shift2).astype(bf16)
    dx2 = cot[...] * token_scale
    cot[...] = dx2
    e2[...] = dx2.astype(bf16)
    da2[...] = jnp.zeros_like(da2)

    def put(h, first, result):
        for block, inside, row, count in cat_pieces(first, result.shape[0]):
            for p in range(4):
                gb[h, block, pl.ds(p * (R // 4) + inside, count), :] = result[
                    row : row + count, p * W : (p + 1) * W
                ].astype(bf16)

    def feed_forward(h, _):
        for copy in weight_copies(h, range(QB + 2, QB + CB)):
            copy.wait()
        up = panels(wc, h, W, D)
        down = panels(wc, h, W + D, D)
        hidden = dot(low2[...], up)
        root = math.sqrt(2.0 / math.pi)
        square = hidden * hidden
        bend = jnp.tanh(root * hidden * (1.0 + 0.044715 * square))
        half = 0.5 * (1.0 + bend)
        active = (hidden * half).astype(bf16)
        slope = half + 0.5 * hidden * (1.0 - bend * bend) * (root + (3.0 * 0.044715 * root) * square)
        acc[...] += dot(active, down)
        back = (dot_cols(e2[...], down) * slope).astype(bf16)
        put(h, W + D, dot_rows(active, e2[...]))
        put(h, W, dot_rows(low2[...], back))
        da2[...] += dot_cols(back, up)
        for copy in grad_copies(h, range(QB + 2, QB + CB)):
            copy.start()
        return 0

    lax.fori_loop(0, shards_all, feed_forward, 0)
    out_delta[...] = acc[...].astype(bf16)

    def norm_backward(grad, scaled, inverse, gain):
        grad_scaled = grad * gain
        centre = jnp.mean(grad_scaled, axis=-1, keepdims=True)
        slope = jnp.mean(grad_scaled * scaled, axis=-1, keepdims=True)
        return inverse * (grad_scaled - centre - scaled * slope)

    grad2 = da2[...]
    norm_grads[...] = jnp.zeros_like(norm_grads)
    norm_grads[2:3, :] = jnp.sum(grad2 * xhat2[...], axis=0, keepdims=True)
    norm_grads[3:4, :] = jnp.sum(grad2, axis=0, keepdims=True)
    change = norm_backward(grad2, xhat2[...], inv2[...], gain2)
    dx1[...] = change
    e1[...] = (cot[...] + change).astype(bf16)
    da1[...] = jnp.zeros_like(da1)

    def attention_back(h, _):
        put(h, 0, dot_rows(att[h], e1[...]))
        d_att = dot_cols(e1[...], panels(wc, h, 0, W)).astype(bf16)
        parts = []
        for i in range(items_here):
            here = slice(i * SEQ, (i + 1) * SEQ)
            query, key, value = qkv[h, 0, here, :], qkv[h, 1, here, :], qkv[h, 2, here, :]
            d_here = d_att[here, :]
            shared = d_here.astype(f32) * att[h, here, :].astype(f32)
            slopes = []
            for a in range(2):
                along = jnp.sum(only(shared, a), axis=-1, keepdims=True)
                slopes.append((probs[h, i, a].astype(f32) * (dot_cols(only(d_here, a), value) - along)).astype(bf16))
            stack = lambda values: jnp.concatenate([only(values, 0), only(values, 1)], axis=0)
            tall = jnp.concatenate(slopes, axis=0)
            d_query = dot(jnp.concatenate(slopes, axis=1), stack(key)) * (1.0 / math.sqrt(HD))
            d_key = dot_rows(tall, stack(query))
            d_value = dot_rows(jnp.concatenate([probs[h, i, 0], probs[h, i, 1]], axis=0), stack(d_here))
            parts.append(jnp.concatenate([d_query, d_key, d_value], axis=1).astype(bf16))
        d_qkv = jnp.concatenate(parts, axis=0)
        d_weight = dot_rows(low1[...], d_qkv).astype(bf16)
        for j in range(QB):
            for p in range(3):
                gb[h, j, p * W : (p + 1) * W, :] = d_weight[j * W : (j + 1) * W, p * W : (p + 1) * W]
        da1[...] += dot_cols(d_qkv, panels(wq, h, 0, D))
        for copy in grad_copies(h, range(QB + 2)):
            copy.start()
        return 0

    lax.fori_loop(0, shards_all, attention_back, 0)
    grad1 = da1[...]
    norm_grads[0:1, :] = jnp.sum(grad1 * xhat1[...], axis=0, keepdims=True)
    norm_grads[1:2, :] = jnp.sum(grad1, axis=0, keepdims=True)
    in_delta[...] = (dx1[...] + norm_backward(grad1, xhat1[...], inv1[...], gain1)).astype(bf16)
    for h in range(shards_all):
        for copy in grad_copies(h, range(QB + CB)):
            copy.wait()


def compute_items(tokens, cotangent, gathered, meta, steps, bands, lens, owners):
    head_count = lax.axis_size("head")
    tokens_here = tokens.shape[0] // head_count
    items_here = tokens_here // SEQ
    slots = gathered.shape[1] * gathered.shape[2] * CAP
    wide = gathered.reshape(4, slots, 3, W, W)
    narrow = gathered.reshape(4, slots, 4, R // 4, W)
    vm = pl.BlockSpec(memory_space=pltpu.VMEM)
    sm = pl.BlockSpec(memory_space=pltpu.SMEM)
    hbm = pl.BlockSpec(memory_space=pl.ANY)
    dma = pltpu.SemaphoreType.DMA
    square = (tokens_here, D)
    return pl.pallas_call(
        compute_kernel,
        name="compute_items",
        out_shape=(
            jax.ShapeDtypeStruct((4, slots, R, W), bf16),
            jax.ShapeDtypeStruct(square, bf16),
            jax.ShapeDtypeStruct(square, bf16),
            jax.ShapeDtypeStruct((8, D), f32),
        ),
        in_specs=[hbm, hbm, hbm, hbm, vm, vm, vm, sm, sm],
        out_specs=(hbm, vm, vm, vm),
        scratch_shapes=[
            pltpu.VMEM((4, 3, D, W), bf16), pltpu.VMEM((4, 4, W + 2 * D, W), bf16),
            pltpu.VMEM(square, f32), pltpu.VMEM(square, f32),
            pltpu.VMEM(square, bf16), pltpu.VMEM(square, f32), pltpu.VMEM((tokens_here, 1), f32),
            pltpu.VMEM((4, 3, tokens_here, W), bf16), pltpu.VMEM((4, items_here, 2, SEQ, SEQ), bf16),
            pltpu.VMEM((4, tokens_here, W), bf16), pltpu.VMEM(square, f32), pltpu.VMEM(square, f32),
            pltpu.VMEM(square, bf16), pltpu.VMEM(square, f32), pltpu.VMEM((tokens_here, 1), f32),
            pltpu.VMEM(square, bf16), pltpu.VMEM(square, f32), pltpu.VMEM(square, f32), pltpu.VMEM(square, bf16),
            pltpu.VMEM(square, f32), pltpu.VMEM((4, QB + CB, R, W), bf16),
            dma((4, QB + CB)), dma((2,)), dma((4, QB + CB)),
        ],
        compiler_params=pltpu.CompilerParams(vmem_limit_bytes=56 << 20),
    )(tokens, cotangent, wide, narrow, meta, steps, bands, lens, owners)


def reduce_kernel(
    grads, out_delta, in_delta, norm_grads, total, out_all, in_all, norm_total,
    held, from_core, rxa, rya, ryb, rxb, rz, n_core, n_x, n_y, n_z, norm_sum,
    l_sem, c_s, c_r, xa_s, xa_r, ya_s, ya_r, yb_s, yb_r, xb_s, xb_r, z_s, z_r, n_s, n_r, o_s, o_r, o_l,
):
    z, y, x, c = place(Sizes)
    nz = Sizes.z
    x_peer, y_peer, core_peer = device(z, y, 1 - x, c), device(z, 1 - y, x, c), device(z, y, x, 1 - c)
    z_peers = [device(lax.rem(z + k, nz), y, x, c) for k in range(1, nz)]
    greet([x_peer, y_peer, core_peer] + z_peers)

    def remote(src, dst, send, recv, peer):
        return pltpu.make_async_remote_copy(
            src_ref=src, dst_ref=dst, send_sem=send, recv_sem=recv, device_id=peer, device_id_type=MESH
        )

    sent = []

    def push(*args):
        copy = remote(*args)
        copy.start()
        sent.append(copy)

    def wait_recv(dst, send, recv):
        remote(dst, dst, send, recv, x_peer).wait_recv()

    def chunk(k):
        return lax.rem(z + 1 + k, nz)

    here, far = x * 2 + c, (1 - x) * 2 + c
    a_rows, b_rows = pl.ds(0, RA), pl.ds(RA, R - RA)
    tokens_here = out_delta.shape[0]
    head = x * 2 + c

    def own_tokens(ref, who):
        return ref.at[pl.ds(pl.multiple_of(who * tokens_here, tokens_here), tokens_here), :]

    for k in range(nz):
        zz = chunk(k)
        for j in range(2):
            mine, theirs = j * 2 + c, j * 2 + 1 - c
            pltpu.make_async_copy(grads.at[mine, zz], held.at[j, zz], l_sem.at[k, j]).start()
            push(grads.at[theirs, zz], from_core.at[j, zz], c_s.at[k, j], c_r.at[k, j], core_peer)

    outs = ((out_delta, out_all), (in_delta, in_all))
    for i, (src, dst) in enumerate(outs):
        pltpu.make_async_copy(src, own_tokens(dst, head), o_l.at[i]).start()
        push(src, own_tokens(dst, head), o_s.at[i, 0], o_r.at[i, 0], x_peer)
        push(src, own_tokens(dst, head), o_s.at[i, 1], o_r.at[i, 1], core_peer)
    push(norm_grads, n_core, n_s.at[0], n_r.at[0], core_peer)

    def add(dst, src, rows, count):
        for r in rows:
            dst(r)[...] = dst(r)[...] + src(r)[...]

    def stage0(k):
        zz = chunk(k)
        for j in range(2):
            pltpu.make_async_copy(grads.at[j * 2 + c, zz], held.at[j, zz], l_sem.at[k, j]).wait()
            wait_recv(from_core.at[j, zz], c_s.at[k, j], c_r.at[k, j])

        def one(i, _):
            j, yy, r = i // (2 * CAP), lax.rem(i // CAP, 2), lax.rem(i, CAP)
            held[j, zz, yy, r] = held[j, zz, yy, r] + from_core[j, zz, yy, r]
            return 0

        lax.fori_loop(0, 2 * 2 * CAP, one, 0)
        push(held.at[1 - x, zz, :, :, a_rows, :], rxa.at[zz], xa_s.at[k], xa_r.at[k], x_peer)
        push(held.at[:, zz, 1 - y, :, b_rows, :], ryb.at[zz], yb_s.at[k], yb_r.at[k], y_peer)

    def stage1(k):
        zz = chunk(k)
        wait_recv(rxa.at[zz], xa_s.at[k], xa_r.at[k])

        def one(i, _):
            yy, r = i // CAP, lax.rem(i, CAP)
            held[x, zz, yy, r, a_rows, :] = held[x, zz, yy, r, a_rows, :] + rxa[zz, yy, r]
            return 0

        lax.fori_loop(0, 2 * CAP, one, 0)
        push(held.at[x, zz, 1 - y, :, a_rows, :], rya.at[zz], ya_s.at[k], ya_r.at[k], y_peer)
        wait_recv(ryb.at[zz], yb_s.at[k], yb_r.at[k])

        def two(i, _):
            j, r = i // CAP, lax.rem(i, CAP)
            held[j, zz, y, r, b_rows, :] = held[j, zz, y, r, b_rows, :] + ryb[zz, j, r]
            return 0

        lax.fori_loop(0, 2 * CAP, two, 0)
        push(held.at[1 - x, zz, y, :, b_rows, :], rxb.at[zz], xb_s.at[k], xb_r.at[k], x_peer)

    def stage2(k):
        zz = chunk(k)
        wait_recv(rya.at[zz], ya_s.at[k], ya_r.at[k])
        wait_recv(rxb.at[zz], xb_s.at[k], xb_r.at[k])

        def one(r, _):
            held[x, zz, y, r, a_rows, :] = held[x, zz, y, r, a_rows, :] + rya[zz, r]
            held[x, zz, y, r, b_rows, :] = held[x, zz, y, r, b_rows, :] + rxb[zz, r]
            return 0

        lax.fori_loop(0, CAP, one, 0)
        if k < nz - 1:
            push(held.at[x, zz, y], rz.at[k], z_s.at[k], z_r.at[k], z_peers[k])

    for step in range(nz + 2):
        if step < nz:
            stage0(step)
        if step == 0:
            wait_recv(n_core, n_s.at[0], n_r.at[0])
            norm_sum[0] = norm_grads[...] + n_core[...]
            push(norm_sum.at[0], n_x, n_s.at[1], n_r.at[1], x_peer)
        if step == 1:
            wait_recv(n_x, n_s.at[1], n_r.at[1])
            norm_sum[1] = norm_sum[0] + n_x[...]
            push(norm_sum.at[1], n_y, n_s.at[2], n_r.at[2], y_peer)
        if step == 2:
            wait_recv(n_y, n_s.at[2], n_r.at[2])
            norm_sum[2] = norm_sum[1] + n_y[...]
            for k, peer in enumerate(z_peers):
                push(norm_sum.at[2], n_z.at[k], n_s.at[3 + k], n_r.at[3 + k], peer)
            for i, (src, dst) in enumerate(outs):
                whose = (1 - x) * 2 + c
                wait_recv(own_tokens(dst, whose), o_s.at[i, 0], o_r.at[i, 0])
                push(own_tokens(dst, whose), own_tokens(dst, whose), o_s.at[i, 2], o_r.at[i, 2], core_peer)
        if 0 <= step - 1 < nz:
            stage1(step - 1)
        if 0 <= step - 2 < nz:
            stage2(step - 2)

    for k in range(nz - 1):
        wait_recv(rz.at[k], z_s.at[k], z_r.at[k])
        wait_recv(n_z.at[k], n_s.at[3 + k], n_r.at[3 + k])
    norm_total[...] = norm_sum[2] + ((n_z[0] + n_z[1]) + n_z[2])

    def last(r, _):
        mine = held[x, z, y, r].astype(f32)
        total[r] = mine + ((rz[0, r].astype(f32) + rz[1, r].astype(f32)) + rz[2, r].astype(f32))
        return 0

    lax.fori_loop(0, CAP, last, 0)
    for i, (src, dst) in enumerate(outs):
        pltpu.make_async_copy(src, own_tokens(dst, head), o_l.at[i]).wait()
        for m, whose in ((1, x * 2 + 1 - c), (2, (1 - x) * 2 + 1 - c)):
            wait_recv(own_tokens(dst, whose), o_s.at[i, m], o_r.at[i, m])
    for copy in sent:
        copy.wait_send()


def reduce_gradients(grads, out_delta, in_delta, norm_grads, tokens_all):
    nz = Sizes.z
    grads = grads.reshape(4, nz, 2, CAP, R, W)
    vm = pl.BlockSpec(memory_space=pltpu.VMEM)
    hbm = pl.BlockSpec(memory_space=pl.ANY)
    dma = pltpu.SemaphoreType.DMA
    rb = R - RA
    vec = pltpu.VMEM((8, D), f32)
    return pl.pallas_call(
        reduce_kernel,
        name="reduce_gradients",
        out_shape=(
            jax.ShapeDtypeStruct((CAP, R, W), f32),
            jax.ShapeDtypeStruct((tokens_all, D), bf16),
            jax.ShapeDtypeStruct((tokens_all, D), bf16),
            jax.ShapeDtypeStruct((8, D), f32),
        ),
        in_specs=[hbm, hbm, hbm, vm],
        out_specs=(vm, hbm, hbm, vm),
        scratch_shapes=[
            pltpu.VMEM((2, nz, 2, CAP, R, W), bf16), pltpu.VMEM((2, nz, 2, CAP, R, W), bf16),
            pltpu.VMEM((nz, 2, CAP, RA, W), bf16), pltpu.VMEM((nz, CAP, RA, W), bf16),
            pltpu.VMEM((nz, 2, CAP, rb, W), bf16), pltpu.VMEM((nz, CAP, rb, W), bf16),
            pltpu.VMEM((nz - 1, CAP, R, W), bf16),
            vec, vec, vec, pltpu.VMEM((nz - 1, 8, D), f32), pltpu.VMEM((3, 8, D), f32),
            dma((nz, 2)), dma((nz, 2)), dma((nz, 2)), dma((nz,)), dma((nz,)), dma((nz,)), dma((nz,)),
            dma((nz,)), dma((nz,)), dma((nz,)), dma((nz,)), dma((nz,)), dma((nz,)), dma((8,)), dma((8,)),
            dma((2, 3)), dma((2, 3)), dma((2,)),
        ],
        compiler_params=pltpu.CompilerParams(collective_id=1, has_side_effects=True, vmem_limit_bytes=48 << 20),
    )(grads, out_delta, in_delta, norm_grads)


def update_kernel(
    total, norm_total, master, first, second, norm_master, norm_first, norm_second, owners,
    new_master, new_first, new_second, new_norm, new_norm_first, new_norm_second, wide, narrow,
):
    dp = lax.axis_index("dp")
    rows = block_rows(owners)
    held = 0
    for j in range(owners.shape[0]):
        held = held + jnp.where(owners[j] == dp, 1, 0)
    for r in range(CAP):
        for p in range(3):
            wide[pl.ds(p, W, stride=3), :] = total[r, p * W : (p + 1) * W, :]
        for p in range(4):
            narrow[pl.ds(p, R // 4, stride=4), :] = total[r, p * (R // 4) : (p + 1) * (R // 4), :]
        grad = jnp.where(slot_is_wide(rows, dp * CAP + r), wide[...], narrow[...])
        results = adamw_update(master[:, r, :], first[:, r, :], second[:, r, :], grad, weight_decay, learn_rate)
        for ref, result in zip((new_master, new_first, new_second), results):
            ref[:, r, :] = jnp.where(r < held, result, 0.0)
    pair = norm_total[:, pl.ds(pl.multiple_of((dp // 2) * W, W), W)]
    mine = jnp.where(lax.rem(dp, 2) == 1, pltpu.roll(pair, W // 2, 1), pair)[0:4, 0 : norm_master.shape[1]]
    results = adamw_update(norm_master[...], norm_first[...], norm_second[...], mine, 0.0, norm_rate)
    for ref, result in zip((new_norm, new_norm_first, new_norm_second), results):
        ref[...] = result


def update_owned(total, norm_total, slots, norms, owners):
    vm = pl.BlockSpec(memory_space=pltpu.VMEM)
    sm = pl.BlockSpec(memory_space=pltpu.SMEM)
    return pl.pallas_call(
        update_kernel,
        name="update_owned",
        out_shape=tuple(jax.ShapeDtypeStruct(a.shape, f32) for a in slots + norms),
        in_specs=[vm] * 8 + [sm],
        out_specs=(vm,) * 6,
        scratch_shapes=[pltpu.VMEM((R, W), f32), pltpu.VMEM((R, W), f32)],
        compiler_params=pltpu.CompilerParams(vmem_limit_bytes=24 << 20),
    )(total, norm_total, *slots, *norms, owners)


def fast_shards(
    tokens, cotangent, timesteps, bands, lengths, owners,
    master_slots, first_slots, second_slots, norm_master, norm_first, norm_second,
):
    def tiles(slots):
        return jnp.transpose(slots.reshape(CAP, R, W), (1, 0, 2))

    def flat(slots):
        return jnp.transpose(slots, (1, 0, 2)).reshape(CAP, R * W)

    steps, bands_row, lens_row = (v.reshape(1, -1) for v in (timesteps, bands, lengths))
    slots = tuple(tiles(s) for s in (master_slots, first_slots, second_slots))
    norms = (norm_master, norm_first, norm_second)
    gathered, meta = gather_weights(slots[0], norm_master, steps, bands_row, lens_row, owners)
    grads, out_delta, in_delta, norm_grads = compute_items(
        tokens, cotangent, gathered, meta, steps, bands_row, lengths, owners
    )
    total, out_all, in_all, norm_total = reduce_gradients(grads, out_delta, in_delta, norm_grads, tokens.shape[0])
    updated = update_owned(total, norm_total, slots, norms, owners)
    table = bands[:, None] == jnp.arange(NBANDS, dtype=jnp.int32)[None, :]
    sums = jnp.sum(meta[:, :, 64:66], axis=0)
    weight_of = jnp.sum(jnp.where(table, sums[None, :, 0], 0.0), axis=1)
    count_of = jnp.sum(jnp.where(table, sums[None, :, 1], 0.0), axis=1)
    scale = jnp.exp(-2.0 * timesteps.astype(f32) / TSTEPS) * count_of / weight_of
    valid = jnp.arange(SEQ, dtype=jnp.int32)[None, :] < lengths[:, None]
    token_scale = jnp.where(valid, scale[:, None], 0.0).reshape(-1, 1)
    return (
        tokens + out_all.astype(f32),
        cotangent * token_scale + in_all.astype(f32),
        *(flat(s) for s in updated[:3]),
        *updated[3:],
    )


def solution(mesh):
    fits = dict(mesh.shape) == {"dp": 8, "head": 4}
    placed = (
        P("dp", None),
        P("dp", None),
        P("dp"),
        P("dp"),
        P("dp"),
        P(),
        P("dp", "head"),
        P("dp", "head"),
        P("dp", "head"),
        P(None, "dp"),
        P(None, "dp"),
        P(None, "dp"),
    )
    return jax.shard_map(
        fast_shards if fits else shards,
        mesh=mesh,
        in_specs=placed,
        out_specs=(
            P("dp", None),
            P("dp", None),
            P("dp", "head"),
            P("dp", "head"),
            P("dp", "head"),
            P(None, "dp"),
            P(None, "dp"),
            P(None, "dp"),
        ),
        check_vma=False,
    )
```

```python
import math

import jax
import jax.numpy as jnp
from jax import lax
from jax.experimental import pallas as pl
from jax.experimental.pallas import tpu as pltpu
from jax.sharding import PartitionSpec as P

D = 512
H = 8
HD = 64
FF = 2048
SEQ = 256
TSTEPS = 1000
NBANDS = 8
CAP = 3
STEP = 5


beta_one = 0.5
beta_two = 0.5
learn_rate = 0.04
norm_rate = 0.4
weight_decay = 0.1
adam_eps = 1e-08
norm_eps = 1e-05


def contract_rows(left_side, right_side):
    return lax.dot_general(
        left_side, right_side, (((0,), (0,)), ((), ())), preferred_element_type=jnp.float32
    )


def contract_cols(left_side, right_side):
    return lax.dot_general(
        left_side, right_side, (((1,), (1,)), ((), ())), preferred_element_type=jnp.float32
    )


def gelu_tanh(values):
    return jax.nn.gelu(values, approximate=True)


def norm_forward(values, gain_row, shift_row):
    average = jnp.mean(values, axis=-1, keepdims=True)
    centred = values - average
    inverse = lax.rsqrt(jnp.mean(centred * centred, axis=-1, keepdims=True) + norm_eps)
    scaled = centred * inverse
    return (scaled * gain_row + shift_row, scaled, inverse)


def norm_backward(grad_normed, scaled, inverse, gain_row):
    grad_scaled = grad_normed * gain_row
    centre_term = jnp.mean(grad_scaled, axis=-1, keepdims=True)
    slope_term = jnp.mean(grad_scaled * scaled, axis=-1, keepdims=True)
    return inverse * (grad_scaled - centre_term - scaled * slope_term)


def slot_rows(owners, capacity):
    block_index = jnp.arange(owners.shape[0], dtype=jnp.int32)
    earlier = (owners[None, :] == owners[:, None]) & (block_index[None, :] < block_index[:, None])
    return owners * capacity + jnp.sum(earlier.astype(jnp.int32), axis=1)


def attention_scores(query_heads, key_heads, key_valid):
    scores = jnp.einsum(
        "gqad,gkad->gaqk", query_heads, key_heads, preferred_element_type=jnp.float32
    ) / math.sqrt(HD)
    return jnp.where(key_valid[:, None, None, :], scores, -1e30)


def adamw_update(weight, first_moment, second, gradient, decay_rate, step_rate):
    new_first = beta_one * first_moment + (1.0 - beta_one) * gradient
    new_second = beta_two * second + (1.0 - beta_two) * gradient * gradient
    first_hat = new_first / (1.0 - beta_one**STEP)
    second_hat = new_second / (1.0 - beta_two**STEP)
    new_weight = weight - step_rate * (
        first_hat / (jnp.sqrt(second_hat) + adam_eps) + decay_rate * weight
    )
    return (new_weight, new_first, new_second)


def shards(
    tokens,
    cotangent,
    timesteps,
    bands,
    lengths,
    owners,
    master_slots,
    first_slots,
    second_slots,
    norm_master,
    norm_first,
    norm_second,
):
    head_count = lax.axis_size("head")
    owner_index = lax.axis_index("dp")
    heads_here = H // head_count
    width_here = heads_here * HD
    units_here = FF // head_count
    block_len = master_slots.shape[1]
    norm_cols = norm_master.shape[1]
    row_count = tokens.shape[0]
    item_count = lengths.shape[0]
    block_count = owners.shape[0]
    slot_row = slot_rows(owners, CAP)
    gathered, norm_whole = (
        lax.all_gather(master_slots.astype(jnp.bfloat16), "dp", axis=0, tiled=True),
        lax.all_gather(norm_master.astype(jnp.bfloat16), "dp", axis=1, tiled=True),
    )
    flat_params = gathered[slot_row].reshape(-1)
    qkv_end = 3 * D * width_here
    out_end = qkv_end + width_here * D
    up_end = out_end + D * units_here
    qkv_weight = flat_params[:qkv_end].reshape(D, 3 * width_here)
    out_weight = flat_params[qkv_end:out_end].reshape(width_here, D)
    up_weight = flat_params[out_end:up_end].reshape(D, units_here)
    down_weight = flat_params[up_end:].reshape(units_here, D)
    norm_params = norm_whole.astype(jnp.float32)
    item_weight = jnp.exp(-2.0 * timesteps.astype(jnp.float32) / TSTEPS)
    item_length = lengths.astype(jnp.float32)
    band_table = (bands[:, None] == jnp.arange(NBANDS, dtype=jnp.int32)[None, :]).astype(
        jnp.float32
    )
    weight_sums, count_sums = lax.psum(
        (
            jnp.sum(band_table * (item_weight * item_length)[:, None], axis=0),
            jnp.sum(band_table * item_length[:, None], axis=0),
        ),
        "dp",
    )
    item_scale = (
        item_weight
        * jnp.sum(band_table * count_sums[None, :], axis=1)
        / jnp.sum(band_table * weight_sums[None, :], axis=1)
    )
    key_valid = jnp.arange(SEQ, dtype=jnp.int32)[None, :] < lengths[:, None]
    token_scale = jnp.where(key_valid, item_scale[:, None], 0.0).reshape(row_count)
    normed_one, scaled_one, inverse_one = norm_forward(tokens, norm_params[0], norm_params[1])
    normed_one_low = normed_one.astype(jnp.bfloat16)
    projected_low = jnp.dot(normed_one_low, qkv_weight, preferred_element_type=jnp.float32).astype(
        jnp.bfloat16
    )
    head_shape = (item_count, SEQ, heads_here, HD)
    query_heads = projected_low[:, :width_here].reshape(head_shape)
    key_heads = projected_low[:, width_here : 2 * width_here].reshape(head_shape)
    value_heads = projected_low[:, 2 * width_here :].reshape(head_shape)
    scores = attention_scores(query_heads, key_heads, key_valid)
    row_max = jnp.max(scores, axis=-1, keepdims=True)
    exp_scores = jnp.exp(scores - row_max)
    row_total = jnp.sum(exp_scores, axis=-1, keepdims=True)
    log_total = row_max + jnp.log(row_total)
    prob_low = (exp_scores / row_total).astype(jnp.bfloat16)
    attended_low = (
        jnp.einsum("gaqk,gkad->gqad", prob_low, value_heads, preferred_element_type=jnp.float32)
        .astype(jnp.bfloat16)
        .reshape(row_count, width_here)
    )
    attn_sum = lax.psum(
        jnp.dot(attended_low, out_weight, preferred_element_type=jnp.float32).astype(jnp.bfloat16),
        "head",
    ).astype(jnp.float32)
    mixed_state = tokens + attn_sum
    normed_two, scaled_two, inverse_two = norm_forward(mixed_state, norm_params[2], norm_params[3])
    normed_two_low = normed_two.astype(jnp.bfloat16)
    hidden = jnp.dot(normed_two_low, up_weight, preferred_element_type=jnp.float32)
    activated, gelu_pull = jax.vjp(gelu_tanh, hidden)
    activated_low = activated.astype(jnp.bfloat16)
    ffn_sum = lax.psum(
        jnp.dot(activated_low, down_weight, preferred_element_type=jnp.float32).astype(
            jnp.bfloat16
        ),
        "head",
    ).astype(jnp.float32)
    block_output = mixed_state + ffn_sum
    grad_state = cotangent * token_scale[:, None]
    grad_low_two = grad_state.astype(jnp.bfloat16)
    grad_down = contract_rows(activated_low, grad_low_two)
    grad_activated = contract_cols(grad_low_two, down_weight)
    grad_hidden_low = gelu_pull(grad_activated)[0].astype(jnp.bfloat16)
    grad_up = contract_rows(normed_two_low, grad_hidden_low)
    grad_normed_two = lax.psum(
        contract_cols(grad_hidden_low, up_weight).astype(jnp.bfloat16), "head"
    ).astype(jnp.float32)
    grad_mixed = grad_state + norm_backward(
        grad_normed_two, scaled_two, inverse_two, norm_params[2]
    )
    grad_low_one = grad_mixed.astype(jnp.bfloat16)
    grad_out_proj = contract_rows(attended_low, grad_low_one)
    grad_attended_low = (
        contract_cols(grad_low_one, out_weight).astype(jnp.bfloat16).reshape(head_shape)
    )
    scores_again = attention_scores(query_heads, key_heads, key_valid)
    probabilities = jnp.exp(scores_again - log_total)
    prob_again_low = probabilities.astype(jnp.bfloat16)
    grad_values = jnp.einsum(
        "gaqk,gqad->gkad", prob_again_low, grad_attended_low, preferred_element_type=jnp.float32
    )
    grad_probs = jnp.einsum(
        "gqad,gkad->gaqk", grad_attended_low, value_heads, preferred_element_type=jnp.float32
    )
    grad_scores_low = (
        probabilities * (grad_probs - jnp.sum(grad_probs * probabilities, axis=-1, keepdims=True))
    ).astype(jnp.bfloat16)
    grad_queries = jnp.einsum(
        "gaqk,gkad->gqad", grad_scores_low, key_heads, preferred_element_type=jnp.float32
    ) / math.sqrt(HD)
    grad_keys = jnp.einsum(
        "gaqk,gqad->gkad", grad_scores_low, query_heads, preferred_element_type=jnp.float32
    ) / math.sqrt(HD)
    grad_projected_low = jnp.concatenate(
        [
            grad_queries.reshape(row_count, width_here),
            grad_keys.reshape(row_count, width_here),
            grad_values.reshape(row_count, width_here),
        ],
        axis=1,
    ).astype(jnp.bfloat16)
    grad_qkv = contract_rows(normed_one_low, grad_projected_low)
    grad_normed_one = lax.psum(
        contract_cols(grad_projected_low, qkv_weight).astype(jnp.bfloat16), "head"
    ).astype(jnp.float32)
    input_grad = grad_mixed + norm_backward(
        grad_normed_one, scaled_one, inverse_one, norm_params[0]
    )
    norm_grads = jnp.stack(
        [
            jnp.sum(grad_normed_one * scaled_one, axis=0),
            jnp.sum(grad_normed_one, axis=0),
            jnp.sum(grad_normed_two * scaled_two, axis=0),
            jnp.sum(grad_normed_two, axis=0),
        ]
    )
    grad_blocks = jnp.concatenate(
        [
            grad_qkv.reshape(-1),
            grad_out_proj.reshape(-1),
            grad_up.reshape(-1),
            grad_down.reshape(-1),
        ]
    ).reshape(block_count, block_len)
    summed, norm_summed = (
        lax.psum(grad_blocks.astype(jnp.bfloat16), "dp").astype(jnp.float32),
        lax.psum(norm_grads.astype(jnp.bfloat16), "dp").astype(jnp.float32),
    )
    landing = jnp.where(owners == owner_index, slot_row - owner_index * CAP, CAP)
    owned_grad = jnp.zeros((CAP, block_len), jnp.float32).at[landing].set(summed, mode="drop")
    norm_owned = lax.dynamic_slice_in_dim(norm_summed, owner_index * norm_cols, norm_cols, 1)
    held_count = jnp.sum((owners == owner_index).astype(jnp.int32))
    used_slot = (jnp.arange(CAP, dtype=jnp.int32) < held_count)[:, None]
    new_master, new_first, new_second = adamw_update(
        master_slots, first_slots, second_slots, owned_grad, weight_decay, learn_rate
    )
    new_master = jnp.where(used_slot, new_master, 0.0)
    new_first = jnp.where(used_slot, new_first, 0.0)
    new_second = jnp.where(used_slot, new_second, 0.0)
    new_norms, new_norm_first, new_norm_second = adamw_update(
        norm_master, norm_first, norm_second, norm_owned, 0.0, norm_rate
    )
    return (
        block_output,
        input_grad,
        new_master,
        new_first,
        new_second,
        new_norms,
        new_norm_first,
        new_norm_second,
    )


W = 128
R = 384
QB = 4
CB = 12
MESH = pl.DeviceIdType.MESH
bf16 = jnp.bfloat16
f32 = jnp.float32


def place(sizes):
    dp = lax.axis_index("dp")
    head = lax.axis_index("head")
    return dp // sizes.y, lax.rem(dp, sizes.y), head // sizes.c, lax.rem(head, sizes.c)


class Sizes:
    z, y, x, c = 4, 2, 2, 2


def device(z, y, x, c):
    return (z * Sizes.y + y, x * Sizes.c + c)


def greet(partners):
    barrier = pltpu.get_barrier_semaphore()
    for partner in partners:
        pl.semaphore_signal(barrier, inc=1, device_id=partner, device_id_type=MESH)
    pl.semaphore_wait(barrier, len(partners))


def block_rows(owners):
    ids = [owners[j] for j in range(owners.shape[0])]
    rows = []
    for j, mine in enumerate(ids):
        row = mine * CAP
        for other in ids[:j]:
            row = row + jnp.where(other == mine, 1, 0)
        rows.append(row)
    return rows


def slot_is_wide(rows, slot_row):
    flag = rows[0] == slot_row
    for row in rows[1:QB]:
        flag = jnp.logical_or(flag, row == slot_row)
    return flag


def dot(left, right):
    return jnp.dot(left, right, preferred_element_type=f32)


def dot_cols(left, right):
    return lax.dot_general(left, right, (((1,), (1,)), ((), ())), preferred_element_type=f32)


def dot_rows(left, right):
    return lax.dot_general(left, right, (((0,), (0,)), ((), ())), preferred_element_type=f32)


def normalise(values):
    centred = values - jnp.mean(values, axis=-1, keepdims=True)
    inverse = lax.rsqrt(jnp.mean(centred * centred, axis=-1, keepdims=True) + norm_eps)
    return centred * inverse, inverse


def panels(ref, h, first, size):
    return jnp.concatenate([ref[h, p, first : first + size, :] for p in range(ref.shape[1])], axis=1)


def cat_pieces(first, size):
    pieces = []
    row = first
    while row < first + size:
        block, inside = divmod(row, R // 4)
        count = min(R // 4 - inside, first + size - row)
        pieces.append((QB + block, inside, row - first, count))
        row += count
    return pieces


RA = 192
GA = 192


def layer_kernel(
    tok_hbm, cot_hbm, master_hbm, norms_hbm, steps_hbm, bands_hbm, lens_row_hbm, lens_hbm, owners_hbm,
    total, out_all, in_all, norm_total,
    wv, master, flat, own, mine, meta, norms_v, steps, bands, lens_row, lens, owners, block_at,
    tok, cot, low1, xhat1, inv1, qkv, probs, att, acc, low2, xhat2, inv2, e2, da2, dx1, e1, da1, out_low, in_low,
    theirs, held, from_core, rxa, sa, rya, sb, ryb, sbx, rxb, fz, rz, norm_part, norm_sum, n_core, n_x, n_y, n_z,
    i_sem, z_s, z_r, ya_s, ya_r, xa_s, xa_r, xb_s, xb_r, yb_s, yb_r, core_s, core_r, m_s, m_r,
    cs, cr, as_, ar, say_s, say_r, sby_s, sby_r, sbx_s, sbx_r, fz_s, fz_r, n_s, n_r, o_s, o_r, o_l,
):
    z, y, x, c = place(Sizes)
    nz = Sizes.z
    dp, head = z * 2 + y, x * 2 + c
    dp_peers = [device(lax.rem(z + k, nz), (y + j) % 2, x, c) for k in range(nz) for j in range(2) if k or j]
    z_peers = [device(lax.rem(z + k, nz), y, x, c) for k in range(1, nz)]
    x_peer, y_peer, core_peer = device(z, y, 1 - x, c), device(z, 1 - y, x, c), device(z, y, x, 1 - c)
    peers = dp_peers + [x_peer, core_peer]
    barrier = pltpu.get_barrier_semaphore()
    for peer in peers:
        pl.semaphore_signal(barrier, inc=1, device_id=peer, device_id_type=MESH)

    tokens_here = tok.shape[0]
    items_here = tokens_here // SEQ
    first_token = pl.multiple_of(head * tokens_here, tokens_here)
    fetches = [
        pltpu.make_async_copy(src, dst, i_sem.at[n])
        for n, (src, dst) in enumerate((
            (owners_hbm, owners), (master_hbm, master), (steps_hbm, steps), (bands_hbm, bands),
            (lens_row_hbm, lens_row), (norms_hbm, norms_v), (lens_hbm, lens),
            (tok_hbm.at[pl.ds(first_token, tokens_here), :], tok),
            (cot_hbm.at[pl.ds(first_token, tokens_here), :], cot),
        ))
    ]
    for fetch in fetches:
        fetch.start()

    def remote(src, dst, send, recv, peer):
        return pltpu.make_async_remote_copy(
            src_ref=src, dst_ref=dst, send_sem=send, recv_sem=recv, device_id=peer, device_id_type=MESH
        )

    sent = []

    def push(*args):
        copy = remote(*args)
        copy.start()
        sent.append(copy)

    def wait_recv(dst, send, recv):
        remote(dst, dst, send, recv, x_peer).wait_recv()

    fetches[0].wait()
    rows = block_rows(owners)
    fetches[1].wait()
    for r in range(CAP):
        flat[...] = master[:, r, :]
        wide = jnp.concatenate([flat[pl.ds(p, W, stride=3), :] for p in range(3)], axis=0)
        narrow = jnp.concatenate([flat[pl.ds(p, R // 4, stride=4), :] for p in range(4)], axis=0)
        own[r] = jnp.where(slot_is_wide(rows, dp * CAP + r), wide, narrow).astype(bf16)

    for n in (2, 3, 4, 5):
        fetches[n].wait()
    items = steps.shape[1]
    item_weight = jnp.exp(-2.0 * steps[...].astype(f32) / TSTEPS)
    item_length = lens_row[...].astype(f32)
    table = bands[...] == lax.broadcasted_iota(jnp.int32, (NBANDS, items), 0)
    ones = table.astype(f32)
    mine[...] = jnp.zeros_like(mine)
    mine[0:4, 0 : W // 2] = norms_v[...]
    mine[:, W // 2 : W // 2 + 1] = jnp.sum(ones * (item_weight * item_length), axis=1, keepdims=True)
    mine[:, W // 2 + 1 : W // 2 + 2] = jnp.sum(ones * item_length, axis=1, keepdims=True)
    meta[dp] = mine[...]

    pl.semaphore_wait(barrier, len(peers))

    shard, far = x * 2 + c, (1 - x) * 2 + c
    part_a, part_b = pl.ds(0, GA), pl.ds(GA, R - GA)

    def slab(sh, zz, yy, part=slice(None)):
        return wv.at[sh, pl.ds((zz * 2 + yy) * CAP, CAP), part, :]

    def order(k):
        return (z, z + 1 - 2 * lax.rem(z, 2), 2 - z // 2, 3 - 3 * (z // 2))[k]

    up, down, inner = z < nz - 1, z > 0, lax.rem(z, nz - 1) != 0
    own_up = remote(own, slab(shard, z, y), z_s.at[0], z_r.at[z], device(z + 1, y, x, c))
    own_down = remote(own, slab(shard, z, y), z_s.at[1], z_r.at[z], device(z - 1, y, x, c))
    pl.when(up)(own_up.start)
    pl.when(down)(own_down.start)
    for k, peer in enumerate(dp_peers):
        push(mine, meta.at[dp], m_s.at[k], m_r.at[k], peer)
    on_ward = []

    def gather0(k):
        zz = order(k)
        if k:
            wait_recv(slab(shard, zz, y), z_s.at[0], z_r.at[zz])
            goal = 3 - z if k == 1 else 3 * (z - 1)
            copy = remote(slab(shard, zz, y), slab(shard, zz, y), z_s.at[1 + k], z_r.at[zz], device(goal, y, x, c))
            pl.when(inner)(copy.start)
            on_ward.append(copy)
        whole = slab(shard, zz, y) if k else own
        first, second = whole.at[:, part_a, :], whole.at[:, part_b, :]
        push(first, slab(shard, zz, y, part_a), ya_s.at[k], ya_r.at[k], y_peer)
        push(second, slab(shard, zz, y, part_b), xb_s.at[k], xb_r.at[k], x_peer)
        push(second, slab(shard, zz, y, part_b), yb_s.at[k, 0], yb_r.at[k, 0], y_peer)
        push(first, slab(shard, zz, y, part_a), xa_s.at[k, 0], xa_r.at[k, 0], x_peer)
        push(whole, slab(shard, zz, y), core_s.at[k, 0], core_r.at[k, 0], core_peer)

    def gather1(k):
        zz = order(k)
        there = slab(shard, zz, 1 - y, part_a)
        wait_recv(there, ya_s.at[k], ya_r.at[k])
        push(there, there, xa_s.at[k, 1], xa_r.at[k, 1], x_peer)
        there = slab(far, zz, y, part_b)
        wait_recv(there, xb_s.at[k], xb_r.at[k])
        push(there, there, yb_s.at[k, 1], yb_r.at[k, 1], y_peer)
        wait_recv(slab(shard, zz, 1 - y, part_b), yb_s.at[k, 0], yb_r.at[k, 0])
        push(slab(shard, zz, 1 - y), slab(shard, zz, 1 - y), core_s.at[k, 1], core_r.at[k, 1], core_peer)

    def gather2(k):
        zz = order(k)
        wait_recv(slab(far, zz, y, part_a), xa_s.at[k, 0], xa_r.at[k, 0])
        push(slab(far, zz, y), slab(far, zz, y), core_s.at[k, 2], core_r.at[k, 2], core_peer)
        wait_recv(slab(far, zz, 1 - y, part_a), xa_s.at[k, 1], xa_r.at[k, 1])
        wait_recv(slab(far, zz, 1 - y, part_b), yb_s.at[k, 1], yb_r.at[k, 1])
        push(slab(far, zz, 1 - y), slab(far, zz, 1 - y), core_s.at[k, 3], core_r.at[k, 3], core_peer)

    own_copy = pltpu.make_async_copy(own, slab(shard, z, y), i_sem.at[9])
    own_copy.start()
    gather0(0)

    for row in range(nz * 2 * CAP):
        block = 0
        for j, block_row in enumerate(rows):
            block = block + jnp.where(block_row == row, j, 0)
        block_at[row] = block
    for k in range(len(dp_peers)):
        wait_recv(meta.at[dp], m_s.at[k], m_r.at[k])
    lane = lax.broadcasted_iota(jnp.int32, (8, W), 1)
    chunks = []
    for pair in range(meta.shape[0] // 2):
        chunks.append(jnp.where(lane < W // 2, meta[2 * pair], pltpu.roll(meta[2 * pair + 1], W // 2, 1)))
    norms = jnp.concatenate(chunks, axis=1).astype(bf16).astype(f32)
    gain1, shift1, gain2, shift2 = (norms[i : i + 1, :] for i in range(4))
    sums = meta[0]
    for d in range(1, meta.shape[0]):
        sums = sums + meta[d]
    weight_of = jnp.sum(jnp.where(table, sums[:, W // 2 : W // 2 + 1], 0.0), axis=0, keepdims=True)
    count_of = jnp.sum(jnp.where(table, sums[:, W // 2 + 1 : W // 2 + 2], 0.0), axis=0, keepdims=True)
    scales = item_weight * count_of / weight_of
    item_lane = lax.broadcasted_iota(jnp.int32, (1, items), 1)
    position = lax.broadcasted_iota(jnp.int32, (SEQ, 1), 0)
    fetches[6].wait()
    columns = []
    for i in range(items_here):
        here = item_lane == head * items_here + i
        scale = jnp.sum(jnp.where(here, scales, 0.0), axis=1, keepdims=True)
        columns.append(jnp.where(position < lens[head * items_here + i], scale, 0.0))
    fetches[7].wait()
    scaled, inverse = normalise(tok[...])
    xhat1[...] = scaled
    inv1[...] = inverse
    low1[...] = (scaled * gain1 + shift1).astype(bf16)
    acc[...] = jnp.zeros_like(acc)
    fetches[8].wait()
    for i, column in enumerate(columns):
        cot[i * SEQ : (i + 1) * SEQ, :] = cot[i * SEQ : (i + 1) * SEQ, :] * column
    e2[...] = cot[...].astype(bf16)
    own_copy.wait()

    for step in range(1, nz + 2):
        if step < nz:
            gather0(step)
        if step - 1 < nz:
            gather1(step - 1)
        if step >= 2:
            gather2(step - 2)

    def core_arrived(kinds):
        for k in range(nz):
            zz = order(k)
            for kind in kinds:
                sh = (x if kind < 2 else 1 - x) * 2 + 1 - c
                wait_recv(slab(sh, zz, y if kind in (0, 2) else 1 - y), core_s.at[k, kind], core_r.at[k, kind])

    head_lane = lax.broadcasted_iota(jnp.int32, (1, W), 1)
    head_masks = [head_lane < HD, head_lane >= HD]
    key_pos = lax.broadcasted_iota(jnp.int32, (1, SEQ), 1)

    def only(values, a):
        return jnp.where(head_masks[a], values, jnp.zeros_like(values))

    def stack(values):
        return jnp.concatenate([only(values, 0), only(values, 1)], axis=0)

    def wide_matrix(h):
        return jnp.concatenate(
            [
                jnp.concatenate([wv[h, rows[j], p * W : (p + 1) * W, :] for j in range(QB)], axis=0)
                for p in range(3)
            ],
            axis=1,
        )

    def narrow_matrix(h, first, size):
        pieces = cat_pieces(first, size)
        return jnp.concatenate(
            [
                jnp.concatenate(
                    [wv[h, rows[b], pl.ds(p * (R // 4) + inside, count), :] for b, inside, _, count in pieces], axis=0
                )
                for p in range(4)
            ],
            axis=1,
        )

    def attention(i, _):
        h = lax.rem(x + i // 2, 2) * 2 + lax.rem(c + i, 2)
        projected = dot(low1[...], wide_matrix(h))
        qkv[h, 0] = (projected[:, :W].astype(bf16).astype(f32) * (1.0 / math.sqrt(HD))).astype(bf16)
        qkv[h, 1] = projected[:, W : 2 * W].astype(bf16)
        qkv[h, 2] = projected[:, 2 * W :].astype(bf16)
        for i in range(items_here):
            here = slice(i * SEQ, (i + 1) * SEQ)
            query, key, value = qkv[h, 0, here, :], qkv[h, 1, here, :], qkv[h, 2, here, :]
            valid = key_pos < lens[head * items_here + i]
            both = []
            for a in range(2):
                scores = jnp.where(valid, dot_cols(only(query, a), key), -1e30)
                exps = jnp.exp(scores - jnp.max(scores, axis=-1, keepdims=True))
                prob = (exps * (1.0 / jnp.sum(exps, axis=-1, keepdims=True))).astype(bf16)
                probs[h, i, a] = prob
                both.append(prob)
            att[h, here, :] = dot(jnp.concatenate(both, axis=1), stack(value)).astype(bf16)
        acc[...] += dot(att[h], narrow_matrix(h, 0, W))
        return 0

    core_arrived((0, 1, 2, 3))
    lax.fori_loop(0, 4, attention, 0)
    acc[...] += tok[...]
    scaled, inverse = normalise(acc[...])
    xhat2[...] = scaled
    inv2[...] = inverse
    low2[...] = (scaled * gain2 + shift2).astype(bf16)
    da2[...] = jnp.zeros_like(da2)

    def shard_of(i):
        return lax.rem(1 - x + i, 2) * 2 + (1 - c if i < 2 else c)

    def put(dst, extra, first, result):
        for block, inside, row, count in cat_pieces(first, result.shape[0]):
            for p in range(4):
                here = pl.ds(p * (R // 4) + inside, count)
                part = result[row : row + count, p * W : (p + 1) * W]
                if extra is not None and (block >= QB + 2 or first < W):
                    part = part + extra[block, here, :].astype(f32)
                dst[block, here, :] = part.astype(bf16)

    def feed_forward(h, dst, extra):
        up_matrix = narrow_matrix(h, W, D)
        down_matrix = narrow_matrix(h, W + D, D)
        hidden = dot(low2[...], up_matrix)
        root = math.sqrt(2.0 / math.pi)
        square = hidden * hidden
        bend = jnp.tanh(root * hidden * (1.0 + 0.044715 * square))
        half = 0.5 * (1.0 + bend)
        active = (hidden * half).astype(bf16)
        slope = half + 0.5 * hidden * (1.0 - bend * bend) * (root + (3.0 * 0.044715 * root) * square)
        acc[...] += dot(active, down_matrix)
        back = (dot_cols(e2[...], down_matrix) * slope).astype(bf16)
        put(dst, extra, W + D, dot_rows(active, e2[...]))
        put(dst, extra, W, dot_rows(low2[...], back))
        da2[...] += dot_cols(back, up_matrix)

    wide_blocks, deep_blocks = pl.ds(0, QB + 2), pl.ds(QB + 2, CB - 2)
    x_part, y_part = pl.ds(0, RA), pl.ds(RA, R - RA)

    def core_push(i, part, n):
        return remote(theirs.at[i, part], from_core.at[i, part], cs.at[n, i], cr.at[n, i], core_peer)

    def ff_theirs(i, _):
        feed_forward(lax.rem(1 - x + i, 2) * 2 + 1 - c, theirs.at[i], None)
        core_push(i, deep_blocks, 0).start()
        return 0

    def x_push(part, n):
        return remote(held.at[0, part, x_part, :], rxa.at[part], as_.at[n], ar.at[n], x_peer)

    def ff_mine(i, _):
        core_push(i, deep_blocks, 0).wait_recv()
        feed_forward(lax.rem(1 - x + i, 2) * 2 + c, held.at[i], from_core.at[i])
        pl.when(i == 0)(x_push(deep_blocks, 0).start)
        return 0

    lax.fori_loop(0, 2, ff_theirs, 0)
    lax.fori_loop(0, 2, ff_mine, 0)

    def own_tokens(ref, who):
        return ref.at[pl.ds(pl.multiple_of(who * tokens_here, tokens_here), tokens_here), :]

    outs = ((out_low, out_all), (in_low, in_all))

    def spread(i):
        src, dst = outs[i]
        pltpu.make_async_copy(src, own_tokens(dst, head), o_l.at[i]).start()
        push(src, own_tokens(dst, head), o_s.at[i, 0], o_r.at[i, 0], x_peer)
        push(src, own_tokens(dst, head), o_s.at[i, 1], o_r.at[i, 1], core_peer)

    out_low[...] = acc[...].astype(bf16)
    spread(0)

    def norm_backward(grad, scaled, inverse, gain):
        grad_scaled = grad * gain
        centre = jnp.mean(grad_scaled, axis=-1, keepdims=True)
        slope = jnp.mean(grad_scaled * scaled, axis=-1, keepdims=True)
        return inverse * (grad_scaled - centre - scaled * slope)

    grad2 = da2[...]
    norm_part[...] = jnp.zeros_like(norm_part)
    norm_part[2:3, :] = jnp.sum(grad2 * xhat2[...], axis=0, keepdims=True)
    norm_part[3:4, :] = jnp.sum(grad2, axis=0, keepdims=True)
    change = cot[...] + norm_backward(grad2, xhat2[...], inv2[...], gain2)
    dx1[...] = change
    e1[...] = change.astype(bf16)
    da1[...] = jnp.zeros_like(da1)

    def attention_back(h, dst, extra):
        put(dst, extra, 0, dot_rows(att[h], e1[...]))
        if extra is not None:
            for p in range(4):
                here = pl.ds(p * (R // 4) + W - R // 4, R // 2 - W)
                dst[QB + 1, here, :] = dst[QB + 1, here, :] + extra[QB + 1, here, :]
        d_att = dot_cols(e1[...], narrow_matrix(h, 0, W)).astype(bf16)
        parts = []
        for i in range(items_here):
            here = slice(i * SEQ, (i + 1) * SEQ)
            query, key, value = qkv[h, 0, here, :], qkv[h, 1, here, :], qkv[h, 2, here, :]
            d_here = d_att[here, :]
            shared = d_here.astype(f32) * att[h, here, :].astype(f32)
            slopes = []
            for a in range(2):
                along = jnp.sum(only(shared, a), axis=-1, keepdims=True)
                slopes.append((probs[h, i, a].astype(f32) * (dot_cols(only(d_here, a), value) - along)).astype(bf16))
            tall = jnp.concatenate(slopes, axis=0)
            d_query = dot(jnp.concatenate(slopes, axis=1), stack(key)) * (1.0 / math.sqrt(HD))
            d_key = dot_rows(tall, stack(query))
            d_value = dot_rows(jnp.concatenate([probs[h, i, 0], probs[h, i, 1]], axis=0), stack(d_here))
            parts.append(jnp.concatenate([d_query, d_key, d_value], axis=1).astype(bf16))
        d_qkv = jnp.concatenate(parts, axis=0)
        d_weight = dot_rows(low1[...], d_qkv)
        for j in range(QB):
            for p in range(3):
                part = d_weight[j * W : (j + 1) * W, p * W : (p + 1) * W]
                if extra is not None:
                    part = part + extra[j, p * W : (p + 1) * W, :].astype(f32)
                dst[j, p * W : (p + 1) * W, :] = part.astype(bf16)
        da1[...] += dot_cols(d_qkv, wide_matrix(h))

    def att_theirs(i, _):
        attention_back(lax.rem(1 - x + i, 2) * 2 + 1 - c, theirs.at[i], None)
        core_push(i, wide_blocks, 1).start()
        return 0

    def att_mine(i, _):
        core_push(i, wide_blocks, 1).wait_recv()
        attention_back(lax.rem(1 - x + i, 2) * 2 + c, held.at[i], from_core.at[i])
        pl.when(i == 0)(x_push(wide_blocks, 1).start)
        return 0

    lax.fori_loop(0, 2, att_theirs, 0)
    lax.fori_loop(0, 2, att_mine, 0)

    def chunk(k):
        return lax.rem(z + 1 + k, nz)

    def block_of(zz, yy, r):
        return block_at[(zz * 2 + yy) * CAP + r]

    for k in range(nz):
        zz = chunk(k)
        for j in range(2):
            for r in range(CAP):
                sb[k, j, r] = held[j, block_of(zz, 1 - y, r), y_part, :]
        push(sb.at[k], ryb.at[k], sby_s.at[k], sby_r.at[k], y_peer)

    grad1 = da1[...]
    norm_part[0:1, :] = jnp.sum(grad1 * xhat1[...], axis=0, keepdims=True)
    norm_part[1:2, :] = jnp.sum(grad1, axis=0, keepdims=True)
    push(norm_part, n_core, n_s.at[0], n_r.at[0], core_peer)
    in_low[...] = (dx1[...] + norm_backward(grad1, xhat1[...], inv1[...], gain1)).astype(bf16)

    x_push(deep_blocks, 0).wait_recv()

    def add_deep(j, _):
        held[1, j, x_part, :] = held[1, j, x_part, :] + rxa[j]
        return 0

    lax.fori_loop(QB + 2, QB + CB, add_deep, 0)
    x_push(wide_blocks, 1).wait_recv()
    lax.fori_loop(0, QB + 2, add_deep, 0)
    for k in range(nz):
        zz = chunk(k)
        for r in range(CAP):
            sa[k, r] = held[1, block_of(zz, 1 - y, r), x_part, :]
        push(sa.at[k], rya.at[k], say_s.at[k], say_r.at[k], y_peer)

    def reduce1(k):
        zz = chunk(k)
        wait_recv(ryb.at[k], sby_s.at[k], sby_r.at[k])
        for r in range(CAP):
            sbx[k, r] = held[0, block_of(zz, y, r), y_part, :] + ryb[k, 0, r]
        push(sbx.at[k], rxb.at[k], sbx_s.at[k], sbx_r.at[k], x_peer)

    def reduce2(k):
        zz = chunk(k)
        wait_recv(rya.at[k], say_s.at[k], say_r.at[k])
        for r in range(CAP):
            fz[k, r, x_part, :] = held[1, block_of(zz, y, r), x_part, :] + rya[k, r]
        wait_recv(rxb.at[k], sbx_s.at[k], sbx_r.at[k])
        for r in range(CAP):
            part = held[1, block_of(zz, y, r), y_part, :].astype(f32) + ryb[k, 1, r].astype(f32)
            fz[k, r, y_part, :] = (part + rxb[k, r].astype(f32)).astype(bf16)
        if k < nz - 1:
            push(fz.at[k], rz.at[k], fz_s.at[k], fz_r.at[k], z_peers[k])

    for k in range(nz):
        reduce1(k)
        if k == 0:
            spread(1)
            wait_recv(n_core, n_s.at[0], n_r.at[0])
            norm_sum[0] = norm_part[...] + n_core[...]
            push(norm_sum.at[0], n_x, n_s.at[1], n_r.at[1], x_peer)
        if k == 1:
            wait_recv(n_x, n_s.at[1], n_r.at[1])
            norm_sum[1] = norm_sum[0] + n_x[...]
            push(norm_sum.at[1], n_y, n_s.at[2], n_r.at[2], y_peer)
        if k == 2:
            wait_recv(n_y, n_s.at[2], n_r.at[2])
            norm_sum[2] = norm_sum[1] + n_y[...]
            for m, peer in enumerate(z_peers):
                push(norm_sum.at[2], n_z.at[m], n_s.at[3 + m], n_r.at[3 + m], peer)
        if k >= 1:
            reduce2(k - 1)

    def pass_on(i):
        src, dst = outs[i]
        there = own_tokens(dst, (1 - x) * 2 + c)
        wait_recv(there, o_s.at[i, 0], o_r.at[i, 0])
        push(there, there, o_s.at[i, 2], o_r.at[i, 2], core_peer)

    pass_on(0)
    reduce2(nz - 1)
    pass_on(1)

    for k in range(nz - 1):
        wait_recv(rz.at[k], fz_s.at[k], fz_r.at[k])
        wait_recv(n_z.at[k], n_s.at[3 + k], n_r.at[3 + k])
    norm_total[...] = norm_sum[2] + ((n_z[0] + n_z[1]) + n_z[2])
    for r in range(CAP):
        others = (rz[0, r].astype(f32) + rz[1, r].astype(f32)) + rz[2, r].astype(f32)
        total[r] = fz[nz - 1, r].astype(f32) + others
    for i, (src, dst) in enumerate(outs):
        pltpu.make_async_copy(src, own_tokens(dst, head), o_l.at[i]).wait()
        for m, whose in ((1, x * 2 + 1 - c), (2, (1 - x) * 2 + 1 - c)):
            wait_recv(own_tokens(dst, whose), o_s.at[i, m], o_r.at[i, m])
    for copy in sent:
        copy.wait_send()
    for copy in on_ward:
        pl.when(inner)(copy.wait_send)
    pl.when(up)(own_up.wait_send)
    pl.when(down)(own_down.wait_send)
    for i in range(2):
        core_push(i, deep_blocks, 0).wait_send()
        core_push(i, wide_blocks, 1).wait_send()
    x_push(deep_blocks, 0).wait_send()
    x_push(wide_blocks, 1).wait_send()


def layer(tokens, cotangent, master, norms, steps, bands, lens_row, lens, owners):
    nz = Sizes.z
    here = tokens.shape[0] // lax.axis_size("head")
    items_here = here // SEQ
    items = lens.shape[0]
    vm = pl.BlockSpec(memory_space=pltpu.VMEM)
    hbm = pl.BlockSpec(memory_space=pltpu.HBM)
    dma = pltpu.SemaphoreType.DMA
    V, S = pltpu.VMEM, pltpu.SMEM
    square = (here, D)
    blocks = QB + CB
    rb = R - RA
    low, full = V(square, bf16), V(square, f32)
    scratch = [
        V((4, nz * 2 * CAP, R, W), bf16), V((R, CAP, W), f32), V((R, W), f32), V((CAP, R, W), bf16),
        V((8, W), f32), V((nz * 2, 8, W), f32), V(norms.shape, f32),
        V((1, items), jnp.int32), V((1, items), jnp.int32), V((1, items), jnp.int32),
        S((items,), jnp.int32), S(owners.shape, jnp.int32), S((nz * 2 * CAP,), jnp.int32),
        full, full, low, full, V((here, 1), f32), V((4, 3, here, W), bf16),
        V((4, items_here, 2, SEQ, SEQ), bf16), V((4, here, W), bf16), full, low, full, V((here, 1), f32),
        low, full, full, low, full, low, low,
        V((2, blocks, R, W), bf16), V((2, blocks, R, W), bf16), V((2, blocks, R, W), bf16),
        V((blocks, RA, W), bf16), V((nz, CAP, RA, W), bf16), V((nz, CAP, RA, W), bf16),
        V((nz, 2, CAP, rb, W), bf16), V((nz, 2, CAP, rb, W), bf16), V((nz, CAP, rb, W), bf16),
        V((nz, CAP, rb, W), bf16), V((nz, CAP, R, W), bf16), V((nz - 1, CAP, R, W), bf16),
        V((8, D), f32), V((3, 8, D), f32), V((8, D), f32), V((8, D), f32), V((8, D), f32), V((nz - 1, 8, D), f32),
        dma((10,)), dma((5,)), dma((nz,)), dma((nz,)), dma((nz,)), dma((nz, 2)), dma((nz, 2)), dma((nz,)), dma((nz,)),
        dma((nz, 2)), dma((nz, 2)), dma((nz, 4)), dma((nz, 4)), dma((8,)), dma((8,)),
        dma((2, 2)), dma((2, 2)), dma((2,)), dma((2,)), dma((nz,)), dma((nz,)), dma((nz,)), dma((nz,)),
        dma((nz,)), dma((nz,)), dma((nz,)), dma((nz,)), dma((8,)), dma((8,)), dma((2, 3)), dma((2, 3)), dma((2,)),
    ]
    return pl.pallas_call(
        layer_kernel,
        name="layer",
        out_shape=(
            jax.ShapeDtypeStruct((CAP, R, W), f32),
            jax.ShapeDtypeStruct(tokens.shape, bf16),
            jax.ShapeDtypeStruct(tokens.shape, bf16),
            jax.ShapeDtypeStruct((8, D), f32),
        ),
        in_specs=[hbm] * 9,
        out_specs=(vm, hbm, hbm, vm),
        scratch_shapes=scratch,
        compiler_params=pltpu.CompilerParams(collective_id=0, has_side_effects=True, vmem_limit_bytes=60 << 20),
    )(tokens, cotangent, master, norms, steps, bands, lens_row, lens, owners)


def update_kernel(
    total, norm_total, master, first, second, norm_master, norm_first, norm_second, owners,
    new_master, new_first, new_second, new_norm, new_norm_first, new_norm_second, wide, narrow,
):
    dp = lax.axis_index("dp")
    rows = block_rows(owners)
    held = 0
    for j in range(owners.shape[0]):
        held = held + jnp.where(owners[j] == dp, 1, 0)
    for r in range(CAP):
        for p in range(3):
            wide[pl.ds(p, W, stride=3), :] = total[r, p * W : (p + 1) * W, :]
        for p in range(4):
            narrow[pl.ds(p, R // 4, stride=4), :] = total[r, p * (R // 4) : (p + 1) * (R // 4), :]
        grad = jnp.where(slot_is_wide(rows, dp * CAP + r), wide[...], narrow[...])
        results = adamw_update(master[:, r, :], first[:, r, :], second[:, r, :], grad, weight_decay, learn_rate)
        for ref, result in zip((new_master, new_first, new_second), results):
            ref[:, r, :] = jnp.where(r < held, result, 0.0)
    pair = norm_total[:, pl.ds(pl.multiple_of((dp // 2) * W, W), W)]
    mine = jnp.where(lax.rem(dp, 2) == 1, pltpu.roll(pair, W // 2, 1), pair)[0:4, 0 : norm_master.shape[1]]
    results = adamw_update(norm_master[...], norm_first[...], norm_second[...], mine, 0.0, norm_rate)
    for ref, result in zip((new_norm, new_norm_first, new_norm_second), results):
        ref[...] = result


def update_owned(total, norm_total, slots, norms, owners):
    vm = pl.BlockSpec(memory_space=pltpu.VMEM)
    sm = pl.BlockSpec(memory_space=pltpu.SMEM)
    return pl.pallas_call(
        update_kernel,
        name="update_owned",
        out_shape=tuple(jax.ShapeDtypeStruct(a.shape, f32) for a in slots + norms),
        in_specs=[vm] * 8 + [sm],
        out_specs=(vm,) * 6,
        scratch_shapes=[pltpu.VMEM((R, W), f32), pltpu.VMEM((R, W), f32)],
        compiler_params=pltpu.CompilerParams(vmem_limit_bytes=24 << 20),
    )(total, norm_total, *slots, *norms, owners)


def fast_shards(
    tokens, cotangent, timesteps, bands, lengths, owners,
    master_slots, first_slots, second_slots, norm_master, norm_first, norm_second,
):
    def tiles(slots):
        return jnp.transpose(slots.reshape(CAP, R, W), (1, 0, 2))

    def flat(slots):
        return jnp.transpose(slots, (1, 0, 2)).reshape(CAP, R * W)

    steps, bands_row, lens_row = (v.reshape(1, -1) for v in (timesteps, bands, lengths))
    slots = tuple(tiles(s) for s in (master_slots, first_slots, second_slots))
    norms = (norm_master, norm_first, norm_second)
    total, out_all, in_all, norm_total = layer(
        tokens, cotangent, slots[0], norm_master, steps, bands_row, lens_row, lengths, owners
    )
    updated = update_owned(total, norm_total, slots, norms, owners)
    return (out_all.astype(f32), in_all.astype(f32), *(flat(s) for s in updated[:3]), *updated[3:])


def solution(mesh):
    fits = dict(mesh.shape) == {"dp": 8, "head": 4}
    placed = (
        P("dp", None),
        P("dp", None),
        P("dp"),
        P("dp"),
        P("dp"),
        P(),
        P("dp", "head"),
        P("dp", "head"),
        P("dp", "head"),
        P(None, "dp"),
        P(None, "dp"),
        P(None, "dp"),
    )
    return jax.shard_map(
        fast_shards if fits else shards,
        mesh=mesh,
        in_specs=placed,
        out_specs=(
            P("dp", None),
            P("dp", None),
            P("dp", "head"),
            P("dp", "head"),
            P("dp", "head"),
            P(None, "dp"),
            P(None, "dp"),
            P(None, "dp"),
        ),
        check_vma=False,
    )
```

```python
import math

import jax
import jax.numpy as jnp
from jax import lax
from jax.experimental import pallas as pl
from jax.experimental.pallas import tpu as pltpu
from jax.sharding import PartitionSpec as P

D = 512
H = 8
HD = 64
FF = 2048
SEQ = 256
TSTEPS = 1000
NBANDS = 8
CAP = 3
STEP = 5


beta_one = 0.5
beta_two = 0.5
learn_rate = 0.04
norm_rate = 0.4
weight_decay = 0.1
adam_eps = 1e-08
norm_eps = 1e-05


def contract_rows(left_side, right_side):
    return lax.dot_general(
        left_side, right_side, (((0,), (0,)), ((), ())), preferred_element_type=jnp.float32
    )


def contract_cols(left_side, right_side):
    return lax.dot_general(
        left_side, right_side, (((1,), (1,)), ((), ())), preferred_element_type=jnp.float32
    )


def gelu_tanh(values):
    return jax.nn.gelu(values, approximate=True)


def norm_forward(values, gain_row, shift_row):
    average = jnp.mean(values, axis=-1, keepdims=True)
    centred = values - average
    inverse = lax.rsqrt(jnp.mean(centred * centred, axis=-1, keepdims=True) + norm_eps)
    scaled = centred * inverse
    return (scaled * gain_row + shift_row, scaled, inverse)


def norm_backward(grad_normed, scaled, inverse, gain_row):
    grad_scaled = grad_normed * gain_row
    centre_term = jnp.mean(grad_scaled, axis=-1, keepdims=True)
    slope_term = jnp.mean(grad_scaled * scaled, axis=-1, keepdims=True)
    return inverse * (grad_scaled - centre_term - scaled * slope_term)


def slot_rows(owners, capacity):
    block_index = jnp.arange(owners.shape[0], dtype=jnp.int32)
    earlier = (owners[None, :] == owners[:, None]) & (block_index[None, :] < block_index[:, None])
    return owners * capacity + jnp.sum(earlier.astype(jnp.int32), axis=1)


def attention_scores(query_heads, key_heads, key_valid):
    scores = jnp.einsum(
        "gqad,gkad->gaqk", query_heads, key_heads, preferred_element_type=jnp.float32
    ) / math.sqrt(HD)
    return jnp.where(key_valid[:, None, None, :], scores, -1e30)


def adamw_update(weight, first_moment, second, gradient, decay_rate, step_rate):
    new_first = beta_one * first_moment + (1.0 - beta_one) * gradient
    new_second = beta_two * second + (1.0 - beta_two) * gradient * gradient
    first_hat = new_first / (1.0 - beta_one**STEP)
    second_hat = new_second / (1.0 - beta_two**STEP)
    new_weight = weight - step_rate * (
        first_hat / (jnp.sqrt(second_hat) + adam_eps) + decay_rate * weight
    )
    return (new_weight, new_first, new_second)


def shards(
    tokens,
    cotangent,
    timesteps,
    bands,
    lengths,
    owners,
    master_slots,
    first_slots,
    second_slots,
    norm_master,
    norm_first,
    norm_second,
):
    head_count = lax.axis_size("head")
    owner_index = lax.axis_index("dp")
    heads_here = H // head_count
    width_here = heads_here * HD
    units_here = FF // head_count
    block_len = master_slots.shape[1]
    norm_cols = norm_master.shape[1]
    row_count = tokens.shape[0]
    item_count = lengths.shape[0]
    block_count = owners.shape[0]
    slot_row = slot_rows(owners, CAP)
    gathered, norm_whole = (
        lax.all_gather(master_slots.astype(jnp.bfloat16), "dp", axis=0, tiled=True),
        lax.all_gather(norm_master.astype(jnp.bfloat16), "dp", axis=1, tiled=True),
    )
    flat_params = gathered[slot_row].reshape(-1)
    qkv_end = 3 * D * width_here
    out_end = qkv_end + width_here * D
    up_end = out_end + D * units_here
    qkv_weight = flat_params[:qkv_end].reshape(D, 3 * width_here)
    out_weight = flat_params[qkv_end:out_end].reshape(width_here, D)
    up_weight = flat_params[out_end:up_end].reshape(D, units_here)
    down_weight = flat_params[up_end:].reshape(units_here, D)
    norm_params = norm_whole.astype(jnp.float32)
    item_weight = jnp.exp(-2.0 * timesteps.astype(jnp.float32) / TSTEPS)
    item_length = lengths.astype(jnp.float32)
    band_table = (bands[:, None] == jnp.arange(NBANDS, dtype=jnp.int32)[None, :]).astype(
        jnp.float32
    )
    weight_sums, count_sums = lax.psum(
        (
            jnp.sum(band_table * (item_weight * item_length)[:, None], axis=0),
            jnp.sum(band_table * item_length[:, None], axis=0),
        ),
        "dp",
    )
    item_scale = (
        item_weight
        * jnp.sum(band_table * count_sums[None, :], axis=1)
        / jnp.sum(band_table * weight_sums[None, :], axis=1)
    )
    key_valid = jnp.arange(SEQ, dtype=jnp.int32)[None, :] < lengths[:, None]
    token_scale = jnp.where(key_valid, item_scale[:, None], 0.0).reshape(row_count)
    normed_one, scaled_one, inverse_one = norm_forward(tokens, norm_params[0], norm_params[1])
    normed_one_low = normed_one.astype(jnp.bfloat16)
    projected_low = jnp.dot(normed_one_low, qkv_weight, preferred_element_type=jnp.float32).astype(
        jnp.bfloat16
    )
    head_shape = (item_count, SEQ, heads_here, HD)
    query_heads = projected_low[:, :width_here].reshape(head_shape)
    key_heads = projected_low[:, width_here : 2 * width_here].reshape(head_shape)
    value_heads = projected_low[:, 2 * width_here :].reshape(head_shape)
    scores = attention_scores(query_heads, key_heads, key_valid)
    row_max = jnp.max(scores, axis=-1, keepdims=True)
    exp_scores = jnp.exp(scores - row_max)
    row_total = jnp.sum(exp_scores, axis=-1, keepdims=True)
    log_total = row_max + jnp.log(row_total)
    prob_low = (exp_scores / row_total).astype(jnp.bfloat16)
    attended_low = (
        jnp.einsum("gaqk,gkad->gqad", prob_low, value_heads, preferred_element_type=jnp.float32)
        .astype(jnp.bfloat16)
        .reshape(row_count, width_here)
    )
    attn_sum = lax.psum(
        jnp.dot(attended_low, out_weight, preferred_element_type=jnp.float32).astype(jnp.bfloat16),
        "head",
    ).astype(jnp.float32)
    mixed_state = tokens + attn_sum
    normed_two, scaled_two, inverse_two = norm_forward(mixed_state, norm_params[2], norm_params[3])
    normed_two_low = normed_two.astype(jnp.bfloat16)
    hidden = jnp.dot(normed_two_low, up_weight, preferred_element_type=jnp.float32)
    activated, gelu_pull = jax.vjp(gelu_tanh, hidden)
    activated_low = activated.astype(jnp.bfloat16)
    ffn_sum = lax.psum(
        jnp.dot(activated_low, down_weight, preferred_element_type=jnp.float32).astype(
            jnp.bfloat16
        ),
        "head",
    ).astype(jnp.float32)
    block_output = mixed_state + ffn_sum
    grad_state = cotangent * token_scale[:, None]
    grad_low_two = grad_state.astype(jnp.bfloat16)
    grad_down = contract_rows(activated_low, grad_low_two)
    grad_activated = contract_cols(grad_low_two, down_weight)
    grad_hidden_low = gelu_pull(grad_activated)[0].astype(jnp.bfloat16)
    grad_up = contract_rows(normed_two_low, grad_hidden_low)
    grad_normed_two = lax.psum(
        contract_cols(grad_hidden_low, up_weight).astype(jnp.bfloat16), "head"
    ).astype(jnp.float32)
    grad_mixed = grad_state + norm_backward(
        grad_normed_two, scaled_two, inverse_two, norm_params[2]
    )
    grad_low_one = grad_mixed.astype(jnp.bfloat16)
    grad_out_proj = contract_rows(attended_low, grad_low_one)
    grad_attended_low = (
        contract_cols(grad_low_one, out_weight).astype(jnp.bfloat16).reshape(head_shape)
    )
    scores_again = attention_scores(query_heads, key_heads, key_valid)
    probabilities = jnp.exp(scores_again - log_total)
    prob_again_low = probabilities.astype(jnp.bfloat16)
    grad_values = jnp.einsum(
        "gaqk,gqad->gkad", prob_again_low, grad_attended_low, preferred_element_type=jnp.float32
    )
    grad_probs = jnp.einsum(
        "gqad,gkad->gaqk", grad_attended_low, value_heads, preferred_element_type=jnp.float32
    )
    grad_scores_low = (
        probabilities * (grad_probs - jnp.sum(grad_probs * probabilities, axis=-1, keepdims=True))
    ).astype(jnp.bfloat16)
    grad_queries = jnp.einsum(
        "gaqk,gkad->gqad", grad_scores_low, key_heads, preferred_element_type=jnp.float32
    ) / math.sqrt(HD)
    grad_keys = jnp.einsum(
        "gaqk,gqad->gkad", grad_scores_low, query_heads, preferred_element_type=jnp.float32
    ) / math.sqrt(HD)
    grad_projected_low = jnp.concatenate(
        [
            grad_queries.reshape(row_count, width_here),
            grad_keys.reshape(row_count, width_here),
            grad_values.reshape(row_count, width_here),
        ],
        axis=1,
    ).astype(jnp.bfloat16)
    grad_qkv = contract_rows(normed_one_low, grad_projected_low)
    grad_normed_one = lax.psum(
        contract_cols(grad_projected_low, qkv_weight).astype(jnp.bfloat16), "head"
    ).astype(jnp.float32)
    input_grad = grad_mixed + norm_backward(
        grad_normed_one, scaled_one, inverse_one, norm_params[0]
    )
    norm_grads = jnp.stack(
        [
            jnp.sum(grad_normed_one * scaled_one, axis=0),
            jnp.sum(grad_normed_one, axis=0),
            jnp.sum(grad_normed_two * scaled_two, axis=0),
            jnp.sum(grad_normed_two, axis=0),
        ]
    )
    grad_blocks = jnp.concatenate(
        [
            grad_qkv.reshape(-1),
            grad_out_proj.reshape(-1),
            grad_up.reshape(-1),
            grad_down.reshape(-1),
        ]
    ).reshape(block_count, block_len)
    summed, norm_summed = (
        lax.psum(grad_blocks.astype(jnp.bfloat16), "dp").astype(jnp.float32),
        lax.psum(norm_grads.astype(jnp.bfloat16), "dp").astype(jnp.float32),
    )
    landing = jnp.where(owners == owner_index, slot_row - owner_index * CAP, CAP)
    owned_grad = jnp.zeros((CAP, block_len), jnp.float32).at[landing].set(summed, mode="drop")
    norm_owned = lax.dynamic_slice_in_dim(norm_summed, owner_index * norm_cols, norm_cols, 1)
    held_count = jnp.sum((owners == owner_index).astype(jnp.int32))
    used_slot = (jnp.arange(CAP, dtype=jnp.int32) < held_count)[:, None]
    new_master, new_first, new_second = adamw_update(
        master_slots, first_slots, second_slots, owned_grad, weight_decay, learn_rate
    )
    new_master = jnp.where(used_slot, new_master, 0.0)
    new_first = jnp.where(used_slot, new_first, 0.0)
    new_second = jnp.where(used_slot, new_second, 0.0)
    new_norms, new_norm_first, new_norm_second = adamw_update(
        norm_master, norm_first, norm_second, norm_owned, 0.0, norm_rate
    )
    return (
        block_output,
        input_grad,
        new_master,
        new_first,
        new_second,
        new_norms,
        new_norm_first,
        new_norm_second,
    )


W = 128
R = 384
QB = 4
CB = 12
MESH = pl.DeviceIdType.MESH
bf16 = jnp.bfloat16
f32 = jnp.float32


def place(sizes):
    dp = lax.axis_index("dp")
    head = lax.axis_index("head")
    return dp // sizes.y, lax.rem(dp, sizes.y), head // sizes.c, lax.rem(head, sizes.c)


class Sizes:
    z, y, x, c = 4, 2, 2, 2


def device(z, y, x, c):
    return (z * Sizes.y + y, x * Sizes.c + c)


def greet(partners):
    barrier = pltpu.get_barrier_semaphore()
    for partner in partners:
        pl.semaphore_signal(barrier, inc=1, device_id=partner, device_id_type=MESH)
    pl.semaphore_wait(barrier, len(partners))


def block_rows(owners):
    ids = [owners[j] for j in range(owners.shape[0])]
    rows = []
    for j, mine in enumerate(ids):
        row = mine * CAP
        for other in ids[:j]:
            row = row + jnp.where(other == mine, 1, 0)
        rows.append(row)
    return rows


def slot_is_wide(rows, slot_row):
    flag = rows[0] == slot_row
    for row in rows[1:QB]:
        flag = jnp.logical_or(flag, row == slot_row)
    return flag


def dot(left, right):
    return jnp.dot(left, right, preferred_element_type=f32)


def dot_cols(left, right):
    return lax.dot_general(left, right, (((1,), (1,)), ((), ())), preferred_element_type=f32)


def dot_rows(left, right):
    return lax.dot_general(left, right, (((0,), (0,)), ((), ())), preferred_element_type=f32)


def normalise(values):
    centred = values - jnp.mean(values, axis=-1, keepdims=True)
    inverse = lax.rsqrt(jnp.mean(centred * centred, axis=-1, keepdims=True) + norm_eps)
    return centred * inverse, inverse


def panels(ref, h, first, size):
    return jnp.concatenate([ref[h, p, first : first + size, :] for p in range(ref.shape[1])], axis=1)


def cat_pieces(first, size):
    pieces = []
    row = first
    while row < first + size:
        block, inside = divmod(row, R // 4)
        count = min(R // 4 - inside, first + size - row)
        pieces.append((QB + block, inside, row - first, count))
        row += count
    return pieces


RA = 192
GA = 192
TILE = 128


def layer_kernel(
    tok_hbm, cot_hbm, master_hbm, norms_hbm, steps_hbm, bands_hbm, lens_row_hbm, lens_hbm, owners_hbm,
    total, out_all, in_all, norm_total,
    wv, master, flat, mine, meta, norms_v, steps, bands, lens_row, lens, owners, block_at,
    tok, cot, low1, xhat1, inv1, qkv, probs, sums, att, acc, low2, xhat2, inv2, e2, actives, slopes, da, e1,
    out_low, in_low,
    grads, from_core, rxa, sa, rya, sb, ryb, sbx, rxb, fz, rz, norm_part, norm_sum, n_core, n_x, n_y, n_z,
    i_sem, z_s, z_r, ya_s, ya_r, xa_s, xa_r, xb_s, xb_r, yb_s, yb_r, core_s, core_r, m_s, m_r,
    cs, cr, as_, ar, say_s, say_r, sby_s, sby_r, sbx_s, sbx_r, fz_s, fz_r, n_s, n_r, o_s, o_r, o_l,
):
    z, y, x, c = place(Sizes)
    nz = Sizes.z
    dp, head = z * 2 + y, x * 2 + c
    dp_peers = [device(lax.rem(z + k, nz), (y + j) % 2, x, c) for k in range(nz) for j in range(2) if k or j]
    x_peer, y_peer, core_peer = device(z, y, 1 - x, c), device(z, 1 - y, x, c), device(z, y, x, 1 - c)
    peers = dp_peers + [x_peer, core_peer]
    barrier = pltpu.get_barrier_semaphore()
    for peer in peers:
        pl.semaphore_signal(barrier, inc=1, device_id=peer, device_id_type=MESH)

    tokens_here = tok.shape[0]
    items_here = tokens_here // SEQ
    tiles = tokens_here // TILE
    first_token = pl.multiple_of(head * tokens_here, tokens_here)
    fetches = [
        pltpu.make_async_copy(src, dst, i_sem.at[n])
        for n, (src, dst) in enumerate((
            (owners_hbm, owners), (master_hbm, master), (steps_hbm, steps), (bands_hbm, bands),
            (lens_row_hbm, lens_row), (norms_hbm, norms_v), (lens_hbm, lens),
            (tok_hbm.at[pl.ds(first_token, tokens_here), :], tok),
            (cot_hbm.at[pl.ds(first_token, tokens_here), :], cot),
        ))
    ]
    for fetch in fetches:
        fetch.start()

    def loop(first, last, body):
        def step(i, _):
            body(i)
            return 0

        lax.fori_loop(first, last, step, 0)

    def remote(src, dst, send, recv, peer):
        return pltpu.make_async_remote_copy(
            src_ref=src, dst_ref=dst, send_sem=send, recv_sem=recv, device_id=peer, device_id_type=MESH
        )

    def same(ref, send, recv, peer):
        return remote(ref, ref, send, recv, peer)

    shard, far = x * 2 + c, (1 - x) * 2 + c
    fetches[0].wait()
    rows = block_rows(owners)
    fetches[1].wait()
    for r in range(CAP):
        flat[...] = master[:, r, :]
        wide = jnp.concatenate([flat[pl.ds(p, W, stride=3), :] for p in range(3)], axis=0)
        narrow = jnp.concatenate([flat[pl.ds(p, R // 4, stride=4), :] for p in range(4)], axis=0)
        wv[shard, dp * CAP + r] = jnp.where(slot_is_wide(rows, dp * CAP + r), wide, narrow).astype(bf16)

    for n in (2, 3, 4, 5):
        fetches[n].wait()
    items = steps.shape[1]
    item_weight = jnp.exp(-2.0 * steps[...].astype(f32) / TSTEPS)
    item_length = lens_row[...].astype(f32)
    table = bands[...] == lax.broadcasted_iota(jnp.int32, (NBANDS, items), 0)
    ones = table.astype(f32)
    mine[...] = jnp.zeros_like(mine)
    mine[0:4, 0 : W // 2] = norms_v[...]
    mine[:, W // 2 : W // 2 + 1] = jnp.sum(ones * (item_weight * item_length), axis=1, keepdims=True)
    mine[:, W // 2 + 1 : W // 2 + 2] = jnp.sum(ones * item_length, axis=1, keepdims=True)
    meta[dp] = mine[...]

    pl.semaphore_wait(barrier, len(peers))

    part_a, part_b = pl.ds(0, GA), pl.ds(GA, R - GA)

    def slab(sh, zz, yy, part=slice(None)):
        return wv.at[sh, pl.ds((zz * 2 + yy) * CAP, CAP), part, :]

    def order(k):
        late, low = k // 2, z // 2
        return (1 - late) * (z + k * (1 - 2 * lax.rem(z, 2))) + late * (k + low * (3 - 2 * k))

    up, down, inner = z < nz - 1, z > 0, lax.rem(z, nz - 1) != 0
    own_up = same(slab(shard, z, y), z_s.at[0], z_r.at[z], device(z + 1, y, x, c))
    own_down = same(slab(shard, z, y), z_s.at[nz], z_r.at[z], device(z - 1, y, x, c))
    pl.when(up)(own_up.start)
    pl.when(down)(own_down.start)

    def meta_copy(k):
        return remote(mine, meta.at[dp], m_s.at[k], m_r.at[k], dp_peers[k])

    for k in range(len(dp_peers)):
        meta_copy(k).start()

    def along_z(k):
        zz = order(k)
        late = k // 2
        goal = (1 - late) * (3 - z) + late * 3 * (z - 1)
        return same(slab(shard, zz, y), z_s.at[k], z_r.at[zz], device(goal, y, x, c))

    def first_copies(k):
        zz = order(k)
        one, two = slab(shard, zz, y, part_a), slab(shard, zz, y, part_b)
        return (
            same(one, ya_s.at[k], ya_r.at[k], y_peer),
            same(two, xb_s.at[k], xb_r.at[k], x_peer),
            same(two, yb_s.at[k, 0], yb_r.at[k, 0], y_peer),
            same(one, xa_s.at[k, 0], xa_r.at[k, 0], x_peer),
            same(slab(shard, zz, y), core_s.at[k, 0], core_r.at[k, 0], core_peer),
        )

    def second_copies(k):
        zz = order(k)
        return (
            same(slab(shard, zz, 1 - y, part_a), xa_s.at[k, 1], xa_r.at[k, 1], x_peer),
            same(slab(far, zz, y, part_b), yb_s.at[k, 1], yb_r.at[k, 1], y_peer),
            same(slab(shard, zz, 1 - y), core_s.at[k, 1], core_r.at[k, 1], core_peer),
        )

    def third_copies(k):
        zz = order(k)
        return (
            same(slab(far, zz, y), core_s.at[k, 2], core_r.at[k, 2], core_peer),
            same(slab(far, zz, 1 - y), core_s.at[k, 3], core_r.at[k, 3], core_peer),
        )

    def gather0(k):
        @pl.when(k > 0)
        def _():
            along_z(k).wait_recv()
            pl.when(inner)(along_z(k).start)

        for copy in first_copies(k):
            copy.start()

    def gather1(k):
        zz = order(k)
        over_x, over_y, core = second_copies(k)
        same(slab(shard, zz, 1 - y, part_a), ya_s.at[k], ya_r.at[k], y_peer).wait_recv()
        over_x.start()
        same(slab(far, zz, y, part_b), xb_s.at[k], xb_r.at[k], x_peer).wait_recv()
        over_y.start()
        same(slab(shard, zz, 1 - y, part_b), yb_s.at[k, 0], yb_r.at[k, 0], y_peer).wait_recv()
        core.start()

    def gather2(k):
        zz = order(k)
        near, apart = third_copies(k)
        same(slab(far, zz, y, part_a), xa_s.at[k, 0], xa_r.at[k, 0], x_peer).wait_recv()
        near.start()
        same(slab(far, zz, 1 - y, part_a), xa_s.at[k, 1], xa_r.at[k, 1], x_peer).wait_recv()
        same(slab(far, zz, 1 - y, part_b), yb_s.at[k, 1], yb_r.at[k, 1], y_peer).wait_recv()
        apart.start()

    gather0(0)

    def find_block(row):
        block = 0
        for j, block_row in enumerate(rows):
            block = block + jnp.where(block_row == row, j, 0)
        block_at[row] = block

    loop(0, nz * 2 * CAP, find_block)
    for k in range(len(dp_peers)):
        meta_copy(k).wait_recv()
    lane = lax.broadcasted_iota(jnp.int32, (8, W), 1)
    chunks = []
    for pair in range(meta.shape[0] // 2):
        chunks.append(jnp.where(lane < W // 2, meta[2 * pair], pltpu.roll(meta[2 * pair + 1], W // 2, 1)))
    norms = jnp.concatenate(chunks, axis=1).astype(bf16).astype(f32)
    gain1, shift1, gain2, shift2 = (norms[i : i + 1, :] for i in range(4))
    band_sums = meta[0]
    for d in range(1, meta.shape[0]):
        band_sums = band_sums + meta[d]
    weight_of = jnp.sum(jnp.where(table, band_sums[:, W // 2 : W // 2 + 1], 0.0), axis=0, keepdims=True)
    count_of = jnp.sum(jnp.where(table, band_sums[:, W // 2 + 1 : W // 2 + 2], 0.0), axis=0, keepdims=True)
    scales = item_weight * count_of / weight_of
    item_lane = lax.broadcasted_iota(jnp.int32, (1, items), 1)
    position = lax.broadcasted_iota(jnp.int32, (TILE, 1), 0)
    fetches[6].wait()
    fetches[7].wait()
    fetches[8].wait()

    def tile(t):
        return pl.ds(pl.multiple_of(t * TILE, TILE), TILE)

    def first_norm(t):
        here = tile(t)
        scaled, inverse = normalise(tok[here, :])
        xhat1[here, :] = scaled
        inv1[here, :] = inverse
        low1[here, :] = (scaled * gain1 + shift1).astype(bf16)
        item = head * items_here + t // (SEQ // TILE)
        scale = jnp.sum(jnp.where(item_lane == item, scales, 0.0), axis=1, keepdims=True)
        inside = position + lax.rem(t, SEQ // TILE) * TILE < lens[item]
        scaled_cot = cot[here, :] * jnp.where(inside, scale, 0.0)
        cot[here, :] = scaled_cot
        e2[here, :] = scaled_cot.astype(bf16)
        acc[here, :] = jnp.zeros((TILE, D), f32)

    loop(0, tiles, first_norm)

    def gather(step):
        pl.when(step < nz)(lambda: gather0(step))
        pl.when(step <= nz)(lambda: gather1(step - 1))
        pl.when(step >= 2)(lambda: gather2(step - 2))

    loop(1, nz + 2, gather)

    def all_here(k):
        zz = order(k)
        for kind, (xx, yy) in enumerate(((x, y), (x, 1 - y), (1 - x, y), (1 - x, 1 - y))):
            same(slab(xx * 2 + 1 - c, zz, yy), core_s.at[k, kind], core_r.at[k, kind], core_peer).wait_recv()

    loop(0, nz, all_here)

    head_lane = lax.broadcasted_iota(jnp.int32, (1, W), 1)
    head_masks = [head_lane < HD, head_lane >= HD]
    key_pos = lax.broadcasted_iota(jnp.int32, (1, SEQ), 1)
    item_rows = [slice(i * SEQ, (i + 1) * SEQ) for i in range(items_here)]

    def only(values, a):
        return jnp.where(head_masks[a], values, jnp.zeros_like(values))

    def stack(values):
        return jnp.concatenate([only(values, 0), only(values, 1)], axis=0)

    def wide_matrix(h):
        return jnp.concatenate(
            [
                jnp.concatenate([wv[h, rows[j], p * W : (p + 1) * W, :] for j in range(QB)], axis=0)
                for p in range(3)
            ],
            axis=1,
        )

    def narrow_matrix(h, first, size):
        pieces = cat_pieces(first, size)
        return jnp.concatenate(
            [
                jnp.concatenate(
                    [wv[h, rows[b], pl.ds(p * (R // 4) + inside, count), :] for b, inside, _, count in pieces], axis=0
                )
                for p in range(4)
            ],
            axis=1,
        )

    key_row = lax.broadcasted_iota(jnp.int32, (2 * SEQ, W), 0)
    head_ones = jnp.where((key_row < SEQ) == head_masks[0], 1.0, 0.0).astype(bf16)

    def attention(h):
        projected = dot(low1[...], wide_matrix(h))
        qkv[h, 0] = (projected[:, :W].astype(bf16).astype(f32) * (1.0 / math.sqrt(HD))).astype(bf16)
        qkv[h, 1] = projected[:, W : 2 * W].astype(bf16)
        qkv[h, 2] = projected[:, 2 * W :].astype(bf16)
        for i, here in enumerate(item_rows):
            query, key, value = qkv[h, 0, here, :], qkv[h, 1, here, :], qkv[h, 2, here, :]
            valid = key_pos < lens[head * items_here + i]
            both = []
            for a in range(2):
                scores = jnp.where(valid, dot_cols(only(query, a), key), -1e30)
                exps = jnp.exp(scores - jnp.max(scores, axis=-1, keepdims=True)).astype(bf16)
                probs[h, i, a] = exps
                both.append(exps)
            mixed = dot(jnp.concatenate(both, axis=1), jnp.concatenate([stack(value), head_ones], axis=1))
            inverse = 1.0 / mixed[:, W:]
            sums[h, here, :] = inverse
            att[h, here, :] = (mixed[:, :W] * inverse).astype(bf16)
        acc[...] += dot(att[h], narrow_matrix(h, 0, W))

    loop(0, 4, attention)

    def second_norm(t):
        here = tile(t)
        state = acc[here, :] + tok[here, :]
        acc[here, :] = state
        scaled, inverse = normalise(state)
        xhat2[here, :] = scaled
        inv2[here, :] = inverse
        low2[here, :] = (scaled * gain2 + shift2).astype(bf16)
        da[here, :] = jnp.zeros((TILE, D), f32)

    loop(0, tiles, second_norm)

    def shard_of(i):
        return lax.rem(1 - x + i, 2) * 2 + lax.rem(c + 1 + i // 2, 2)

    def feed_forward(i):
        h = shard_of(i)
        hidden = dot(low2[...], narrow_matrix(h, W, D))
        root = math.sqrt(2.0 / math.pi)
        square = hidden * hidden
        bend = jnp.tanh(root * hidden * (1.0 + 0.044715 * square))
        half = 0.5 * (1.0 + bend)
        active = (hidden * half).astype(bf16)
        slope = half + 0.5 * hidden * (1.0 - bend * bend) * (root + (3.0 * 0.044715 * root) * square)
        actives[i] = active
        slopes[i] = slope.astype(bf16)
        acc[...] += dot(active, narrow_matrix(h, W + D, D))

    loop(0, 4, feed_forward)

    def own_tokens(ref, who):
        return ref.at[pl.ds(pl.multiple_of(who * tokens_here, tokens_here), tokens_here), :]

    outs = ((out_low, out_all), (in_low, in_all))

    def out_copies(i):
        src, dst = outs[i]
        there, across = own_tokens(dst, head), own_tokens(dst, (1 - x) * 2 + c)
        return (
            pltpu.make_async_copy(src, there, o_l.at[i]),
            remote(src, there, o_s.at[i, 0], o_r.at[i, 0], x_peer),
            remote(src, there, o_s.at[i, 1], o_r.at[i, 1], core_peer),
            same(across, o_s.at[i, 2], o_r.at[i, 2], core_peer),
        )

    out_low[...] = acc[...].astype(bf16)
    for copy in out_copies(0)[:3]:
        copy.start()

    def put(i, first, result):
        for block, inside, row, count in cat_pieces(first, result.shape[0]):
            for p in range(4):
                here = pl.ds(p * (R // 4) + inside, count)
                grads[i, block, here, :] = result[row : row + count, p * W : (p + 1) * W].astype(bf16)

    deep, low = (QB + 2, CB - 2), (0, QB + 2)
    x_part, y_part = pl.ds(0, RA), pl.ds(RA, R - RA)

    def core_push(i, n):
        part = pl.ds(*(deep, low)[n])
        return remote(grads.at[i, part], from_core.at[i, part], cs.at[n, i], cr.at[n, i], core_peer)

    def x_push(n):
        part = pl.ds(*(deep, low)[n])
        return remote(grads.at[2, part, x_part, :], rxa.at[part], as_.at[n], ar.at[n], x_peer)

    def hand_over(i, n):
        first, count = (deep, low)[n]
        pl.when(i < 2)(lambda: core_push(i, n).start())

        @pl.when(i >= 2)
        def _():
            core_push(i - 2, n).wait_recv()

            def add(j):
                grads[i, j] = grads[i, j] + from_core[i - 2, j]

            loop(first, first + count, add)
            pl.when(i == 2)(lambda: x_push(n).start())

    def feed_forward_back(i):
        h = shard_of(i)
        back = (dot_cols(e2[...], narrow_matrix(h, W + D, D)) * slopes[i].astype(f32)).astype(bf16)
        put(i, W + D, dot_rows(actives[i], e2[...]))
        put(i, W, dot_rows(low2[...], back))
        da[...] += dot_cols(back, narrow_matrix(h, W, D))
        hand_over(i, 0)

    loop(0, 4, feed_forward_back)

    def norm_backward(grad, scaled, inverse, gain):
        grad_scaled = grad * gain
        centre = jnp.mean(grad_scaled, axis=-1, keepdims=True)
        slope = jnp.mean(grad_scaled * scaled, axis=-1, keepdims=True)
        return inverse * (grad_scaled - centre - scaled * slope)

    norm_part[...] = jnp.zeros_like(norm_part)

    def second_norm_back(t):
        here = tile(t)
        grad, scaled = da[here, :], xhat2[here, :]
        norm_part[2:3, :] += jnp.sum(grad * scaled, axis=0, keepdims=True)
        norm_part[3:4, :] += jnp.sum(grad, axis=0, keepdims=True)
        change = cot[here, :] + norm_backward(grad, scaled, inv2[here, :], gain2)
        cot[here, :] = change
        e1[here, :] = change.astype(bf16)
        da[here, :] = jnp.zeros((TILE, D), f32)

    loop(0, tiles, second_norm_back)

    def attention_back(i):
        h = shard_of(i)
        put(i, 0, dot_rows(att[h], e1[...]))
        d_all = dot_cols(e1[...], narrow_matrix(h, 0, W)) * sums[h]
        shared_all = (d_all * att[h].astype(f32)).astype(bf16)
        d_all = d_all.astype(bf16)
        parts = []
        for m, here in enumerate(item_rows):
            query, key, value = qkv[h, 0, here, :], qkv[h, 1, here, :], qkv[h, 2, here, :]
            d_here, shared = d_all[here, :], shared_all[here, :]
            against = jnp.concatenate([value, jnp.full((SEQ, W), -1.0, bf16)], axis=1)
            d_scores = []
            for a in range(2):
                change = dot_cols(jnp.concatenate([only(d_here, a), only(shared, a)], axis=1), against)
                d_scores.append((probs[h, m, a].astype(f32) * change).astype(bf16))
            d_query = dot(jnp.concatenate(d_scores, axis=1), stack(key)) * (1.0 / math.sqrt(HD))
            d_key = dot_rows(jnp.concatenate(d_scores, axis=0), stack(query))
            d_value = dot_rows(jnp.concatenate([probs[h, m, 0], probs[h, m, 1]], axis=0), stack(d_here))
            parts.append(jnp.concatenate([d_query, d_key, d_value], axis=1).astype(bf16))
        d_qkv = jnp.concatenate(parts, axis=0)
        d_weight = dot_rows(low1[...], d_qkv).astype(bf16)
        for j in range(QB):
            for p in range(3):
                grads[i, j, p * W : (p + 1) * W, :] = d_weight[j * W : (j + 1) * W, p * W : (p + 1) * W]
        da[...] += dot_cols(d_qkv, wide_matrix(h))
        hand_over(i, 1)

    loop(0, 4, attention_back)

    def chunk(k):
        return lax.rem(z + 1 + k, nz)

    def block_of(k, yy, r):
        return block_at[(chunk(k) * 2 + yy) * CAP + r]

    def over_y_first(k):
        return remote(sb.at[k], ryb.at[k], sby_s.at[k], sby_r.at[k], y_peer)

    def over_x_last(k):
        return remote(sbx.at[k], rxb.at[k], sbx_s.at[k], sbx_r.at[k], x_peer)

    def over_y_last(k):
        return remote(sa.at[k], rya.at[k], say_s.at[k], say_r.at[k], y_peer)

    def over_z(k):
        return remote(fz.at[k], rz.at[k], fz_s.at[k], fz_r.at[k], device(chunk(k), y, x, c))

    def send_b(k):
        for r in range(CAP):
            block = block_of(k, 1 - y, r)
            for j in range(2):
                sb[k, j, r] = grads[2 + j, block, y_part, :]
        over_y_first(k).start()

    loop(0, nz, send_b)

    def first_norm_back(t):
        here = tile(t)
        grad, scaled = da[here, :], xhat1[here, :]
        norm_part[0:1, :] += jnp.sum(grad * scaled, axis=0, keepdims=True)
        norm_part[1:2, :] += jnp.sum(grad, axis=0, keepdims=True)
        in_low[here, :] = (cot[here, :] + norm_backward(grad, scaled, inv1[here, :], gain1)).astype(bf16)

    loop(0, tiles, first_norm_back)
    for copy in out_copies(1)[:3]:
        copy.start()

    def norm_copies():
        z_peers = [device(lax.rem(z + k, nz), y, x, c) for k in range(1, nz)]
        return [
            remote(norm_part, n_core, n_s.at[0], n_r.at[0], core_peer),
            remote(norm_sum.at[0], n_x, n_s.at[1], n_r.at[1], x_peer),
            remote(norm_sum.at[1], n_y, n_s.at[2], n_r.at[2], y_peer),
        ] + [remote(norm_sum.at[2], n_z.at[k], n_s.at[3 + k], n_r.at[3 + k], p) for k, p in enumerate(z_peers)]

    norm_copies()[0].start()

    for n in range(2):
        x_push(n).wait_recv()

    def add_x(j):
        grads[3, j, x_part, :] = grads[3, j, x_part, :] + rxa[j]

    loop(0, QB + CB, add_x)

    def send_a(k):
        for r in range(CAP):
            sa[k, r] = grads[3, block_of(k, 1 - y, r), x_part, :]
        over_y_last(k).start()

    loop(0, nz, send_a)

    norm_copies()[0].wait_recv()
    norm_sum[0] = norm_part[...] + n_core[...]
    norm_copies()[1].start()

    def reduce1(k):
        over_y_first(k).wait_recv()
        for r in range(CAP):
            sbx[k, r] = grads[2, block_of(k, y, r), y_part, :] + ryb[k, 0, r]
        over_x_last(k).start()

    def reduce2(k):
        over_y_last(k).wait_recv()
        over_x_last(k).wait_recv()
        for r in range(CAP):
            block = block_of(k, y, r)
            fz[k, r, x_part, :] = grads[3, block, x_part, :] + rya[k, r]
            part = grads[3, block, y_part, :].astype(f32) + ryb[k, 1, r].astype(f32)
            fz[k, r, y_part, :] = (part + rxb[k, r].astype(f32)).astype(bf16)
        pl.when(k < nz - 1)(lambda: over_z(k).start())

    def reduce_step(k):
        pl.when(k < nz)(lambda: reduce1(k))
        pl.when(k >= 1)(lambda: reduce2(k - 1))

    loop(0, 2, reduce_step)
    norm_copies()[1].wait_recv()
    norm_sum[1] = norm_sum[0] + n_x[...]
    norm_copies()[2].start()
    for i in range(2):
        if i == 0:
            out_copies(i)[1].wait_recv()
            out_copies(i)[3].start()
    loop(2, 4, reduce_step)
    norm_copies()[2].wait_recv()
    norm_sum[2] = norm_sum[1] + n_y[...]
    for copy in norm_copies()[3:]:
        copy.start()
    loop(4, nz + 1, reduce_step)
    out_copies(1)[1].wait_recv()
    out_copies(1)[3].start()

    for k in range(nz - 1):
        over_z(k).wait_recv()
        norm_copies()[3 + k].wait_recv()
    norm_total[...] = norm_sum[2] + ((n_z[0] + n_z[1]) + n_z[2])

    def last(r):
        others = (rz[0, r].astype(f32) + rz[1, r].astype(f32)) + rz[2, r].astype(f32)
        total[r] = fz[nz - 1, r].astype(f32) + others

    loop(0, CAP, last)

    for i in range(2):
        local, _, over_core, again = out_copies(i)
        local.wait()
        over_core.wait_recv()
        again.wait_recv()
        for copy in out_copies(i)[1:]:
            copy.wait_send()
    for copy in norm_copies():
        copy.wait_send()
    for k in range(len(dp_peers)):
        meta_copy(k).wait_send()
    pl.when(up)(own_up.wait_send)
    pl.when(down)(own_down.wait_send)

    def sent(k):
        for copy in first_copies(k) + second_copies(k) + third_copies(k):
            copy.wait_send()
        pl.when(jnp.logical_and(k > 0, inner))(along_z(k).wait_send)
        for copy in (over_y_first(k), over_x_last(k), over_y_last(k)):
            copy.wait_send()
        pl.when(k < nz - 1)(over_z(k).wait_send)

    loop(0, nz, sent)
    for n in range(2):
        x_push(n).wait_send()
        for i in range(2):
            core_push(i, n).wait_send()


def layer(tokens, cotangent, master, norms, steps, bands, lens_row, lens, owners):
    nz = Sizes.z
    here = tokens.shape[0] // lax.axis_size("head")
    items_here = here // SEQ
    items = lens.shape[0]
    vm = pl.BlockSpec(memory_space=pltpu.VMEM)
    hbm = pl.BlockSpec(memory_space=pltpu.HBM)
    dma = pltpu.SemaphoreType.DMA
    V, S = pltpu.VMEM, pltpu.SMEM
    square = (here, D)
    blocks = QB + CB
    rb = R - RA
    low, full = V(square, bf16), V(square, f32)
    scratch = [
        V((4, nz * 2 * CAP, R, W), bf16), V((R, CAP, W), f32), V((R, W), f32),
        V((8, W), f32), V((nz * 2, 8, W), f32), V(norms.shape, f32),
        V((1, items), jnp.int32), V((1, items), jnp.int32), V((1, items), jnp.int32),
        S((items,), jnp.int32), S(owners.shape, jnp.int32), S((nz * 2 * CAP,), jnp.int32),
        full, full, low, full, V((here, 1), f32), V((4, 3, here, W), bf16),
        V((4, items_here, 2, SEQ, SEQ), bf16), V((4, here, W), f32), V((4, here, W), bf16),
        full, low, full, V((here, 1), f32), low, V((4, here, D), bf16), V((4, here, D), bf16), full, low, low, low,
        V((4, blocks, R, W), bf16), V((2, blocks, R, W), bf16),
        V((blocks, RA, W), bf16), V((nz, CAP, RA, W), bf16), V((nz, CAP, RA, W), bf16),
        V((nz, 2, CAP, rb, W), bf16), V((nz, 2, CAP, rb, W), bf16), V((nz, CAP, rb, W), bf16),
        V((nz, CAP, rb, W), bf16), V((nz, CAP, R, W), bf16), V((nz - 1, CAP, R, W), bf16),
        V((8, D), f32), V((3, 8, D), f32), V((8, D), f32), V((8, D), f32), V((8, D), f32), V((nz - 1, 8, D), f32),
        dma((9,)), dma((nz + 1,)), dma((nz,)), dma((nz,)), dma((nz,)), dma((nz, 2)), dma((nz, 2)), dma((nz,)), dma((nz,)),
        dma((nz, 2)), dma((nz, 2)), dma((nz, 4)), dma((nz, 4)), dma((8,)), dma((8,)),
        dma((2, 2)), dma((2, 2)), dma((2,)), dma((2,)), dma((nz,)), dma((nz,)), dma((nz,)), dma((nz,)),
        dma((nz,)), dma((nz,)), dma((nz,)), dma((nz,)), dma((8,)), dma((8,)), dma((2, 3)), dma((2, 3)), dma((2,)),
    ]
    return pl.pallas_call(
        layer_kernel,
        name="layer",
        out_shape=(
            jax.ShapeDtypeStruct((CAP, R, W), f32),
            jax.ShapeDtypeStruct(tokens.shape, bf16),
            jax.ShapeDtypeStruct(tokens.shape, bf16),
            jax.ShapeDtypeStruct((8, D), f32),
        ),
        in_specs=[hbm] * 9,
        out_specs=(vm, hbm, hbm, vm),
        scratch_shapes=scratch,
        compiler_params=pltpu.CompilerParams(collective_id=0, has_side_effects=True, vmem_limit_bytes=56 << 20),
    )(tokens, cotangent, master, norms, steps, bands, lens_row, lens, owners)


def finish_kernel(
    total_hbm, norm_hbm, master_hbm, first_hbm, second_hbm, norm_m, norm_f, norm_s, owners_hbm, out_all, in_all,
    block_output, input_grad, new_master, new_first, new_second, new_norm, new_norm_first, new_norm_second,
    out_low, in_low, out_full, in_full, states, results, flat, grad, total, norm_total, norm_master, norm_first, norm_second, owners, l_sem, s_sem, i_sem, r_sem,
):
    pieces = l_sem.shape[1]
    size = out_low.shape[0] // pieces
    pairs = ((out_all, out_low, out_full, block_output), (in_all, in_low, in_full, input_grad))

    def piece(p):
        return pl.ds(pl.multiple_of(p * size, size), size)

    def fetch(n, p):
        return pltpu.make_async_copy(pairs[n][0].at[piece(p), :], pairs[n][1].at[piece(p), :], l_sem.at[n, p])

    def store(n, p):
        return pltpu.make_async_copy(pairs[n][2].at[piece(p), :], pairs[n][3].at[piece(p), :], s_sem.at[n, p])

    small_copies = [
        pltpu.make_async_copy(src, dst, i_sem.at[3 + i])
        for i, (src, dst) in enumerate((
            (owners_hbm, owners), (total_hbm, total), (norm_hbm, norm_total),
            (norm_m, norm_master), (norm_f, norm_first), (norm_s, norm_second),
        ))
    ]
    state_copies = [
        pltpu.make_async_copy(src, states.at[i], i_sem.at[i]) for i, src in enumerate((master_hbm, first_hbm, second_hbm))
    ]
    result_copies = [
        pltpu.make_async_copy(results.at[i], dst, r_sem.at[i]) for i, dst in enumerate((new_master, new_first, new_second))
    ]

    def loop(count, body):
        def step(i, _):
            body(i)
            return 0

        lax.fori_loop(0, count, step, 0)

    for copy in small_copies:
        copy.start()
    loop(pieces, lambda p: fetch(0, p).start())
    for copy in state_copies:
        copy.start()
    loop(pieces, lambda p: fetch(1, p).start())

    dp = lax.axis_index("dp")
    small_copies[0].wait()
    rows = block_rows(owners)
    held = 0
    for j in range(owners.shape[0]):
        held = held + jnp.where(owners[j] == dp, 1, 0)

    def spread(r):
        is_wide = slot_is_wide(rows, dp * CAP + r)

        @pl.when(is_wide)
        def _():
            for p in range(3):
                flat[pl.ds(p, W, stride=3), :] = total[r, p * W : (p + 1) * W, :]

        @pl.when(jnp.logical_not(is_wide))
        def _():
            for p in range(4):
                flat[pl.ds(p, R // 4, stride=4), :] = total[r, p * (R // 4) : (p + 1) * (R // 4), :]

    small_copies[1].wait()
    for r in range(CAP):
        spread(r)
        grad[:, r, :] = flat[...]

    def convert(n, p):
        fetch(n, p).wait()
        _, low, full, _ = pairs[n]
        full[piece(p), :] = low[piece(p), :].astype(f32)
        store(n, p).start()

    loop(pieces, lambda p: convert(0, p))
    for copy in state_copies:
        copy.wait()
    step = 32
    slot = lax.broadcasted_iota(jnp.int32, (step, CAP, W), 1)

    def update(i):
        here = pl.ds(pl.multiple_of(i * step, step), step)
        new = adamw_update(states[0, here], states[1, here], states[2, here], grad[here], weight_decay, learn_rate)
        for n in range(3):
            results[n, here] = jnp.where(slot < held, new[n], 0.0)

    loop(R // step, update)
    for copy in result_copies:
        copy.start()
    for copy in small_copies[2:]:
        copy.wait()
    pair = norm_total[:, pl.ds(pl.multiple_of((dp // 2) * W, W), W)]
    mine = jnp.where(lax.rem(dp, 2) == 1, pltpu.roll(pair, W // 2, 1), pair)[0:4, 0 : norm_master.shape[1]]
    new = adamw_update(norm_master[...], norm_first[...], norm_second[...], mine, 0.0, norm_rate)
    for ref, value in zip((new_norm, new_norm_first, new_norm_second), new):
        ref[...] = value
    loop(pieces, lambda p: convert(1, p))
    for n in range(2):
        loop(pieces, lambda p: store(n, p).wait())
    for copy in result_copies:
        copy.wait()


def finish(total, norm_total, slots, norms, owners, out_all, in_all):
    vm = pl.BlockSpec(memory_space=pltpu.VMEM)
    hbm = pl.BlockSpec(memory_space=pltpu.HBM)
    dma = pltpu.SemaphoreType.DMA
    V = pltpu.VMEM
    pieces = 8
    shape = out_all.shape
    return pl.pallas_call(
        finish_kernel,
        name="finish",
        out_shape=(
            (jax.ShapeDtypeStruct(shape, f32),) * 2 + tuple(jax.ShapeDtypeStruct(a.shape, f32) for a in slots + norms)
        ),
        in_specs=[hbm] * 11,
        out_specs=(hbm,) * 5 + (vm,) * 3,
        scratch_shapes=[
            V(shape, bf16), V(shape, bf16), V(shape, f32), V(shape, f32), V((3, R, CAP, W), f32), V((3, R, CAP, W), f32),
            V((R, W), f32), V((R, CAP, W), f32),
            V(total.shape, f32), V(norm_total.shape, f32), *(V(a.shape, f32) for a in norms),
            pltpu.SMEM(owners.shape, jnp.int32), dma((2, pieces)), dma((2, pieces)), dma((9,)), dma((3,)),
        ],
        compiler_params=pltpu.CompilerParams(vmem_limit_bytes=60 << 20),
    )(total, norm_total, *slots, *norms, owners, out_all, in_all)


def fast_shards(
    tokens, cotangent, timesteps, bands, lengths, owners,
    master_slots, first_slots, second_slots, norm_master, norm_first, norm_second,
):
    def tiles(slots):
        return jnp.transpose(slots.reshape(CAP, R, W), (1, 0, 2))

    def flat(slots):
        return jnp.transpose(slots, (1, 0, 2)).reshape(CAP, R * W)

    steps, bands_row, lens_row = (v.reshape(1, -1) for v in (timesteps, bands, lengths))
    slots = tuple(tiles(s) for s in (master_slots, first_slots, second_slots))
    norms = (norm_master, norm_first, norm_second)
    total, out_all, in_all, norm_total = layer(
        tokens, cotangent, slots[0], norm_master, steps, bands_row, lens_row, lengths, owners
    )
    results = finish(total, norm_total, slots, norms, owners, out_all, in_all)
    return (*results[:2], *(flat(s) for s in results[2:5]), *results[5:])


def solution(mesh):
    fits = dict(mesh.shape) == {"dp": 8, "head": 4}
    placed = (
        P("dp", None),
        P("dp", None),
        P("dp"),
        P("dp"),
        P("dp"),
        P(),
        P("dp", "head"),
        P("dp", "head"),
        P("dp", "head"),
        P(None, "dp"),
        P(None, "dp"),
        P(None, "dp"),
    )
    return jax.shard_map(
        fast_shards if fits else shards,
        mesh=mesh,
        in_specs=placed,
        out_specs=(
            P("dp", None),
            P("dp", None),
            P("dp", "head"),
            P("dp", "head"),
            P("dp", "head"),
            P(None, "dp"),
            P(None, "dp"),
            P(None, "dp"),
        ),
        check_vma=False,
    )
```

```python
import math

import jax
import jax.numpy as jnp
from jax import lax
from jax.experimental import pallas as pl
from jax.experimental.pallas import tpu as pltpu
from jax.sharding import PartitionSpec as P

D = 512
H = 8
HD = 64
FF = 2048
SEQ = 256
TSTEPS = 1000
NBANDS = 8
CAP = 3
STEP = 5


beta_one = 0.5
beta_two = 0.5
learn_rate = 0.04
norm_rate = 0.4
weight_decay = 0.1
adam_eps = 1e-08
norm_eps = 1e-05


def contract_rows(left_side, right_side):
    return lax.dot_general(
        left_side, right_side, (((0,), (0,)), ((), ())), preferred_element_type=jnp.float32
    )


def contract_cols(left_side, right_side):
    return lax.dot_general(
        left_side, right_side, (((1,), (1,)), ((), ())), preferred_element_type=jnp.float32
    )


def gelu_tanh(values):
    return jax.nn.gelu(values, approximate=True)


def norm_forward(values, gain_row, shift_row):
    average = jnp.mean(values, axis=-1, keepdims=True)
    centred = values - average
    inverse = lax.rsqrt(jnp.mean(centred * centred, axis=-1, keepdims=True) + norm_eps)
    scaled = centred * inverse
    return (scaled * gain_row + shift_row, scaled, inverse)


def norm_backward(grad_normed, scaled, inverse, gain_row):
    grad_scaled = grad_normed * gain_row
    centre_term = jnp.mean(grad_scaled, axis=-1, keepdims=True)
    slope_term = jnp.mean(grad_scaled * scaled, axis=-1, keepdims=True)
    return inverse * (grad_scaled - centre_term - scaled * slope_term)


def slot_rows(owners, capacity):
    block_index = jnp.arange(owners.shape[0], dtype=jnp.int32)
    earlier = (owners[None, :] == owners[:, None]) & (block_index[None, :] < block_index[:, None])
    return owners * capacity + jnp.sum(earlier.astype(jnp.int32), axis=1)


def attention_scores(query_heads, key_heads, key_valid):
    scores = jnp.einsum(
        "gqad,gkad->gaqk", query_heads, key_heads, preferred_element_type=jnp.float32
    ) / math.sqrt(HD)
    return jnp.where(key_valid[:, None, None, :], scores, -1e30)


def adamw_update(weight, first_moment, second, gradient, decay_rate, step_rate):
    new_first = beta_one * first_moment + (1.0 - beta_one) * gradient
    new_second = beta_two * second + (1.0 - beta_two) * gradient * gradient
    first_hat = new_first / (1.0 - beta_one**STEP)
    second_hat = new_second / (1.0 - beta_two**STEP)
    new_weight = weight - step_rate * (
        first_hat / (jnp.sqrt(second_hat) + adam_eps) + decay_rate * weight
    )
    return (new_weight, new_first, new_second)


def shards(
    tokens,
    cotangent,
    timesteps,
    bands,
    lengths,
    owners,
    master_slots,
    first_slots,
    second_slots,
    norm_master,
    norm_first,
    norm_second,
):
    head_count = lax.axis_size("head")
    owner_index = lax.axis_index("dp")
    heads_here = H // head_count
    width_here = heads_here * HD
    units_here = FF // head_count
    block_len = master_slots.shape[1]
    norm_cols = norm_master.shape[1]
    row_count = tokens.shape[0]
    item_count = lengths.shape[0]
    block_count = owners.shape[0]
    slot_row = slot_rows(owners, CAP)
    gathered, norm_whole = (
        lax.all_gather(master_slots.astype(jnp.bfloat16), "dp", axis=0, tiled=True),
        lax.all_gather(norm_master.astype(jnp.bfloat16), "dp", axis=1, tiled=True),
    )
    flat_params = gathered[slot_row].reshape(-1)
    qkv_end = 3 * D * width_here
    out_end = qkv_end + width_here * D
    up_end = out_end + D * units_here
    qkv_weight = flat_params[:qkv_end].reshape(D, 3 * width_here)
    out_weight = flat_params[qkv_end:out_end].reshape(width_here, D)
    up_weight = flat_params[out_end:up_end].reshape(D, units_here)
    down_weight = flat_params[up_end:].reshape(units_here, D)
    norm_params = norm_whole.astype(jnp.float32)
    item_weight = jnp.exp(-2.0 * timesteps.astype(jnp.float32) / TSTEPS)
    item_length = lengths.astype(jnp.float32)
    band_table = (bands[:, None] == jnp.arange(NBANDS, dtype=jnp.int32)[None, :]).astype(
        jnp.float32
    )
    weight_sums, count_sums = lax.psum(
        (
            jnp.sum(band_table * (item_weight * item_length)[:, None], axis=0),
            jnp.sum(band_table * item_length[:, None], axis=0),
        ),
        "dp",
    )
    item_scale = (
        item_weight
        * jnp.sum(band_table * count_sums[None, :], axis=1)
        / jnp.sum(band_table * weight_sums[None, :], axis=1)
    )
    key_valid = jnp.arange(SEQ, dtype=jnp.int32)[None, :] < lengths[:, None]
    token_scale = jnp.where(key_valid, item_scale[:, None], 0.0).reshape(row_count)
    normed_one, scaled_one, inverse_one = norm_forward(tokens, norm_params[0], norm_params[1])
    normed_one_low = normed_one.astype(jnp.bfloat16)
    projected_low = jnp.dot(normed_one_low, qkv_weight, preferred_element_type=jnp.float32).astype(
        jnp.bfloat16
    )
    head_shape = (item_count, SEQ, heads_here, HD)
    query_heads = projected_low[:, :width_here].reshape(head_shape)
    key_heads = projected_low[:, width_here : 2 * width_here].reshape(head_shape)
    value_heads = projected_low[:, 2 * width_here :].reshape(head_shape)
    scores = attention_scores(query_heads, key_heads, key_valid)
    row_max = jnp.max(scores, axis=-1, keepdims=True)
    exp_scores = jnp.exp(scores - row_max)
    row_total = jnp.sum(exp_scores, axis=-1, keepdims=True)
    log_total = row_max + jnp.log(row_total)
    prob_low = (exp_scores / row_total).astype(jnp.bfloat16)
    attended_low = (
        jnp.einsum("gaqk,gkad->gqad", prob_low, value_heads, preferred_element_type=jnp.float32)
        .astype(jnp.bfloat16)
        .reshape(row_count, width_here)
    )
    attn_sum = lax.psum(
        jnp.dot(attended_low, out_weight, preferred_element_type=jnp.float32).astype(jnp.bfloat16),
        "head",
    ).astype(jnp.float32)
    mixed_state = tokens + attn_sum
    normed_two, scaled_two, inverse_two = norm_forward(mixed_state, norm_params[2], norm_params[3])
    normed_two_low = normed_two.astype(jnp.bfloat16)
    hidden = jnp.dot(normed_two_low, up_weight, preferred_element_type=jnp.float32)
    activated, gelu_pull = jax.vjp(gelu_tanh, hidden)
    activated_low = activated.astype(jnp.bfloat16)
    ffn_sum = lax.psum(
        jnp.dot(activated_low, down_weight, preferred_element_type=jnp.float32).astype(
            jnp.bfloat16
        ),
        "head",
    ).astype(jnp.float32)
    block_output = mixed_state + ffn_sum
    grad_state = cotangent * token_scale[:, None]
    grad_low_two = grad_state.astype(jnp.bfloat16)
    grad_down = contract_rows(activated_low, grad_low_two)
    grad_activated = contract_cols(grad_low_two, down_weight)
    grad_hidden_low = gelu_pull(grad_activated)[0].astype(jnp.bfloat16)
    grad_up = contract_rows(normed_two_low, grad_hidden_low)
    grad_normed_two = lax.psum(
        contract_cols(grad_hidden_low, up_weight).astype(jnp.bfloat16), "head"
    ).astype(jnp.float32)
    grad_mixed = grad_state + norm_backward(
        grad_normed_two, scaled_two, inverse_two, norm_params[2]
    )
    grad_low_one = grad_mixed.astype(jnp.bfloat16)
    grad_out_proj = contract_rows(attended_low, grad_low_one)
    grad_attended_low = (
        contract_cols(grad_low_one, out_weight).astype(jnp.bfloat16).reshape(head_shape)
    )
    scores_again = attention_scores(query_heads, key_heads, key_valid)
    probabilities = jnp.exp(scores_again - log_total)
    prob_again_low = probabilities.astype(jnp.bfloat16)
    grad_values = jnp.einsum(
        "gaqk,gqad->gkad", prob_again_low, grad_attended_low, preferred_element_type=jnp.float32
    )
    grad_probs = jnp.einsum(
        "gqad,gkad->gaqk", grad_attended_low, value_heads, preferred_element_type=jnp.float32
    )
    grad_scores_low = (
        probabilities * (grad_probs - jnp.sum(grad_probs * probabilities, axis=-1, keepdims=True))
    ).astype(jnp.bfloat16)
    grad_queries = jnp.einsum(
        "gaqk,gkad->gqad", grad_scores_low, key_heads, preferred_element_type=jnp.float32
    ) / math.sqrt(HD)
    grad_keys = jnp.einsum(
        "gaqk,gqad->gkad", grad_scores_low, query_heads, preferred_element_type=jnp.float32
    ) / math.sqrt(HD)
    grad_projected_low = jnp.concatenate(
        [
            grad_queries.reshape(row_count, width_here),
            grad_keys.reshape(row_count, width_here),
            grad_values.reshape(row_count, width_here),
        ],
        axis=1,
    ).astype(jnp.bfloat16)
    grad_qkv = contract_rows(normed_one_low, grad_projected_low)
    grad_normed_one = lax.psum(
        contract_cols(grad_projected_low, qkv_weight).astype(jnp.bfloat16), "head"
    ).astype(jnp.float32)
    input_grad = grad_mixed + norm_backward(
        grad_normed_one, scaled_one, inverse_one, norm_params[0]
    )
    norm_grads = jnp.stack(
        [
            jnp.sum(grad_normed_one * scaled_one, axis=0),
            jnp.sum(grad_normed_one, axis=0),
            jnp.sum(grad_normed_two * scaled_two, axis=0),
            jnp.sum(grad_normed_two, axis=0),
        ]
    )
    grad_blocks = jnp.concatenate(
        [
            grad_qkv.reshape(-1),
            grad_out_proj.reshape(-1),
            grad_up.reshape(-1),
            grad_down.reshape(-1),
        ]
    ).reshape(block_count, block_len)
    summed, norm_summed = (
        lax.psum(grad_blocks.astype(jnp.bfloat16), "dp").astype(jnp.float32),
        lax.psum(norm_grads.astype(jnp.bfloat16), "dp").astype(jnp.float32),
    )
    landing = jnp.where(owners == owner_index, slot_row - owner_index * CAP, CAP)
    owned_grad = jnp.zeros((CAP, block_len), jnp.float32).at[landing].set(summed, mode="drop")
    norm_owned = lax.dynamic_slice_in_dim(norm_summed, owner_index * norm_cols, norm_cols, 1)
    held_count = jnp.sum((owners == owner_index).astype(jnp.int32))
    used_slot = (jnp.arange(CAP, dtype=jnp.int32) < held_count)[:, None]
    new_master, new_first, new_second = adamw_update(
        master_slots, first_slots, second_slots, owned_grad, weight_decay, learn_rate
    )
    new_master = jnp.where(used_slot, new_master, 0.0)
    new_first = jnp.where(used_slot, new_first, 0.0)
    new_second = jnp.where(used_slot, new_second, 0.0)
    new_norms, new_norm_first, new_norm_second = adamw_update(
        norm_master, norm_first, norm_second, norm_owned, 0.0, norm_rate
    )
    return (
        block_output,
        input_grad,
        new_master,
        new_first,
        new_second,
        new_norms,
        new_norm_first,
        new_norm_second,
    )


W = 128
R = 384
QB = 4
CB = 12
MESH = pl.DeviceIdType.MESH
bf16 = jnp.bfloat16
f32 = jnp.float32


def place(sizes):
    dp = lax.axis_index("dp")
    head = lax.axis_index("head")
    return dp // sizes.y, lax.rem(dp, sizes.y), head // sizes.c, lax.rem(head, sizes.c)


class Sizes:
    z, y, x, c = 4, 2, 2, 2


def device(z, y, x, c):
    return (z * Sizes.y + y, x * Sizes.c + c)


def greet(partners):
    barrier = pltpu.get_barrier_semaphore()
    for partner in partners:
        pl.semaphore_signal(barrier, inc=1, device_id=partner, device_id_type=MESH)
    pl.semaphore_wait(barrier, len(partners))


def block_rows(owners):
    ids = [owners[j] for j in range(owners.shape[0])]
    rows = []
    for j, mine in enumerate(ids):
        row = mine * CAP
        for other in ids[:j]:
            row = row + jnp.where(other == mine, 1, 0)
        rows.append(row)
    return rows


def slot_is_wide(rows, slot_row):
    flag = rows[0] == slot_row
    for row in rows[1:QB]:
        flag = jnp.logical_or(flag, row == slot_row)
    return flag


def dot(left, right):
    return jnp.dot(left, right, preferred_element_type=f32)


def dot_cols(left, right):
    return lax.dot_general(left, right, (((1,), (1,)), ((), ())), preferred_element_type=f32)


def dot_rows(left, right):
    return lax.dot_general(left, right, (((0,), (0,)), ((), ())), preferred_element_type=f32)


def normalise(values):
    centred = values - jnp.mean(values, axis=-1, keepdims=True)
    inverse = lax.rsqrt(jnp.mean(centred * centred, axis=-1, keepdims=True) + norm_eps)
    return centred * inverse, inverse


def panels(ref, h, first, size):
    return jnp.concatenate([ref[h, p, first : first + size, :] for p in range(ref.shape[1])], axis=1)


def cat_pieces(first, size):
    pieces = []
    row = first
    while row < first + size:
        block, inside = divmod(row, R // 4)
        count = min(R // 4 - inside, first + size - row)
        pieces.append((QB + block, inside, row - first, count))
        row += count
    return pieces


RA = 288
GA = 192
TILE = 128


def layer_kernel(
    tok_hbm, cot_hbm, master_hbm, norms_hbm, steps_hbm, bands_hbm, lens_row_hbm, lens_hbm, owners_hbm,
    total, out_all, in_all, norm_total,
    wv, master, flat, mine, meta, norms_v, steps, bands, lens_row, lens, owners, block_at,
    tok, cot, low1, xhat1, inv1, qkv, probs, sums, att, acc, low2, xhat2, inv2, e2, da, e1,
    out_low, in_low,
    grads, from_core, rxa, sa, rya, sb, ryb, sbx, rxb, fz, rz, norm_part, norm_sum, n_core, n_x, n_y, n_z,
    i_sem, z_s, z_r, ya_s, ya_r, xa_s, xa_r, xb_s, xb_r, yb_s, yb_r, core_s, core_r, m_s, m_r,
    cs, cr, as_, ar, say_s, say_r, sby_s, sby_r, sbx_s, sbx_r, fz_s, fz_r, n_s, n_r, o_s, o_r, o_l,
):
    z, y, x, c = place(Sizes)
    nz = Sizes.z
    dp, head = z * 2 + y, x * 2 + c
    dp_peers = [device(lax.rem(z + k, nz), (y + j) % 2, x, c) for k in range(nz) for j in range(2) if k or j]
    x_peer, y_peer, core_peer = device(z, y, 1 - x, c), device(z, 1 - y, x, c), device(z, y, x, 1 - c)
    peers = dp_peers + [x_peer, core_peer]
    barrier = pltpu.get_barrier_semaphore()
    for peer in peers:
        pl.semaphore_signal(barrier, inc=1, device_id=peer, device_id_type=MESH)

    tokens_here = tok.shape[1]
    items_here = tokens_here // SEQ
    tiles = tokens_here // TILE

    def whose(p):
        return lax.rem(x + p, 2) * 2 + c

    def tokens_of(ref, who):
        return ref.at[pl.ds(pl.multiple_of(who * tokens_here, tokens_here), tokens_here), :]

    fetches = [
        pltpu.make_async_copy(src, dst, i_sem.at[n])
        for n, (src, dst) in enumerate((
            (owners_hbm, owners), (master_hbm, master), (steps_hbm, steps), (bands_hbm, bands),
            (lens_row_hbm, lens_row), (norms_hbm, norms_v), (lens_hbm, lens),
            (tokens_of(tok_hbm, whose(0)), tok.at[0]), (tokens_of(cot_hbm, whose(0)), cot.at[0]),
            (tokens_of(tok_hbm, whose(1)), tok.at[1]), (tokens_of(cot_hbm, whose(1)), cot.at[1]),
        ))
    ]
    for fetch in fetches:
        fetch.start()

    def loop(first, last, body):
        def step(i, _):
            body(i)
            return 0

        lax.fori_loop(first, last, step, 0)

    def remote(src, dst, send, recv, peer):
        return pltpu.make_async_remote_copy(
            src_ref=src, dst_ref=dst, send_sem=send, recv_sem=recv, device_id=peer, device_id_type=MESH
        )

    def same(ref, send, recv, peer):
        return remote(ref, ref, send, recv, peer)

    shard, far = x * 2 + c, (1 - x) * 2 + c
    fetches[0].wait()
    rows = block_rows(owners)
    fetches[1].wait()
    for r in range(CAP):
        flat[...] = master[:, r, :]
        wide = jnp.concatenate([flat[pl.ds(p, W, stride=3), :] for p in range(3)], axis=0)
        narrow = jnp.concatenate([flat[pl.ds(p, R // 4, stride=4), :] for p in range(4)], axis=0)
        wv[shard, dp * CAP + r] = jnp.where(slot_is_wide(rows, dp * CAP + r), wide, narrow).astype(bf16)

    for n in (2, 3, 4, 5):
        fetches[n].wait()
    items = steps.shape[1]
    item_weight = jnp.exp(-2.0 * steps[...].astype(f32) / TSTEPS)
    item_length = lens_row[...].astype(f32)
    table = bands[...] == lax.broadcasted_iota(jnp.int32, (NBANDS, items), 0)
    ones = table.astype(f32)
    mine[...] = jnp.zeros_like(mine)
    mine[0:4, 0 : W // 2] = norms_v[...]
    mine[:, W // 2 : W // 2 + 1] = jnp.sum(ones * (item_weight * item_length), axis=1, keepdims=True)
    mine[:, W // 2 + 1 : W // 2 + 2] = jnp.sum(ones * item_length, axis=1, keepdims=True)
    meta[dp] = mine[...]

    pl.semaphore_wait(barrier, len(peers))

    part_a, part_b = pl.ds(0, GA), pl.ds(GA, R - GA)

    def slab(sh, zz, yy, part=slice(None)):
        return wv.at[sh, pl.ds((zz * 2 + yy) * CAP, CAP), part, :]

    def order(k):
        late, low = k // 2, z // 2
        return (1 - late) * (z + k * (1 - 2 * lax.rem(z, 2))) + late * (k + low * (3 - 2 * k))

    up, down, inner = z < nz - 1, z > 0, lax.rem(z, nz - 1) != 0
    own_up = same(slab(shard, z, y), z_s.at[0], z_r.at[z], device(z + 1, y, x, c))
    own_down = same(slab(shard, z, y), z_s.at[nz], z_r.at[z], device(z - 1, y, x, c))
    pl.when(up)(own_up.start)
    pl.when(down)(own_down.start)

    def meta_copy(k):
        return remote(mine, meta.at[dp], m_s.at[k], m_r.at[k], dp_peers[k])

    for k in range(len(dp_peers)):
        meta_copy(k).start()

    def along_z(k):
        zz = order(k)
        late = k // 2
        goal = (1 - late) * (3 - z) + late * 3 * (z - 1)
        return same(slab(shard, zz, y), z_s.at[k], z_r.at[zz], device(goal, y, x, c))

    def first_copies(k):
        zz = order(k)
        one, two = slab(shard, zz, y, part_a), slab(shard, zz, y, part_b)
        return (
            same(one, ya_s.at[k], ya_r.at[k], y_peer),
            same(two, xb_s.at[k], xb_r.at[k], x_peer),
            same(two, yb_s.at[k, 0], yb_r.at[k, 0], y_peer),
            same(one, xa_s.at[k, 0], xa_r.at[k, 0], x_peer),
            same(slab(shard, zz, y), core_s.at[k, 0], core_r.at[k, 0], core_peer),
        )

    def second_copies(k):
        zz = order(k)
        return (
            same(slab(shard, zz, 1 - y, part_a), xa_s.at[k, 1], xa_r.at[k, 1], x_peer),
            same(slab(far, zz, y, part_b), yb_s.at[k, 1], yb_r.at[k, 1], y_peer),
            same(slab(shard, zz, 1 - y), core_s.at[k, 1], core_r.at[k, 1], core_peer),
        )

    def third_copies(k):
        zz = order(k)
        return (
            same(slab(far, zz, y), core_s.at[k, 2], core_r.at[k, 2], core_peer),
            same(slab(far, zz, 1 - y), core_s.at[k, 3], core_r.at[k, 3], core_peer),
        )

    def gather0(k):
        @pl.when(k > 0)
        def _():
            along_z(k).wait_recv()
            pl.when(inner)(along_z(k).start)

        for copy in first_copies(k):
            copy.start()

    def gather1(k):
        zz = order(k)
        over_x, over_y, core = second_copies(k)
        same(slab(shard, zz, 1 - y, part_a), ya_s.at[k], ya_r.at[k], y_peer).wait_recv()
        over_x.start()
        same(slab(far, zz, y, part_b), xb_s.at[k], xb_r.at[k], x_peer).wait_recv()
        over_y.start()
        same(slab(shard, zz, 1 - y, part_b), yb_s.at[k, 0], yb_r.at[k, 0], y_peer).wait_recv()
        core.start()

    def gather2(k):
        zz = order(k)
        near, apart = third_copies(k)
        same(slab(far, zz, y, part_a), xa_s.at[k, 0], xa_r.at[k, 0], x_peer).wait_recv()
        near.start()
        same(slab(far, zz, 1 - y, part_a), xa_s.at[k, 1], xa_r.at[k, 1], x_peer).wait_recv()
        same(slab(far, zz, 1 - y, part_b), yb_s.at[k, 1], yb_r.at[k, 1], y_peer).wait_recv()
        apart.start()

    gather0(0)

    def find_block(row):
        block = 0
        for j, block_row in enumerate(rows):
            block = block + jnp.where(block_row == row, j, 0)
        block_at[row] = block

    loop(0, nz * 2 * CAP, find_block)
    for k in range(len(dp_peers)):
        meta_copy(k).wait_recv()
    lane = lax.broadcasted_iota(jnp.int32, (8, W), 1)
    chunks = []
    for pair in range(meta.shape[0] // 2):
        chunks.append(jnp.where(lane < W // 2, meta[2 * pair], pltpu.roll(meta[2 * pair + 1], W // 2, 1)))
    norms = jnp.concatenate(chunks, axis=1).astype(bf16).astype(f32)
    gain1, shift1, gain2, shift2 = (norms[i : i + 1, :] for i in range(4))
    band_sums = meta[0]
    for d in range(1, meta.shape[0]):
        band_sums = band_sums + meta[d]
    weight_of = jnp.sum(jnp.where(table, band_sums[:, W // 2 : W // 2 + 1], 0.0), axis=0, keepdims=True)
    count_of = jnp.sum(jnp.where(table, band_sums[:, W // 2 + 1 : W // 2 + 2], 0.0), axis=0, keepdims=True)
    scales = item_weight * count_of / weight_of
    item_lane = lax.broadcasted_iota(jnp.int32, (1, items), 1)
    position = lax.broadcasted_iota(jnp.int32, (TILE, 1), 0)
    for n in range(6, 11):
        fetches[n].wait()

    def tile(t):
        return pl.ds(pl.multiple_of(t * TILE, TILE), TILE)

    def first_norm(i):
        p, t = i // tiles, lax.rem(i, tiles)
        here = tile(t)
        scaled, inverse = normalise(tok[p, here, :])
        xhat1[p, here, :] = scaled
        inv1[p, here, :] = inverse
        low1[p, here, :] = (scaled * gain1 + shift1).astype(bf16)
        item = whose(p) * items_here + t // (SEQ // TILE)
        scale = jnp.sum(jnp.where(item_lane == item, scales, 0.0), axis=1, keepdims=True)
        inside = position + lax.rem(t, SEQ // TILE) * TILE < lens[item]
        scaled_cot = cot[p, here, :] * jnp.where(inside, scale, 0.0)
        cot[p, here, :] = scaled_cot
        e2[p, here, :] = scaled_cot.astype(bf16)

    loop(0, 2 * tiles, first_norm)

    def gather(step):
        pl.when(step < nz)(lambda: gather0(step))
        pl.when(step <= nz)(lambda: gather1(step - 1))
        pl.when(step >= 2)(lambda: gather2(step - 2))

    loop(1, nz + 2, gather)

    def all_here(k):
        zz = order(k)
        for kind, (xx, yy) in enumerate(((x, y), (x, 1 - y), (1 - x, y), (1 - x, 1 - y))):
            same(slab(xx * 2 + 1 - c, zz, yy), core_s.at[k, kind], core_r.at[k, kind], core_peer).wait_recv()

    loop(0, nz, all_here)

    head_lane = lax.broadcasted_iota(jnp.int32, (1, W), 1)
    head_masks = [head_lane < HD, head_lane >= HD]
    key_pos = lax.broadcasted_iota(jnp.int32, (1, SEQ), 1)
    item_rows = [slice(i * SEQ, (i + 1) * SEQ) for i in range(items_here)]

    def only(values, a):
        return jnp.where(head_masks[a], values, jnp.zeros_like(values))

    def stack(values):
        return jnp.concatenate([only(values, 0), only(values, 1)], axis=0)

    def wide_matrix(h):
        return jnp.concatenate(
            [
                jnp.concatenate([wv[h, rows[j], p * W : (p + 1) * W, :] for j in range(QB)], axis=0)
                for p in range(3)
            ],
            axis=1,
        )

    def narrow_matrix(h, first, size):
        pieces = cat_pieces(first, size)
        return jnp.concatenate(
            [
                jnp.concatenate(
                    [wv[h, rows[b], pl.ds(p * (R // 4) + inside, count), :] for b, inside, _, count in pieces], axis=0
                )
                for p in range(4)
            ],
            axis=1,
        )

    deep, low = (QB + 2, CB - 2), (0, QB + 2)
    x_part, y_part = pl.ds(0, RA), pl.ds(RA, R - RA)

    def core_push(j, n):
        part = pl.ds(*(deep, low)[n])
        return remote(grads.at[j, part], from_core.at[j, part], cs.at[n, j], cr.at[n, j], core_peer)

    def x_push(n):
        part = pl.ds(*(deep, low)[n])
        return remote(grads.at[2, part, x_part, :], rxa.at[part], as_.at[n], ar.at[n], x_peer)

    def hand_over(i, n):
        first, count = (deep, low)[n]
        pl.when(i < 2)(lambda: core_push(i, n).start())

        @pl.when(i >= 2)
        def _():
            core_push(i - 2, n).wait_recv()

            def add(block):
                grads[i, block] = grads[i, block] + from_core[i - 2, block]

            loop(first, first + count, add)
            pl.when(i == 2)(lambda: x_push(n).start())

    pair_z, cross_z = z + 1 - 2 * lax.rem(z, 2), lax.rem(z + 2, nz)

    def chunk(k):
        return lax.rem(pair_z + lax.rem(k, 2) * (z - pair_z) + 2 * (1 - k // 2), nz)

    def block_of(k, yy, r):
        return block_at[(chunk(k) * 2 + yy) * CAP + r]

    def over_y_first(k):
        return remote(sb.at[k], ryb.at[k], sby_s.at[k], sby_r.at[k], y_peer)

    def over_x_last(k):
        return remote(sbx.at[k], rxb.at[k], sbx_s.at[k], sbx_r.at[k], x_peer)

    def over_y_last(k):
        return remote(sa.at[k], rya.at[k], say_s.at[k], say_r.at[k], y_peer)

    def over_z(k):
        goal = pair_z + lax.rem(k, 2) * (cross_z - pair_z)
        return remote(fz.at[k], rz.at[k], fz_s.at[k], fz_r.at[k], device(goal, y, x, c))

    def norm_copies():
        z_peers = [device(lax.rem(z + k, nz), y, x, c) for k in range(1, nz)]
        return [
            remote(norm_part, n_core, n_s.at[0], n_r.at[0], core_peer),
            remote(norm_sum.at[0], n_x, n_s.at[1], n_r.at[1], x_peer),
            remote(norm_sum.at[1], n_y, n_s.at[2], n_r.at[2], y_peer),
        ] + [remote(norm_sum.at[2], n_z.at[k], n_s.at[3 + k], n_r.at[3 + k], p) for k, p in enumerate(z_peers)]

    def send_b(k):
        for r in range(CAP):
            block = block_of(k, 1 - y, r)
            for j in range(2):
                sb[k, j, r] = grads[2 + j, block, y_part, :]
        over_y_first(k).start()

    def add_x(j):
        grads[3, j, x_part, :] = grads[3, j, x_part, :] + rxa[j]

    def send_a(k):
        for r in range(CAP):
            sa[k, r] = grads[3, block_of(k, 1 - y, r), x_part, :]
        over_y_last(k).start()

    def reduce1(k):
        over_y_first(k).wait_recv()
        for r in range(CAP):
            sbx[k, r] = grads[2, block_of(k, y, r), y_part, :] + ryb[k, 0, r]
        over_x_last(k).start()

    def reduce2(k):
        over_y_last(k).wait_recv()
        over_x_last(k).wait_recv()
        for r in range(CAP):
            block = block_of(k, y, r)
            fz[k, r, x_part, :] = grads[3, block, x_part, :] + rya[k, r]
            part = grads[3, block, y_part, :].astype(f32) + ryb[k, 1, r].astype(f32)
            fz[k, r, y_part, :] = (part + rxb[k, r].astype(f32)).astype(bf16)
        pl.when(lax.rem(k, 2) == 0)(lambda: over_z(k).start())

    def cross():
        over_z(0).wait_recv()
        for r in range(CAP):
            fz[1, r] = fz[1, r] + rz[0, r]
        over_z(1).start()

    key_row = lax.broadcasted_iota(jnp.int32, (2 * SEQ, W), 0)
    head_ones = jnp.where((key_row < SEQ) == head_masks[0], 1.0, 0.0).astype(bf16)

    def attention(p, h):
        projected = dot(low1[p], wide_matrix(h))
        qkv[h, 0] = (projected[:, :W].astype(bf16).astype(f32) * (1.0 / math.sqrt(HD))).astype(bf16)
        qkv[h, 1] = projected[:, W : 2 * W].astype(bf16)
        qkv[h, 2] = projected[:, 2 * W :].astype(bf16)
        for i, here in enumerate(item_rows):
            query, key, value = qkv[h, 0, here, :], qkv[h, 1, here, :], qkv[h, 2, here, :]
            valid = key_pos < lens[whose(p) * items_here + i]
            both = []
            for a in range(2):
                scores = jnp.where(valid, dot_cols(only(query, a), key), -1e30)
                exps = jnp.exp(scores - jnp.max(scores, axis=-1, keepdims=True)).astype(bf16)
                probs[h, i, a] = exps
                both.append(exps)
            mixed = dot(jnp.concatenate(both, axis=1), jnp.concatenate([stack(value), head_ones], axis=1))
            inverse = 1.0 / mixed[:, W:]
            sums[h, here, :] = inverse
            att[h, here, :] = (mixed[:, :W] * inverse).astype(bf16)
        acc[...] += dot(att[h], narrow_matrix(h, 0, W))

    def put(i, first, result):
        for block, inside, row, count in cat_pieces(first, result.shape[0]):
            for p in range(4):
                here = pl.ds(p * (R // 4) + inside, count)
                grads[i, block, here, :] = result[row : row + count, p * W : (p + 1) * W].astype(bf16)

    def shard_of(p, i):
        return lax.rem(1 + x + p + i, 2) * 2 + lax.rem(c + 1 + i // 2, 2)

    def feed_forward(p, i):
        h = shard_of(p, i)
        up_matrix, down_matrix = narrow_matrix(h, W, D), narrow_matrix(h, W + D, D)
        hidden = dot(low2[...], up_matrix)
        root = math.sqrt(2.0 / math.pi)
        square = hidden * hidden
        bend = jnp.tanh(root * hidden * (1.0 + 0.044715 * square))
        half = 0.5 * (1.0 + bend)
        active = (hidden * half).astype(bf16)
        slope = half + 0.5 * hidden * (1.0 - bend * bend) * (root + (3.0 * 0.044715 * root) * square)
        acc[...] += dot(active, down_matrix)
        back = (dot_cols(e2[p], down_matrix) * slope).astype(bf16)
        da[...] += dot_cols(back, up_matrix)
        if p == 0:
            put(i, W + D, dot_rows(active, e2[p]))
            put(i, W, dot_rows(low2[...], back))
            hand_over(i, 0)

    def attention_back(p, i):
        h = shard_of(p, i)
        d_all = dot_cols(e1[...], narrow_matrix(h, 0, W)) * sums[h]
        shared_all = (d_all * att[h].astype(f32)).astype(bf16)
        d_all = d_all.astype(bf16)
        parts = []
        for m, here in enumerate(item_rows):
            query, key, value = qkv[h, 0, here, :], qkv[h, 1, here, :], qkv[h, 2, here, :]
            d_here, shared = d_all[here, :], shared_all[here, :]
            against = jnp.concatenate([value, jnp.full((SEQ, W), -1.0, bf16)], axis=1)
            d_scores = []
            for a in range(2):
                change = dot_cols(jnp.concatenate([only(d_here, a), only(shared, a)], axis=1), against)
                d_scores.append((probs[h, m, a].astype(f32) * change).astype(bf16))
            d_query = dot(jnp.concatenate(d_scores, axis=1), stack(key)) * (1.0 / math.sqrt(HD))
            d_key = dot_rows(jnp.concatenate(d_scores, axis=0), stack(query))
            d_value = dot_rows(jnp.concatenate([probs[h, m, 0], probs[h, m, 1]], axis=0), stack(d_here))
            parts.append(jnp.concatenate([d_query, d_key, d_value], axis=1).astype(bf16))
        d_qkv = jnp.concatenate(parts, axis=0)
        da[...] += dot_cols(d_qkv, wide_matrix(h))
        if p == 0:
            put(i, 0, dot_rows(att[h], e1[...]))
            d_weight = dot_rows(low1[p], d_qkv).astype(bf16)
            for j in range(QB):
                for m in range(3):
                    grads[i, j, m * W : (m + 1) * W, :] = d_weight[j * W : (j + 1) * W, m * W : (m + 1) * W]
            hand_over(i, 1)

    def norm_backward(grad, scaled, inverse, gain):
        grad_scaled = grad * gain
        centre = jnp.mean(grad_scaled, axis=-1, keepdims=True)
        slope = jnp.mean(grad_scaled * scaled, axis=-1, keepdims=True)
        return inverse * (grad_scaled - centre - scaled * slope)

    def add_norm(p, row, grad, scaled):
        if p == 0:
            norm_part[row : row + 1, :] += jnp.sum(grad * scaled, axis=0, keepdims=True)
            norm_part[row + 1 : row + 2, :] += jnp.sum(grad, axis=0, keepdims=True)

    norm_part[...] = jnp.zeros_like(norm_part)

    def out_copies(p, n):
        src, dst = ((out_low, out_all), (in_low, in_all))[n]
        there = tokens_of(dst, whose(p))
        return (
            pltpu.make_async_copy(src.at[p], there, o_l.at[p, n]),
            remote(src.at[p], there, o_s.at[p, n], o_r.at[p, n], core_peer),
        )

    def layer_pass(p):
        if p == 1:
            loop(0, nz, send_b)
            norm_copies()[0].start()

        acc[...] = jnp.zeros_like(acc)
        loop(0, 4, lambda h: attention(p, h))

        def second_norm(t):
            here = tile(t)
            state = acc[here, :] + tok[p, here, :]
            acc[here, :] = state
            scaled, inverse = normalise(state)
            xhat2[here, :] = scaled
            inv2[here, :] = inverse
            low2[here, :] = (scaled * gain2 + shift2).astype(bf16)
            da[here, :] = jnp.zeros((TILE, D), f32)

        loop(0, tiles, second_norm)
        loop(0, 4, lambda i: feed_forward(p, i))
        out_low[p] = acc[...].astype(bf16)
        for copy in out_copies(p, 0):
            copy.start()

        if p == 1:
            norm_copies()[0].wait_recv()
            norm_sum[0] = norm_part[...] + n_core[...]
            norm_copies()[1].start()
            for n in range(2):
                x_push(n).wait_recv()
            loop(0, QB + CB, add_x)
            loop(0, nz, send_a)
            loop(0, nz, reduce1)
            norm_copies()[1].wait_recv()
            norm_sum[1] = norm_sum[0] + n_x[...]
            norm_copies()[2].start()


        def second_norm_back(t):
            here = tile(t)
            grad, scaled = da[here, :], xhat2[here, :]
            add_norm(p, 2, grad, scaled)
            change = cot[p, here, :] + norm_backward(grad, scaled, inv2[here, :], gain2)
            cot[p, here, :] = change
            e1[here, :] = change.astype(bf16)
            da[here, :] = jnp.zeros((TILE, D), f32)

        loop(0, tiles, second_norm_back)
        if p == 1:
            reduce2(0)

        def attention_step(i):
            attention_back(p, i)
            if p == 1:
                pl.when(i < 2)(lambda: reduce2(i + 1))
                pl.when(i == 1)(cross)

        loop(0, 4, attention_step)

        def first_norm_back(t):
            here = tile(t)
            grad, scaled = da[here, :], xhat1[p, here, :]
            add_norm(p, 0, grad, scaled)
            in_low[p, here, :] = (cot[p, here, :] + norm_backward(grad, scaled, inv1[p, here, :], gain1)).astype(bf16)

        loop(0, tiles, first_norm_back)
        for copy in out_copies(p, 1):
            copy.start()

    layer_pass(0)
    layer_pass(1)
    norm_copies()[2].wait_recv()
    norm_sum[2] = norm_sum[1] + n_y[...]
    for copy in norm_copies()[3:]:
        copy.start()
    reduce2(nz - 1)

    for k in range(nz - 1):
        norm_copies()[3 + k].wait_recv()
    over_z(2).wait_recv()
    over_z(1).wait_recv()
    norm_total[...] = norm_sum[2] + ((n_z[0] + n_z[1]) + n_z[2])

    def last(r):
        others = rz[1, r].astype(f32) + rz[2, r].astype(f32)
        total[r] = fz[nz - 1, r].astype(f32) + others

    loop(0, CAP, last)

    for p in range(2):
        for n in range(2):
            local, over_core = out_copies(p, n)
            local.wait()
            over_core.wait()
    for copy in norm_copies():
        copy.wait_send()
    for k in range(len(dp_peers)):
        meta_copy(k).wait_send()
    pl.when(up)(own_up.wait_send)
    pl.when(down)(own_down.wait_send)

    def sent(k):
        for copy in first_copies(k) + second_copies(k) + third_copies(k):
            copy.wait_send()
        pl.when(jnp.logical_and(k > 0, inner))(along_z(k).wait_send)
        for copy in (over_y_first(k), over_x_last(k), over_y_last(k)):
            copy.wait_send()
        pl.when(k < nz - 1)(over_z(k).wait_send)

    loop(0, nz, sent)
    for n in range(2):
        x_push(n).wait_send()
        for j in range(2):
            core_push(j, n).wait_send()


def layer(tokens, cotangent, master, norms, steps, bands, lens_row, lens, owners):
    nz = Sizes.z
    here = tokens.shape[0] // lax.axis_size("head")
    items_here = here // SEQ
    items = lens.shape[0]
    vm = pl.BlockSpec(memory_space=pltpu.VMEM)
    hbm = pl.BlockSpec(memory_space=pltpu.HBM)
    dma = pltpu.SemaphoreType.DMA
    V, S = pltpu.VMEM, pltpu.SMEM
    square = (here, D)
    blocks = QB + CB
    rb = R - RA
    low, full, two_low, two = V(square, bf16), V(square, f32), V((2, *square), bf16), V((2, *square), f32)
    scratch = [
        V((4, nz * 2 * CAP, R, W), bf16), V((R, CAP, W), f32), V((R, W), f32),
        V((8, W), f32), V((nz * 2, 8, W), f32), V(norms.shape, f32),
        V((1, items), jnp.int32), V((1, items), jnp.int32), V((1, items), jnp.int32),
        S((items,), jnp.int32), S(owners.shape, jnp.int32), S((nz * 2 * CAP,), jnp.int32),
        two, two, two_low, two, V((2, here, 1), f32), V((4, 3, here, W), bf16),
        V((4, items_here, 2, SEQ, SEQ), bf16), V((4, here, W), f32), V((4, here, W), bf16),
        full, low, full, V((here, 1), f32), two_low,
        full, low, two_low, two_low,
        V((4, blocks, R, W), bf16), V((2, blocks, R, W), bf16),
        V((blocks, RA, W), bf16), V((nz, CAP, RA, W), bf16), V((nz, CAP, RA, W), bf16),
        V((nz, 2, CAP, rb, W), bf16), V((nz, 2, CAP, rb, W), bf16), V((nz, CAP, rb, W), bf16),
        V((nz, CAP, rb, W), bf16), V((nz, CAP, R, W), bf16), V((nz - 1, CAP, R, W), bf16),
        V((8, D), f32), V((3, 8, D), f32), V((8, D), f32), V((8, D), f32), V((8, D), f32), V((nz - 1, 8, D), f32),
        dma((11,)), dma((nz + 1,)), dma((nz,)), dma((nz,)), dma((nz,)), dma((nz, 2)), dma((nz, 2)), dma((nz,)), dma((nz,)),
        dma((nz, 2)), dma((nz, 2)), dma((nz, 4)), dma((nz, 4)), dma((8,)), dma((8,)),
        dma((2, 2)), dma((2, 2)), dma((2,)), dma((2,)), dma((nz,)), dma((nz,)), dma((nz,)), dma((nz,)),
        dma((nz,)), dma((nz,)), dma((nz,)), dma((nz,)), dma((8,)), dma((8,)), dma((2, 2)), dma((2, 2)), dma((2, 2)),
    ]
    return pl.pallas_call(
        layer_kernel,
        name="layer",
        out_shape=(
            jax.ShapeDtypeStruct((CAP, R, W), f32),
            jax.ShapeDtypeStruct(tokens.shape, bf16),
            jax.ShapeDtypeStruct(tokens.shape, bf16),
            jax.ShapeDtypeStruct((8, D), f32),
        ),
        in_specs=[hbm] * 9,
        out_specs=(vm, hbm, hbm, vm),
        scratch_shapes=scratch,
        compiler_params=pltpu.CompilerParams(collective_id=0, has_side_effects=True, vmem_limit_bytes=56 << 20),
    )(tokens, cotangent, master, norms, steps, bands, lens_row, lens, owners)


def finish_kernel(
    total_hbm, norm_hbm, master_hbm, first_hbm, second_hbm, norm_m, norm_f, norm_s, owners_hbm, out_all, in_all,
    block_output, input_grad, new_master, new_first, new_second, new_norm, new_norm_first, new_norm_second,
    out_low, in_low, out_full, in_full, states, results, flat, grad, total, norm_total, norm_master, norm_first, norm_second, owners, l_sem, s_sem, i_sem, r_sem,
):
    pieces = l_sem.shape[1]
    size = out_low.shape[0] // pieces
    pairs = ((out_all, out_low, out_full, block_output), (in_all, in_low, in_full, input_grad))

    def piece(p):
        return pl.ds(pl.multiple_of(p * size, size), size)

    def fetch(n, p):
        return pltpu.make_async_copy(pairs[n][0].at[piece(p), :], pairs[n][1].at[piece(p), :], l_sem.at[n, p])

    def store(n, p):
        return pltpu.make_async_copy(pairs[n][2].at[piece(p), :], pairs[n][3].at[piece(p), :], s_sem.at[n, p])

    small_copies = [
        pltpu.make_async_copy(src, dst, i_sem.at[3 + i])
        for i, (src, dst) in enumerate((
            (owners_hbm, owners), (total_hbm, total), (norm_hbm, norm_total),
            (norm_m, norm_master), (norm_f, norm_first), (norm_s, norm_second),
        ))
    ]
    state_copies = [
        pltpu.make_async_copy(src, states.at[i], i_sem.at[i]) for i, src in enumerate((master_hbm, first_hbm, second_hbm))
    ]
    result_copies = [
        pltpu.make_async_copy(results.at[i], dst, r_sem.at[i]) for i, dst in enumerate((new_master, new_first, new_second))
    ]

    def loop(count, body):
        def step(i, _):
            body(i)
            return 0

        lax.fori_loop(0, count, step, 0)

    for copy in small_copies:
        copy.start()
    loop(pieces, lambda p: fetch(0, p).start())
    for copy in state_copies:
        copy.start()
    loop(pieces, lambda p: fetch(1, p).start())

    dp = lax.axis_index("dp")
    small_copies[0].wait()
    rows = block_rows(owners)
    held = 0
    for j in range(owners.shape[0]):
        held = held + jnp.where(owners[j] == dp, 1, 0)

    def spread(r):
        is_wide = slot_is_wide(rows, dp * CAP + r)

        @pl.when(is_wide)
        def _():
            for p in range(3):
                flat[pl.ds(p, W, stride=3), :] = total[r, p * W : (p + 1) * W, :]

        @pl.when(jnp.logical_not(is_wide))
        def _():
            for p in range(4):
                flat[pl.ds(p, R // 4, stride=4), :] = total[r, p * (R // 4) : (p + 1) * (R // 4), :]

    small_copies[1].wait()
    for r in range(CAP):
        spread(r)
        grad[:, r, :] = flat[...]

    def convert(n, p):
        fetch(n, p).wait()
        _, low, full, _ = pairs[n]
        full[piece(p), :] = low[piece(p), :].astype(f32)
        store(n, p).start()

    loop(pieces, lambda p: convert(0, p))
    for copy in state_copies:
        copy.wait()
    step = 32
    slot = lax.broadcasted_iota(jnp.int32, (step, CAP, W), 1)

    def update(i):
        here = pl.ds(pl.multiple_of(i * step, step), step)
        new = adamw_update(states[0, here], states[1, here], states[2, here], grad[here], weight_decay, learn_rate)
        for n in range(3):
            results[n, here] = jnp.where(slot < held, new[n], 0.0)

    loop(R // step, update)
    for copy in result_copies:
        copy.start()
    for copy in small_copies[2:]:
        copy.wait()
    pair = norm_total[:, pl.ds(pl.multiple_of((dp // 2) * W, W), W)]
    mine = jnp.where(lax.rem(dp, 2) == 1, pltpu.roll(pair, W // 2, 1), pair)[0:4, 0 : norm_master.shape[1]]
    new = adamw_update(norm_master[...], norm_first[...], norm_second[...], mine, 0.0, norm_rate)
    for ref, value in zip((new_norm, new_norm_first, new_norm_second), new):
        ref[...] = value
    loop(pieces, lambda p: convert(1, p))
    for n in range(2):
        loop(pieces, lambda p: store(n, p).wait())
    for copy in result_copies:
        copy.wait()


def finish(total, norm_total, slots, norms, owners, out_all, in_all):
    vm = pl.BlockSpec(memory_space=pltpu.VMEM)
    hbm = pl.BlockSpec(memory_space=pltpu.HBM)
    dma = pltpu.SemaphoreType.DMA
    V = pltpu.VMEM
    pieces = 8
    shape = out_all.shape
    return pl.pallas_call(
        finish_kernel,
        name="finish",
        out_shape=(
            (jax.ShapeDtypeStruct(shape, f32),) * 2 + tuple(jax.ShapeDtypeStruct(a.shape, f32) for a in slots + norms)
        ),
        in_specs=[hbm] * 11,
        out_specs=(hbm,) * 5 + (vm,) * 3,
        scratch_shapes=[
            V(shape, bf16), V(shape, bf16), V(shape, f32), V(shape, f32), V((3, R, CAP, W), f32), V((3, R, CAP, W), f32),
            V((R, W), f32), V((R, CAP, W), f32),
            V(total.shape, f32), V(norm_total.shape, f32), *(V(a.shape, f32) for a in norms),
            pltpu.SMEM(owners.shape, jnp.int32), dma((2, pieces)), dma((2, pieces)), dma((9,)), dma((3,)),
        ],
        compiler_params=pltpu.CompilerParams(vmem_limit_bytes=60 << 20),
    )(total, norm_total, *slots, *norms, owners, out_all, in_all)


def fast_shards(
    tokens, cotangent, timesteps, bands, lengths, owners,
    master_slots, first_slots, second_slots, norm_master, norm_first, norm_second,
):
    def tiles(slots):
        return jnp.transpose(slots.reshape(CAP, R, W), (1, 0, 2))

    def flat(slots):
        return jnp.transpose(slots, (1, 0, 2)).reshape(CAP, R * W)

    steps, bands_row, lens_row = (v.reshape(1, -1) for v in (timesteps, bands, lengths))
    slots = tuple(tiles(s) for s in (master_slots, first_slots, second_slots))
    norms = (norm_master, norm_first, norm_second)
    total, out_all, in_all, norm_total = layer(
        tokens, cotangent, slots[0], norm_master, steps, bands_row, lens_row, lengths, owners
    )
    results = finish(total, norm_total, slots, norms, owners, out_all, in_all)
    return (*results[:2], *(flat(s) for s in results[2:5]), *results[5:])


def solution(mesh):
    fits = dict(mesh.shape) == {"dp": 8, "head": 4}
    placed = (
        P("dp", None),
        P("dp", None),
        P("dp"),
        P("dp"),
        P("dp"),
        P(),
        P("dp", "head"),
        P("dp", "head"),
        P("dp", "head"),
        P(None, "dp"),
        P(None, "dp"),
        P(None, "dp"),
    )
    return jax.shard_map(
        fast_shards if fits else shards,
        mesh=mesh,
        in_specs=placed,
        out_specs=(
            P("dp", None),
            P("dp", None),
            P("dp", "head"),
            P("dp", "head"),
            P("dp", "head"),
            P(None, "dp"),
            P(None, "dp"),
            P(None, "dp"),
        ),
        check_vma=False,
    )
```

```python
import math

import jax
import jax.numpy as jnp
from jax import lax
from jax.experimental import pallas as pl
from jax.experimental.pallas import tpu as pltpu
from jax.sharding import PartitionSpec as P

D = 512
H = 8
HD = 64
FF = 2048
SEQ = 256
TSTEPS = 1000
NBANDS = 8
CAP = 3
STEP = 5


beta_one = 0.5
beta_two = 0.5
learn_rate = 0.04
norm_rate = 0.4
weight_decay = 0.1
adam_eps = 1e-08
norm_eps = 1e-05


def contract_rows(left_side, right_side):
    return lax.dot_general(
        left_side, right_side, (((0,), (0,)), ((), ())), preferred_element_type=jnp.float32
    )


def contract_cols(left_side, right_side):
    return lax.dot_general(
        left_side, right_side, (((1,), (1,)), ((), ())), preferred_element_type=jnp.float32
    )


def gelu_tanh(values):
    return jax.nn.gelu(values, approximate=True)


def norm_forward(values, gain_row, shift_row):
    average = jnp.mean(values, axis=-1, keepdims=True)
    centred = values - average
    inverse = lax.rsqrt(jnp.mean(centred * centred, axis=-1, keepdims=True) + norm_eps)
    scaled = centred * inverse
    return (scaled * gain_row + shift_row, scaled, inverse)


def norm_backward(grad_normed, scaled, inverse, gain_row):
    grad_scaled = grad_normed * gain_row
    centre_term = jnp.mean(grad_scaled, axis=-1, keepdims=True)
    slope_term = jnp.mean(grad_scaled * scaled, axis=-1, keepdims=True)
    return inverse * (grad_scaled - centre_term - scaled * slope_term)


def slot_rows(owners, capacity):
    block_index = jnp.arange(owners.shape[0], dtype=jnp.int32)
    earlier = (owners[None, :] == owners[:, None]) & (block_index[None, :] < block_index[:, None])
    return owners * capacity + jnp.sum(earlier.astype(jnp.int32), axis=1)


def attention_scores(query_heads, key_heads, key_valid):
    scores = jnp.einsum(
        "gqad,gkad->gaqk", query_heads, key_heads, preferred_element_type=jnp.float32
    ) / math.sqrt(HD)
    return jnp.where(key_valid[:, None, None, :], scores, -1e30)


def adamw_update(weight, first_moment, second, gradient, decay_rate, step_rate):
    new_first = beta_one * first_moment + (1.0 - beta_one) * gradient
    new_second = beta_two * second + (1.0 - beta_two) * gradient * gradient
    first_hat = new_first / (1.0 - beta_one**STEP)
    second_hat = new_second / (1.0 - beta_two**STEP)
    new_weight = weight - step_rate * (
        first_hat / (jnp.sqrt(second_hat) + adam_eps) + decay_rate * weight
    )
    return (new_weight, new_first, new_second)


def shards(
    tokens,
    cotangent,
    timesteps,
    bands,
    lengths,
    owners,
    master_slots,
    first_slots,
    second_slots,
    norm_master,
    norm_first,
    norm_second,
):
    head_count = lax.axis_size("head")
    owner_index = lax.axis_index("dp")
    heads_here = H // head_count
    width_here = heads_here * HD
    units_here = FF // head_count
    block_len = master_slots.shape[1]
    norm_cols = norm_master.shape[1]
    row_count = tokens.shape[0]
    item_count = lengths.shape[0]
    block_count = owners.shape[0]
    slot_row = slot_rows(owners, CAP)
    gathered, norm_whole = (
        lax.all_gather(master_slots.astype(jnp.bfloat16), "dp", axis=0, tiled=True),
        lax.all_gather(norm_master.astype(jnp.bfloat16), "dp", axis=1, tiled=True),
    )
    flat_params = gathered[slot_row].reshape(-1)
    qkv_end = 3 * D * width_here
    out_end = qkv_end + width_here * D
    up_end = out_end + D * units_here
    qkv_weight = flat_params[:qkv_end].reshape(D, 3 * width_here)
    out_weight = flat_params[qkv_end:out_end].reshape(width_here, D)
    up_weight = flat_params[out_end:up_end].reshape(D, units_here)
    down_weight = flat_params[up_end:].reshape(units_here, D)
    norm_params = norm_whole.astype(jnp.float32)
    item_weight = jnp.exp(-2.0 * timesteps.astype(jnp.float32) / TSTEPS)
    item_length = lengths.astype(jnp.float32)
    band_table = (bands[:, None] == jnp.arange(NBANDS, dtype=jnp.int32)[None, :]).astype(
        jnp.float32
    )
    weight_sums, count_sums = lax.psum(
        (
            jnp.sum(band_table * (item_weight * item_length)[:, None], axis=0),
            jnp.sum(band_table * item_length[:, None], axis=0),
        ),
        "dp",
    )
    item_scale = (
        item_weight
        * jnp.sum(band_table * count_sums[None, :], axis=1)
        / jnp.sum(band_table * weight_sums[None, :], axis=1)
    )
    key_valid = jnp.arange(SEQ, dtype=jnp.int32)[None, :] < lengths[:, None]
    token_scale = jnp.where(key_valid, item_scale[:, None], 0.0).reshape(row_count)
    normed_one, scaled_one, inverse_one = norm_forward(tokens, norm_params[0], norm_params[1])
    normed_one_low = normed_one.astype(jnp.bfloat16)
    projected_low = jnp.dot(normed_one_low, qkv_weight, preferred_element_type=jnp.float32).astype(
        jnp.bfloat16
    )
    head_shape = (item_count, SEQ, heads_here, HD)
    query_heads = projected_low[:, :width_here].reshape(head_shape)
    key_heads = projected_low[:, width_here : 2 * width_here].reshape(head_shape)
    value_heads = projected_low[:, 2 * width_here :].reshape(head_shape)
    scores = attention_scores(query_heads, key_heads, key_valid)
    row_max = jnp.max(scores, axis=-1, keepdims=True)
    exp_scores = jnp.exp(scores - row_max)
    row_total = jnp.sum(exp_scores, axis=-1, keepdims=True)
    log_total = row_max + jnp.log(row_total)
    prob_low = (exp_scores / row_total).astype(jnp.bfloat16)
    attended_low = (
        jnp.einsum("gaqk,gkad->gqad", prob_low, value_heads, preferred_element_type=jnp.float32)
        .astype(jnp.bfloat16)
        .reshape(row_count, width_here)
    )
    attn_sum = lax.psum(
        jnp.dot(attended_low, out_weight, preferred_element_type=jnp.float32).astype(jnp.bfloat16),
        "head",
    ).astype(jnp.float32)
    mixed_state = tokens + attn_sum
    normed_two, scaled_two, inverse_two = norm_forward(mixed_state, norm_params[2], norm_params[3])
    normed_two_low = normed_two.astype(jnp.bfloat16)
    hidden = jnp.dot(normed_two_low, up_weight, preferred_element_type=jnp.float32)
    activated, gelu_pull = jax.vjp(gelu_tanh, hidden)
    activated_low = activated.astype(jnp.bfloat16)
    ffn_sum = lax.psum(
        jnp.dot(activated_low, down_weight, preferred_element_type=jnp.float32).astype(
            jnp.bfloat16
        ),
        "head",
    ).astype(jnp.float32)
    block_output = mixed_state + ffn_sum
    grad_state = cotangent * token_scale[:, None]
    grad_low_two = grad_state.astype(jnp.bfloat16)
    grad_down = contract_rows(activated_low, grad_low_two)
    grad_activated = contract_cols(grad_low_two, down_weight)
    grad_hidden_low = gelu_pull(grad_activated)[0].astype(jnp.bfloat16)
    grad_up = contract_rows(normed_two_low, grad_hidden_low)
    grad_normed_two = lax.psum(
        contract_cols(grad_hidden_low, up_weight).astype(jnp.bfloat16), "head"
    ).astype(jnp.float32)
    grad_mixed = grad_state + norm_backward(
        grad_normed_two, scaled_two, inverse_two, norm_params[2]
    )
    grad_low_one = grad_mixed.astype(jnp.bfloat16)
    grad_out_proj = contract_rows(attended_low, grad_low_one)
    grad_attended_low = (
        contract_cols(grad_low_one, out_weight).astype(jnp.bfloat16).reshape(head_shape)
    )
    scores_again = attention_scores(query_heads, key_heads, key_valid)
    probabilities = jnp.exp(scores_again - log_total)
    prob_again_low = probabilities.astype(jnp.bfloat16)
    grad_values = jnp.einsum(
        "gaqk,gqad->gkad", prob_again_low, grad_attended_low, preferred_element_type=jnp.float32
    )
    grad_probs = jnp.einsum(
        "gqad,gkad->gaqk", grad_attended_low, value_heads, preferred_element_type=jnp.float32
    )
    grad_scores_low = (
        probabilities * (grad_probs - jnp.sum(grad_probs * probabilities, axis=-1, keepdims=True))
    ).astype(jnp.bfloat16)
    grad_queries = jnp.einsum(
        "gaqk,gkad->gqad", grad_scores_low, key_heads, preferred_element_type=jnp.float32
    ) / math.sqrt(HD)
    grad_keys = jnp.einsum(
        "gaqk,gqad->gkad", grad_scores_low, query_heads, preferred_element_type=jnp.float32
    ) / math.sqrt(HD)
    grad_projected_low = jnp.concatenate(
        [
            grad_queries.reshape(row_count, width_here),
            grad_keys.reshape(row_count, width_here),
            grad_values.reshape(row_count, width_here),
        ],
        axis=1,
    ).astype(jnp.bfloat16)
    grad_qkv = contract_rows(normed_one_low, grad_projected_low)
    grad_normed_one = lax.psum(
        contract_cols(grad_projected_low, qkv_weight).astype(jnp.bfloat16), "head"
    ).astype(jnp.float32)
    input_grad = grad_mixed + norm_backward(
        grad_normed_one, scaled_one, inverse_one, norm_params[0]
    )
    norm_grads = jnp.stack(
        [
            jnp.sum(grad_normed_one * scaled_one, axis=0),
            jnp.sum(grad_normed_one, axis=0),
            jnp.sum(grad_normed_two * scaled_two, axis=0),
            jnp.sum(grad_normed_two, axis=0),
        ]
    )
    grad_blocks = jnp.concatenate(
        [
            grad_qkv.reshape(-1),
            grad_out_proj.reshape(-1),
            grad_up.reshape(-1),
            grad_down.reshape(-1),
        ]
    ).reshape(block_count, block_len)
    summed, norm_summed = (
        lax.psum(grad_blocks.astype(jnp.bfloat16), "dp").astype(jnp.float32),
        lax.psum(norm_grads.astype(jnp.bfloat16), "dp").astype(jnp.float32),
    )
    landing = jnp.where(owners == owner_index, slot_row - owner_index * CAP, CAP)
    owned_grad = jnp.zeros((CAP, block_len), jnp.float32).at[landing].set(summed, mode="drop")
    norm_owned = lax.dynamic_slice_in_dim(norm_summed, owner_index * norm_cols, norm_cols, 1)
    held_count = jnp.sum((owners == owner_index).astype(jnp.int32))
    used_slot = (jnp.arange(CAP, dtype=jnp.int32) < held_count)[:, None]
    new_master, new_first, new_second = adamw_update(
        master_slots, first_slots, second_slots, owned_grad, weight_decay, learn_rate
    )
    new_master = jnp.where(used_slot, new_master, 0.0)
    new_first = jnp.where(used_slot, new_first, 0.0)
    new_second = jnp.where(used_slot, new_second, 0.0)
    new_norms, new_norm_first, new_norm_second = adamw_update(
        norm_master, norm_first, norm_second, norm_owned, 0.0, norm_rate
    )
    return (
        block_output,
        input_grad,
        new_master,
        new_first,
        new_second,
        new_norms,
        new_norm_first,
        new_norm_second,
    )


W = 128
R = 384
QB = 4
CB = 12
MESH = pl.DeviceIdType.MESH
bf16 = jnp.bfloat16
f32 = jnp.float32


def place(sizes):
    dp = lax.axis_index("dp")
    head = lax.axis_index("head")
    return dp // sizes.y, lax.rem(dp, sizes.y), head // sizes.c, lax.rem(head, sizes.c)


class Sizes:
    z, y, x, c = 4, 2, 2, 2


def device(z, y, x, c):
    return (z * Sizes.y + y, x * Sizes.c + c)


def greet(partners):
    barrier = pltpu.get_barrier_semaphore()
    for partner in partners:
        pl.semaphore_signal(barrier, inc=1, device_id=partner, device_id_type=MESH)
    pl.semaphore_wait(barrier, len(partners))


def block_rows(owners):
    ids = [owners[j] for j in range(owners.shape[0])]
    rows = []
    for j, mine in enumerate(ids):
        row = mine * CAP
        for other in ids[:j]:
            row = row + jnp.where(other == mine, 1, 0)
        rows.append(row)
    return rows


def slot_is_wide(rows, slot_row):
    flag = rows[0] == slot_row
    for row in rows[1:QB]:
        flag = jnp.logical_or(flag, row == slot_row)
    return flag


def dot(left, right):
    return jnp.dot(left, right, preferred_element_type=f32)


def dot_cols(left, right):
    return lax.dot_general(left, right, (((1,), (1,)), ((), ())), preferred_element_type=f32)


def dot_rows(left, right):
    return lax.dot_general(left, right, (((0,), (0,)), ((), ())), preferred_element_type=f32)


def normalise(values):
    centred = values - jnp.mean(values, axis=-1, keepdims=True)
    inverse = lax.rsqrt(jnp.mean(centred * centred, axis=-1, keepdims=True) + norm_eps)
    return centred * inverse, inverse


def panels(ref, h, first, size):
    return jnp.concatenate([ref[h, p, first : first + size, :] for p in range(ref.shape[1])], axis=1)


def cat_pieces(first, size):
    pieces = []
    row = first
    while row < first + size:
        block, inside = divmod(row, R // 4)
        count = min(R // 4 - inside, first + size - row)
        pieces.append((QB + block, inside, row - first, count))
        row += count
    return pieces


RA = 288
GA, GB = 176, 336
TILE = 128


def layer_kernel(
    tok_hbm, cot_hbm, master_hbm, norms_hbm, steps_hbm, bands_hbm, lens_row_hbm, lens_hbm, owners_hbm,
    total, out_all, in_all, norm_total,
    wv, master, flat, mine, meta, norms_v, steps, bands, lens_row, lens, owners, block_at,
    tok, cot, low1, xhat1, inv1, qkv, probs, sums, att, acc, low2, xhat2, inv2, e2, actives, d_qkvs, da, e1,
    out_low, in_low,
    grads, from_core, rxa, sa, rya, sb, ryb, sbx, rxb, fz, rz, norm_part, norm_sum, n_core, n_x, n_y, n_z,
    i_sem, z_s, z_r, ya_s, ya_r, xa_s, xa_r, xb_s, xb_r, yb_s, yb_r, core_s, core_r, m_s, m_r,
    c_s, c_r, zc_s, zc_r, cc_s, cc_r,
    cs, cr, as_, ar, say_s, say_r, sby_s, sby_r, sbx_s, sbx_r, fz_s, fz_r, n_s, n_r, o_s, o_r, o_l,
):
    z, y, x, c = place(Sizes)
    nz = Sizes.z
    dp, head = z * 2 + y, x * 2 + c
    dp_peers = [device(lax.rem(z + k, nz), (y + j) % 2, x, c) for k in range(nz) for j in range(2) if k or j]
    x_peer, y_peer, core_peer = device(z, y, 1 - x, c), device(z, 1 - y, x, c), device(z, y, x, 1 - c)
    peers = dp_peers + [x_peer, core_peer]
    barrier = pltpu.get_barrier_semaphore()
    for peer in peers:
        pl.semaphore_signal(barrier, inc=1, device_id=peer, device_id_type=MESH)

    tokens_here = tok.shape[1]
    items_here = tokens_here // SEQ
    tiles = tokens_here // TILE

    def whose(p):
        return lax.rem(x + p, 2) * 2 + c

    def tokens_of(ref, who):
        return ref.at[pl.ds(pl.multiple_of(who * tokens_here, tokens_here), tokens_here), :]

    fetches = [
        pltpu.make_async_copy(src, dst, i_sem.at[n])
        for n, (src, dst) in enumerate((
            (owners_hbm, owners), (master_hbm, master), (steps_hbm, steps), (bands_hbm, bands),
            (lens_row_hbm, lens_row), (norms_hbm, norms_v), (lens_hbm, lens),
            (tokens_of(tok_hbm, whose(0)), tok.at[0]), (tokens_of(cot_hbm, whose(0)), cot.at[0]),
            (tokens_of(tok_hbm, whose(1)), tok.at[1]), (tokens_of(cot_hbm, whose(1)), cot.at[1]),
        ))
    ]
    for fetch in fetches:
        fetch.start()

    def loop(first, last, body):
        def step(i, _):
            body(i)
            return 0

        lax.fori_loop(first, last, step, 0)

    def remote(src, dst, send, recv, peer):
        return pltpu.make_async_remote_copy(
            src_ref=src, dst_ref=dst, send_sem=send, recv_sem=recv, device_id=peer, device_id_type=MESH
        )

    def same(ref, send, recv, peer):
        return remote(ref, ref, send, recv, peer)

    shard, far = x * 2 + c, (1 - x) * 2 + c
    fetches[0].wait()
    rows = block_rows(owners)
    fetches[1].wait()
    for r in range(CAP):
        flat[...] = master[:, r, :]
        wide = jnp.concatenate([flat[pl.ds(p, W, stride=3), :] for p in range(3)], axis=0)
        narrow = jnp.concatenate([flat[pl.ds(p, R // 4, stride=4), :] for p in range(4)], axis=0)
        wv[shard, dp * CAP + r] = jnp.where(slot_is_wide(rows, dp * CAP + r), wide, narrow).astype(bf16)

    for n in (2, 3, 4, 5):
        fetches[n].wait()
    items = steps.shape[1]
    item_weight = jnp.exp(-2.0 * steps[...].astype(f32) / TSTEPS)
    item_length = lens_row[...].astype(f32)
    table = bands[...] == lax.broadcasted_iota(jnp.int32, (NBANDS, items), 0)
    ones = table.astype(f32)
    mine[...] = jnp.zeros_like(mine)
    mine[0:4, 0 : W // 2] = norms_v[...]
    mine[:, W // 2 : W // 2 + 1] = jnp.sum(ones * (item_weight * item_length), axis=1, keepdims=True)
    mine[:, W // 2 + 1 : W // 2 + 2] = jnp.sum(ones * item_length, axis=1, keepdims=True)
    meta[dp] = mine[...]

    pl.semaphore_wait(barrier, len(peers))

    part_a, part_b, part_ab, part_c = pl.ds(0, GA), pl.ds(GA, GB - GA), pl.ds(0, GB), pl.ds(GB, R - GB)

    def slab(sh, zz, yy, part=slice(None)):
        return wv.at[sh, pl.ds((zz * 2 + yy) * CAP, CAP), part, :]

    def order(k):
        late, low = k // 2, z // 2
        return (1 - late) * (z + k * (1 - 2 * lax.rem(z, 2))) + late * (k + low * (3 - 2 * k))

    up, down, inner = z < nz - 1, z > 0, lax.rem(z, nz - 1) != 0
    own_up = same(slab(shard, z, y, part_ab), z_s.at[0], z_r.at[z], device(z + 1, y, x, c))
    own_down = same(slab(shard, z, y, part_ab), z_s.at[nz], z_r.at[z], device(z - 1, y, x, c))
    pl.when(up)(own_up.start)
    pl.when(down)(own_down.start)

    def meta_copy(k):
        return remote(mine, meta.at[dp], m_s.at[k], m_r.at[k], dp_peers[k])

    for k in range(len(dp_peers)):
        meta_copy(k).start()

    def along_z(k):
        zz = order(k)
        late = k // 2
        goal = (1 - late) * (3 - z) + late * 3 * (z - 1)
        return same(slab(shard, zz, y, part_ab), z_s.at[k], z_r.at[zz], device(goal, y, x, c))

    def both(j, zz):
        return wv.at[lax.rem(x + j, 2) * 2 + c, pl.ds(zz * 2 * CAP, 2 * CAP), part_c, :]

    def last_z(j, n):
        return same(both(j, z), zc_s.at[j, n], zc_r.at[j, n], device(lax.rem(z + n, nz), y, x, c))

    def last_here(j, n):
        zz = lax.rem(z + nz - n, nz)
        return same(both(j, zz), zc_s.at[j, n], zc_r.at[j, n], x_peer)

    def last_core(j, n):
        return same(both(j, lax.rem(z + nz - n, nz)), cc_s.at[j, n], cc_r.at[j, n], core_peer)

    own_c = slab(shard, z, y, part_c)
    c_copies = (
        same(own_c, c_s.at[0], c_r.at[0], y_peer),
        same(own_c, c_s.at[1], c_r.at[1], x_peer),
        same(slab(shard, z, 1 - y, part_c), c_s.at[2], c_r.at[2], x_peer),
    )

    def first_copies(k):
        zz = order(k)
        one, two = slab(shard, zz, y, part_a), slab(shard, zz, y, part_b)
        return (
            same(one, ya_s.at[k], ya_r.at[k], y_peer),
            same(two, xb_s.at[k], xb_r.at[k], x_peer),
            same(two, yb_s.at[k, 0], yb_r.at[k, 0], y_peer),
            same(one, xa_s.at[k, 0], xa_r.at[k, 0], x_peer),
            same(slab(shard, zz, y, part_ab), core_s.at[k, 0], core_r.at[k, 0], core_peer),
        )

    def second_copies(k):
        zz = order(k)
        return (
            same(slab(shard, zz, 1 - y, part_a), xa_s.at[k, 1], xa_r.at[k, 1], x_peer),
            same(slab(far, zz, y, part_b), yb_s.at[k, 1], yb_r.at[k, 1], y_peer),
            same(slab(shard, zz, 1 - y, part_ab), core_s.at[k, 1], core_r.at[k, 1], core_peer),
        )

    def third_copies(k):
        zz = order(k)
        return (
            same(slab(far, zz, y, part_ab), core_s.at[k, 2], core_r.at[k, 2], core_peer),
            same(slab(far, zz, 1 - y, part_ab), core_s.at[k, 3], core_r.at[k, 3], core_peer),
        )

    def gather0(k):
        @pl.when(k > 0)
        def _():
            along_z(k).wait_recv()
            pl.when(inner)(along_z(k).start)

        for copy in first_copies(k):
            copy.start()

    def gather1(k):
        zz = order(k)
        over_x, over_y, core = second_copies(k)
        same(slab(shard, zz, 1 - y, part_a), ya_s.at[k], ya_r.at[k], y_peer).wait_recv()
        over_x.start()
        same(slab(far, zz, y, part_b), xb_s.at[k], xb_r.at[k], x_peer).wait_recv()
        over_y.start()
        same(slab(shard, zz, 1 - y, part_b), yb_s.at[k, 0], yb_r.at[k, 0], y_peer).wait_recv()
        core.start()

    def gather2(k):
        zz = order(k)
        near, apart = third_copies(k)
        same(slab(far, zz, y, part_a), xa_s.at[k, 0], xa_r.at[k, 0], x_peer).wait_recv()
        near.start()
        same(slab(far, zz, 1 - y, part_a), xa_s.at[k, 1], xa_r.at[k, 1], x_peer).wait_recv()
        same(slab(far, zz, 1 - y, part_b), yb_s.at[k, 1], yb_r.at[k, 1], y_peer).wait_recv()
        apart.start()

    c_copies[0].start()
    c_copies[1].start()
    gather0(0)

    def gather_last(n):
        for j in range(2):
            last_here(j, n).wait_recv()
            last_core(j, n).start()

    def find_block(row):
        block = 0
        for j, block_row in enumerate(rows):
            block = block + jnp.where(block_row == row, j, 0)
        block_at[row] = block

    loop(0, nz * 2 * CAP, find_block)
    for k in range(len(dp_peers)):
        meta_copy(k).wait_recv()
    lane = lax.broadcasted_iota(jnp.int32, (8, W), 1)
    chunks = []
    for pair in range(meta.shape[0] // 2):
        chunks.append(jnp.where(lane < W // 2, meta[2 * pair], pltpu.roll(meta[2 * pair + 1], W // 2, 1)))
    norms = jnp.concatenate(chunks, axis=1).astype(bf16).astype(f32)
    gain1, shift1, gain2, shift2 = (norms[i : i + 1, :] for i in range(4))
    band_sums = meta[0]
    for d in range(1, meta.shape[0]):
        band_sums = band_sums + meta[d]
    weight_of = jnp.sum(jnp.where(table, band_sums[:, W // 2 : W // 2 + 1], 0.0), axis=0, keepdims=True)
    count_of = jnp.sum(jnp.where(table, band_sums[:, W // 2 + 1 : W // 2 + 2], 0.0), axis=0, keepdims=True)
    scales = item_weight * count_of / weight_of
    item_lane = lax.broadcasted_iota(jnp.int32, (1, items), 1)
    position = lax.broadcasted_iota(jnp.int32, (TILE, 1), 0)
    for n in range(6, 11):
        fetches[n].wait()

    def tile(t):
        return pl.ds(pl.multiple_of(t * TILE, TILE), TILE)

    def first_norm(i):
        p, t = i // tiles, lax.rem(i, tiles)
        here = tile(t)
        scaled, inverse = normalise(tok[p, here, :])
        xhat1[p, here, :] = scaled
        inv1[p, here, :] = inverse
        low1[p, here, :] = (scaled * gain1 + shift1).astype(bf16)
        item = whose(p) * items_here + t // (SEQ // TILE)
        scale = jnp.sum(jnp.where(item_lane == item, scales, 0.0), axis=1, keepdims=True)
        inside = position + lax.rem(t, SEQ // TILE) * TILE < lens[item]
        scaled_cot = cot[p, here, :] * jnp.where(inside, scale, 0.0)
        cot[p, here, :] = scaled_cot
        e2[p, here, :] = scaled_cot.astype(bf16)

    c_copies[0].wait_recv()
    c_copies[2].start()
    loop(0, 2 * tiles, first_norm)
    c_copies[1].wait_recv()
    c_copies[2].wait_recv()
    for j in range(2):
        last_core(j, 0).start()

    def gather(step):
        pl.when(step < nz)(lambda: gather0(step))

        @pl.when(step == nz - 1)
        def _():
            for j in range(2):
                for n in range(1, nz):
                    last_z(j, n).start()

        pl.when(step <= nz)(lambda: gather1(step - 1))
        pl.when(step >= 2)(lambda: gather2(step - 2))

    loop(1, nz + 2, gather)
    loop(1, nz, gather_last)

    def all_here(k):
        zz = order(k)
        for kind, (xx, yy) in enumerate(((x, y), (x, 1 - y), (1 - x, y), (1 - x, 1 - y))):
            same(slab(xx * 2 + 1 - c, zz, yy, part_ab), core_s.at[k, kind], core_r.at[k, kind], core_peer).wait_recv()
        for j in range(2):
            last_core(j, k).wait_recv()

    loop(0, nz, all_here)

    head_lane = lax.broadcasted_iota(jnp.int32, (1, W), 1)
    head_masks = [head_lane < HD, head_lane >= HD]
    key_pos = lax.broadcasted_iota(jnp.int32, (1, SEQ), 1)
    item_rows = [slice(i * SEQ, (i + 1) * SEQ) for i in range(items_here)]

    def only(values, a):
        return jnp.where(head_masks[a], values, jnp.zeros_like(values))

    def stack(values):
        return jnp.concatenate([only(values, 0), only(values, 1)], axis=0)

    def wide_matrix(h):
        return jnp.concatenate(
            [
                jnp.concatenate([wv[h, rows[j], p * W : (p + 1) * W, :] for j in range(QB)], axis=0)
                for p in range(3)
            ],
            axis=1,
        )

    def narrow_matrix(h, first, size):
        pieces = cat_pieces(first, size)
        return jnp.concatenate(
            [
                jnp.concatenate(
                    [wv[h, rows[b], pl.ds(p * (R // 4) + inside, count), :] for b, inside, _, count in pieces], axis=0
                )
                for p in range(4)
            ],
            axis=1,
        )

    deep, low = (QB + 2, CB - 2), (0, QB + 2)
    x_part, y_part = pl.ds(0, RA), pl.ds(RA, R - RA)

    def core_push(j, n):
        part = pl.ds(*(deep, low)[n])
        return remote(grads.at[j, part], from_core.at[j, part], cs.at[n, j], cr.at[n, j], core_peer)

    def x_push(n):
        part = pl.ds(*(deep, low)[n])
        return remote(grads.at[2, part, x_part, :], rxa.at[part], as_.at[n], ar.at[n], x_peer)

    def hand_over(i, n):
        first, count = (deep, low)[n]
        pl.when(i < 2)(lambda: core_push(i, n).start())

        @pl.when(i >= 2)
        def _():
            core_push(i - 2, n).wait_recv()

            def add(block):
                grads[i, block] = grads[i, block] + from_core[i - 2, block]

            loop(first, first + count, add)
            pl.when(i == 2)(lambda: x_push(n).start())

    pair_z, cross_z = z + 1 - 2 * lax.rem(z, 2), lax.rem(z + 2, nz)

    def chunk(k):
        return lax.rem(pair_z + lax.rem(k, 2) * (z - pair_z) + 2 * (1 - k // 2), nz)

    def block_of(k, yy, r):
        return block_at[(chunk(k) * 2 + yy) * CAP + r]

    def over_y_first(k):
        return remote(sb.at[k], ryb.at[k], sby_s.at[k], sby_r.at[k], y_peer)

    def over_x_last(k):
        return remote(sbx.at[k], rxb.at[k], sbx_s.at[k], sbx_r.at[k], x_peer)

    def over_y_last(k):
        return remote(sa.at[k], rya.at[k], say_s.at[k], say_r.at[k], y_peer)

    def over_z(k, r):
        goal = pair_z + lax.rem(k, 2) * (cross_z - pair_z)
        return remote(fz.at[k, r], rz.at[k, r], fz_s.at[k, r], fz_r.at[k, r], device(goal, y, x, c))

    def norm_copies():
        z_peers = [device(lax.rem(z + k, nz), y, x, c) for k in range(1, nz)]
        return [
            remote(norm_part, n_core, n_s.at[0], n_r.at[0], core_peer),
            remote(norm_sum.at[0], n_x, n_s.at[1], n_r.at[1], x_peer),
            remote(norm_sum.at[1], n_y, n_s.at[2], n_r.at[2], y_peer),
        ] + [remote(norm_sum.at[2], n_z.at[k], n_s.at[3 + k], n_r.at[3 + k], p) for k, p in enumerate(z_peers)]

    def send_b(k):
        for r in range(CAP):
            block = block_of(k, 1 - y, r)
            for j in range(2):
                sb[k, j, r] = grads[2 + j, block, y_part, :]
        over_y_first(k).start()

    def add_x(j):
        grads[3, j, x_part, :] = grads[3, j, x_part, :] + rxa[j]

    def send_a(k):
        for r in range(CAP):
            sa[k, r] = grads[3, block_of(k, 1 - y, r), x_part, :]
        over_y_last(k).start()

    def reduce1(k):
        over_y_first(k).wait_recv()
        for r in range(CAP):
            sbx[k, r] = grads[2, block_of(k, y, r), y_part, :] + ryb[k, 0, r]
        over_x_last(k).start()

    def reduce2(k):
        over_y_last(k).wait_recv()
        over_x_last(k).wait_recv()
        for r in range(CAP):
            block = block_of(k, y, r)
            fz[k, r, x_part, :] = grads[3, block, x_part, :] + rya[k, r]
            part = grads[3, block, y_part, :].astype(f32) + ryb[k, 1, r].astype(f32)
            fz[k, r, y_part, :] = (part + rxb[k, r].astype(f32)).astype(bf16)
            pl.when(lax.rem(k, 2) == 0)(over_z(k, r).start)

    def cross():
        for r in range(CAP):
            over_z(0, r).wait_recv()
            fz[1, r] = fz[1, r] + rz[0, r]
            over_z(1, r).start()

    key_row = lax.broadcasted_iota(jnp.int32, (2 * SEQ, W), 0)
    head_ones = jnp.where((key_row < SEQ) == head_masks[0], 1.0, 0.0).astype(bf16)

    def attention(p, h):
        projected = dot(low1[p], wide_matrix(h))
        qkv[h, 0] = (projected[:, :W].astype(bf16).astype(f32) * (1.0 / math.sqrt(HD))).astype(bf16)
        qkv[h, 1] = projected[:, W : 2 * W].astype(bf16)
        qkv[h, 2] = projected[:, 2 * W :].astype(bf16)
        for i, here in enumerate(item_rows):
            query, key, value = qkv[h, 0, here, :], qkv[h, 1, here, :], qkv[h, 2, here, :]
            valid = key_pos < lens[whose(p) * items_here + i]
            both = []
            for a in range(2):
                scores = jnp.where(valid, dot_cols(only(query, a), key), -1e30)
                exps = jnp.exp(scores - jnp.max(scores, axis=-1, keepdims=True)).astype(bf16)
                probs[h, i, a] = exps
                both.append(exps)
            mixed = dot(jnp.concatenate(both, axis=1), jnp.concatenate([stack(value), head_ones], axis=1))
            inverse = 1.0 / mixed[:, W:]
            sums[h, here, :] = inverse
            att[h, here, :] = (mixed[:, :W] * inverse).astype(bf16)
        acc[...] += dot(att[h], narrow_matrix(h, 0, W))

    def put(i, first, result):
        for block, inside, row, count in cat_pieces(first, result.shape[0]):
            for p in range(4):
                here = pl.ds(p * (R // 4) + inside, count)
                grads[i, block, here, :] = result[row : row + count, p * W : (p + 1) * W].astype(bf16)

    def shard_of(p, i):
        return lax.rem(1 + x + p + i, 2) * 2 + lax.rem(c + 1 + i // 2, 2)

    def feed_forward(p, i):
        h = shard_of(p, i)
        up_matrix, down_matrix = narrow_matrix(h, W, D), narrow_matrix(h, W + D, D)
        hidden = dot(low2[...], up_matrix)
        root = math.sqrt(2.0 / math.pi)
        square = hidden * hidden
        bend = jnp.tanh(root * hidden * (1.0 + 0.044715 * square))
        half = 0.5 * (1.0 + bend)
        active = (hidden * half).astype(bf16)
        slope = half + 0.5 * hidden * (1.0 - bend * bend) * (root + (3.0 * 0.044715 * root) * square)
        if p == 0:
            actives[i] = active
        else:
            acc[...] += dot(active, down_matrix)
        back = (dot_cols(e2[p], down_matrix) * slope).astype(bf16)
        da[...] += dot_cols(back, up_matrix)
        if p == 0:
            put(i, W + D, dot_rows(active, e2[p]))
            put(i, W, dot_rows(low2[...], back))
            hand_over(i, 0)

    def attention_back(p, i):
        h = shard_of(p, i)
        d_all = dot_cols(e1[...], narrow_matrix(h, 0, W)) * sums[h]
        shared_all = (d_all * att[h].astype(f32)).astype(bf16)
        d_all = d_all.astype(bf16)
        parts = []
        for m, here in enumerate(item_rows):
            query, key, value = qkv[h, 0, here, :], qkv[h, 1, here, :], qkv[h, 2, here, :]
            d_here, shared = d_all[here, :], shared_all[here, :]
            against = jnp.concatenate([value, jnp.full((SEQ, W), -1.0, bf16)], axis=1)
            d_scores = []
            for a in range(2):
                change = dot_cols(jnp.concatenate([only(d_here, a), only(shared, a)], axis=1), against)
                d_scores.append((probs[h, m, a].astype(f32) * change).astype(bf16))
            d_query = dot(jnp.concatenate(d_scores, axis=1), stack(key)) * (1.0 / math.sqrt(HD))
            d_key = dot_rows(jnp.concatenate(d_scores, axis=0), stack(query))
            d_value = dot_rows(jnp.concatenate([probs[h, m, 0], probs[h, m, 1]], axis=0), stack(d_here))
            parts.append(jnp.concatenate([d_query, d_key, d_value], axis=1).astype(bf16))
        d_qkv = jnp.concatenate(parts, axis=0)
        if p == 0:
            d_qkvs[i] = d_qkv
            put(i, 0, dot_rows(att[h], e1[...]))
            d_weight = dot_rows(low1[p], d_qkv).astype(bf16)
            for j in range(QB):
                for m in range(3):
                    grads[i, j, m * W : (m + 1) * W, :] = d_weight[j * W : (j + 1) * W, m * W : (m + 1) * W]
            hand_over(i, 1)
        else:
            da[...] += dot_cols(d_qkv, wide_matrix(h))

    def late_output(i):
        acc[...] += dot(actives[i], narrow_matrix(shard_of(0, i), W + D, D))

    def late_input(i):
        da[...] += dot_cols(d_qkvs[i], wide_matrix(shard_of(0, i)))

    def norm_backward(grad, scaled, inverse, gain):
        grad_scaled = grad * gain
        centre = jnp.mean(grad_scaled, axis=-1, keepdims=True)
        slope = jnp.mean(grad_scaled * scaled, axis=-1, keepdims=True)
        return inverse * (grad_scaled - centre - scaled * slope)

    def add_norm(p, row, grad, scaled):
        if p == 0:
            norm_part[row : row + 1, :] += jnp.sum(grad * scaled, axis=0, keepdims=True)
            norm_part[row + 1 : row + 2, :] += jnp.sum(grad, axis=0, keepdims=True)

    norm_part[...] = jnp.zeros_like(norm_part)

    def out_copies(p, n):
        src, dst = ((out_low, out_all), (in_low, in_all))[n]
        there = tokens_of(dst, whose(p))
        return (
            pltpu.make_async_copy(src.at[p], there, o_l.at[p, n]),
            remote(src.at[p], there, o_s.at[p, n], o_r.at[p, n], core_peer),
        )

    def block_result(p):
        out_low[p] = acc[...].astype(bf16)
        for copy in out_copies(p, 0):
            copy.start()

    def input_result(p):
        def first_norm_back(t):
            here = tile(t)
            grad, scaled = da[here, :], xhat1[p, here, :]
            add_norm(p, 0, grad, scaled)
            in_low[p, here, :] = (cot[p, here, :] + norm_backward(grad, scaled, inv1[p, here, :], gain1)).astype(bf16)

        loop(0, tiles, first_norm_back)
        for copy in out_copies(p, 1):
            copy.start()

    def layer_pass(p):
        acc[...] = jnp.zeros_like(acc)
        loop(0, 4, lambda h: attention(p, h))

        def second_norm(t):
            here = tile(t)
            state = acc[here, :] + tok[p, here, :]
            acc[here, :] = state
            scaled, inverse = normalise(state)
            xhat2[here, :] = scaled
            inv2[here, :] = inverse
            low2[here, :] = (scaled * gain2 + shift2).astype(bf16)
            da[here, :] = jnp.zeros((TILE, D), f32)

        loop(0, tiles, second_norm)
        loop(0, 4, lambda i: feed_forward(p, i))
        if p == 1:
            block_result(1)
            for n in range(2):
                x_push(n).wait_recv()
            loop(0, QB + CB, add_x)
            loop(0, nz, send_a)
            loop(0, nz, reduce1)
            norm_copies()[0].wait_recv()
            norm_sum[0] = norm_part[...] + n_core[...]
            norm_copies()[1].start()

        def second_norm_back(t):
            here = tile(t)
            grad, scaled = da[here, :], xhat2[here, :]
            add_norm(p, 2, grad, scaled)
            change = cot[p, here, :] + norm_backward(grad, scaled, inv2[here, :], gain2)
            cot[p, here, :] = change
            e1[here, :] = change.astype(bf16)
            da[here, :] = jnp.zeros((TILE, D), f32)

        loop(0, tiles, second_norm_back)
        if p == 1:
            norm_copies()[1].wait_recv()
            norm_sum[1] = norm_sum[0] + n_x[...]
            norm_copies()[2].start()
            reduce2(0)

        def attention_step(i):
            attention_back(p, i)
            if p == 1:
                pl.when(i == 0)(lambda: reduce2(1))

                @pl.when(i == 1)
                def _():
                    cross()
                    reduce2(2)

        loop(0, 4, attention_step)

    layer_pass(0)
    loop(0, nz, send_b)
    loop(0, 4, late_output)
    block_result(0)
    loop(0, 4, late_input)
    input_result(0)
    norm_copies()[0].start()
    layer_pass(1)
    input_result(1)
    norm_copies()[2].wait_recv()
    norm_sum[2] = norm_sum[1] + n_y[...]
    for copy in norm_copies()[3:]:
        copy.start()
    reduce2(nz - 1)

    for k in range(nz - 1):
        norm_copies()[3 + k].wait_recv()
    for r in range(CAP):
        over_z(2, r).wait_recv()
        over_z(1, r).wait_recv()
    norm_total[...] = norm_sum[2] + ((n_z[0] + n_z[1]) + n_z[2])

    def last(r):
        others = rz[1, r].astype(f32) + rz[2, r].astype(f32)
        total[r] = fz[nz - 1, r].astype(f32) + others

    loop(0, CAP, last)

    for p in range(2):
        for n in range(2):
            local, over_core = out_copies(p, n)
            local.wait()
            over_core.wait()
    for copy in norm_copies():
        copy.wait_send()
    for k in range(len(dp_peers)):
        meta_copy(k).wait_send()
    pl.when(up)(own_up.wait_send)
    pl.when(down)(own_down.wait_send)
    for copy in c_copies:
        copy.wait_send()

    def sent(k):
        for copy in first_copies(k) + second_copies(k) + third_copies(k):
            copy.wait_send()
        pl.when(jnp.logical_and(k > 0, inner))(along_z(k).wait_send)
        for j in range(2):
            last_core(j, k).wait_send()
            pl.when(k > 0)(last_z(j, k).wait_send)
        for copy in (over_y_first(k), over_x_last(k), over_y_last(k)):
            copy.wait_send()
        for r in range(CAP):
            pl.when(k < nz - 1)(over_z(k, r).wait_send)

    loop(0, nz, sent)
    for n in range(2):
        x_push(n).wait_send()
        for j in range(2):
            core_push(j, n).wait_send()


def layer(tokens, cotangent, master, norms, steps, bands, lens_row, lens, owners):
    nz = Sizes.z
    here = tokens.shape[0] // lax.axis_size("head")
    items_here = here // SEQ
    items = lens.shape[0]
    vm = pl.BlockSpec(memory_space=pltpu.VMEM)
    hbm = pl.BlockSpec(memory_space=pltpu.HBM)
    dma = pltpu.SemaphoreType.DMA
    V, S = pltpu.VMEM, pltpu.SMEM
    square = (here, D)
    blocks = QB + CB
    rb = R - RA
    low, full, two_low, two = V(square, bf16), V(square, f32), V((2, *square), bf16), V((2, *square), f32)
    scratch = [
        V((4, nz * 2 * CAP, R, W), bf16), V((R, CAP, W), f32), V((R, W), f32),
        V((8, W), f32), V((nz * 2, 8, W), f32), V(norms.shape, f32),
        V((1, items), jnp.int32), V((1, items), jnp.int32), V((1, items), jnp.int32),
        S((items,), jnp.int32), S(owners.shape, jnp.int32), S((nz * 2 * CAP,), jnp.int32),
        two, two, two_low, two, V((2, here, 1), f32), V((4, 3, here, W), bf16),
        V((4, items_here, 2, SEQ, SEQ), bf16), V((4, here, W), f32), V((4, here, W), bf16),
        full, low, full, V((here, 1), f32), two_low,
        V((4, here, D), bf16), V((4, here, 3 * W), bf16), full, low, two_low, two_low,
        V((4, blocks, R, W), bf16), V((2, blocks, R, W), bf16),
        V((blocks, RA, W), bf16), V((nz, CAP, RA, W), bf16), V((nz, CAP, RA, W), bf16),
        V((nz, 2, CAP, rb, W), bf16), V((nz, 2, CAP, rb, W), bf16), V((nz, CAP, rb, W), bf16),
        V((nz, CAP, rb, W), bf16), V((nz, CAP, R, W), bf16), V((nz - 1, CAP, R, W), bf16),
        V((8, D), f32), V((3, 8, D), f32), V((8, D), f32), V((8, D), f32), V((8, D), f32), V((nz - 1, 8, D), f32),
        dma((11,)), dma((nz + 1,)), dma((nz,)), dma((nz,)), dma((nz,)), dma((nz, 2)), dma((nz, 2)), dma((nz,)), dma((nz,)),
        dma((nz, 2)), dma((nz, 2)), dma((nz, 4)), dma((nz, 4)), dma((8,)), dma((8,)),
        dma((3,)), dma((3,)), dma((2, nz)), dma((2, nz)), dma((2, nz)), dma((2, nz)),
        dma((2, 2)), dma((2, 2)), dma((2,)), dma((2,)), dma((nz,)), dma((nz,)), dma((nz,)), dma((nz,)),
        dma((nz,)), dma((nz,)), dma((nz, CAP)), dma((nz, CAP)), dma((8,)), dma((8,)), dma((2, 2)), dma((2, 2)), dma((2, 2)),
    ]
    return pl.pallas_call(
        layer_kernel,
        name="layer",
        out_shape=(
            jax.ShapeDtypeStruct((CAP, R, W), f32),
            jax.ShapeDtypeStruct(tokens.shape, bf16),
            jax.ShapeDtypeStruct(tokens.shape, bf16),
            jax.ShapeDtypeStruct((8, D), f32),
        ),
        in_specs=[hbm] * 9,
        out_specs=(vm, hbm, hbm, vm),
        scratch_shapes=scratch,
        compiler_params=pltpu.CompilerParams(collective_id=0, has_side_effects=True, vmem_limit_bytes=56 << 20),
    )(tokens, cotangent, master, norms, steps, bands, lens_row, lens, owners)


def finish_kernel(
    total_hbm, norm_hbm, master_hbm, first_hbm, second_hbm, norm_m, norm_f, norm_s, owners_hbm, out_all, in_all,
    block_output, input_grad, new_master, new_first, new_second, new_norm, new_norm_first, new_norm_second,
    out_low, in_low, out_full, in_full, states, results, flat, grad, total, norm_total, norm_master, norm_first, norm_second, owners, l_sem, s_sem, i_sem, r_sem,
):
    pieces = l_sem.shape[1]
    size = out_low.shape[0] // pieces
    pairs = ((out_all, out_low, out_full, block_output), (in_all, in_low, in_full, input_grad))

    def piece(p):
        return pl.ds(pl.multiple_of(p * size, size), size)

    def fetch(n, p):
        return pltpu.make_async_copy(pairs[n][0].at[piece(p), :], pairs[n][1].at[piece(p), :], l_sem.at[n, p])

    def store(n, p):
        return pltpu.make_async_copy(pairs[n][2].at[piece(p), :], pairs[n][3].at[piece(p), :], s_sem.at[n, p])

    small_copies = [
        pltpu.make_async_copy(src, dst, i_sem.at[3 + i])
        for i, (src, dst) in enumerate((
            (owners_hbm, owners), (total_hbm, total), (norm_hbm, norm_total),
            (norm_m, norm_master), (norm_f, norm_first), (norm_s, norm_second),
        ))
    ]
    state_copies = [
        pltpu.make_async_copy(src, states.at[i], i_sem.at[i]) for i, src in enumerate((master_hbm, first_hbm, second_hbm))
    ]
    result_copies = [
        pltpu.make_async_copy(results.at[i], dst, r_sem.at[i]) for i, dst in enumerate((new_master, new_first, new_second))
    ]

    def loop(count, body):
        def step(i, _):
            body(i)
            return 0

        lax.fori_loop(0, count, step, 0)

    for copy in small_copies:
        copy.start()
    loop(pieces, lambda p: fetch(0, p).start())
    for copy in state_copies:
        copy.start()
    loop(pieces, lambda p: fetch(1, p).start())

    dp = lax.axis_index("dp")
    small_copies[0].wait()
    rows = block_rows(owners)
    held = 0
    for j in range(owners.shape[0]):
        held = held + jnp.where(owners[j] == dp, 1, 0)

    def spread(r):
        is_wide = slot_is_wide(rows, dp * CAP + r)

        @pl.when(is_wide)
        def _():
            for p in range(3):
                flat[pl.ds(p, W, stride=3), :] = total[r, p * W : (p + 1) * W, :]

        @pl.when(jnp.logical_not(is_wide))
        def _():
            for p in range(4):
                flat[pl.ds(p, R // 4, stride=4), :] = total[r, p * (R // 4) : (p + 1) * (R // 4), :]

    small_copies[1].wait()
    for r in range(CAP):
        spread(r)
        grad[:, r, :] = flat[...]

    def convert(n, p):
        fetch(n, p).wait()
        _, low, full, _ = pairs[n]
        full[piece(p), :] = low[piece(p), :].astype(f32)
        store(n, p).start()

    loop(pieces, lambda p: convert(0, p))
    for copy in state_copies:
        copy.wait()
    step = 32
    slot = lax.broadcasted_iota(jnp.int32, (step, CAP, W), 1)

    def update(i):
        here = pl.ds(pl.multiple_of(i * step, step), step)
        new = adamw_update(states[0, here], states[1, here], states[2, here], grad[here], weight_decay, learn_rate)
        for n in range(3):
            results[n, here] = jnp.where(slot < held, new[n], 0.0)

    loop(R // step, update)
    for copy in result_copies:
        copy.start()
    for copy in small_copies[2:]:
        copy.wait()
    pair = norm_total[:, pl.ds(pl.multiple_of((dp // 2) * W, W), W)]
    mine = jnp.where(lax.rem(dp, 2) == 1, pltpu.roll(pair, W // 2, 1), pair)[0:4, 0 : norm_master.shape[1]]
    new = adamw_update(norm_master[...], norm_first[...], norm_second[...], mine, 0.0, norm_rate)
    for ref, value in zip((new_norm, new_norm_first, new_norm_second), new):
        ref[...] = value
    loop(pieces, lambda p: convert(1, p))
    for n in range(2):
        loop(pieces, lambda p: store(n, p).wait())
    for copy in result_copies:
        copy.wait()


def finish(total, norm_total, slots, norms, owners, out_all, in_all):
    vm = pl.BlockSpec(memory_space=pltpu.VMEM)
    hbm = pl.BlockSpec(memory_space=pltpu.HBM)
    dma = pltpu.SemaphoreType.DMA
    V = pltpu.VMEM
    pieces = 8
    shape = out_all.shape
    return pl.pallas_call(
        finish_kernel,
        name="finish",
        out_shape=(
            (jax.ShapeDtypeStruct(shape, f32),) * 2 + tuple(jax.ShapeDtypeStruct(a.shape, f32) for a in slots + norms)
        ),
        in_specs=[hbm] * 11,
        out_specs=(hbm,) * 5 + (vm,) * 3,
        scratch_shapes=[
            V(shape, bf16), V(shape, bf16), V(shape, f32), V(shape, f32), V((3, R, CAP, W), f32), V((3, R, CAP, W), f32),
            V((R, W), f32), V((R, CAP, W), f32),
            V(total.shape, f32), V(norm_total.shape, f32), *(V(a.shape, f32) for a in norms),
            pltpu.SMEM(owners.shape, jnp.int32), dma((2, pieces)), dma((2, pieces)), dma((9,)), dma((3,)),
        ],
        compiler_params=pltpu.CompilerParams(vmem_limit_bytes=60 << 20),
    )(total, norm_total, *slots, *norms, owners, out_all, in_all)


def fast_shards(
    tokens, cotangent, timesteps, bands, lengths, owners,
    master_slots, first_slots, second_slots, norm_master, norm_first, norm_second,
):
    def tiles(slots):
        return jnp.transpose(slots.reshape(CAP, R, W), (1, 0, 2))

    def flat(slots):
        return jnp.transpose(slots, (1, 0, 2)).reshape(CAP, R * W)

    steps, bands_row, lens_row = (v.reshape(1, -1) for v in (timesteps, bands, lengths))
    slots = tuple(tiles(s) for s in (master_slots, first_slots, second_slots))
    norms = (norm_master, norm_first, norm_second)
    total, out_all, in_all, norm_total = layer(
        tokens, cotangent, slots[0], norm_master, steps, bands_row, lens_row, lengths, owners
    )
    results = finish(total, norm_total, slots, norms, owners, out_all, in_all)
    return (*results[:2], *(flat(s) for s in results[2:5]), *results[5:])


def solution(mesh):
    fits = dict(mesh.shape) == {"dp": 8, "head": 4}
    placed = (
        P("dp", None),
        P("dp", None),
        P("dp"),
        P("dp"),
        P("dp"),
        P(),
        P("dp", "head"),
        P("dp", "head"),
        P("dp", "head"),
        P(None, "dp"),
        P(None, "dp"),
        P(None, "dp"),
    )
    return jax.shard_map(
        fast_shards if fits else shards,
        mesh=mesh,
        in_specs=placed,
        out_specs=(
            P("dp", None),
            P("dp", None),
            P("dp", "head"),
            P("dp", "head"),
            P("dp", "head"),
            P(None, "dp"),
            P(None, "dp"),
            P(None, "dp"),
        ),
        check_vma=False,
    )
```

```python
import math

import jax
import jax.numpy as jnp
from jax import lax
from jax.experimental import pallas as pl
from jax.experimental.pallas import tpu as pltpu
from jax.sharding import PartitionSpec as P

D = 512
H = 8
HD = 64
FF = 2048
SEQ = 256
TSTEPS = 1000
NBANDS = 8
CAP = 3
STEP = 5


beta_one = 0.5
beta_two = 0.5
learn_rate = 0.04
norm_rate = 0.4
weight_decay = 0.1
adam_eps = 1e-08
norm_eps = 1e-05


def contract_rows(left_side, right_side):
    return lax.dot_general(
        left_side, right_side, (((0,), (0,)), ((), ())), preferred_element_type=jnp.float32
    )


def contract_cols(left_side, right_side):
    return lax.dot_general(
        left_side, right_side, (((1,), (1,)), ((), ())), preferred_element_type=jnp.float32
    )


def gelu_tanh(values):
    return jax.nn.gelu(values, approximate=True)


def norm_forward(values, gain_row, shift_row):
    average = jnp.mean(values, axis=-1, keepdims=True)
    centred = values - average
    inverse = lax.rsqrt(jnp.mean(centred * centred, axis=-1, keepdims=True) + norm_eps)
    scaled = centred * inverse
    return (scaled * gain_row + shift_row, scaled, inverse)


def norm_backward(grad_normed, scaled, inverse, gain_row):
    grad_scaled = grad_normed * gain_row
    centre_term = jnp.mean(grad_scaled, axis=-1, keepdims=True)
    slope_term = jnp.mean(grad_scaled * scaled, axis=-1, keepdims=True)
    return inverse * (grad_scaled - centre_term - scaled * slope_term)


def slot_rows(owners, capacity):
    block_index = jnp.arange(owners.shape[0], dtype=jnp.int32)
    earlier = (owners[None, :] == owners[:, None]) & (block_index[None, :] < block_index[:, None])
    return owners * capacity + jnp.sum(earlier.astype(jnp.int32), axis=1)


def attention_scores(query_heads, key_heads, key_valid):
    scores = jnp.einsum(
        "gqad,gkad->gaqk", query_heads, key_heads, preferred_element_type=jnp.float32
    ) / math.sqrt(HD)
    return jnp.where(key_valid[:, None, None, :], scores, -1e30)


def adamw_update(weight, first_moment, second, gradient, decay_rate, step_rate):
    new_first = beta_one * first_moment + (1.0 - beta_one) * gradient
    new_second = beta_two * second + (1.0 - beta_two) * gradient * gradient
    first_hat = new_first / (1.0 - beta_one**STEP)
    second_hat = new_second / (1.0 - beta_two**STEP)
    new_weight = weight - step_rate * (
        first_hat / (jnp.sqrt(second_hat) + adam_eps) + decay_rate * weight
    )
    return (new_weight, new_first, new_second)


def shards(
    tokens,
    cotangent,
    timesteps,
    bands,
    lengths,
    owners,
    master_slots,
    first_slots,
    second_slots,
    norm_master,
    norm_first,
    norm_second,
):
    head_count = lax.axis_size("head")
    owner_index = lax.axis_index("dp")
    heads_here = H // head_count
    width_here = heads_here * HD
    units_here = FF // head_count
    block_len = master_slots.shape[1]
    norm_cols = norm_master.shape[1]
    row_count = tokens.shape[0]
    item_count = lengths.shape[0]
    block_count = owners.shape[0]
    slot_row = slot_rows(owners, CAP)
    gathered, norm_whole = (
        lax.all_gather(master_slots.astype(jnp.bfloat16), "dp", axis=0, tiled=True),
        lax.all_gather(norm_master.astype(jnp.bfloat16), "dp", axis=1, tiled=True),
    )
    flat_params = gathered[slot_row].reshape(-1)
    qkv_end = 3 * D * width_here
    out_end = qkv_end + width_here * D
    up_end = out_end + D * units_here
    qkv_weight = flat_params[:qkv_end].reshape(D, 3 * width_here)
    out_weight = flat_params[qkv_end:out_end].reshape(width_here, D)
    up_weight = flat_params[out_end:up_end].reshape(D, units_here)
    down_weight = flat_params[up_end:].reshape(units_here, D)
    norm_params = norm_whole.astype(jnp.float32)
    item_weight = jnp.exp(-2.0 * timesteps.astype(jnp.float32) / TSTEPS)
    item_length = lengths.astype(jnp.float32)
    band_table = (bands[:, None] == jnp.arange(NBANDS, dtype=jnp.int32)[None, :]).astype(
        jnp.float32
    )
    weight_sums, count_sums = lax.psum(
        (
            jnp.sum(band_table * (item_weight * item_length)[:, None], axis=0),
            jnp.sum(band_table * item_length[:, None], axis=0),
        ),
        "dp",
    )
    item_scale = (
        item_weight
        * jnp.sum(band_table * count_sums[None, :], axis=1)
        / jnp.sum(band_table * weight_sums[None, :], axis=1)
    )
    key_valid = jnp.arange(SEQ, dtype=jnp.int32)[None, :] < lengths[:, None]
    token_scale = jnp.where(key_valid, item_scale[:, None], 0.0).reshape(row_count)
    normed_one, scaled_one, inverse_one = norm_forward(tokens, norm_params[0], norm_params[1])
    normed_one_low = normed_one.astype(jnp.bfloat16)
    projected_low = jnp.dot(normed_one_low, qkv_weight, preferred_element_type=jnp.float32).astype(
        jnp.bfloat16
    )
    head_shape = (item_count, SEQ, heads_here, HD)
    query_heads = projected_low[:, :width_here].reshape(head_shape)
    key_heads = projected_low[:, width_here : 2 * width_here].reshape(head_shape)
    value_heads = projected_low[:, 2 * width_here :].reshape(head_shape)
    scores = attention_scores(query_heads, key_heads, key_valid)
    row_max = jnp.max(scores, axis=-1, keepdims=True)
    exp_scores = jnp.exp(scores - row_max)
    row_total = jnp.sum(exp_scores, axis=-1, keepdims=True)
    log_total = row_max + jnp.log(row_total)
    prob_low = (exp_scores / row_total).astype(jnp.bfloat16)
    attended_low = (
        jnp.einsum("gaqk,gkad->gqad", prob_low, value_heads, preferred_element_type=jnp.float32)
        .astype(jnp.bfloat16)
        .reshape(row_count, width_here)
    )
    attn_sum = lax.psum(
        jnp.dot(attended_low, out_weight, preferred_element_type=jnp.float32).astype(jnp.bfloat16),
        "head",
    ).astype(jnp.float32)
    mixed_state = tokens + attn_sum
    normed_two, scaled_two, inverse_two = norm_forward(mixed_state, norm_params[2], norm_params[3])
    normed_two_low = normed_two.astype(jnp.bfloat16)
    hidden = jnp.dot(normed_two_low, up_weight, preferred_element_type=jnp.float32)
    activated, gelu_pull = jax.vjp(gelu_tanh, hidden)
    activated_low = activated.astype(jnp.bfloat16)
    ffn_sum = lax.psum(
        jnp.dot(activated_low, down_weight, preferred_element_type=jnp.float32).astype(
            jnp.bfloat16
        ),
        "head",
    ).astype(jnp.float32)
    block_output = mixed_state + ffn_sum
    grad_state = cotangent * token_scale[:, None]
    grad_low_two = grad_state.astype(jnp.bfloat16)
    grad_down = contract_rows(activated_low, grad_low_two)
    grad_activated = contract_cols(grad_low_two, down_weight)
    grad_hidden_low = gelu_pull(grad_activated)[0].astype(jnp.bfloat16)
    grad_up = contract_rows(normed_two_low, grad_hidden_low)
    grad_normed_two = lax.psum(
        contract_cols(grad_hidden_low, up_weight).astype(jnp.bfloat16), "head"
    ).astype(jnp.float32)
    grad_mixed = grad_state + norm_backward(
        grad_normed_two, scaled_two, inverse_two, norm_params[2]
    )
    grad_low_one = grad_mixed.astype(jnp.bfloat16)
    grad_out_proj = contract_rows(attended_low, grad_low_one)
    grad_attended_low = (
        contract_cols(grad_low_one, out_weight).astype(jnp.bfloat16).reshape(head_shape)
    )
    scores_again = attention_scores(query_heads, key_heads, key_valid)
    probabilities = jnp.exp(scores_again - log_total)
    prob_again_low = probabilities.astype(jnp.bfloat16)
    grad_values = jnp.einsum(
        "gaqk,gqad->gkad", prob_again_low, grad_attended_low, preferred_element_type=jnp.float32
    )
    grad_probs = jnp.einsum(
        "gqad,gkad->gaqk", grad_attended_low, value_heads, preferred_element_type=jnp.float32
    )
    grad_scores_low = (
        probabilities * (grad_probs - jnp.sum(grad_probs * probabilities, axis=-1, keepdims=True))
    ).astype(jnp.bfloat16)
    grad_queries = jnp.einsum(
        "gaqk,gkad->gqad", grad_scores_low, key_heads, preferred_element_type=jnp.float32
    ) / math.sqrt(HD)
    grad_keys = jnp.einsum(
        "gaqk,gqad->gkad", grad_scores_low, query_heads, preferred_element_type=jnp.float32
    ) / math.sqrt(HD)
    grad_projected_low = jnp.concatenate(
        [
            grad_queries.reshape(row_count, width_here),
            grad_keys.reshape(row_count, width_here),
            grad_values.reshape(row_count, width_here),
        ],
        axis=1,
    ).astype(jnp.bfloat16)
    grad_qkv = contract_rows(normed_one_low, grad_projected_low)
    grad_normed_one = lax.psum(
        contract_cols(grad_projected_low, qkv_weight).astype(jnp.bfloat16), "head"
    ).astype(jnp.float32)
    input_grad = grad_mixed + norm_backward(
        grad_normed_one, scaled_one, inverse_one, norm_params[0]
    )
    norm_grads = jnp.stack(
        [
            jnp.sum(grad_normed_one * scaled_one, axis=0),
            jnp.sum(grad_normed_one, axis=0),
            jnp.sum(grad_normed_two * scaled_two, axis=0),
            jnp.sum(grad_normed_two, axis=0),
        ]
    )
    grad_blocks = jnp.concatenate(
        [
            grad_qkv.reshape(-1),
            grad_out_proj.reshape(-1),
            grad_up.reshape(-1),
            grad_down.reshape(-1),
        ]
    ).reshape(block_count, block_len)
    summed, norm_summed = (
        lax.psum(grad_blocks.astype(jnp.bfloat16), "dp").astype(jnp.float32),
        lax.psum(norm_grads.astype(jnp.bfloat16), "dp").astype(jnp.float32),
    )
    landing = jnp.where(owners == owner_index, slot_row - owner_index * CAP, CAP)
    owned_grad = jnp.zeros((CAP, block_len), jnp.float32).at[landing].set(summed, mode="drop")
    norm_owned = lax.dynamic_slice_in_dim(norm_summed, owner_index * norm_cols, norm_cols, 1)
    held_count = jnp.sum((owners == owner_index).astype(jnp.int32))
    used_slot = (jnp.arange(CAP, dtype=jnp.int32) < held_count)[:, None]
    new_master, new_first, new_second = adamw_update(
        master_slots, first_slots, second_slots, owned_grad, weight_decay, learn_rate
    )
    new_master = jnp.where(used_slot, new_master, 0.0)
    new_first = jnp.where(used_slot, new_first, 0.0)
    new_second = jnp.where(used_slot, new_second, 0.0)
    new_norms, new_norm_first, new_norm_second = adamw_update(
        norm_master, norm_first, norm_second, norm_owned, 0.0, norm_rate
    )
    return (
        block_output,
        input_grad,
        new_master,
        new_first,
        new_second,
        new_norms,
        new_norm_first,
        new_norm_second,
    )


W = 128
R = 384
QB = 4
CB = 12
MESH = pl.DeviceIdType.MESH
bf16 = jnp.bfloat16
f32 = jnp.float32


def place(sizes):
    dp = lax.axis_index("dp")
    head = lax.axis_index("head")
    return dp // sizes.y, lax.rem(dp, sizes.y), head // sizes.c, lax.rem(head, sizes.c)


class Sizes:
    z, y, x, c = 4, 2, 2, 2


def device(z, y, x, c):
    return (z * Sizes.y + y, x * Sizes.c + c)


def greet(partners):
    barrier = pltpu.get_barrier_semaphore()
    for partner in partners:
        pl.semaphore_signal(barrier, inc=1, device_id=partner, device_id_type=MESH)
    pl.semaphore_wait(barrier, len(partners))


def block_rows(owners):
    ids = [owners[j] for j in range(owners.shape[0])]
    rows = []
    for j, mine in enumerate(ids):
        row = mine * CAP
        for other in ids[:j]:
            row = row + jnp.where(other == mine, 1, 0)
        rows.append(row)
    return rows


def slot_is_wide(rows, slot_row):
    flag = rows[0] == slot_row
    for row in rows[1:QB]:
        flag = jnp.logical_or(flag, row == slot_row)
    return flag


def dot(left, right):
    return jnp.dot(left, right, preferred_element_type=f32)


def dot_cols(left, right):
    return lax.dot_general(left, right, (((1,), (1,)), ((), ())), preferred_element_type=f32)


def dot_rows(left, right):
    return lax.dot_general(left, right, (((0,), (0,)), ((), ())), preferred_element_type=f32)


def normalise(values):
    centred = values - jnp.mean(values, axis=-1, keepdims=True)
    inverse = lax.rsqrt(jnp.mean(centred * centred, axis=-1, keepdims=True) + norm_eps)
    return centred * inverse, inverse


def panels(ref, h, first, size):
    return jnp.concatenate([ref[h, p, first : first + size, :] for p in range(ref.shape[1])], axis=1)


def cat_pieces(first, size):
    pieces = []
    row = first
    while row < first + size:
        block, inside = divmod(row, R // 4)
        count = min(R // 4 - inside, first + size - row)
        pieces.append((QB + block, inside, row - first, count))
        row += count
    return pieces


RA, RB = 192, 288
GA, GB = 176, 336
TILE = 128


def layer_kernel(
    tok_hbm, cot_hbm, master_hbm, norms_hbm, steps_hbm, bands_hbm, lens_row_hbm, lens_hbm, owners_hbm,
    total, out_all, in_all, norm_total,
    wv, master, flat, mine, meta, norms_v, steps, bands, lens_row, lens, owners, block_at,
    tok, cot, low1, xhat1, inv1, qkv, probs, sums, att, acc, low2, xhat2, inv2, e2, actives, d_qkvs, da, e1,
    out_low, in_low,
    grads, from_core, rxa, sa, rya, sb, ryb, sbx, rxb, fz, rz, sc, rc, ryc, rxc, norm_part, norm_sum, n_core, n_x, n_y, n_z,
    i_sem, z_s, z_r, ya_s, ya_r, xa_s, xa_r, xb_s, xb_r, yb_s, yb_r, core_s, core_r, m_s, m_r,
    c_s, c_r, zc_s, zc_r, cc_s, cc_r, sc_s, sc_r, cy_s, cy_r, cx_s, cx_r,
    cs, cr, as_, ar, say_s, say_r, sby_s, sby_r, sbx_s, sbx_r, fz_s, fz_r, n_s, n_r, o_s, o_r, o_l,
):
    z, y, x, c = place(Sizes)
    nz = Sizes.z
    dp, head = z * 2 + y, x * 2 + c
    dp_peers = [device(lax.rem(z + k, nz), (y + j) % 2, x, c) for k in range(nz) for j in range(2) if k or j]
    x_peer, y_peer, core_peer = device(z, y, 1 - x, c), device(z, 1 - y, x, c), device(z, y, x, 1 - c)
    peers = dp_peers + [x_peer, core_peer]
    barrier = pltpu.get_barrier_semaphore()
    for peer in peers:
        pl.semaphore_signal(barrier, inc=1, device_id=peer, device_id_type=MESH)

    tokens_here = tok.shape[1]
    items_here = tokens_here // SEQ
    tiles = tokens_here // TILE

    def whose(p):
        return lax.rem(x + p, 2) * 2 + c

    def tokens_of(ref, who):
        return ref.at[pl.ds(pl.multiple_of(who * tokens_here, tokens_here), tokens_here), :]

    fetches = [
        pltpu.make_async_copy(src, dst, i_sem.at[n])
        for n, (src, dst) in enumerate((
            (owners_hbm, owners), (master_hbm, master), (steps_hbm, steps), (bands_hbm, bands),
            (lens_row_hbm, lens_row), (norms_hbm, norms_v), (lens_hbm, lens),
            (tokens_of(tok_hbm, whose(0)), tok.at[0]), (tokens_of(cot_hbm, whose(0)), cot.at[0]),
            (tokens_of(tok_hbm, whose(1)), tok.at[1]), (tokens_of(cot_hbm, whose(1)), cot.at[1]),
        ))
    ]
    for fetch in fetches:
        fetch.start()

    def loop(first, last, body):
        def step(i, _):
            body(i)
            return 0

        lax.fori_loop(first, last, step, 0)

    def remote(src, dst, send, recv, peer):
        return pltpu.make_async_remote_copy(
            src_ref=src, dst_ref=dst, send_sem=send, recv_sem=recv, device_id=peer, device_id_type=MESH
        )

    def same(ref, send, recv, peer):
        return remote(ref, ref, send, recv, peer)

    shard, far = x * 2 + c, (1 - x) * 2 + c
    fetches[0].wait()
    rows = block_rows(owners)
    fetches[1].wait()
    for r in range(CAP):
        flat[...] = master[:, r, :]
        wide = jnp.concatenate([flat[pl.ds(p, W, stride=3), :] for p in range(3)], axis=0)
        narrow = jnp.concatenate([flat[pl.ds(p, R // 4, stride=4), :] for p in range(4)], axis=0)
        wv[shard, dp * CAP + r] = jnp.where(slot_is_wide(rows, dp * CAP + r), wide, narrow).astype(bf16)

    for n in (2, 3, 4, 5):
        fetches[n].wait()
    items = steps.shape[1]
    item_weight = jnp.exp(-2.0 * steps[...].astype(f32) / TSTEPS)
    item_length = lens_row[...].astype(f32)
    table = bands[...] == lax.broadcasted_iota(jnp.int32, (NBANDS, items), 0)
    ones = table.astype(f32)
    mine[...] = jnp.zeros_like(mine)
    mine[0:4, 0 : W // 2] = norms_v[...]
    mine[:, W // 2 : W // 2 + 1] = jnp.sum(ones * (item_weight * item_length), axis=1, keepdims=True)
    mine[:, W // 2 + 1 : W // 2 + 2] = jnp.sum(ones * item_length, axis=1, keepdims=True)
    meta[dp] = mine[...]

    pl.semaphore_wait(barrier, len(peers))

    part_a, part_b, part_ab, part_c = pl.ds(0, GA), pl.ds(GA, GB - GA), pl.ds(0, GB), pl.ds(GB, R - GB)

    def slab(sh, zz, yy, part=slice(None)):
        return wv.at[sh, pl.ds((zz * 2 + yy) * CAP, CAP), part, :]

    def order(k):
        late, low = k // 2, z // 2
        return (1 - late) * (z + k * (1 - 2 * lax.rem(z, 2))) + late * (k + low * (3 - 2 * k))

    up, down, inner = z < nz - 1, z > 0, lax.rem(z, nz - 1) != 0
    own_up = same(slab(shard, z, y, part_ab), z_s.at[0], z_r.at[z], device(z + 1, y, x, c))
    own_down = same(slab(shard, z, y, part_ab), z_s.at[nz], z_r.at[z], device(z - 1, y, x, c))
    pl.when(up)(own_up.start)
    pl.when(down)(own_down.start)

    def meta_copy(k):
        return remote(mine, meta.at[dp], m_s.at[k], m_r.at[k], dp_peers[k])

    for k in range(len(dp_peers)):
        meta_copy(k).start()

    def along_z(k):
        zz = order(k)
        late = k // 2
        goal = (1 - late) * (3 - z) + late * 3 * (z - 1)
        return same(slab(shard, zz, y, part_ab), z_s.at[k], z_r.at[zz], device(goal, y, x, c))

    def both(j, zz):
        return wv.at[lax.rem(x + j, 2) * 2 + c, pl.ds(zz * 2 * CAP, 2 * CAP), part_c, :]

    def last_z(j, n):
        return same(both(j, z), zc_s.at[j, n], zc_r.at[j, n], device(lax.rem(z + n, nz), y, x, c))

    def last_here(j, n):
        zz = lax.rem(z + nz - n, nz)
        return same(both(j, zz), zc_s.at[j, n], zc_r.at[j, n], x_peer)

    def last_core(j, n):
        return same(both(j, lax.rem(z + nz - n, nz)), cc_s.at[j, n], cc_r.at[j, n], core_peer)

    own_c = slab(shard, z, y, part_c)
    c_copies = (
        same(own_c, c_s.at[0], c_r.at[0], y_peer),
        same(own_c, c_s.at[1], c_r.at[1], x_peer),
        same(slab(shard, z, 1 - y, part_c), c_s.at[2], c_r.at[2], x_peer),
    )

    def first_copies(k):
        zz = order(k)
        one, two = slab(shard, zz, y, part_a), slab(shard, zz, y, part_b)
        return (
            same(one, ya_s.at[k], ya_r.at[k], y_peer),
            same(two, xb_s.at[k], xb_r.at[k], x_peer),
            same(two, yb_s.at[k, 0], yb_r.at[k, 0], y_peer),
            same(one, xa_s.at[k, 0], xa_r.at[k, 0], x_peer),
            same(slab(shard, zz, y, part_ab), core_s.at[k, 0], core_r.at[k, 0], core_peer),
        )

    def second_copies(k):
        zz = order(k)
        return (
            same(slab(shard, zz, 1 - y, part_a), xa_s.at[k, 1], xa_r.at[k, 1], x_peer),
            same(slab(far, zz, y, part_b), yb_s.at[k, 1], yb_r.at[k, 1], y_peer),
            same(slab(shard, zz, 1 - y, part_ab), core_s.at[k, 1], core_r.at[k, 1], core_peer),
        )

    def third_copies(k):
        zz = order(k)
        return (
            same(slab(far, zz, y, part_ab), core_s.at[k, 2], core_r.at[k, 2], core_peer),
            same(slab(far, zz, 1 - y, part_ab), core_s.at[k, 3], core_r.at[k, 3], core_peer),
        )

    def gather0(k):
        @pl.when(k > 0)
        def _():
            along_z(k).wait_recv()
            pl.when(inner)(along_z(k).start)

        for copy in first_copies(k):
            copy.start()

    def gather1(k):
        zz = order(k)
        over_x, over_y, core = second_copies(k)
        same(slab(shard, zz, 1 - y, part_a), ya_s.at[k], ya_r.at[k], y_peer).wait_recv()
        over_x.start()
        same(slab(far, zz, y, part_b), xb_s.at[k], xb_r.at[k], x_peer).wait_recv()
        over_y.start()
        same(slab(shard, zz, 1 - y, part_b), yb_s.at[k, 0], yb_r.at[k, 0], y_peer).wait_recv()
        core.start()

    def gather2(k):
        zz = order(k)
        near, apart = third_copies(k)
        same(slab(far, zz, y, part_a), xa_s.at[k, 0], xa_r.at[k, 0], x_peer).wait_recv()
        near.start()
        same(slab(far, zz, 1 - y, part_a), xa_s.at[k, 1], xa_r.at[k, 1], x_peer).wait_recv()
        same(slab(far, zz, 1 - y, part_b), yb_s.at[k, 1], yb_r.at[k, 1], y_peer).wait_recv()
        apart.start()

    c_copies[0].start()
    c_copies[1].start()
    gather0(0)

    def gather_last(n):
        for j in range(2):
            last_here(j, n).wait_recv()
            last_core(j, n).start()

    def find_block(row):
        block = 0
        for j, block_row in enumerate(rows):
            block = block + jnp.where(block_row == row, j, 0)
        block_at[row] = block

    loop(0, nz * 2 * CAP, find_block)
    for k in range(len(dp_peers)):
        meta_copy(k).wait_recv()
    lane = lax.broadcasted_iota(jnp.int32, (8, W), 1)
    chunks = []
    for pair in range(meta.shape[0] // 2):
        chunks.append(jnp.where(lane < W // 2, meta[2 * pair], pltpu.roll(meta[2 * pair + 1], W // 2, 1)))
    norms = jnp.concatenate(chunks, axis=1).astype(bf16).astype(f32)
    gain1, shift1, gain2, shift2 = (norms[i : i + 1, :] for i in range(4))
    band_sums = meta[0]
    for d in range(1, meta.shape[0]):
        band_sums = band_sums + meta[d]
    weight_of = jnp.sum(jnp.where(table, band_sums[:, W // 2 : W // 2 + 1], 0.0), axis=0, keepdims=True)
    count_of = jnp.sum(jnp.where(table, band_sums[:, W // 2 + 1 : W // 2 + 2], 0.0), axis=0, keepdims=True)
    scales = item_weight * count_of / weight_of
    item_lane = lax.broadcasted_iota(jnp.int32, (1, items), 1)
    position = lax.broadcasted_iota(jnp.int32, (TILE, 1), 0)
    for n in range(6, 11):
        fetches[n].wait()

    def tile(t):
        return pl.ds(pl.multiple_of(t * TILE, TILE), TILE)

    def first_norm(i):
        p, t = i // tiles, lax.rem(i, tiles)
        here = tile(t)
        scaled, inverse = normalise(tok[p, here, :])
        xhat1[p, here, :] = scaled
        inv1[p, here, :] = inverse
        low1[p, here, :] = (scaled * gain1 + shift1).astype(bf16)
        item = whose(p) * items_here + t // (SEQ // TILE)
        scale = jnp.sum(jnp.where(item_lane == item, scales, 0.0), axis=1, keepdims=True)
        inside = position + lax.rem(t, SEQ // TILE) * TILE < lens[item]
        scaled_cot = cot[p, here, :] * jnp.where(inside, scale, 0.0)
        cot[p, here, :] = scaled_cot
        e2[p, here, :] = scaled_cot.astype(bf16)

    c_copies[0].wait_recv()
    c_copies[2].start()
    loop(0, 2 * tiles, first_norm)
    c_copies[1].wait_recv()
    c_copies[2].wait_recv()
    for j in range(2):
        last_core(j, 0).start()

    def gather(step):
        pl.when(step < nz)(lambda: gather0(step))

        @pl.when(step == nz - 1)
        def _():
            for j in range(2):
                for n in range(1, nz):
                    last_z(j, n).start()

        pl.when(step <= nz)(lambda: gather1(step - 1))
        pl.when(step >= 2)(lambda: gather2(step - 2))

    loop(1, nz + 2, gather)
    loop(1, nz, gather_last)

    def all_here(k):
        zz = order(k)
        for kind, (xx, yy) in enumerate(((x, y), (x, 1 - y), (1 - x, y), (1 - x, 1 - y))):
            same(slab(xx * 2 + 1 - c, zz, yy, part_ab), core_s.at[k, kind], core_r.at[k, kind], core_peer).wait_recv()
        for j in range(2):
            last_core(j, k).wait_recv()

    loop(0, nz, all_here)

    head_lane = lax.broadcasted_iota(jnp.int32, (1, W), 1)
    head_masks = [head_lane < HD, head_lane >= HD]
    key_pos = lax.broadcasted_iota(jnp.int32, (1, SEQ), 1)
    item_rows = [slice(i * SEQ, (i + 1) * SEQ) for i in range(items_here)]

    def only(values, a):
        return jnp.where(head_masks[a], values, jnp.zeros_like(values))

    def stack(values):
        return jnp.concatenate([only(values, 0), only(values, 1)], axis=0)

    def wide_matrix(h):
        return jnp.concatenate(
            [
                jnp.concatenate([wv[h, rows[j], p * W : (p + 1) * W, :] for j in range(QB)], axis=0)
                for p in range(3)
            ],
            axis=1,
        )

    def narrow_matrix(h, first, size):
        pieces = cat_pieces(first, size)
        return jnp.concatenate(
            [
                jnp.concatenate(
                    [wv[h, rows[b], pl.ds(p * (R // 4) + inside, count), :] for b, inside, _, count in pieces], axis=0
                )
                for p in range(4)
            ],
            axis=1,
        )

    deep, low = (QB + 2, CB - 2), (0, QB + 2)
    x_part, y_part, z_part = pl.ds(0, RA), pl.ds(RA, RB - RA), pl.ds(RB, R - RB)

    def core_push(j, n):
        part = pl.ds(*(deep, low)[n])
        return remote(grads.at[j, part], from_core.at[j, part], cs.at[n, j], cr.at[n, j], core_peer)

    def x_push(n):
        part = pl.ds(*(deep, low)[n])
        return remote(grads.at[2, part, x_part, :], rxa.at[part], as_.at[n], ar.at[n], x_peer)

    def hand_over(i, n):
        first, count = (deep, low)[n]
        pl.when(i < 2)(lambda: core_push(i, n).start())

        @pl.when(i >= 2)
        def _():
            core_push(i - 2, n).wait_recv()

            def add(block):
                grads[i, block] = grads[i, block] + from_core[i - 2, block]

            loop(first, first + count, add)
            pl.when(i == 2)(lambda: x_push(n).start())

    pair_z, cross_z = z + 1 - 2 * lax.rem(z, 2), lax.rem(z + 2, nz)

    def chunk(k):
        return lax.rem(pair_z + lax.rem(k, 2) * (z - pair_z) + 2 * (1 - k // 2), nz)

    def block_of(k, yy, r):
        return block_at[(chunk(k) * 2 + yy) * CAP + r]

    def over_y_first(k):
        return remote(sb.at[k], ryb.at[k], sby_s.at[k], sby_r.at[k], y_peer)

    def over_x_last(k):
        return remote(sbx.at[k], rxb.at[k], sbx_s.at[k], sbx_r.at[k], x_peer)

    def over_y_last(k):
        return remote(sa.at[k], rya.at[k], say_s.at[k], say_r.at[k], y_peer)

    def over_z(k, r):
        goal = pair_z + lax.rem(k, 2) * (cross_z - pair_z)
        return remote(fz.at[k, r], rz.at[k, r], fz_s.at[k, r], fz_r.at[k, r], device(goal, y, x, c))

    def z_first(k):
        goal = pair_z + lax.rem(k, 2) * (cross_z - pair_z)
        return remote(sc.at[k], rc.at[k], sc_s.at[k], sc_r.at[k], device(goal, y, x, c))

    def z_then_y():
        return remote(sc.at[nz - 1, :, 1 - y], ryc, cy_s, cy_r, y_peer)

    def z_then_x():
        return remote(sc.at[nz - 1, 0, y], rxc, cx_s, cx_r, x_peer)

    def send_c(k):
        for r in range(2 * CAP):
            block = block_of(k, r // CAP, r % CAP)
            for j in range(2):
                sc[k, j, r // CAP, r % CAP] = grads[2 + j, block, z_part, :]
        pl.when(k == 0)(lambda: z_first(k).start())

    def cross_c():
        z_first(0).wait_recv()
        for j in range(2):
            sc[1, j] = sc[1, j] + rc[0, j]
        z_first(1).start()
        z_first(2).start()

    def own_c():
        z_first(1).wait_recv()
        z_first(2).wait_recv()
        for j in range(2):
            sc[nz - 1, j] = sc[nz - 1, j] + (rc[1, j].astype(f32) + rc[2, j].astype(f32)).astype(bf16)
        z_then_y().start()

    def y_c():
        z_then_y().wait_recv()
        for j in range(2):
            sc[nz - 1, j, y] = sc[nz - 1, j, y] + ryc[j]
        z_then_x().start()

    def norm_copies():
        z_peers = [device(lax.rem(z + k, nz), y, x, c) for k in range(1, nz)]
        return [
            remote(norm_part, n_core, n_s.at[0], n_r.at[0], core_peer),
            remote(norm_sum.at[0], n_x, n_s.at[1], n_r.at[1], x_peer),
            remote(norm_sum.at[1], n_y, n_s.at[2], n_r.at[2], y_peer),
        ] + [remote(norm_sum.at[2], n_z.at[k], n_s.at[3 + k], n_r.at[3 + k], p) for k, p in enumerate(z_peers)]

    def send_b(k):
        for r in range(CAP):
            block = block_of(k, 1 - y, r)
            for j in range(2):
                sb[k, j, r] = grads[2 + j, block, y_part, :]
        over_y_first(k).start()

    def add_x(j):
        grads[3, j, x_part, :] = grads[3, j, x_part, :] + rxa[j]

    def send_a(k):
        for r in range(CAP):
            sa[k, r] = grads[3, block_of(k, 1 - y, r), x_part, :]
        over_y_last(k).start()

    def reduce1(k):
        over_y_first(k).wait_recv()
        for r in range(CAP):
            sbx[k, r] = grads[2, block_of(k, y, r), y_part, :] + ryb[k, 0, r]
        over_x_last(k).start()

    def reduce2(k):
        over_y_last(k).wait_recv()
        over_x_last(k).wait_recv()
        for r in range(CAP):
            block = block_of(k, y, r)
            fz[k, r, x_part, :] = grads[3, block, x_part, :] + rya[k, r]
            part = grads[3, block, y_part, :].astype(f32) + ryb[k, 1, r].astype(f32)
            fz[k, r, y_part, :] = (part + rxb[k, r].astype(f32)).astype(bf16)
            pl.when(lax.rem(k, 2) == 0)(over_z(k, r).start)

    def cross():
        for r in range(CAP):
            over_z(0, r).wait_recv()
            fz[1, r] = fz[1, r] + rz[0, r]
            over_z(1, r).start()

    key_row = lax.broadcasted_iota(jnp.int32, (2 * SEQ, W), 0)
    head_ones = jnp.where((key_row < SEQ) == head_masks[0], 1.0, 0.0).astype(bf16)

    def attention(p, h):
        projected = dot(low1[p], wide_matrix(h))
        qkv[h, 0] = (projected[:, :W].astype(bf16).astype(f32) * (1.0 / math.sqrt(HD))).astype(bf16)
        qkv[h, 1] = projected[:, W : 2 * W].astype(bf16)
        qkv[h, 2] = projected[:, 2 * W :].astype(bf16)
        for i, here in enumerate(item_rows):
            query, key, value = qkv[h, 0, here, :], qkv[h, 1, here, :], qkv[h, 2, here, :]
            valid = key_pos < lens[whose(p) * items_here + i]
            both = []
            for a in range(2):
                scores = jnp.where(valid, dot_cols(only(query, a), key), -1e30)
                exps = jnp.exp(scores - jnp.max(scores, axis=-1, keepdims=True)).astype(bf16)
                probs[h, i, a] = exps
                both.append(exps)
            mixed = dot(jnp.concatenate(both, axis=1), jnp.concatenate([stack(value), head_ones], axis=1))
            inverse = 1.0 / mixed[:, W:]
            sums[h, here, :] = inverse
            att[h, here, :] = (mixed[:, :W] * inverse).astype(bf16)
        acc[...] += dot(att[h], narrow_matrix(h, 0, W))

    def put(i, first, result):
        for block, inside, row, count in cat_pieces(first, result.shape[0]):
            for p in range(4):
                here = pl.ds(p * (R // 4) + inside, count)
                grads[i, block, here, :] = result[row : row + count, p * W : (p + 1) * W].astype(bf16)

    def shard_of(p, i):
        return lax.rem(1 + x + p + i, 2) * 2 + lax.rem(c + 1 + i // 2, 2)

    def feed_forward(p, i):
        h = shard_of(p, i)
        up_matrix, down_matrix = narrow_matrix(h, W, D), narrow_matrix(h, W + D, D)
        hidden = dot(low2[...], up_matrix)
        root = math.sqrt(2.0 / math.pi)
        square = hidden * hidden
        bend = jnp.tanh(root * hidden * (1.0 + 0.044715 * square))
        half = 0.5 * (1.0 + bend)
        active = (hidden * half).astype(bf16)
        slope = half + 0.5 * hidden * (1.0 - bend * bend) * (root + (3.0 * 0.044715 * root) * square)
        if p == 0:
            actives[i] = active
        else:
            acc[...] += dot(active, down_matrix)
        back = (dot_cols(e2[p], down_matrix) * slope).astype(bf16)
        da[...] += dot_cols(back, up_matrix)
        if p == 0:
            put(i, W + D, dot_rows(active, e2[p]))
            put(i, W, dot_rows(low2[...], back))
            hand_over(i, 0)

    def attention_back(p, i):
        h = shard_of(p, i)
        d_all = dot_cols(e1[...], narrow_matrix(h, 0, W)) * sums[h]
        shared_all = (d_all * att[h].astype(f32)).astype(bf16)
        d_all = d_all.astype(bf16)
        parts = []
        for m, here in enumerate(item_rows):
            query, key, value = qkv[h, 0, here, :], qkv[h, 1, here, :], qkv[h, 2, here, :]
            d_here, shared = d_all[here, :], shared_all[here, :]
            against = jnp.concatenate([value, jnp.full((SEQ, W), -1.0, bf16)], axis=1)
            d_scores = []
            for a in range(2):
                change = dot_cols(jnp.concatenate([only(d_here, a), only(shared, a)], axis=1), against)
                d_scores.append((probs[h, m, a].astype(f32) * change).astype(bf16))
            d_query = dot(jnp.concatenate(d_scores, axis=1), stack(key)) * (1.0 / math.sqrt(HD))
            d_key = dot_rows(jnp.concatenate(d_scores, axis=0), stack(query))
            d_value = dot_rows(jnp.concatenate([probs[h, m, 0], probs[h, m, 1]], axis=0), stack(d_here))
            parts.append(jnp.concatenate([d_query, d_key, d_value], axis=1).astype(bf16))
        d_qkv = jnp.concatenate(parts, axis=0)
        if p == 0:
            d_qkvs[i] = d_qkv
            put(i, 0, dot_rows(att[h], e1[...]))
            d_weight = dot_rows(low1[p], d_qkv).astype(bf16)
            for j in range(QB):
                for m in range(3):
                    grads[i, j, m * W : (m + 1) * W, :] = d_weight[j * W : (j + 1) * W, m * W : (m + 1) * W]
            hand_over(i, 1)
        else:
            da[...] += dot_cols(d_qkv, wide_matrix(h))

    def late_output(i):
        acc[...] += dot(actives[i], narrow_matrix(shard_of(0, i), W + D, D))

    def late_input(i):
        da[...] += dot_cols(d_qkvs[i], wide_matrix(shard_of(0, i)))

    def norm_backward(grad, scaled, inverse, gain):
        grad_scaled = grad * gain
        centre = jnp.mean(grad_scaled, axis=-1, keepdims=True)
        slope = jnp.mean(grad_scaled * scaled, axis=-1, keepdims=True)
        return inverse * (grad_scaled - centre - scaled * slope)

    def add_norm(p, row, grad, scaled):
        if p == 0:
            norm_part[row : row + 1, :] += jnp.sum(grad * scaled, axis=0, keepdims=True)
            norm_part[row + 1 : row + 2, :] += jnp.sum(grad, axis=0, keepdims=True)

    norm_part[...] = jnp.zeros_like(norm_part)

    def out_copies(p, n):
        src, dst = ((out_low, out_all), (in_low, in_all))[n]
        there = tokens_of(dst, whose(p))
        return (
            pltpu.make_async_copy(src.at[p], there, o_l.at[p, n]),
            remote(src.at[p], there, o_s.at[p, n], o_r.at[p, n], core_peer),
        )

    def block_result(p):
        out_low[p] = acc[...].astype(bf16)
        for copy in out_copies(p, 0):
            copy.start()

    def input_result(p):
        def first_norm_back(t):
            here = tile(t)
            grad, scaled = da[here, :], xhat1[p, here, :]
            add_norm(p, 0, grad, scaled)
            in_low[p, here, :] = (cot[p, here, :] + norm_backward(grad, scaled, inv1[p, here, :], gain1)).astype(bf16)

        loop(0, tiles, first_norm_back)
        for copy in out_copies(p, 1):
            copy.start()

    def layer_pass(p):
        acc[...] = jnp.zeros_like(acc)
        loop(0, 4, lambda h: attention(p, h))
        if p == 1:
            cross_c()

        def second_norm(t):
            here = tile(t)
            state = acc[here, :] + tok[p, here, :]
            acc[here, :] = state
            scaled, inverse = normalise(state)
            xhat2[here, :] = scaled
            inv2[here, :] = inverse
            low2[here, :] = (scaled * gain2 + shift2).astype(bf16)
            da[here, :] = jnp.zeros((TILE, D), f32)

        loop(0, tiles, second_norm)
        if p == 1:
            for n in range(2):
                x_push(n).wait_recv()
            loop(0, QB + CB, add_x)
            loop(0, nz, send_a)
            loop(0, nz, reduce1)
        loop(0, 4, lambda i: feed_forward(p, i))
        if p == 1:
            block_result(1)
            norm_copies()[0].wait_recv()
            norm_sum[0] = norm_part[...] + n_core[...]
            norm_copies()[1].start()

        def second_norm_back(t):
            here = tile(t)
            grad, scaled = da[here, :], xhat2[here, :]
            add_norm(p, 2, grad, scaled)
            change = cot[p, here, :] + norm_backward(grad, scaled, inv2[here, :], gain2)
            cot[p, here, :] = change
            e1[here, :] = change.astype(bf16)
            da[here, :] = jnp.zeros((TILE, D), f32)

        loop(0, tiles, second_norm_back)
        if p == 1:
            norm_copies()[1].wait_recv()
            norm_sum[1] = norm_sum[0] + n_x[...]
            norm_copies()[2].start()
            reduce2(0)

        def attention_step(i):
            attention_back(p, i)
            if p == 1:
                @pl.when(i == 0)
                def _():
                    own_c()
                    reduce2(1)

                @pl.when(i == 1)
                def _():
                    cross()
                    reduce2(2)
                    y_c()

        loop(0, 4, attention_step)

    layer_pass(0)
    loop(0, nz, send_c)
    loop(0, nz, send_b)
    loop(0, 4, late_output)
    block_result(0)
    loop(0, 4, late_input)
    input_result(0)
    norm_copies()[0].start()
    layer_pass(1)
    input_result(1)

    norm_copies()[2].wait_recv()
    norm_sum[2] = norm_sum[1] + n_y[...]
    for copy in norm_copies()[3:]:
        copy.start()
    reduce2(nz - 1)

    for k in range(nz - 1):
        norm_copies()[3 + k].wait_recv()
    z_then_x().wait_recv()
    for r in range(CAP):
        over_z(2, r).wait_recv()
        over_z(1, r).wait_recv()
    norm_total[...] = norm_sum[2] + ((n_z[0] + n_z[1]) + n_z[2])

    def last(r):
        others = rz[1, r].astype(f32) + rz[2, r].astype(f32)
        total[r, pl.ds(0, RB), :] = fz[nz - 1, r].astype(f32) + others
        total[r, z_part, :] = sc[nz - 1, 1, y, r].astype(f32) + rxc[r].astype(f32)

    loop(0, CAP, last)

    for p in range(2):
        for n in range(2):
            local, over_core = out_copies(p, n)
            local.wait()
            over_core.wait()
    for copy in norm_copies():
        copy.wait_send()
    for k in range(len(dp_peers)):
        meta_copy(k).wait_send()
    pl.when(up)(own_up.wait_send)
    pl.when(down)(own_down.wait_send)
    for copy in c_copies:
        copy.wait_send()

    def sent(k):
        for copy in first_copies(k) + second_copies(k) + third_copies(k):
            copy.wait_send()
        pl.when(jnp.logical_and(k > 0, inner))(along_z(k).wait_send)
        for j in range(2):
            last_core(j, k).wait_send()
            pl.when(k > 0)(last_z(j, k).wait_send)
        for copy in (over_y_first(k), over_x_last(k), over_y_last(k)):
            copy.wait_send()
        pl.when(k < nz - 1)(z_first(k).wait_send)
        for r in range(CAP):
            pl.when(k < nz - 1)(over_z(k, r).wait_send)

    loop(0, nz, sent)
    z_then_y().wait_send()
    z_then_x().wait_send()
    for n in range(2):
        x_push(n).wait_send()
        for j in range(2):
            core_push(j, n).wait_send()


def layer(tokens, cotangent, master, norms, steps, bands, lens_row, lens, owners):
    nz = Sizes.z
    here = tokens.shape[0] // lax.axis_size("head")
    items_here = here // SEQ
    items = lens.shape[0]
    vm = pl.BlockSpec(memory_space=pltpu.VMEM)
    hbm = pl.BlockSpec(memory_space=pltpu.HBM)
    dma = pltpu.SemaphoreType.DMA
    V, S = pltpu.VMEM, pltpu.SMEM
    square = (here, D)
    blocks = QB + CB
    rb = RB - RA
    low, full, two_low, two = V(square, bf16), V(square, f32), V((2, *square), bf16), V((2, *square), f32)
    scratch = [
        V((4, nz * 2 * CAP, R, W), bf16), V((R, CAP, W), f32), V((R, W), f32),
        V((8, W), f32), V((nz * 2, 8, W), f32), V(norms.shape, f32),
        V((1, items), jnp.int32), V((1, items), jnp.int32), V((1, items), jnp.int32),
        S((items,), jnp.int32), S(owners.shape, jnp.int32), S((nz * 2 * CAP,), jnp.int32),
        two, two, two_low, two, V((2, here, 1), f32), V((4, 3, here, W), bf16),
        V((4, items_here, 2, SEQ, SEQ), bf16), V((4, here, W), f32), V((4, here, W), bf16),
        full, low, full, V((here, 1), f32), two_low,
        V((4, here, D), bf16), V((4, here, 3 * W), bf16), full, low, two_low, two_low,
        V((4, blocks, R, W), bf16), V((2, blocks, R, W), bf16),
        V((blocks, RA, W), bf16), V((nz, CAP, RA, W), bf16), V((nz, CAP, RA, W), bf16),
        V((nz, 2, CAP, rb, W), bf16), V((nz, 2, CAP, rb, W), bf16), V((nz, CAP, rb, W), bf16),
        V((nz, CAP, rb, W), bf16), V((nz, CAP, RB, W), bf16), V((nz - 1, CAP, RB, W), bf16),
        V((nz, 2, 2, CAP, R - RB, W), bf16), V((nz - 1, 2, 2, CAP, R - RB, W), bf16),
        V((2, CAP, R - RB, W), bf16), V((CAP, R - RB, W), bf16),
        V((8, D), f32), V((3, 8, D), f32), V((8, D), f32), V((8, D), f32), V((8, D), f32), V((nz - 1, 8, D), f32),
        dma((11,)), dma((nz + 1,)), dma((nz,)), dma((nz,)), dma((nz,)), dma((nz, 2)), dma((nz, 2)), dma((nz,)), dma((nz,)),
        dma((nz, 2)), dma((nz, 2)), dma((nz, 4)), dma((nz, 4)), dma((8,)), dma((8,)),
        dma((3,)), dma((3,)), dma((2, nz)), dma((2, nz)), dma((2, nz)), dma((2, nz)),
        dma((nz,)), dma((nz,)), dma, dma, dma, dma,
        dma((2, 2)), dma((2, 2)), dma((2,)), dma((2,)), dma((nz,)), dma((nz,)), dma((nz,)), dma((nz,)),
        dma((nz,)), dma((nz,)), dma((nz, CAP)), dma((nz, CAP)), dma((8,)), dma((8,)), dma((2, 2)), dma((2, 2)), dma((2, 2)),
    ]
    return pl.pallas_call(
        layer_kernel,
        name="layer",
        out_shape=(
            jax.ShapeDtypeStruct((CAP, R, W), f32),
            jax.ShapeDtypeStruct(tokens.shape, bf16),
            jax.ShapeDtypeStruct(tokens.shape, bf16),
            jax.ShapeDtypeStruct((8, D), f32),
        ),
        in_specs=[hbm] * 9,
        out_specs=(vm, hbm, hbm, vm),
        scratch_shapes=scratch,
        compiler_params=pltpu.CompilerParams(collective_id=0, has_side_effects=True, vmem_limit_bytes=56 << 20),
    )(tokens, cotangent, master, norms, steps, bands, lens_row, lens, owners)


def finish_kernel(
    total_hbm, norm_hbm, master_hbm, first_hbm, second_hbm, norm_m, norm_f, norm_s, owners_hbm, out_all, in_all,
    block_output, input_grad, new_master, new_first, new_second, new_norm, new_norm_first, new_norm_second,
    out_low, in_low, out_full, in_full, states, results, flat, grad, total, norm_total, norm_master, norm_first, norm_second, owners, l_sem, s_sem, i_sem, r_sem,
):
    pieces = l_sem.shape[1]
    size = out_low.shape[0] // pieces
    pairs = ((out_all, out_low, out_full, block_output), (in_all, in_low, in_full, input_grad))

    def piece(p):
        return pl.ds(pl.multiple_of(p * size, size), size)

    def fetch(n, p):
        return pltpu.make_async_copy(pairs[n][0].at[piece(p), :], pairs[n][1].at[piece(p), :], l_sem.at[n, p])

    def store(n, p):
        return pltpu.make_async_copy(pairs[n][2].at[piece(p), :], pairs[n][3].at[piece(p), :], s_sem.at[n, p])

    small_copies = [
        pltpu.make_async_copy(src, dst, i_sem.at[3 + i])
        for i, (src, dst) in enumerate((
            (owners_hbm, owners), (total_hbm, total), (norm_hbm, norm_total),
            (norm_m, norm_master), (norm_f, norm_first), (norm_s, norm_second),
        ))
    ]
    state_copies = [
        pltpu.make_async_copy(src, states.at[i], i_sem.at[i]) for i, src in enumerate((master_hbm, first_hbm, second_hbm))
    ]
    result_copies = [
        pltpu.make_async_copy(results.at[i], dst, r_sem.at[i]) for i, dst in enumerate((new_master, new_first, new_second))
    ]

    def loop(count, body):
        def step(i, _):
            body(i)
            return 0

        lax.fori_loop(0, count, step, 0)

    for copy in small_copies:
        copy.start()
    loop(pieces, lambda p: fetch(0, p).start())
    for copy in state_copies:
        copy.start()
    loop(pieces, lambda p: fetch(1, p).start())

    dp = lax.axis_index("dp")
    small_copies[0].wait()
    rows = block_rows(owners)
    held = 0
    for j in range(owners.shape[0]):
        held = held + jnp.where(owners[j] == dp, 1, 0)

    def spread(r):
        is_wide = slot_is_wide(rows, dp * CAP + r)

        @pl.when(is_wide)
        def _():
            for p in range(3):
                flat[pl.ds(p, W, stride=3), :] = total[r, p * W : (p + 1) * W, :]

        @pl.when(jnp.logical_not(is_wide))
        def _():
            for p in range(4):
                flat[pl.ds(p, R // 4, stride=4), :] = total[r, p * (R // 4) : (p + 1) * (R // 4), :]

    small_copies[1].wait()
    for r in range(CAP):
        spread(r)
        grad[:, r, :] = flat[...]

    def convert(n, p):
        fetch(n, p).wait()
        _, low, full, _ = pairs[n]
        full[piece(p), :] = low[piece(p), :].astype(f32)
        store(n, p).start()

    loop(pieces, lambda p: convert(0, p))
    for copy in state_copies:
        copy.wait()
    step = 32
    slot = lax.broadcasted_iota(jnp.int32, (step, CAP, W), 1)

    def update(i):
        here = pl.ds(pl.multiple_of(i * step, step), step)
        new = adamw_update(states[0, here], states[1, here], states[2, here], grad[here], weight_decay, learn_rate)
        for n in range(3):
            results[n, here] = jnp.where(slot < held, new[n], 0.0)

    loop(R // step, update)
    for copy in result_copies:
        copy.start()
    for copy in small_copies[2:]:
        copy.wait()
    pair = norm_total[:, pl.ds(pl.multiple_of((dp // 2) * W, W), W)]
    mine = jnp.where(lax.rem(dp, 2) == 1, pltpu.roll(pair, W // 2, 1), pair)[0:4, 0 : norm_master.shape[1]]
    new = adamw_update(norm_master[...], norm_first[...], norm_second[...], mine, 0.0, norm_rate)
    for ref, value in zip((new_norm, new_norm_first, new_norm_second), new):
        ref[...] = value
    loop(pieces, lambda p: convert(1, p))
    for n in range(2):
        loop(pieces, lambda p: store(n, p).wait())
    for copy in result_copies:
        copy.wait()


def finish(total, norm_total, slots, norms, owners, out_all, in_all):
    vm = pl.BlockSpec(memory_space=pltpu.VMEM)
    hbm = pl.BlockSpec(memory_space=pltpu.HBM)
    dma = pltpu.SemaphoreType.DMA
    V = pltpu.VMEM
    pieces = 8
    shape = out_all.shape
    return pl.pallas_call(
        finish_kernel,
        name="finish",
        out_shape=(
            (jax.ShapeDtypeStruct(shape, f32),) * 2 + tuple(jax.ShapeDtypeStruct(a.shape, f32) for a in slots + norms)
        ),
        in_specs=[hbm] * 11,
        out_specs=(hbm,) * 5 + (vm,) * 3,
        scratch_shapes=[
            V(shape, bf16), V(shape, bf16), V(shape, f32), V(shape, f32), V((3, R, CAP, W), f32), V((3, R, CAP, W), f32),
            V((R, W), f32), V((R, CAP, W), f32),
            V(total.shape, f32), V(norm_total.shape, f32), *(V(a.shape, f32) for a in norms),
            pltpu.SMEM(owners.shape, jnp.int32), dma((2, pieces)), dma((2, pieces)), dma((9,)), dma((3,)),
        ],
        compiler_params=pltpu.CompilerParams(vmem_limit_bytes=60 << 20),
    )(total, norm_total, *slots, *norms, owners, out_all, in_all)


def fast_shards(
    tokens, cotangent, timesteps, bands, lengths, owners,
    master_slots, first_slots, second_slots, norm_master, norm_first, norm_second,
):
    def tiles(slots):
        return jnp.transpose(slots.reshape(CAP, R, W), (1, 0, 2))

    def flat(slots):
        return jnp.transpose(slots, (1, 0, 2)).reshape(CAP, R * W)

    steps, bands_row, lens_row = (v.reshape(1, -1) for v in (timesteps, bands, lengths))
    slots = tuple(tiles(s) for s in (master_slots, first_slots, second_slots))
    norms = (norm_master, norm_first, norm_second)
    total, out_all, in_all, norm_total = layer(
        tokens, cotangent, slots[0], norm_master, steps, bands_row, lens_row, lengths, owners
    )
    results = finish(total, norm_total, slots, norms, owners, out_all, in_all)
    return (*results[:2], *(flat(s) for s in results[2:5]), *results[5:])


def solution(mesh):
    fits = dict(mesh.shape) == {"dp": 8, "head": 4}
    placed = (
        P("dp", None),
        P("dp", None),
        P("dp"),
        P("dp"),
        P("dp"),
        P(),
        P("dp", "head"),
        P("dp", "head"),
        P("dp", "head"),
        P(None, "dp"),
        P(None, "dp"),
        P(None, "dp"),
    )
    return jax.shard_map(
        fast_shards if fits else shards,
        mesh=mesh,
        in_specs=placed,
        out_specs=(
            P("dp", None),
            P("dp", None),
            P("dp", "head"),
            P("dp", "head"),
            P("dp", "head"),
            P(None, "dp"),
            P(None, "dp"),
            P(None, "dp"),
        ),
        check_vma=False,
    )
```

```python
import math

import jax
import jax.numpy as jnp
from jax import lax
from jax.experimental import pallas as pl
from jax.experimental.pallas import tpu as pltpu
from jax.sharding import PartitionSpec as P

D = 512
H = 8
HD = 64
FF = 2048
SEQ = 256
TSTEPS = 1000
NBANDS = 8
CAP = 3
STEP = 5


beta_one = 0.5
beta_two = 0.5
learn_rate = 0.04
norm_rate = 0.4
weight_decay = 0.1
adam_eps = 1e-08
norm_eps = 1e-05


def contract_rows(left_side, right_side):
    return lax.dot_general(
        left_side, right_side, (((0,), (0,)), ((), ())), preferred_element_type=jnp.float32
    )


def contract_cols(left_side, right_side):
    return lax.dot_general(
        left_side, right_side, (((1,), (1,)), ((), ())), preferred_element_type=jnp.float32
    )


def gelu_tanh(values):
    return jax.nn.gelu(values, approximate=True)


def norm_forward(values, gain_row, shift_row):
    average = jnp.mean(values, axis=-1, keepdims=True)
    centred = values - average
    inverse = lax.rsqrt(jnp.mean(centred * centred, axis=-1, keepdims=True) + norm_eps)
    scaled = centred * inverse
    return (scaled * gain_row + shift_row, scaled, inverse)


def norm_backward(grad_normed, scaled, inverse, gain_row):
    grad_scaled = grad_normed * gain_row
    centre_term = jnp.mean(grad_scaled, axis=-1, keepdims=True)
    slope_term = jnp.mean(grad_scaled * scaled, axis=-1, keepdims=True)
    return inverse * (grad_scaled - centre_term - scaled * slope_term)


def slot_rows(owners, capacity):
    block_index = jnp.arange(owners.shape[0], dtype=jnp.int32)
    earlier = (owners[None, :] == owners[:, None]) & (block_index[None, :] < block_index[:, None])
    return owners * capacity + jnp.sum(earlier.astype(jnp.int32), axis=1)


def attention_scores(query_heads, key_heads, key_valid):
    scores = jnp.einsum(
        "gqad,gkad->gaqk", query_heads, key_heads, preferred_element_type=jnp.float32
    ) / math.sqrt(HD)
    return jnp.where(key_valid[:, None, None, :], scores, -1e30)


def adamw_update(weight, first_moment, second, gradient, decay_rate, step_rate):
    new_first = beta_one * first_moment + (1.0 - beta_one) * gradient
    new_second = beta_two * second + (1.0 - beta_two) * gradient * gradient
    first_hat = new_first / (1.0 - beta_one**STEP)
    second_hat = new_second / (1.0 - beta_two**STEP)
    new_weight = weight - step_rate * (
        first_hat / (jnp.sqrt(second_hat) + adam_eps) + decay_rate * weight
    )
    return (new_weight, new_first, new_second)


def shards(
    tokens,
    cotangent,
    timesteps,
    bands,
    lengths,
    owners,
    master_slots,
    first_slots,
    second_slots,
    norm_master,
    norm_first,
    norm_second,
):
    head_count = lax.axis_size("head")
    owner_index = lax.axis_index("dp")
    heads_here = H // head_count
    width_here = heads_here * HD
    units_here = FF // head_count
    block_len = master_slots.shape[1]
    norm_cols = norm_master.shape[1]
    row_count = tokens.shape[0]
    item_count = lengths.shape[0]
    block_count = owners.shape[0]
    slot_row = slot_rows(owners, CAP)
    gathered, norm_whole = (
        lax.all_gather(master_slots.astype(jnp.bfloat16), "dp", axis=0, tiled=True),
        lax.all_gather(norm_master.astype(jnp.bfloat16), "dp", axis=1, tiled=True),
    )
    flat_params = gathered[slot_row].reshape(-1)
    qkv_end = 3 * D * width_here
    out_end = qkv_end + width_here * D
    up_end = out_end + D * units_here
    qkv_weight = flat_params[:qkv_end].reshape(D, 3 * width_here)
    out_weight = flat_params[qkv_end:out_end].reshape(width_here, D)
    up_weight = flat_params[out_end:up_end].reshape(D, units_here)
    down_weight = flat_params[up_end:].reshape(units_here, D)
    norm_params = norm_whole.astype(jnp.float32)
    item_weight = jnp.exp(-2.0 * timesteps.astype(jnp.float32) / TSTEPS)
    item_length = lengths.astype(jnp.float32)
    band_table = (bands[:, None] == jnp.arange(NBANDS, dtype=jnp.int32)[None, :]).astype(
        jnp.float32
    )
    weight_sums, count_sums = lax.psum(
        (
            jnp.sum(band_table * (item_weight * item_length)[:, None], axis=0),
            jnp.sum(band_table * item_length[:, None], axis=0),
        ),
        "dp",
    )
    item_scale = (
        item_weight
        * jnp.sum(band_table * count_sums[None, :], axis=1)
        / jnp.sum(band_table * weight_sums[None, :], axis=1)
    )
    key_valid = jnp.arange(SEQ, dtype=jnp.int32)[None, :] < lengths[:, None]
    token_scale = jnp.where(key_valid, item_scale[:, None], 0.0).reshape(row_count)
    normed_one, scaled_one, inverse_one = norm_forward(tokens, norm_params[0], norm_params[1])
    normed_one_low = normed_one.astype(jnp.bfloat16)
    projected_low = jnp.dot(normed_one_low, qkv_weight, preferred_element_type=jnp.float32).astype(
        jnp.bfloat16
    )
    head_shape = (item_count, SEQ, heads_here, HD)
    query_heads = projected_low[:, :width_here].reshape(head_shape)
    key_heads = projected_low[:, width_here : 2 * width_here].reshape(head_shape)
    value_heads = projected_low[:, 2 * width_here :].reshape(head_shape)
    scores = attention_scores(query_heads, key_heads, key_valid)
    row_max = jnp.max(scores, axis=-1, keepdims=True)
    exp_scores = jnp.exp(scores - row_max)
    row_total = jnp.sum(exp_scores, axis=-1, keepdims=True)
    log_total = row_max + jnp.log(row_total)
    prob_low = (exp_scores / row_total).astype(jnp.bfloat16)
    attended_low = (
        jnp.einsum("gaqk,gkad->gqad", prob_low, value_heads, preferred_element_type=jnp.float32)
        .astype(jnp.bfloat16)
        .reshape(row_count, width_here)
    )
    attn_sum = lax.psum(
        jnp.dot(attended_low, out_weight, preferred_element_type=jnp.float32).astype(jnp.bfloat16),
        "head",
    ).astype(jnp.float32)
    mixed_state = tokens + attn_sum
    normed_two, scaled_two, inverse_two = norm_forward(mixed_state, norm_params[2], norm_params[3])
    normed_two_low = normed_two.astype(jnp.bfloat16)
    hidden = jnp.dot(normed_two_low, up_weight, preferred_element_type=jnp.float32)
    activated, gelu_pull = jax.vjp(gelu_tanh, hidden)
    activated_low = activated.astype(jnp.bfloat16)
    ffn_sum = lax.psum(
        jnp.dot(activated_low, down_weight, preferred_element_type=jnp.float32).astype(
            jnp.bfloat16
        ),
        "head",
    ).astype(jnp.float32)
    block_output = mixed_state + ffn_sum
    grad_state = cotangent * token_scale[:, None]
    grad_low_two = grad_state.astype(jnp.bfloat16)
    grad_down = contract_rows(activated_low, grad_low_two)
    grad_activated = contract_cols(grad_low_two, down_weight)
    grad_hidden_low = gelu_pull(grad_activated)[0].astype(jnp.bfloat16)
    grad_up = contract_rows(normed_two_low, grad_hidden_low)
    grad_normed_two = lax.psum(
        contract_cols(grad_hidden_low, up_weight).astype(jnp.bfloat16), "head"
    ).astype(jnp.float32)
    grad_mixed = grad_state + norm_backward(
        grad_normed_two, scaled_two, inverse_two, norm_params[2]
    )
    grad_low_one = grad_mixed.astype(jnp.bfloat16)
    grad_out_proj = contract_rows(attended_low, grad_low_one)
    grad_attended_low = (
        contract_cols(grad_low_one, out_weight).astype(jnp.bfloat16).reshape(head_shape)
    )
    scores_again = attention_scores(query_heads, key_heads, key_valid)
    probabilities = jnp.exp(scores_again - log_total)
    prob_again_low = probabilities.astype(jnp.bfloat16)
    grad_values = jnp.einsum(
        "gaqk,gqad->gkad", prob_again_low, grad_attended_low, preferred_element_type=jnp.float32
    )
    grad_probs = jnp.einsum(
        "gqad,gkad->gaqk", grad_attended_low, value_heads, preferred_element_type=jnp.float32
    )
    grad_scores_low = (
        probabilities * (grad_probs - jnp.sum(grad_probs * probabilities, axis=-1, keepdims=True))
    ).astype(jnp.bfloat16)
    grad_queries = jnp.einsum(
        "gaqk,gkad->gqad", grad_scores_low, key_heads, preferred_element_type=jnp.float32
    ) / math.sqrt(HD)
    grad_keys = jnp.einsum(
        "gaqk,gqad->gkad", grad_scores_low, query_heads, preferred_element_type=jnp.float32
    ) / math.sqrt(HD)
    grad_projected_low = jnp.concatenate(
        [
            grad_queries.reshape(row_count, width_here),
            grad_keys.reshape(row_count, width_here),
            grad_values.reshape(row_count, width_here),
        ],
        axis=1,
    ).astype(jnp.bfloat16)
    grad_qkv = contract_rows(normed_one_low, grad_projected_low)
    grad_normed_one = lax.psum(
        contract_cols(grad_projected_low, qkv_weight).astype(jnp.bfloat16), "head"
    ).astype(jnp.float32)
    input_grad = grad_mixed + norm_backward(
        grad_normed_one, scaled_one, inverse_one, norm_params[0]
    )
    norm_grads = jnp.stack(
        [
            jnp.sum(grad_normed_one * scaled_one, axis=0),
            jnp.sum(grad_normed_one, axis=0),
            jnp.sum(grad_normed_two * scaled_two, axis=0),
            jnp.sum(grad_normed_two, axis=0),
        ]
    )
    grad_blocks = jnp.concatenate(
        [
            grad_qkv.reshape(-1),
            grad_out_proj.reshape(-1),
            grad_up.reshape(-1),
            grad_down.reshape(-1),
        ]
    ).reshape(block_count, block_len)
    summed, norm_summed = (
        lax.psum(grad_blocks.astype(jnp.bfloat16), "dp").astype(jnp.float32),
        lax.psum(norm_grads.astype(jnp.bfloat16), "dp").astype(jnp.float32),
    )
    landing = jnp.where(owners == owner_index, slot_row - owner_index * CAP, CAP)
    owned_grad = jnp.zeros((CAP, block_len), jnp.float32).at[landing].set(summed, mode="drop")
    norm_owned = lax.dynamic_slice_in_dim(norm_summed, owner_index * norm_cols, norm_cols, 1)
    held_count = jnp.sum((owners == owner_index).astype(jnp.int32))
    used_slot = (jnp.arange(CAP, dtype=jnp.int32) < held_count)[:, None]
    new_master, new_first, new_second = adamw_update(
        master_slots, first_slots, second_slots, owned_grad, weight_decay, learn_rate
    )
    new_master = jnp.where(used_slot, new_master, 0.0)
    new_first = jnp.where(used_slot, new_first, 0.0)
    new_second = jnp.where(used_slot, new_second, 0.0)
    new_norms, new_norm_first, new_norm_second = adamw_update(
        norm_master, norm_first, norm_second, norm_owned, 0.0, norm_rate
    )
    return (
        block_output,
        input_grad,
        new_master,
        new_first,
        new_second,
        new_norms,
        new_norm_first,
        new_norm_second,
    )


W = 128
R = 384
QB = 4
CB = 12
MESH = pl.DeviceIdType.MESH
bf16 = jnp.bfloat16
f32 = jnp.float32


def place(sizes):
    dp = lax.axis_index("dp")
    head = lax.axis_index("head")
    return dp // sizes.y, lax.rem(dp, sizes.y), head // sizes.c, lax.rem(head, sizes.c)


class Sizes:
    z, y, x, c = 4, 2, 2, 2


def device(z, y, x, c):
    return (z * Sizes.y + y, x * Sizes.c + c)


def block_rows(owners):
    ids = [owners[j] for j in range(owners.shape[0])]
    rows = []
    for j, mine in enumerate(ids):
        row = mine * CAP
        for other in ids[:j]:
            row = row + jnp.where(other == mine, 1, 0)
        rows.append(row)
    return rows


def slot_is_wide(rows, slot_row):
    flag = rows[0] == slot_row
    for row in rows[1:QB]:
        flag = jnp.logical_or(flag, row == slot_row)
    return flag


def dot(left, right):
    return jnp.dot(left, right, preferred_element_type=f32)


def dot_cols(left, right):
    return lax.dot_general(left, right, (((1,), (1,)), ((), ())), preferred_element_type=f32)


def dot_rows(left, right):
    return lax.dot_general(left, right, (((0,), (0,)), ((), ())), preferred_element_type=f32)


def normalise(values):
    centred = values - jnp.mean(values, axis=-1, keepdims=True)
    inverse = lax.rsqrt(jnp.mean(centred * centred, axis=-1, keepdims=True) + norm_eps)
    return centred * inverse, inverse


def panels(ref, h, first, size):
    return jnp.concatenate([ref[h, p, first : first + size, :] for p in range(ref.shape[1])], axis=1)


def cat_pieces(first, size):
    pieces = []
    row = first
    while row < first + size:
        block, inside = divmod(row, R // 4)
        count = min(R // 4 - inside, first + size - row)
        pieces.append((QB + block, inside, row - first, count))
        row += count
    return pieces


RA, RB = 224, 304
GA, GB = 176, 336
TILE = 128


def layer_kernel(
    tok_hbm, cot_hbm, master_hbm, norms_hbm, steps_hbm, bands_hbm, lens_row_hbm, lens_hbm, owners_hbm,
    total, out_all, in_all, norm_total,
    wv, master, flat, mine, meta, norms_v, steps, bands, lens_row, lens, owners, block_at,
    tok, cot, low1, xhat1, inv1, qkv, probs, sums, att, acc, low2, xhat2, inv2, e2, actives, d_qkvs, da, e1,
    out_low, in_low,
    grads, from_core, rxa, sa, rya, sb, ryb, sbx, rxb, fz, rz, sc, rc, ryc, rxc, norm_part, norm_sum, n_core, n_x, n_y, n_z,
    i_sem, z_s, z_r, ya_s, ya_r, xa_s, xa_r, xb_s, xb_r, yb_s, yb_r, core_s, core_r, m_s, m_r,
    c_s, c_r, zc_s, zc_r, cc_s, cc_r, sc_s, sc_r, cy_s, cy_r, cx_s, cx_r,
    cs, cr, as_, ar, say_s, say_r, sby_s, sby_r, sbx_s, sbx_r, fz_s, fz_r, n_s, n_r, o_s, o_r, o_l,
):
    z, y, x, c = place(Sizes)
    nz = Sizes.z
    dp, head = z * 2 + y, x * 2 + c
    dp_peers = [device(lax.rem(z + k, nz), (y + j) % 2, x, c) for k in range(nz) for j in range(2) if k or j]
    x_peer, y_peer, core_peer = device(z, y, 1 - x, c), device(z, 1 - y, x, c), device(z, y, x, 1 - c)
    peers = dp_peers + [x_peer, core_peer]
    barrier = pltpu.get_barrier_semaphore()
    for peer in peers:
        pl.semaphore_signal(barrier, inc=1, device_id=peer, device_id_type=MESH)

    tokens_here = tok.shape[1]
    items_here = tokens_here // SEQ
    tiles = tokens_here // TILE

    def whose(p):
        return lax.rem(x + p, 2) * 2 + c

    def tokens_of(ref, who):
        return ref.at[pl.ds(pl.multiple_of(who * tokens_here, tokens_here), tokens_here), :]

    fetches = [
        pltpu.make_async_copy(src, dst, i_sem.at[n])
        for n, (src, dst) in enumerate((
            (owners_hbm, owners), (master_hbm, master), (steps_hbm, steps), (bands_hbm, bands),
            (lens_row_hbm, lens_row), (norms_hbm, norms_v), (lens_hbm, lens),
            (tokens_of(tok_hbm, whose(0)), tok.at[0]), (tokens_of(cot_hbm, whose(0)), cot.at[0]),
            (tokens_of(tok_hbm, whose(1)), tok.at[1]), (tokens_of(cot_hbm, whose(1)), cot.at[1]),
        ))
    ]
    for fetch in fetches:
        fetch.start()

    def loop(first, last, body):
        def step(i, _):
            body(i)
            return 0

        lax.fori_loop(first, last, step, 0)

    def remote(src, dst, send, recv, peer):
        return pltpu.make_async_remote_copy(
            src_ref=src, dst_ref=dst, send_sem=send, recv_sem=recv, device_id=peer, device_id_type=MESH
        )

    def same(ref, send, recv, peer):
        return remote(ref, ref, send, recv, peer)

    shard, far = x * 2 + c, (1 - x) * 2 + c
    fetches[0].wait()
    rows = block_rows(owners)
    fetches[1].wait()
    for r in range(CAP):
        flat[...] = master[:, r, :]
        wide = jnp.concatenate([flat[pl.ds(p, W, stride=3), :] for p in range(3)], axis=0)
        narrow = jnp.concatenate([flat[pl.ds(p, R // 4, stride=4), :] for p in range(4)], axis=0)
        wv[shard, dp * CAP + r] = jnp.where(slot_is_wide(rows, dp * CAP + r), wide, narrow).astype(bf16)

    for n in (2, 3, 4, 5):
        fetches[n].wait()
    items = steps.shape[1]
    item_weight = jnp.exp(-2.0 * steps[...].astype(f32) / TSTEPS)
    item_length = lens_row[...].astype(f32)
    table = bands[...] == lax.broadcasted_iota(jnp.int32, (NBANDS, items), 0)
    ones = table.astype(f32)
    mine[...] = jnp.zeros_like(mine)
    mine[0:4, 0 : W // 2] = norms_v[...]
    mine[:, W // 2 : W // 2 + 1] = jnp.sum(ones * (item_weight * item_length), axis=1, keepdims=True)
    mine[:, W // 2 + 1 : W // 2 + 2] = jnp.sum(ones * item_length, axis=1, keepdims=True)
    meta[dp] = mine[...]

    pl.semaphore_wait(barrier, len(peers))

    part_a, part_b, part_ab, part_c = pl.ds(0, GA), pl.ds(GA, GB - GA), pl.ds(0, GB), pl.ds(GB, R - GB)

    def slab(sh, zz, yy, part=slice(None)):
        return wv.at[sh, pl.ds((zz * 2 + yy) * CAP, CAP), part, :]

    def order(k):
        late, low = k // 2, z // 2
        return (1 - late) * (z + k * (1 - 2 * lax.rem(z, 2))) + late * (k + low * (3 - 2 * k))

    up, down, inner = z < nz - 1, z > 0, lax.rem(z, nz - 1) != 0
    own_up = same(slab(shard, z, y, part_ab), z_s.at[0], z_r.at[z], device(z + 1, y, x, c))
    own_down = same(slab(shard, z, y, part_ab), z_s.at[nz], z_r.at[z], device(z - 1, y, x, c))
    pl.when(up)(own_up.start)
    pl.when(down)(own_down.start)

    def meta_copy(k):
        return remote(mine, meta.at[dp], m_s.at[k], m_r.at[k], dp_peers[k])

    for k in range(len(dp_peers)):
        meta_copy(k).start()

    def along_z(k):
        zz = order(k)
        late = k // 2
        goal = (1 - late) * (3 - z) + late * 3 * (z - 1)
        return same(slab(shard, zz, y, part_ab), z_s.at[k], z_r.at[zz], device(goal, y, x, c))

    def both(j, zz):
        return wv.at[lax.rem(x + j, 2) * 2 + c, pl.ds(zz * 2 * CAP, 2 * CAP), part_c, :]

    def last_z(j, n):
        return same(both(j, z), zc_s.at[j, n], zc_r.at[j, n], device(lax.rem(z + n, nz), y, x, c))

    def last_here(j, n):
        zz = lax.rem(z + nz - n, nz)
        return same(both(j, zz), zc_s.at[j, n], zc_r.at[j, n], x_peer)

    def last_core(j, n):
        return same(both(j, lax.rem(z + nz - n, nz)), cc_s.at[j, n], cc_r.at[j, n], core_peer)

    own_c = slab(shard, z, y, part_c)
    c_copies = (
        same(own_c, c_s.at[0], c_r.at[0], y_peer),
        same(own_c, c_s.at[1], c_r.at[1], x_peer),
        same(slab(shard, z, 1 - y, part_c), c_s.at[2], c_r.at[2], x_peer),
    )

    def first_copies(k):
        zz = order(k)
        one, two = slab(shard, zz, y, part_a), slab(shard, zz, y, part_b)
        return (
            same(one, ya_s.at[k], ya_r.at[k], y_peer),
            same(two, xb_s.at[k], xb_r.at[k], x_peer),
            same(two, yb_s.at[k, 0], yb_r.at[k, 0], y_peer),
            same(one, xa_s.at[k, 0], xa_r.at[k, 0], x_peer),
            same(slab(shard, zz, y, part_ab), core_s.at[k, 0], core_r.at[k, 0], core_peer),
        )

    def second_copies(k):
        zz = order(k)
        return (
            same(slab(shard, zz, 1 - y, part_a), xa_s.at[k, 1], xa_r.at[k, 1], x_peer),
            same(slab(far, zz, y, part_b), yb_s.at[k, 1], yb_r.at[k, 1], y_peer),
            same(slab(shard, zz, 1 - y, part_ab), core_s.at[k, 1], core_r.at[k, 1], core_peer),
        )

    def third_copies(k):
        zz = order(k)
        return (
            same(slab(far, zz, y, part_ab), core_s.at[k, 2], core_r.at[k, 2], core_peer),
            same(slab(far, zz, 1 - y, part_ab), core_s.at[k, 3], core_r.at[k, 3], core_peer),
        )

    def gather0(k):
        @pl.when(k > 0)
        def _():
            along_z(k).wait_recv()
            pl.when(inner)(along_z(k).start)

        for copy in first_copies(k):
            copy.start()

    def gather1(k):
        zz = order(k)
        over_x, over_y, core = second_copies(k)
        same(slab(shard, zz, 1 - y, part_a), ya_s.at[k], ya_r.at[k], y_peer).wait_recv()
        over_x.start()
        same(slab(far, zz, y, part_b), xb_s.at[k], xb_r.at[k], x_peer).wait_recv()
        over_y.start()
        same(slab(shard, zz, 1 - y, part_b), yb_s.at[k, 0], yb_r.at[k, 0], y_peer).wait_recv()
        core.start()

    def gather2(k):
        zz = order(k)
        near, apart = third_copies(k)
        same(slab(far, zz, y, part_a), xa_s.at[k, 0], xa_r.at[k, 0], x_peer).wait_recv()
        near.start()
        same(slab(far, zz, 1 - y, part_a), xa_s.at[k, 1], xa_r.at[k, 1], x_peer).wait_recv()
        same(slab(far, zz, 1 - y, part_b), yb_s.at[k, 1], yb_r.at[k, 1], y_peer).wait_recv()
        apart.start()

    c_copies[0].start()
    c_copies[1].start()
    gather0(0)

    def gather_last(n):
        for j in range(2):
            last_here(j, n).wait_recv()
            last_core(j, n).start()

    def find_block(row):
        block = 0
        for j, block_row in enumerate(rows):
            block = block + jnp.where(block_row == row, j, 0)
        block_at[row] = block

    loop(0, nz * 2 * CAP, find_block)
    for k in range(len(dp_peers)):
        meta_copy(k).wait_recv()
    lane = lax.broadcasted_iota(jnp.int32, (8, W), 1)
    chunks = []
    for pair in range(meta.shape[0] // 2):
        chunks.append(jnp.where(lane < W // 2, meta[2 * pair], pltpu.roll(meta[2 * pair + 1], W // 2, 1)))
    norms = jnp.concatenate(chunks, axis=1).astype(bf16).astype(f32)
    gain1, shift1, gain2, shift2 = (norms[i : i + 1, :] for i in range(4))
    band_sums = meta[0]
    for d in range(1, meta.shape[0]):
        band_sums = band_sums + meta[d]
    weight_of = jnp.sum(jnp.where(table, band_sums[:, W // 2 : W // 2 + 1], 0.0), axis=0, keepdims=True)
    count_of = jnp.sum(jnp.where(table, band_sums[:, W // 2 + 1 : W // 2 + 2], 0.0), axis=0, keepdims=True)
    scales = item_weight * count_of / weight_of
    item_lane = lax.broadcasted_iota(jnp.int32, (1, items), 1)
    position = lax.broadcasted_iota(jnp.int32, (TILE, 1), 0)
    for n in range(6, 11):
        fetches[n].wait()

    def tile(t):
        return pl.ds(pl.multiple_of(t * TILE, TILE), TILE)

    def first_norm(i):
        p, t = i // tiles, lax.rem(i, tiles)
        here = tile(t)
        scaled, inverse = normalise(tok[p, here, :])
        xhat1[p, here, :] = scaled
        inv1[p, here, :] = inverse
        low1[p, here, :] = (scaled * gain1 + shift1).astype(bf16)
        item = whose(p) * items_here + t // (SEQ // TILE)
        scale = jnp.sum(jnp.where(item_lane == item, scales, 0.0), axis=1, keepdims=True)
        inside = position + lax.rem(t, SEQ // TILE) * TILE < lens[item]
        scaled_cot = cot[p, here, :] * jnp.where(inside, scale, 0.0)
        cot[p, here, :] = scaled_cot
        e2[p, here, :] = scaled_cot.astype(bf16)

    c_copies[0].wait_recv()
    c_copies[2].start()
    loop(0, 2 * tiles, first_norm)
    c_copies[1].wait_recv()
    c_copies[2].wait_recv()
    for j in range(2):
        last_core(j, 0).start()

    def gather(step):
        pl.when(step < nz)(lambda: gather0(step))

        @pl.when(step == nz - 1)
        def _():
            for j in range(2):
                for n in range(1, nz):
                    last_z(j, n).start()

        pl.when(step <= nz)(lambda: gather1(step - 1))
        pl.when(step >= 2)(lambda: gather2(step - 2))

    loop(1, nz + 2, gather)
    loop(1, nz, gather_last)

    def all_here(k):
        zz = order(k)
        for kind, (xx, yy) in enumerate(((x, y), (x, 1 - y), (1 - x, y), (1 - x, 1 - y))):
            same(slab(xx * 2 + 1 - c, zz, yy, part_ab), core_s.at[k, kind], core_r.at[k, kind], core_peer).wait_recv()
        for j in range(2):
            last_core(j, k).wait_recv()

    loop(0, nz, all_here)

    head_lane = lax.broadcasted_iota(jnp.int32, (1, W), 1)
    head_masks = [head_lane < HD, head_lane >= HD]
    key_pos = lax.broadcasted_iota(jnp.int32, (1, SEQ), 1)
    item_rows = [slice(i * SEQ, (i + 1) * SEQ) for i in range(items_here)]

    def only(values, a):
        return jnp.where(head_masks[a], values, jnp.zeros_like(values))

    def stack(values):
        return jnp.concatenate([only(values, 0), only(values, 1)], axis=0)

    def wide_matrix(h):
        return jnp.concatenate(
            [
                jnp.concatenate([wv[h, rows[j], p * W : (p + 1) * W, :] for j in range(QB)], axis=0)
                for p in range(3)
            ],
            axis=1,
        )

    def narrow_matrix(h, first, size):
        pieces = cat_pieces(first, size)
        return jnp.concatenate(
            [
                jnp.concatenate(
                    [wv[h, rows[b], pl.ds(p * (R // 4) + inside, count), :] for b, inside, _, count in pieces], axis=0
                )
                for p in range(4)
            ],
            axis=1,
        )

    deep, low = (QB + 2, CB - 2), (0, QB + 2)
    x_part, y_part, z_part = pl.ds(0, RA), pl.ds(RA, RB - RA), pl.ds(RB, R - RB)

    def core_push(j, n):
        part = pl.ds(*(deep, low)[n])
        return remote(grads.at[j, part], from_core.at[j, part], cs.at[n, j], cr.at[n, j], core_peer)

    def x_push(n):
        part = pl.ds(*(deep, low)[n])
        return remote(grads.at[2, part, x_part, :], rxa.at[part], as_.at[n], ar.at[n], x_peer)

    def hand_over(i, n):
        first, count = (deep, low)[n]
        pl.when(i < 2)(lambda: core_push(i, n).start())

        @pl.when(i >= 2)
        def _():
            core_push(i - 2, n).wait_recv()

            def add(block):
                grads[i, block] = grads[i, block] + from_core[i - 2, block]

            loop(first, first + count, add)
            pl.when(i == 2)(lambda: x_push(n).start())

    pair_z, cross_z = z + 1 - 2 * lax.rem(z, 2), lax.rem(z + 2, nz)

    def chunk(k):
        return lax.rem(pair_z + lax.rem(k, 2) * (z - pair_z) + 2 * (1 - k // 2), nz)

    def block_of(k, yy, r):
        return block_at[(chunk(k) * 2 + yy) * CAP + r]

    def over_y_first(k):
        return remote(sb.at[k], ryb.at[k], sby_s.at[k], sby_r.at[k], y_peer)

    def over_x_last(k):
        return remote(sbx.at[k], rxb.at[k], sbx_s.at[k], sbx_r.at[k], x_peer)

    def over_y_last(k):
        return remote(sa.at[k], rya.at[k], say_s.at[k], say_r.at[k], y_peer)

    def over_z(k, r):
        goal = pair_z + lax.rem(k, 2) * (cross_z - pair_z)
        return remote(fz.at[k, r], rz.at[k, r], fz_s.at[k, r], fz_r.at[k, r], device(goal, y, x, c))

    def z_first(k):
        goal = pair_z + lax.rem(k, 2) * (cross_z - pair_z)
        return remote(sc.at[k], rc.at[k], sc_s.at[k], sc_r.at[k], device(goal, y, x, c))

    def z_then_y():
        return remote(sc.at[nz - 1, :, 1 - y], ryc, cy_s, cy_r, y_peer)

    def z_then_x():
        return remote(sc.at[nz - 1, 0, y], rxc, cx_s, cx_r, x_peer)

    def send_c(k):
        for r in range(2 * CAP):
            block = block_of(k, r // CAP, r % CAP)
            for j in range(2):
                sc[k, j, r // CAP, r % CAP] = grads[2 + j, block, z_part, :]
        pl.when(lax.rem(k, 2) == 0)(lambda: z_first(k).start())

    def cross_c():
        z_first(0).wait_recv()
        for j in range(2):
            sc[1, j] = sc[1, j] + rc[0, j]
        z_first(1).start()

    def own_c():
        z_first(1).wait_recv()
        z_first(2).wait_recv()
        for j in range(2):
            sc[nz - 1, j] = sc[nz - 1, j] + (rc[1, j].astype(f32) + rc[2, j].astype(f32)).astype(bf16)
        z_then_y().start()

    def y_c():
        z_then_y().wait_recv()
        for j in range(2):
            sc[nz - 1, j, y] = sc[nz - 1, j, y] + ryc[j]
        z_then_x().start()

    def norm_copies():
        z_peers = [device(lax.rem(z + k, nz), y, x, c) for k in range(1, nz)]
        return [
            remote(norm_part, n_core, n_s.at[0], n_r.at[0], core_peer),
            remote(norm_sum.at[0], n_x, n_s.at[1], n_r.at[1], x_peer),
            remote(norm_sum.at[1], n_y, n_s.at[2], n_r.at[2], y_peer),
        ] + [remote(norm_sum.at[2], n_z.at[k], n_s.at[3 + k], n_r.at[3 + k], p) for k, p in enumerate(z_peers)]

    def send_b(k):
        for r in range(CAP):
            block = block_of(k, 1 - y, r)
            for j in range(2):
                sb[k, j, r] = grads[2 + j, block, y_part, :]
        over_y_first(k).start()

    def add_x(j):
        grads[3, j, x_part, :] = grads[3, j, x_part, :] + rxa[j]

    def send_a(k):
        for r in range(CAP):
            sa[k, r] = grads[3, block_of(k, 1 - y, r), x_part, :]
        over_y_last(k).start()

    def reduce1(k):
        over_y_first(k).wait_recv()
        for r in range(CAP):
            sbx[k, r] = grads[2, block_of(k, y, r), y_part, :] + ryb[k, 0, r]
        over_x_last(k).start()

    def reduce2(k):
        over_y_last(k).wait_recv()
        over_x_last(k).wait_recv()
        for r in range(CAP):
            block = block_of(k, y, r)
            fz[k, r, x_part, :] = grads[3, block, x_part, :] + rya[k, r]
            part = grads[3, block, y_part, :].astype(f32) + ryb[k, 1, r].astype(f32)
            fz[k, r, y_part, :] = (part + rxb[k, r].astype(f32)).astype(bf16)
            pl.when(lax.rem(k, 2) == 0)(over_z(k, r).start)

    def cross():
        for r in range(CAP):
            over_z(0, r).wait_recv()
            fz[1, r] = fz[1, r] + rz[0, r]
            over_z(1, r).start()

    key_row = lax.broadcasted_iota(jnp.int32, (2 * SEQ, W), 0)
    head_ones = jnp.where((key_row < SEQ) == head_masks[0], 1.0, 0.0).astype(bf16)

    def attention(p, h):
        projected = dot(low1[p], wide_matrix(h))
        qkv[h, 0] = (projected[:, :W].astype(bf16).astype(f32) * (1.0 / math.sqrt(HD))).astype(bf16)
        qkv[h, 1] = projected[:, W : 2 * W].astype(bf16)
        qkv[h, 2] = projected[:, 2 * W :].astype(bf16)
        for i, here in enumerate(item_rows):
            query, key, value = qkv[h, 0, here, :], qkv[h, 1, here, :], qkv[h, 2, here, :]
            valid = key_pos < lens[whose(p) * items_here + i]
            both = []
            for a in range(2):
                scores = jnp.where(valid, dot_cols(only(query, a), key), -1e30)
                exps = jnp.exp(scores - jnp.max(scores, axis=-1, keepdims=True)).astype(bf16)
                probs[h, i, a] = exps
                both.append(exps)
            mixed = dot(jnp.concatenate(both, axis=1), jnp.concatenate([stack(value), head_ones], axis=1))
            inverse = 1.0 / mixed[:, W:]
            sums[h, here, :] = inverse
            att[h, here, :] = (mixed[:, :W] * inverse).astype(bf16)
        acc[...] += dot(att[h], narrow_matrix(h, 0, W))

    def put(i, first, result):
        for block, inside, row, count in cat_pieces(first, result.shape[0]):
            for p in range(4):
                here = pl.ds(p * (R // 4) + inside, count)
                grads[i, block, here, :] = result[row : row + count, p * W : (p + 1) * W].astype(bf16)

    def shard_of(p, i):
        return lax.rem(1 + x + p + i, 2) * 2 + lax.rem(c + 1 + i // 2, 2)

    def feed_forward(p, i):
        h = shard_of(p, i)
        up_matrix, down_matrix = narrow_matrix(h, W, D), narrow_matrix(h, W + D, D)
        hidden = dot(low2[...], up_matrix)
        root = math.sqrt(2.0 / math.pi)
        square = hidden * hidden
        bend = jnp.tanh(root * hidden * (1.0 + 0.044715 * square))
        half = 0.5 * (1.0 + bend)
        active = (hidden * half).astype(bf16)
        slope = half + 0.5 * hidden * (1.0 - bend * bend) * (root + (3.0 * 0.044715 * root) * square)
        if p == 0:
            actives[i] = active
        else:
            acc[...] += dot(active, down_matrix)
        back = (dot_cols(e2[p], down_matrix) * slope).astype(bf16)
        da[...] += dot_cols(back, up_matrix)
        if p == 0:
            put(i, W + D, dot_rows(active, e2[p]))
            put(i, W, dot_rows(low2[...], back))
            hand_over(i, 0)

    def attention_back(p, i):
        h = shard_of(p, i)
        d_all = dot_cols(e1[...], narrow_matrix(h, 0, W)) * sums[h]
        shared_all = (d_all * att[h].astype(f32)).astype(bf16)
        d_all = d_all.astype(bf16)
        parts = []
        for m, here in enumerate(item_rows):
            query, key, value = qkv[h, 0, here, :], qkv[h, 1, here, :], qkv[h, 2, here, :]
            d_here, shared = d_all[here, :], shared_all[here, :]
            against = jnp.concatenate([value, jnp.full((SEQ, W), -1.0, bf16)], axis=1)
            d_scores = []
            for a in range(2):
                change = dot_cols(jnp.concatenate([only(d_here, a), only(shared, a)], axis=1), against)
                d_scores.append((probs[h, m, a].astype(f32) * change).astype(bf16))
            d_query = dot(jnp.concatenate(d_scores, axis=1), stack(key)) * (1.0 / math.sqrt(HD))
            d_key = dot_rows(jnp.concatenate(d_scores, axis=0), stack(query))
            d_value = dot_rows(jnp.concatenate([probs[h, m, 0], probs[h, m, 1]], axis=0), stack(d_here))
            parts.append(jnp.concatenate([d_query, d_key, d_value], axis=1).astype(bf16))
        d_qkv = jnp.concatenate(parts, axis=0)
        if p == 0:
            d_qkvs[i] = d_qkv
            put(i, 0, dot_rows(att[h], e1[...]))
            d_weight = dot_rows(low1[p], d_qkv).astype(bf16)
            for j in range(QB):
                for m in range(3):
                    grads[i, j, m * W : (m + 1) * W, :] = d_weight[j * W : (j + 1) * W, m * W : (m + 1) * W]
            hand_over(i, 1)
        else:
            da[...] += dot_cols(d_qkv, wide_matrix(h))

    def late_output(i):
        acc[...] += dot(actives[i], narrow_matrix(shard_of(0, i), W + D, D))

    def late_input(i):
        da[...] += dot_cols(d_qkvs[i], wide_matrix(shard_of(0, i)))

    def norm_backward(grad, scaled, inverse, gain):
        grad_scaled = grad * gain
        centre = jnp.mean(grad_scaled, axis=-1, keepdims=True)
        slope = jnp.mean(grad_scaled * scaled, axis=-1, keepdims=True)
        return inverse * (grad_scaled - centre - scaled * slope)

    def add_norm(p, row, grad, scaled):
        if p == 0:
            norm_part[row : row + 1, :] += jnp.sum(grad * scaled, axis=0, keepdims=True)
            norm_part[row + 1 : row + 2, :] += jnp.sum(grad, axis=0, keepdims=True)

    norm_part[...] = jnp.zeros_like(norm_part)

    def out_copies(p, n):
        src, dst = ((out_low, out_all), (in_low, in_all))[n]
        there = tokens_of(dst, whose(p))
        return (
            pltpu.make_async_copy(src.at[p], there, o_l.at[p, n]),
            remote(src.at[p], there, o_s.at[p, n], o_r.at[p, n], core_peer),
        )

    def block_result(p):
        out_low[p] = acc[...].astype(bf16)
        for copy in out_copies(p, 0):
            copy.start()

    def input_result(p):
        def first_norm_back(t):
            here = tile(t)
            grad, scaled = da[here, :], xhat1[p, here, :]
            add_norm(p, 0, grad, scaled)
            in_low[p, here, :] = (cot[p, here, :] + norm_backward(grad, scaled, inv1[p, here, :], gain1)).astype(bf16)

        loop(0, tiles, first_norm_back)
        for copy in out_copies(p, 1):
            copy.start()

    def layer_pass(p):
        acc[...] = jnp.zeros_like(acc)
        loop(0, 4, lambda h: attention(p, h))

        def second_norm(t):
            here = tile(t)
            state = acc[here, :] + tok[p, here, :]
            acc[here, :] = state
            scaled, inverse = normalise(state)
            xhat2[here, :] = scaled
            inv2[here, :] = inverse
            low2[here, :] = (scaled * gain2 + shift2).astype(bf16)
            da[here, :] = jnp.zeros((TILE, D), f32)

        loop(0, tiles, second_norm)
        if p == 1:
            for n in range(2):
                x_push(n).wait_recv()
            loop(0, QB + CB, add_x)
            loop(0, nz, send_a)
            loop(0, nz, reduce1)
        loop(0, 4, lambda i: feed_forward(p, i))
        if p == 1:
            block_result(1)
            own_c()
            reduce2(0)
            norm_copies()[0].wait_recv()
            norm_sum[0] = norm_part[...] + n_core[...]
            norm_copies()[1].start()

        def second_norm_back(t):
            here = tile(t)
            grad, scaled = da[here, :], xhat2[here, :]
            add_norm(p, 2, grad, scaled)
            change = cot[p, here, :] + norm_backward(grad, scaled, inv2[here, :], gain2)
            cot[p, here, :] = change
            e1[here, :] = change.astype(bf16)
            da[here, :] = jnp.zeros((TILE, D), f32)

        loop(0, tiles, second_norm_back)
        if p == 1:
            norm_copies()[1].wait_recv()
            norm_sum[1] = norm_sum[0] + n_x[...]
            norm_copies()[2].start()
            reduce2(1)
            cross()

        def attention_step(i):
            attention_back(p, i)
            if p == 1:
                @pl.when(i == 1)
                def _():
                    reduce2(2)
                    y_c()

        loop(0, 4, attention_step)

    layer_pass(0)
    loop(0, nz, send_c)
    loop(0, nz, send_b)
    loop(0, 4, late_output)
    block_result(0)
    loop(0, 4, late_input)
    input_result(0)
    cross_c()
    norm_copies()[0].start()
    layer_pass(1)
    input_result(1)

    norm_copies()[2].wait_recv()
    norm_sum[2] = norm_sum[1] + n_y[...]
    for copy in norm_copies()[3:]:
        copy.start()
    reduce2(nz - 1)

    for k in range(nz - 1):
        norm_copies()[3 + k].wait_recv()
    z_then_x().wait_recv()
    for r in range(CAP):
        over_z(2, r).wait_recv()
        over_z(1, r).wait_recv()
    norm_total[...] = norm_sum[2] + ((n_z[0] + n_z[1]) + n_z[2])

    def last(r):
        others = rz[1, r].astype(f32) + rz[2, r].astype(f32)
        total[r, pl.ds(0, RB), :] = fz[nz - 1, r].astype(f32) + others
        total[r, z_part, :] = sc[nz - 1, 1, y, r].astype(f32) + rxc[r].astype(f32)

    loop(0, CAP, last)

    for p in range(2):
        for n in range(2):
            local, over_core = out_copies(p, n)
            local.wait()
            over_core.wait()
    for copy in norm_copies():
        copy.wait_send()
    for k in range(len(dp_peers)):
        meta_copy(k).wait_send()
    pl.when(up)(own_up.wait_send)
    pl.when(down)(own_down.wait_send)
    for copy in c_copies:
        copy.wait_send()

    def sent(k):
        for copy in first_copies(k) + second_copies(k) + third_copies(k):
            copy.wait_send()
        pl.when(jnp.logical_and(k > 0, inner))(along_z(k).wait_send)
        for j in range(2):
            last_core(j, k).wait_send()
            pl.when(k > 0)(last_z(j, k).wait_send)
        for copy in (over_y_first(k), over_x_last(k), over_y_last(k)):
            copy.wait_send()
        pl.when(k < nz - 1)(z_first(k).wait_send)
        for r in range(CAP):
            pl.when(k < nz - 1)(over_z(k, r).wait_send)

    loop(0, nz, sent)
    z_then_y().wait_send()
    z_then_x().wait_send()
    for n in range(2):
        x_push(n).wait_send()
        for j in range(2):
            core_push(j, n).wait_send()


def layer(tokens, cotangent, master, norms, steps, bands, lens_row, lens, owners):
    nz = Sizes.z
    here = tokens.shape[0] // lax.axis_size("head")
    items_here = here // SEQ
    items = lens.shape[0]
    vm = pl.BlockSpec(memory_space=pltpu.VMEM)
    hbm = pl.BlockSpec(memory_space=pltpu.HBM)
    dma = pltpu.SemaphoreType.DMA
    V, S = pltpu.VMEM, pltpu.SMEM
    square = (here, D)
    blocks = QB + CB
    rb = RB - RA
    low, full, two_low, two = V(square, bf16), V(square, f32), V((2, *square), bf16), V((2, *square), f32)
    scratch = [
        V((4, nz * 2 * CAP, R, W), bf16), V((R, CAP, W), f32), V((R, W), f32),
        V((8, W), f32), V((nz * 2, 8, W), f32), V(norms.shape, f32),
        V((1, items), jnp.int32), V((1, items), jnp.int32), V((1, items), jnp.int32),
        S((items,), jnp.int32), S(owners.shape, jnp.int32), S((nz * 2 * CAP,), jnp.int32),
        two, two, two_low, two, V((2, here, 1), f32), V((4, 3, here, W), bf16),
        V((4, items_here, 2, SEQ, SEQ), bf16), V((4, here, W), f32), V((4, here, W), bf16),
        full, low, full, V((here, 1), f32), two_low,
        V((4, here, D), bf16), V((4, here, 3 * W), bf16), full, low, two_low, two_low,
        V((4, blocks, R, W), bf16), V((2, blocks, R, W), bf16),
        V((blocks, RA, W), bf16), V((nz, CAP, RA, W), bf16), V((nz, CAP, RA, W), bf16),
        V((nz, 2, CAP, rb, W), bf16), V((nz, 2, CAP, rb, W), bf16), V((nz, CAP, rb, W), bf16),
        V((nz, CAP, rb, W), bf16), V((nz, CAP, RB, W), bf16), V((nz - 1, CAP, RB, W), bf16),
        V((nz, 2, 2, CAP, R - RB, W), bf16), V((nz - 1, 2, 2, CAP, R - RB, W), bf16),
        V((2, CAP, R - RB, W), bf16), V((CAP, R - RB, W), bf16),
        V((8, D), f32), V((3, 8, D), f32), V((8, D), f32), V((8, D), f32), V((8, D), f32), V((nz - 1, 8, D), f32),
        dma((11,)), dma((nz + 1,)), dma((nz,)), dma((nz,)), dma((nz,)), dma((nz, 2)), dma((nz, 2)), dma((nz,)), dma((nz,)),
        dma((nz, 2)), dma((nz, 2)), dma((nz, 4)), dma((nz, 4)), dma((8,)), dma((8,)),
        dma((3,)), dma((3,)), dma((2, nz)), dma((2, nz)), dma((2, nz)), dma((2, nz)),
        dma((nz,)), dma((nz,)), dma, dma, dma, dma,
        dma((2, 2)), dma((2, 2)), dma((2,)), dma((2,)), dma((nz,)), dma((nz,)), dma((nz,)), dma((nz,)),
        dma((nz,)), dma((nz,)), dma((nz, CAP)), dma((nz, CAP)), dma((8,)), dma((8,)), dma((2, 2)), dma((2, 2)), dma((2, 2)),
    ]
    return pl.pallas_call(
        layer_kernel,
        name="layer",
        out_shape=(
            jax.ShapeDtypeStruct((CAP, R, W), f32),
            jax.ShapeDtypeStruct(tokens.shape, bf16),
            jax.ShapeDtypeStruct(tokens.shape, bf16),
            jax.ShapeDtypeStruct((8, D), f32),
        ),
        in_specs=[hbm] * 9,
        out_specs=(vm, hbm, hbm, vm),
        scratch_shapes=scratch,
        compiler_params=pltpu.CompilerParams(collective_id=0, has_side_effects=True, vmem_limit_bytes=56 << 20),
    )(tokens, cotangent, master, norms, steps, bands, lens_row, lens, owners)


def finish_kernel(
    total_hbm, norm_hbm, master_hbm, first_hbm, second_hbm, norm_m, norm_f, norm_s, owners_hbm, out_all, in_all,
    block_output, input_grad, new_master, new_first, new_second, new_norm, new_norm_first, new_norm_second,
    out_low, in_low, out_full, in_full, states, results, flat, grad, total, norm_total, norm_master, norm_first, norm_second, owners, l_sem, s_sem, i_sem, r_sem,
):
    pieces = l_sem.shape[1]
    size = out_low.shape[0] // pieces
    pairs = ((out_all, out_low, out_full, block_output), (in_all, in_low, in_full, input_grad))

    def piece(p):
        return pl.ds(pl.multiple_of(p * size, size), size)

    def fetch(n, p):
        return pltpu.make_async_copy(pairs[n][0].at[piece(p), :], pairs[n][1].at[piece(p), :], l_sem.at[n, p])

    def store(n, p):
        return pltpu.make_async_copy(pairs[n][2].at[piece(p), :], pairs[n][3].at[piece(p), :], s_sem.at[n, p])

    small_copies = [
        pltpu.make_async_copy(src, dst, i_sem.at[3 + i])
        for i, (src, dst) in enumerate((
            (owners_hbm, owners), (total_hbm, total), (norm_hbm, norm_total),
            (norm_m, norm_master), (norm_f, norm_first), (norm_s, norm_second),
        ))
    ]
    state_copies = [
        pltpu.make_async_copy(src, states.at[i], i_sem.at[i]) for i, src in enumerate((master_hbm, first_hbm, second_hbm))
    ]
    result_copies = [
        pltpu.make_async_copy(results.at[i], dst, r_sem.at[i]) for i, dst in enumerate((new_master, new_first, new_second))
    ]

    def loop(count, body):
        def step(i, _):
            body(i)
            return 0

        lax.fori_loop(0, count, step, 0)

    for copy in small_copies:
        copy.start()
    loop(pieces, lambda p: fetch(0, p).start())
    for copy in state_copies:
        copy.start()
    loop(pieces, lambda p: fetch(1, p).start())

    dp = lax.axis_index("dp")
    small_copies[0].wait()
    rows = block_rows(owners)
    held = 0
    for j in range(owners.shape[0]):
        held = held + jnp.where(owners[j] == dp, 1, 0)

    def spread(r):
        is_wide = slot_is_wide(rows, dp * CAP + r)

        @pl.when(is_wide)
        def _():
            for p in range(3):
                flat[pl.ds(p, W, stride=3), :] = total[r, p * W : (p + 1) * W, :]

        @pl.when(jnp.logical_not(is_wide))
        def _():
            for p in range(4):
                flat[pl.ds(p, R // 4, stride=4), :] = total[r, p * (R // 4) : (p + 1) * (R // 4), :]

    small_copies[1].wait()
    for r in range(CAP):
        spread(r)
        grad[:, r, :] = flat[...]

    def convert(n, p):
        fetch(n, p).wait()
        _, low, full, _ = pairs[n]
        full[piece(p), :] = low[piece(p), :].astype(f32)
        store(n, p).start()

    loop(pieces, lambda p: convert(0, p))
    for copy in state_copies:
        copy.wait()
    step = 32
    slot = lax.broadcasted_iota(jnp.int32, (step, CAP, W), 1)

    def update(i):
        here = pl.ds(pl.multiple_of(i * step, step), step)
        new = adamw_update(states[0, here], states[1, here], states[2, here], grad[here], weight_decay, learn_rate)
        for n in range(3):
            results[n, here] = jnp.where(slot < held, new[n], 0.0)

    loop(R // step, update)
    for copy in result_copies:
        copy.start()
    for copy in small_copies[2:]:
        copy.wait()
    pair = norm_total[:, pl.ds(pl.multiple_of((dp // 2) * W, W), W)]
    mine = jnp.where(lax.rem(dp, 2) == 1, pltpu.roll(pair, W // 2, 1), pair)[0:4, 0 : norm_master.shape[1]]
    new = adamw_update(norm_master[...], norm_first[...], norm_second[...], mine, 0.0, norm_rate)
    for ref, value in zip((new_norm, new_norm_first, new_norm_second), new):
        ref[...] = value
    loop(pieces, lambda p: convert(1, p))
    for n in range(2):
        loop(pieces, lambda p: store(n, p).wait())
    for copy in result_copies:
        copy.wait()


def finish(total, norm_total, slots, norms, owners, out_all, in_all):
    vm = pl.BlockSpec(memory_space=pltpu.VMEM)
    hbm = pl.BlockSpec(memory_space=pltpu.HBM)
    dma = pltpu.SemaphoreType.DMA
    V = pltpu.VMEM
    pieces = 8
    shape = out_all.shape
    return pl.pallas_call(
        finish_kernel,
        name="finish",
        out_shape=(
            (jax.ShapeDtypeStruct(shape, f32),) * 2 + tuple(jax.ShapeDtypeStruct(a.shape, f32) for a in slots + norms)
        ),
        in_specs=[hbm] * 11,
        out_specs=(hbm,) * 5 + (vm,) * 3,
        scratch_shapes=[
            V(shape, bf16), V(shape, bf16), V(shape, f32), V(shape, f32), V((3, R, CAP, W), f32), V((3, R, CAP, W), f32),
            V((R, W), f32), V((R, CAP, W), f32),
            V(total.shape, f32), V(norm_total.shape, f32), *(V(a.shape, f32) for a in norms),
            pltpu.SMEM(owners.shape, jnp.int32), dma((2, pieces)), dma((2, pieces)), dma((9,)), dma((3,)),
        ],
        compiler_params=pltpu.CompilerParams(vmem_limit_bytes=60 << 20),
    )(total, norm_total, *slots, *norms, owners, out_all, in_all)


def fast_shards(
    tokens, cotangent, timesteps, bands, lengths, owners,
    master_slots, first_slots, second_slots, norm_master, norm_first, norm_second,
):
    def tiles(slots):
        return jnp.transpose(slots.reshape(CAP, R, W), (1, 0, 2))

    def flat(slots):
        return jnp.transpose(slots, (1, 0, 2)).reshape(CAP, R * W)

    steps, bands_row, lens_row = (v.reshape(1, -1) for v in (timesteps, bands, lengths))
    slots = tuple(tiles(s) for s in (master_slots, first_slots, second_slots))
    norms = (norm_master, norm_first, norm_second)
    total, out_all, in_all, norm_total = layer(
        tokens, cotangent, slots[0], norm_master, steps, bands_row, lens_row, lengths, owners
    )
    results = finish(total, norm_total, slots, norms, owners, out_all, in_all)
    return (*results[:2], *(flat(s) for s in results[2:5]), *results[5:])


def solution(mesh):
    fits = dict(mesh.shape) == {"dp": 8, "head": 4}
    placed = (
        P("dp", None),
        P("dp", None),
        P("dp"),
        P("dp"),
        P("dp"),
        P(),
        P("dp", "head"),
        P("dp", "head"),
        P("dp", "head"),
        P(None, "dp"),
        P(None, "dp"),
        P(None, "dp"),
    )
    return jax.shard_map(
        fast_shards if fits else shards,
        mesh=mesh,
        in_specs=placed,
        out_specs=(
            P("dp", None),
            P("dp", None),
            P("dp", "head"),
            P("dp", "head"),
            P("dp", "head"),
            P(None, "dp"),
            P(None, "dp"),
            P(None, "dp"),
        ),
        check_vma=False,
    )
```

```python
import math

import jax
import jax.numpy as jnp
from jax import lax
from jax.experimental import pallas as pl
from jax.experimental.pallas import tpu as pltpu
from jax.sharding import PartitionSpec as P

D = 512
H = 8
HD = 64
FF = 2048
SEQ = 256
TSTEPS = 1000
NBANDS = 8
CAP = 3
STEP = 5


beta_one = 0.5
beta_two = 0.5
learn_rate = 0.04
norm_rate = 0.4
weight_decay = 0.1
adam_eps = 1e-08
norm_eps = 1e-05


def contract_rows(left_side, right_side):
    return lax.dot_general(
        left_side, right_side, (((0,), (0,)), ((), ())), preferred_element_type=jnp.float32
    )


def contract_cols(left_side, right_side):
    return lax.dot_general(
        left_side, right_side, (((1,), (1,)), ((), ())), preferred_element_type=jnp.float32
    )


def gelu_tanh(values):
    return jax.nn.gelu(values, approximate=True)


def norm_forward(values, gain_row, shift_row):
    average = jnp.mean(values, axis=-1, keepdims=True)
    centred = values - average
    inverse = lax.rsqrt(jnp.mean(centred * centred, axis=-1, keepdims=True) + norm_eps)
    scaled = centred * inverse
    return (scaled * gain_row + shift_row, scaled, inverse)


def norm_backward(grad_normed, scaled, inverse, gain_row):
    grad_scaled = grad_normed * gain_row
    centre_term = jnp.mean(grad_scaled, axis=-1, keepdims=True)
    slope_term = jnp.mean(grad_scaled * scaled, axis=-1, keepdims=True)
    return inverse * (grad_scaled - centre_term - scaled * slope_term)


def slot_rows(owners, capacity):
    block_index = jnp.arange(owners.shape[0], dtype=jnp.int32)
    earlier = (owners[None, :] == owners[:, None]) & (block_index[None, :] < block_index[:, None])
    return owners * capacity + jnp.sum(earlier.astype(jnp.int32), axis=1)


def attention_scores(query_heads, key_heads, key_valid):
    scores = jnp.einsum(
        "gqad,gkad->gaqk", query_heads, key_heads, preferred_element_type=jnp.float32
    ) / math.sqrt(HD)
    return jnp.where(key_valid[:, None, None, :], scores, -1e30)


def adamw_update(weight, first_moment, second, gradient, decay_rate, step_rate):
    new_first = beta_one * first_moment + (1.0 - beta_one) * gradient
    new_second = beta_two * second + (1.0 - beta_two) * gradient * gradient
    first_hat = new_first / (1.0 - beta_one**STEP)
    second_hat = new_second / (1.0 - beta_two**STEP)
    new_weight = weight - step_rate * (
        first_hat / (jnp.sqrt(second_hat) + adam_eps) + decay_rate * weight
    )
    return (new_weight, new_first, new_second)


def shards(
    tokens,
    cotangent,
    timesteps,
    bands,
    lengths,
    owners,
    master_slots,
    first_slots,
    second_slots,
    norm_master,
    norm_first,
    norm_second,
):
    head_count = lax.axis_size("head")
    owner_index = lax.axis_index("dp")
    heads_here = H // head_count
    width_here = heads_here * HD
    units_here = FF // head_count
    block_len = master_slots.shape[1]
    norm_cols = norm_master.shape[1]
    row_count = tokens.shape[0]
    item_count = lengths.shape[0]
    block_count = owners.shape[0]
    slot_row = slot_rows(owners, CAP)
    gathered, norm_whole = (
        lax.all_gather(master_slots.astype(jnp.bfloat16), "dp", axis=0, tiled=True),
        lax.all_gather(norm_master.astype(jnp.bfloat16), "dp", axis=1, tiled=True),
    )
    flat_params = gathered[slot_row].reshape(-1)
    qkv_end = 3 * D * width_here
    out_end = qkv_end + width_here * D
    up_end = out_end + D * units_here
    qkv_weight = flat_params[:qkv_end].reshape(D, 3 * width_here)
    out_weight = flat_params[qkv_end:out_end].reshape(width_here, D)
    up_weight = flat_params[out_end:up_end].reshape(D, units_here)
    down_weight = flat_params[up_end:].reshape(units_here, D)
    norm_params = norm_whole.astype(jnp.float32)
    item_weight = jnp.exp(-2.0 * timesteps.astype(jnp.float32) / TSTEPS)
    item_length = lengths.astype(jnp.float32)
    band_table = (bands[:, None] == jnp.arange(NBANDS, dtype=jnp.int32)[None, :]).astype(
        jnp.float32
    )
    weight_sums, count_sums = lax.psum(
        (
            jnp.sum(band_table * (item_weight * item_length)[:, None], axis=0),
            jnp.sum(band_table * item_length[:, None], axis=0),
        ),
        "dp",
    )
    item_scale = (
        item_weight
        * jnp.sum(band_table * count_sums[None, :], axis=1)
        / jnp.sum(band_table * weight_sums[None, :], axis=1)
    )
    key_valid = jnp.arange(SEQ, dtype=jnp.int32)[None, :] < lengths[:, None]
    token_scale = jnp.where(key_valid, item_scale[:, None], 0.0).reshape(row_count)
    normed_one, scaled_one, inverse_one = norm_forward(tokens, norm_params[0], norm_params[1])
    normed_one_low = normed_one.astype(jnp.bfloat16)
    projected_low = jnp.dot(normed_one_low, qkv_weight, preferred_element_type=jnp.float32).astype(
        jnp.bfloat16
    )
    head_shape = (item_count, SEQ, heads_here, HD)
    query_heads = projected_low[:, :width_here].reshape(head_shape)
    key_heads = projected_low[:, width_here : 2 * width_here].reshape(head_shape)
    value_heads = projected_low[:, 2 * width_here :].reshape(head_shape)
    scores = attention_scores(query_heads, key_heads, key_valid)
    row_max = jnp.max(scores, axis=-1, keepdims=True)
    exp_scores = jnp.exp(scores - row_max)
    row_total = jnp.sum(exp_scores, axis=-1, keepdims=True)
    log_total = row_max + jnp.log(row_total)
    prob_low = (exp_scores / row_total).astype(jnp.bfloat16)
    attended_low = (
        jnp.einsum("gaqk,gkad->gqad", prob_low, value_heads, preferred_element_type=jnp.float32)
        .astype(jnp.bfloat16)
        .reshape(row_count, width_here)
    )
    attn_sum = lax.psum(
        jnp.dot(attended_low, out_weight, preferred_element_type=jnp.float32).astype(jnp.bfloat16),
        "head",
    ).astype(jnp.float32)
    mixed_state = tokens + attn_sum
    normed_two, scaled_two, inverse_two = norm_forward(mixed_state, norm_params[2], norm_params[3])
    normed_two_low = normed_two.astype(jnp.bfloat16)
    hidden = jnp.dot(normed_two_low, up_weight, preferred_element_type=jnp.float32)
    activated, gelu_pull = jax.vjp(gelu_tanh, hidden)
    activated_low = activated.astype(jnp.bfloat16)
    ffn_sum = lax.psum(
        jnp.dot(activated_low, down_weight, preferred_element_type=jnp.float32).astype(
            jnp.bfloat16
        ),
        "head",
    ).astype(jnp.float32)
    block_output = mixed_state + ffn_sum
    grad_state = cotangent * token_scale[:, None]
    grad_low_two = grad_state.astype(jnp.bfloat16)
    grad_down = contract_rows(activated_low, grad_low_two)
    grad_activated = contract_cols(grad_low_two, down_weight)
    grad_hidden_low = gelu_pull(grad_activated)[0].astype(jnp.bfloat16)
    grad_up = contract_rows(normed_two_low, grad_hidden_low)
    grad_normed_two = lax.psum(
        contract_cols(grad_hidden_low, up_weight).astype(jnp.bfloat16), "head"
    ).astype(jnp.float32)
    grad_mixed = grad_state + norm_backward(
        grad_normed_two, scaled_two, inverse_two, norm_params[2]
    )
    grad_low_one = grad_mixed.astype(jnp.bfloat16)
    grad_out_proj = contract_rows(attended_low, grad_low_one)
    grad_attended_low = (
        contract_cols(grad_low_one, out_weight).astype(jnp.bfloat16).reshape(head_shape)
    )
    scores_again = attention_scores(query_heads, key_heads, key_valid)
    probabilities = jnp.exp(scores_again - log_total)
    prob_again_low = probabilities.astype(jnp.bfloat16)
    grad_values = jnp.einsum(
        "gaqk,gqad->gkad", prob_again_low, grad_attended_low, preferred_element_type=jnp.float32
    )
    grad_probs = jnp.einsum(
        "gqad,gkad->gaqk", grad_attended_low, value_heads, preferred_element_type=jnp.float32
    )
    grad_scores_low = (
        probabilities * (grad_probs - jnp.sum(grad_probs * probabilities, axis=-1, keepdims=True))
    ).astype(jnp.bfloat16)
    grad_queries = jnp.einsum(
        "gaqk,gkad->gqad", grad_scores_low, key_heads, preferred_element_type=jnp.float32
    ) / math.sqrt(HD)
    grad_keys = jnp.einsum(
        "gaqk,gqad->gkad", grad_scores_low, query_heads, preferred_element_type=jnp.float32
    ) / math.sqrt(HD)
    grad_projected_low = jnp.concatenate(
        [
            grad_queries.reshape(row_count, width_here),
            grad_keys.reshape(row_count, width_here),
            grad_values.reshape(row_count, width_here),
        ],
        axis=1,
    ).astype(jnp.bfloat16)
    grad_qkv = contract_rows(normed_one_low, grad_projected_low)
    grad_normed_one = lax.psum(
        contract_cols(grad_projected_low, qkv_weight).astype(jnp.bfloat16), "head"
    ).astype(jnp.float32)
    input_grad = grad_mixed + norm_backward(
        grad_normed_one, scaled_one, inverse_one, norm_params[0]
    )
    norm_grads = jnp.stack(
        [
            jnp.sum(grad_normed_one * scaled_one, axis=0),
            jnp.sum(grad_normed_one, axis=0),
            jnp.sum(grad_normed_two * scaled_two, axis=0),
            jnp.sum(grad_normed_two, axis=0),
        ]
    )
    grad_blocks = jnp.concatenate(
        [
            grad_qkv.reshape(-1),
            grad_out_proj.reshape(-1),
            grad_up.reshape(-1),
            grad_down.reshape(-1),
        ]
    ).reshape(block_count, block_len)
    summed, norm_summed = (
        lax.psum(grad_blocks.astype(jnp.bfloat16), "dp").astype(jnp.float32),
        lax.psum(norm_grads.astype(jnp.bfloat16), "dp").astype(jnp.float32),
    )
    landing = jnp.where(owners == owner_index, slot_row - owner_index * CAP, CAP)
    owned_grad = jnp.zeros((CAP, block_len), jnp.float32).at[landing].set(summed, mode="drop")
    norm_owned = lax.dynamic_slice_in_dim(norm_summed, owner_index * norm_cols, norm_cols, 1)
    held_count = jnp.sum((owners == owner_index).astype(jnp.int32))
    used_slot = (jnp.arange(CAP, dtype=jnp.int32) < held_count)[:, None]
    new_master, new_first, new_second = adamw_update(
        master_slots, first_slots, second_slots, owned_grad, weight_decay, learn_rate
    )
    new_master = jnp.where(used_slot, new_master, 0.0)
    new_first = jnp.where(used_slot, new_first, 0.0)
    new_second = jnp.where(used_slot, new_second, 0.0)
    new_norms, new_norm_first, new_norm_second = adamw_update(
        norm_master, norm_first, norm_second, norm_owned, 0.0, norm_rate
    )
    return (
        block_output,
        input_grad,
        new_master,
        new_first,
        new_second,
        new_norms,
        new_norm_first,
        new_norm_second,
    )


W = 128
R = 384
QB = 4
CB = 12
MESH = pl.DeviceIdType.MESH
bf16 = jnp.bfloat16
f32 = jnp.float32


def place(sizes):
    dp = lax.axis_index("dp")
    head = lax.axis_index("head")
    return dp // sizes.y, lax.rem(dp, sizes.y), head // sizes.c, lax.rem(head, sizes.c)


class Sizes:
    z, y, x, c = 4, 2, 2, 2


def device(z, y, x, c):
    return (z * Sizes.y + y, x * Sizes.c + c)


def block_rows(owners):
    ids = [owners[j] for j in range(owners.shape[0])]
    rows = []
    for j, mine in enumerate(ids):
        row = mine * CAP
        for other in ids[:j]:
            row = row + jnp.where(other == mine, 1, 0)
        rows.append(row)
    return rows


def slot_is_wide(rows, slot_row):
    flag = rows[0] == slot_row
    for row in rows[1:QB]:
        flag = jnp.logical_or(flag, row == slot_row)
    return flag


def dot(left, right):
    return jnp.dot(left, right, preferred_element_type=f32)


def dot_cols(left, right):
    return lax.dot_general(left, right, (((1,), (1,)), ((), ())), preferred_element_type=f32)


def dot_rows(left, right):
    return lax.dot_general(left, right, (((0,), (0,)), ((), ())), preferred_element_type=f32)


def normalise(values):
    centred = values - jnp.mean(values, axis=-1, keepdims=True)
    inverse = lax.rsqrt(jnp.mean(centred * centred, axis=-1, keepdims=True) + norm_eps)
    return centred * inverse, inverse


def panels(ref, h, first, size):
    return jnp.concatenate([ref[h, p, first : first + size, :] for p in range(ref.shape[1])], axis=1)


def cat_pieces(first, size):
    pieces = []
    row = first
    while row < first + size:
        block, inside = divmod(row, R // 4)
        count = min(R // 4 - inside, first + size - row)
        pieces.append((QB + block, inside, row - first, count))
        row += count
    return pieces


RA, RB = 224, 304
GA, GB = 176, 336
TILE = 128


def layer_kernel(
    tok_hbm, cot_hbm, master_hbm, norms_hbm, steps_hbm, bands_hbm, lens_row_hbm, lens_hbm, owners_hbm,
    total, out_all, in_all, norm_total,
    wv, master, flat, mine, meta, norms_v, steps, bands, lens_row, lens, owners, block_at,
    tok, cot, low1, xhat1, inv1, qkv, probs, sums, att, acc, low2, xhat2, inv2, e2, actives, d_qkvs, da, e1,
    out_low, in_low,
    grads, from_core, rxa, sa, rya, sb, ryb, sbx, rxb, fz, rz, sc, rc, ryc, rxc, norm_part, norm_sum, n_core, n_x, n_y, n_z,
    i_sem, z_s, z_r, ya_s, ya_r, xa_s, xa_r, xb_s, xb_r, yb_s, yb_r, core_s, core_r, m_s, m_r,
    c_s, c_r, zc_s, zc_r, cc_s, cc_r, sc_s, sc_r, cy_s, cy_r, cx_s, cx_r,
    cs, cr, as_, ar, say_s, say_r, sby_s, sby_r, sbx_s, sbx_r, fz_s, fz_r, n_s, n_r, o_s, o_r, o_l,
):
    z, y, x, c = place(Sizes)
    nz = Sizes.z
    dp, head = z * 2 + y, x * 2 + c
    dp_peers = [device(lax.rem(z + k, nz), (y + j) % 2, x, c) for k in range(nz) for j in range(2) if k or j]
    x_peer, y_peer, core_peer = device(z, y, 1 - x, c), device(z, 1 - y, x, c), device(z, y, x, 1 - c)
    peers = dp_peers + [x_peer, core_peer]
    barrier = pltpu.get_barrier_semaphore()
    for peer in peers:
        pl.semaphore_signal(barrier, inc=1, device_id=peer, device_id_type=MESH)

    tokens_here = tok.shape[1]
    items_here = tokens_here // SEQ
    tiles = tokens_here // TILE

    def whose(p):
        return lax.rem(x + p, 2) * 2 + c

    def tokens_of(ref, who):
        return ref.at[pl.ds(pl.multiple_of(who * tokens_here, tokens_here), tokens_here), :]

    fetches = [
        pltpu.make_async_copy(src, dst, i_sem.at[n])
        for n, (src, dst) in enumerate((
            (owners_hbm, owners), (master_hbm, master), (steps_hbm, steps), (bands_hbm, bands),
            (lens_row_hbm, lens_row), (norms_hbm, norms_v), (lens_hbm, lens),
            (tokens_of(tok_hbm, whose(0)), tok.at[0]), (tokens_of(cot_hbm, whose(0)), cot.at[0]),
            (tokens_of(tok_hbm, whose(1)), tok.at[1]), (tokens_of(cot_hbm, whose(1)), cot.at[1]),
        ))
    ]
    for fetch in fetches:
        fetch.start()

    def loop(first, last, body):
        def step(i, _):
            body(i)
            return 0

        lax.fori_loop(first, last, step, 0)

    def remote(src, dst, send, recv, peer):
        return pltpu.make_async_remote_copy(
            src_ref=src, dst_ref=dst, send_sem=send, recv_sem=recv, device_id=peer, device_id_type=MESH
        )

    def same(ref, send, recv, peer):
        return remote(ref, ref, send, recv, peer)

    shard, far = x * 2 + c, (1 - x) * 2 + c
    fetches[0].wait()
    rows = block_rows(owners)
    fetches[1].wait()
    for r in range(CAP):
        flat[...] = master[:, r, :]
        wide = jnp.concatenate([flat[pl.ds(p, W, stride=3), :] for p in range(3)], axis=0)
        narrow = jnp.concatenate([flat[pl.ds(p, R // 4, stride=4), :] for p in range(4)], axis=0)
        wv[shard, dp * CAP + r] = jnp.where(slot_is_wide(rows, dp * CAP + r), wide, narrow).astype(bf16)

    for n in (2, 3, 4, 5):
        fetches[n].wait()
    items = steps.shape[1]
    item_weight = jnp.exp(-2.0 * steps[...].astype(f32) / TSTEPS)
    item_length = lens_row[...].astype(f32)
    table = bands[...] == lax.broadcasted_iota(jnp.int32, (NBANDS, items), 0)
    ones = table.astype(f32)
    mine[...] = jnp.zeros_like(mine)
    mine[0:4, 0 : W // 2] = norms_v[...]
    mine[:, W // 2 : W // 2 + 1] = jnp.sum(ones * (item_weight * item_length), axis=1, keepdims=True)
    mine[:, W // 2 + 1 : W // 2 + 2] = jnp.sum(ones * item_length, axis=1, keepdims=True)
    meta[dp] = mine[...]

    pl.semaphore_wait(barrier, len(peers))

    part_a, part_b, part_ab, part_c = pl.ds(0, GA), pl.ds(GA, GB - GA), pl.ds(0, GB), pl.ds(GB, R - GB)

    def slab(sh, zz, yy, part=slice(None)):
        return wv.at[sh, pl.ds((zz * 2 + yy) * CAP, CAP), part, :]

    def order(k):
        late, low = k // 2, z // 2
        return (1 - late) * (z + k * (1 - 2 * lax.rem(z, 2))) + late * (k + low * (3 - 2 * k))

    up, down, inner = z < nz - 1, z > 0, lax.rem(z, nz - 1) != 0
    own_up = same(slab(shard, z, y, part_ab), z_s.at[0], z_r.at[z], device(z + 1, y, x, c))
    own_down = same(slab(shard, z, y, part_ab), z_s.at[nz], z_r.at[z], device(z - 1, y, x, c))
    pl.when(up)(own_up.start)
    pl.when(down)(own_down.start)

    def meta_copy(k):
        return remote(mine, meta.at[dp], m_s.at[k], m_r.at[k], dp_peers[k])

    for k in range(len(dp_peers)):
        meta_copy(k).start()

    def along_z(k):
        zz = order(k)
        late = k // 2
        goal = (1 - late) * (3 - z) + late * 3 * (z - 1)
        return same(slab(shard, zz, y, part_ab), z_s.at[k], z_r.at[zz], device(goal, y, x, c))

    def both(j, zz):
        return wv.at[lax.rem(x + j, 2) * 2 + c, pl.ds(zz * 2 * CAP, 2 * CAP), part_c, :]

    def last_z(j, n):
        return same(both(j, z), zc_s.at[j, n], zc_r.at[j, n], device(lax.rem(z + n, nz), y, x, c))

    def last_here(j, n):
        zz = lax.rem(z + nz - n, nz)
        return same(both(j, zz), zc_s.at[j, n], zc_r.at[j, n], x_peer)

    def last_core(j, n):
        return same(both(j, lax.rem(z + nz - n, nz)), cc_s.at[j, n], cc_r.at[j, n], core_peer)

    own_c = slab(shard, z, y, part_c)
    c_copies = (
        same(own_c, c_s.at[0], c_r.at[0], y_peer),
        same(own_c, c_s.at[1], c_r.at[1], x_peer),
        same(slab(shard, z, 1 - y, part_c), c_s.at[2], c_r.at[2], x_peer),
    )

    def first_copies(k):
        zz = order(k)
        one, two = slab(shard, zz, y, part_a), slab(shard, zz, y, part_b)
        return (
            same(one, ya_s.at[k], ya_r.at[k], y_peer),
            same(two, xb_s.at[k], xb_r.at[k], x_peer),
            same(two, yb_s.at[k, 0], yb_r.at[k, 0], y_peer),
            same(one, xa_s.at[k, 0], xa_r.at[k, 0], x_peer),
            same(slab(shard, zz, y, part_ab), core_s.at[k, 0], core_r.at[k, 0], core_peer),
        )

    def second_copies(k):
        zz = order(k)
        return (
            same(slab(shard, zz, 1 - y, part_a), xa_s.at[k, 1], xa_r.at[k, 1], x_peer),
            same(slab(far, zz, y, part_b), yb_s.at[k, 1], yb_r.at[k, 1], y_peer),
            same(slab(shard, zz, 1 - y, part_ab), core_s.at[k, 1], core_r.at[k, 1], core_peer),
        )

    def third_copies(k):
        zz = order(k)
        return (
            same(slab(far, zz, y, part_ab), core_s.at[k, 2], core_r.at[k, 2], core_peer),
            same(slab(far, zz, 1 - y, part_ab), core_s.at[k, 3], core_r.at[k, 3], core_peer),
        )

    def gather0(k):
        @pl.when(k > 0)
        def _():
            along_z(k).wait_recv()
            pl.when(inner)(along_z(k).start)

        for copy in first_copies(k):
            copy.start()

    def gather1(k):
        zz = order(k)
        over_x, over_y, core = second_copies(k)
        same(slab(shard, zz, 1 - y, part_a), ya_s.at[k], ya_r.at[k], y_peer).wait_recv()
        over_x.start()
        same(slab(far, zz, y, part_b), xb_s.at[k], xb_r.at[k], x_peer).wait_recv()
        over_y.start()
        same(slab(shard, zz, 1 - y, part_b), yb_s.at[k, 0], yb_r.at[k, 0], y_peer).wait_recv()
        core.start()

    def gather2(k):
        zz = order(k)
        near, apart = third_copies(k)
        same(slab(far, zz, y, part_a), xa_s.at[k, 0], xa_r.at[k, 0], x_peer).wait_recv()
        near.start()
        same(slab(far, zz, 1 - y, part_a), xa_s.at[k, 1], xa_r.at[k, 1], x_peer).wait_recv()
        same(slab(far, zz, 1 - y, part_b), yb_s.at[k, 1], yb_r.at[k, 1], y_peer).wait_recv()
        apart.start()

    c_copies[0].start()
    c_copies[1].start()
    gather0(0)

    def gather_last(n):
        for j in range(2):
            last_here(j, n).wait_recv()
            last_core(j, n).start()

    def find_block(row):
        block = 0
        for j, block_row in enumerate(rows):
            block = block + jnp.where(block_row == row, j, 0)
        block_at[row] = block

    loop(0, nz * 2 * CAP, find_block)
    for k in range(len(dp_peers)):
        meta_copy(k).wait_recv()
    lane = lax.broadcasted_iota(jnp.int32, (8, W), 1)
    chunks = []
    for pair in range(meta.shape[0] // 2):
        chunks.append(jnp.where(lane < W // 2, meta[2 * pair], pltpu.roll(meta[2 * pair + 1], W // 2, 1)))
    norms = jnp.concatenate(chunks, axis=1).astype(bf16).astype(f32)
    gain1, shift1, gain2, shift2 = (norms[i : i + 1, :] for i in range(4))
    band_sums = meta[0]
    for d in range(1, meta.shape[0]):
        band_sums = band_sums + meta[d]
    weight_of = jnp.sum(jnp.where(table, band_sums[:, W // 2 : W // 2 + 1], 0.0), axis=0, keepdims=True)
    count_of = jnp.sum(jnp.where(table, band_sums[:, W // 2 + 1 : W // 2 + 2], 0.0), axis=0, keepdims=True)
    scales = item_weight * count_of / weight_of
    item_lane = lax.broadcasted_iota(jnp.int32, (1, items), 1)
    position = lax.broadcasted_iota(jnp.int32, (TILE, 1), 0)
    for n in range(6, 11):
        fetches[n].wait()

    def tile(t):
        return pl.ds(pl.multiple_of(t * TILE, TILE), TILE)

    def first_norm(i):
        p, t = i // tiles, lax.rem(i, tiles)
        here = tile(t)
        scaled, inverse = normalise(tok[p, here, :])
        xhat1[p, here, :] = scaled
        inv1[p, here, :] = inverse
        low1[p, here, :] = (scaled * gain1 + shift1).astype(bf16)
        item = whose(p) * items_here + t // (SEQ // TILE)
        scale = jnp.sum(jnp.where(item_lane == item, scales, 0.0), axis=1, keepdims=True)
        inside = position + lax.rem(t, SEQ // TILE) * TILE < lens[item]
        scaled_cot = cot[p, here, :] * jnp.where(inside, scale, 0.0)
        cot[p, here, :] = scaled_cot
        e2[p, here, :] = scaled_cot.astype(bf16)

    c_copies[0].wait_recv()
    c_copies[2].start()
    loop(0, 2 * tiles, first_norm)
    c_copies[1].wait_recv()
    c_copies[2].wait_recv()
    for j in range(2):
        last_core(j, 0).start()

    def gather(step):
        pl.when(step < nz)(lambda: gather0(step))

        @pl.when(step == nz - 1)
        def _():
            for j in range(2):
                for n in range(1, nz):
                    last_z(j, n).start()

        pl.when(step <= nz)(lambda: gather1(step - 1))
        pl.when(step >= 2)(lambda: gather2(step - 2))

    loop(1, nz + 2, gather)
    loop(1, nz, gather_last)

    def all_here(k):
        zz = order(k)
        for kind, (xx, yy) in enumerate(((x, y), (x, 1 - y), (1 - x, y), (1 - x, 1 - y))):
            same(slab(xx * 2 + 1 - c, zz, yy, part_ab), core_s.at[k, kind], core_r.at[k, kind], core_peer).wait_recv()
        for j in range(2):
            last_core(j, k).wait_recv()

    loop(0, nz, all_here)

    head_lane = lax.broadcasted_iota(jnp.int32, (1, W), 1)
    head_masks = [head_lane < HD, head_lane >= HD]
    key_pos = lax.broadcasted_iota(jnp.int32, (1, SEQ), 1)
    item_rows = [slice(i * SEQ, (i + 1) * SEQ) for i in range(items_here)]

    def only(values, a):
        return jnp.where(head_masks[a], values, jnp.zeros_like(values))

    def stack(values):
        return jnp.concatenate([only(values, 0), only(values, 1)], axis=0)

    def wide_matrix(h):
        return jnp.concatenate(
            [
                jnp.concatenate([wv[h, rows[j], p * W : (p + 1) * W, :] for j in range(QB)], axis=0)
                for p in range(3)
            ],
            axis=1,
        )

    def narrow_matrix(h, first, size):
        pieces = cat_pieces(first, size)
        return jnp.concatenate(
            [
                jnp.concatenate(
                    [wv[h, rows[b], pl.ds(p * (R // 4) + inside, count), :] for b, inside, _, count in pieces], axis=0
                )
                for p in range(4)
            ],
            axis=1,
        )

    deep, low = (QB + 2, CB - 2), (0, QB + 2)
    x_part, y_part, z_part = pl.ds(0, RA), pl.ds(RA, RB - RA), pl.ds(RB, R - RB)

    def core_push(j, n):
        part = pl.ds(*(deep, low)[n])
        return remote(grads.at[j, part], from_core.at[j, part], cs.at[n, j], cr.at[n, j], core_peer)

    def x_push(n):
        part = pl.ds(*(deep, low)[n])
        return remote(grads.at[2, part, x_part, :], rxa.at[part], as_.at[n], ar.at[n], x_peer)

    def hand_over(i, n):
        first, count = (deep, low)[n]
        pl.when(i < 2)(lambda: core_push(i, n).start())

        @pl.when(i >= 2)
        def _():
            core_push(i - 2, n).wait_recv()

            def add(block):
                grads[i, block] = grads[i, block] + from_core[i - 2, block]

            loop(first, first + count, add)
            pl.when(i == 2)(lambda: x_push(n).start())

    pair_z, cross_z = z + 1 - 2 * lax.rem(z, 2), lax.rem(z + 2, nz)

    def chunk(k):
        return lax.rem(pair_z + lax.rem(k, 2) * (z - pair_z) + 2 * (1 - k // 2), nz)

    def block_of(k, yy, r):
        return block_at[(chunk(k) * 2 + yy) * CAP + r]

    def over_y_first(k):
        return remote(sb.at[k], ryb.at[k], sby_s.at[k], sby_r.at[k], y_peer)

    def over_x_last(k):
        return remote(sbx.at[k], rxb.at[k], sbx_s.at[k], sbx_r.at[k], x_peer)

    def over_y_last(k):
        return remote(sa.at[k], rya.at[k], say_s.at[k], say_r.at[k], y_peer)

    def over_z(k, r):
        goal = pair_z + lax.rem(k, 2) * (cross_z - pair_z)
        return remote(fz.at[k, r], rz.at[k, r], fz_s.at[k, r], fz_r.at[k, r], device(goal, y, x, c))

    def z_first(k):
        goal = pair_z + lax.rem(k, 2) * (cross_z - pair_z)
        return remote(sc.at[k], rc.at[k], sc_s.at[k], sc_r.at[k], device(goal, y, x, c))

    def z_then_y():
        return remote(sc.at[nz - 1, :, 1 - y], ryc, cy_s, cy_r, y_peer)

    def z_then_x():
        return remote(sc.at[nz - 1, 0, y], rxc, cx_s, cx_r, x_peer)

    def send_c(k):
        for r in range(2 * CAP):
            block = block_of(k, r // CAP, r % CAP)
            for j in range(2):
                sc[k, j, r // CAP, r % CAP] = grads[2 + j, block, z_part, :]
        pl.when(lax.rem(k, 2) == 0)(lambda: z_first(k).start())

    def cross_c():
        z_first(0).wait_recv()
        for j in range(2):
            sc[1, j] = sc[1, j] + rc[0, j]
        z_first(1).start()

    def own_c():
        z_first(1).wait_recv()
        z_first(2).wait_recv()
        for j in range(2):
            sc[nz - 1, j] = sc[nz - 1, j] + (rc[1, j].astype(f32) + rc[2, j].astype(f32)).astype(bf16)
        z_then_y().start()

    def y_c():
        z_then_y().wait_recv()
        for j in range(2):
            sc[nz - 1, j, y] = sc[nz - 1, j, y] + ryc[j]
        z_then_x().start()

    def norm_copies():
        z_peers = [device(lax.rem(z + k, nz), y, x, c) for k in range(1, nz)]
        return [
            remote(norm_part, n_core, n_s.at[0], n_r.at[0], core_peer),
            remote(norm_sum.at[0], n_x, n_s.at[1], n_r.at[1], x_peer),
            remote(norm_sum.at[1], n_y, n_s.at[2], n_r.at[2], y_peer),
        ] + [remote(norm_sum.at[2], n_z.at[k], n_s.at[3 + k], n_r.at[3 + k], p) for k, p in enumerate(z_peers)]

    def send_b(k):
        for r in range(CAP):
            block = block_of(k, 1 - y, r)
            for j in range(2):
                sb[k, j, r] = grads[2 + j, block, y_part, :]
        over_y_first(k).start()

    def add_x(j):
        grads[3, j, x_part, :] = grads[3, j, x_part, :] + rxa[j]

    def send_a(k):
        for r in range(CAP):
            sa[k, r] = grads[3, block_of(k, 1 - y, r), x_part, :]
        over_y_last(k).start()

    def reduce1(k):
        over_y_first(k).wait_recv()
        for r in range(CAP):
            sbx[k, r] = grads[2, block_of(k, y, r), y_part, :] + ryb[k, 0, r]
        over_x_last(k).start()

    def reduce2(k):
        over_y_last(k).wait_recv()
        over_x_last(k).wait_recv()
        for r in range(CAP):
            block = block_of(k, y, r)
            fz[k, r, x_part, :] = grads[3, block, x_part, :] + rya[k, r]
            part = grads[3, block, y_part, :].astype(f32) + ryb[k, 1, r].astype(f32)
            fz[k, r, y_part, :] = (part + rxb[k, r].astype(f32)).astype(bf16)
            pl.when(lax.rem(k, 2) == 0)(over_z(k, r).start)

    def cross():
        for r in range(CAP):
            over_z(0, r).wait_recv()
            fz[1, r] = fz[1, r] + rz[0, r]
            over_z(1, r).start()

    key_row = lax.broadcasted_iota(jnp.int32, (2 * SEQ, W), 0)
    head_ones = jnp.where((key_row < SEQ) == head_masks[0], 1.0, 0.0).astype(bf16)

    def attention(p, h):
        projected = dot(low1[p], wide_matrix(h))
        qkv[h, 0] = (projected[:, :W].astype(bf16).astype(f32) * (1.0 / math.sqrt(HD))).astype(bf16)
        qkv[h, 1] = projected[:, W : 2 * W].astype(bf16)
        qkv[h, 2] = projected[:, 2 * W :].astype(bf16)
        for i, here in enumerate(item_rows):
            query, key, value = qkv[h, 0, here, :], qkv[h, 1, here, :], qkv[h, 2, here, :]
            valid = key_pos < lens[whose(p) * items_here + i]
            both = []
            for a in range(2):
                scores = jnp.where(valid, dot_cols(only(query, a), key), -1e30)
                exps = jnp.exp(scores - jnp.max(scores, axis=-1, keepdims=True)).astype(bf16)
                probs[h, i, a] = exps
                both.append(exps)
            mixed = dot(jnp.concatenate(both, axis=1), jnp.concatenate([stack(value), head_ones], axis=1))
            inverse = 1.0 / mixed[:, W:]
            sums[h, here, :] = inverse
            att[h, here, :] = (mixed[:, :W] * inverse).astype(bf16)
        acc[...] += dot(att[h], narrow_matrix(h, 0, W))

    def put(i, first, result):
        for block, inside, row, count in cat_pieces(first, result.shape[0]):
            for p in range(4):
                here = pl.ds(p * (R // 4) + inside, count)
                grads[i, block, here, :] = result[row : row + count, p * W : (p + 1) * W].astype(bf16)

    def shard_of(p, i):
        return lax.rem(1 + x + p + i, 2) * 2 + lax.rem(c + 1 + i // 2, 2)

    def feed_forward(p, i):
        h = shard_of(p, i)
        up_matrix, down_matrix = narrow_matrix(h, W, D), narrow_matrix(h, W + D, D)
        hidden = dot(low2[...], up_matrix)
        root = math.sqrt(2.0 / math.pi)
        square = hidden * hidden
        bend = jnp.tanh(root * hidden * (1.0 + 0.044715 * square))
        half = 0.5 * (1.0 + bend)
        active = (hidden * half).astype(bf16)
        slope = half + 0.5 * hidden * (1.0 - bend * bend) * (root + (3.0 * 0.044715 * root) * square)
        if p == 0:
            actives[i] = active
        else:
            acc[...] += dot(active, down_matrix)
        back = (dot_cols(e2[p], down_matrix) * slope).astype(bf16)
        da[...] += dot_cols(back, up_matrix)
        if p == 0:
            put(i, W + D, dot_rows(active, e2[p]))
            put(i, W, dot_rows(low2[...], back))
            hand_over(i, 0)

    def attention_back(p, i):
        h = shard_of(p, i)
        d_all = dot_cols(e1[...], narrow_matrix(h, 0, W)) * sums[h]
        shared_all = (d_all * att[h].astype(f32)).astype(bf16)
        d_all = d_all.astype(bf16)
        parts = []
        for m, here in enumerate(item_rows):
            query, key, value = qkv[h, 0, here, :], qkv[h, 1, here, :], qkv[h, 2, here, :]
            d_here, shared = d_all[here, :], shared_all[here, :]
            against = jnp.concatenate([value, jnp.full((SEQ, W), -1.0, bf16)], axis=1)
            d_scores = []
            for a in range(2):
                change = dot_cols(jnp.concatenate([only(d_here, a), only(shared, a)], axis=1), against)
                d_scores.append((probs[h, m, a].astype(f32) * change).astype(bf16))
            d_query = dot(jnp.concatenate(d_scores, axis=1), stack(key)) * (1.0 / math.sqrt(HD))
            d_key = dot_rows(jnp.concatenate(d_scores, axis=0), stack(query))
            d_value = dot_rows(jnp.concatenate([probs[h, m, 0], probs[h, m, 1]], axis=0), stack(d_here))
            parts.append(jnp.concatenate([d_query, d_key, d_value], axis=1).astype(bf16))
        d_qkv = jnp.concatenate(parts, axis=0)
        if p == 0:
            d_qkvs[i] = d_qkv
            put(i, 0, dot_rows(att[h], e1[...]))
            d_weight = dot_rows(low1[p], d_qkv).astype(bf16)
            for j in range(QB):
                for m in range(3):
                    grads[i, j, m * W : (m + 1) * W, :] = d_weight[j * W : (j + 1) * W, m * W : (m + 1) * W]
            hand_over(i, 1)
        else:
            da[...] += dot_cols(d_qkv, wide_matrix(h))

    def late_output(i):
        acc[...] += dot(actives[i], narrow_matrix(shard_of(0, i), W + D, D))

    def late_input(i):
        da[...] += dot_cols(d_qkvs[i], wide_matrix(shard_of(0, i)))

    def norm_backward(grad, scaled, inverse, gain):
        grad_scaled = grad * gain
        centre = jnp.mean(grad_scaled, axis=-1, keepdims=True)
        slope = jnp.mean(grad_scaled * scaled, axis=-1, keepdims=True)
        return inverse * (grad_scaled - centre - scaled * slope)

    def add_norm(p, row, grad, scaled):
        if p == 0:
            norm_part[row : row + 1, :] += jnp.sum(grad * scaled, axis=0, keepdims=True)
            norm_part[row + 1 : row + 2, :] += jnp.sum(grad, axis=0, keepdims=True)

    norm_part[...] = jnp.zeros_like(norm_part)

    def out_copies(p, n):
        src, dst = ((out_low, out_all), (in_low, in_all))[n]
        there = tokens_of(dst, whose(p))
        return (
            pltpu.make_async_copy(src.at[p], there, o_l.at[p, n]),
            remote(src.at[p], there, o_s.at[p, n], o_r.at[p, n], core_peer),
        )

    def block_result(p):
        out_low[p] = acc[...].astype(bf16)
        for copy in out_copies(p, 0):
            copy.start()

    def input_result(p):
        def first_norm_back(t):
            here = tile(t)
            grad, scaled = da[here, :], xhat1[p, here, :]
            add_norm(p, 0, grad, scaled)
            in_low[p, here, :] = (cot[p, here, :] + norm_backward(grad, scaled, inv1[p, here, :], gain1)).astype(bf16)

        loop(0, tiles, first_norm_back)
        for copy in out_copies(p, 1):
            copy.start()

    def layer_pass(p):
        acc[...] = jnp.zeros_like(acc)
        loop(0, 4, lambda h: attention(p, h))

        def second_norm(t):
            here = tile(t)
            state = acc[here, :] + tok[p, here, :]
            acc[here, :] = state
            scaled, inverse = normalise(state)
            xhat2[here, :] = scaled
            inv2[here, :] = inverse
            low2[here, :] = (scaled * gain2 + shift2).astype(bf16)
            da[here, :] = jnp.zeros((TILE, D), f32)

        loop(0, tiles, second_norm)
        if p == 1:
            for n in range(2):
                x_push(n).wait_recv()
            loop(0, QB + CB, add_x)
            loop(0, nz, send_a)
            loop(0, nz, reduce1)
        loop(0, 4, lambda i: feed_forward(p, i))
        if p == 1:
            block_result(1)
            own_c()
            reduce2(0)
            norm_copies()[0].wait_recv()
            norm_sum[0] = norm_part[...] + n_core[...]
            norm_copies()[1].start()

        def second_norm_back(t):
            here = tile(t)
            grad, scaled = da[here, :], xhat2[here, :]
            add_norm(p, 2, grad, scaled)
            change = cot[p, here, :] + norm_backward(grad, scaled, inv2[here, :], gain2)
            cot[p, here, :] = change
            e1[here, :] = change.astype(bf16)
            da[here, :] = jnp.zeros((TILE, D), f32)

        loop(0, tiles, second_norm_back)
        if p == 1:
            norm_copies()[1].wait_recv()
            norm_sum[1] = norm_sum[0] + n_x[...]
            norm_copies()[2].start()
            reduce2(1)
            cross()

        def attention_step(i):
            attention_back(p, i)
            if p == 1:
                @pl.when(i == 1)
                def _():
                    reduce2(2)
                    y_c()

        loop(0, 4, attention_step)

    layer_pass(0)
    loop(0, nz, send_c)
    loop(0, nz, send_b)
    loop(0, 4, late_output)
    block_result(0)
    loop(0, 4, late_input)
    input_result(0)
    cross_c()
    norm_copies()[0].start()
    layer_pass(1)
    input_result(1)

    norm_copies()[2].wait_recv()
    norm_sum[2] = norm_sum[1] + n_y[...]
    for copy in norm_copies()[3:]:
        copy.start()
    reduce2(nz - 1)

    for k in range(nz - 1):
        norm_copies()[3 + k].wait_recv()
    z_then_x().wait_recv()
    for r in range(CAP):
        over_z(2, r).wait_recv()
        over_z(1, r).wait_recv()
    norm_total[...] = norm_sum[2] + ((n_z[0] + n_z[1]) + n_z[2])

    def last(r):
        others = rz[1, r].astype(f32) + rz[2, r].astype(f32)
        total[r, pl.ds(0, RB), :] = fz[nz - 1, r].astype(f32) + others
        total[r, z_part, :] = sc[nz - 1, 1, y, r].astype(f32) + rxc[r].astype(f32)

    loop(0, CAP, last)

    for p in range(2):
        for n in range(2):
            local, over_core = out_copies(p, n)
            local.wait()
            over_core.wait()
    for copy in norm_copies():
        copy.wait_send()
    for k in range(len(dp_peers)):
        meta_copy(k).wait_send()
    pl.when(up)(own_up.wait_send)
    pl.when(down)(own_down.wait_send)
    for copy in c_copies:
        copy.wait_send()

    def sent(k):
        for copy in first_copies(k) + second_copies(k) + third_copies(k):
            copy.wait_send()
        pl.when(jnp.logical_and(k > 0, inner))(along_z(k).wait_send)
        for j in range(2):
            last_core(j, k).wait_send()
            pl.when(k > 0)(last_z(j, k).wait_send)
        for copy in (over_y_first(k), over_x_last(k), over_y_last(k)):
            copy.wait_send()
        pl.when(k < nz - 1)(z_first(k).wait_send)
        for r in range(CAP):
            pl.when(k < nz - 1)(over_z(k, r).wait_send)

    loop(0, nz, sent)
    z_then_y().wait_send()
    z_then_x().wait_send()
    for n in range(2):
        x_push(n).wait_send()
        for j in range(2):
            core_push(j, n).wait_send()


def layer(tokens, cotangent, master, norms, steps, bands, lens_row, lens, owners):
    nz = Sizes.z
    here = tokens.shape[0] // lax.axis_size("head")
    items_here = here // SEQ
    items = lens.shape[0]
    vm = pl.BlockSpec(memory_space=pltpu.VMEM)
    hbm = pl.BlockSpec(memory_space=pltpu.HBM)
    dma = pltpu.SemaphoreType.DMA
    V, S = pltpu.VMEM, pltpu.SMEM
    square = (here, D)
    blocks = QB + CB
    rb = RB - RA
    low, full, two_low, two = V(square, bf16), V(square, f32), V((2, *square), bf16), V((2, *square), f32)
    scratch = [
        V((4, nz * 2 * CAP, R, W), bf16), V((R, CAP, W), f32), V((R, W), f32),
        V((8, W), f32), V((nz * 2, 8, W), f32), V(norms.shape, f32),
        V((1, items), jnp.int32), V((1, items), jnp.int32), V((1, items), jnp.int32),
        S((items,), jnp.int32), S(owners.shape, jnp.int32), S((nz * 2 * CAP,), jnp.int32),
        two, two, two_low, two, V((2, here, 1), f32), V((4, 3, here, W), bf16),
        V((4, items_here, 2, SEQ, SEQ), bf16), V((4, here, W), f32), V((4, here, W), bf16),
        full, low, full, V((here, 1), f32), two_low,
        V((4, here, D), bf16), V((4, here, 3 * W), bf16), full, low, two_low, two_low,
        V((4, blocks, R, W), bf16), V((2, blocks, R, W), bf16),
        V((blocks, RA, W), bf16), V((nz, CAP, RA, W), bf16), V((nz, CAP, RA, W), bf16),
        V((nz, 2, CAP, rb, W), bf16), V((nz, 2, CAP, rb, W), bf16), V((nz, CAP, rb, W), bf16),
        V((nz, CAP, rb, W), bf16), V((nz, CAP, RB, W), bf16), V((nz - 1, CAP, RB, W), bf16),
        V((nz, 2, 2, CAP, R - RB, W), bf16), V((nz - 1, 2, 2, CAP, R - RB, W), bf16),
        V((2, CAP, R - RB, W), bf16), V((CAP, R - RB, W), bf16),
        V((8, D), f32), V((3, 8, D), f32), V((8, D), f32), V((8, D), f32), V((8, D), f32), V((nz - 1, 8, D), f32),
        dma((11,)), dma((nz + 1,)), dma((nz,)), dma((nz,)), dma((nz,)), dma((nz, 2)), dma((nz, 2)), dma((nz,)), dma((nz,)),
        dma((nz, 2)), dma((nz, 2)), dma((nz, 4)), dma((nz, 4)), dma((8,)), dma((8,)),
        dma((3,)), dma((3,)), dma((2, nz)), dma((2, nz)), dma((2, nz)), dma((2, nz)),
        dma((nz,)), dma((nz,)), dma, dma, dma, dma,
        dma((2, 2)), dma((2, 2)), dma((2,)), dma((2,)), dma((nz,)), dma((nz,)), dma((nz,)), dma((nz,)),
        dma((nz,)), dma((nz,)), dma((nz, CAP)), dma((nz, CAP)), dma((8,)), dma((8,)), dma((2, 2)), dma((2, 2)), dma((2, 2)),
    ]
    return pl.pallas_call(
        layer_kernel,
        name="layer",
        out_shape=(
            jax.ShapeDtypeStruct((CAP, R, W), f32),
            jax.ShapeDtypeStruct(tokens.shape, bf16),
            jax.ShapeDtypeStruct(tokens.shape, bf16),
            jax.ShapeDtypeStruct((8, D), f32),
        ),
        in_specs=[hbm] * 9,
        out_specs=(vm, hbm, hbm, vm),
        scratch_shapes=scratch,
        compiler_params=pltpu.CompilerParams(collective_id=0, has_side_effects=True, vmem_limit_bytes=56 << 20),
    )(tokens, cotangent, master, norms, steps, bands, lens_row, lens, owners)


def finish_kernel(
    total_hbm, norm_hbm, master_hbm, first_hbm, second_hbm, norm_m, norm_f, norm_s, owners_hbm, out_all, in_all,
    block_output, input_grad, new_master, new_first, new_second, new_norm, new_norm_first, new_norm_second,
    out_low, in_low, out_full, in_full, states, results, flat, grad, total, norm_total, norm_master, norm_first, norm_second, owners, l_sem, s_sem, i_sem, r_sem,
):
    pieces = l_sem.shape[1]
    size = out_low.shape[0] // pieces
    pairs = ((out_all, out_low, out_full, block_output), (in_all, in_low, in_full, input_grad))

    def piece(p):
        return pl.ds(pl.multiple_of(p * size, size), size)

    def fetch(n, p):
        return pltpu.make_async_copy(pairs[n][0].at[piece(p), :], pairs[n][1].at[piece(p), :], l_sem.at[n, p])

    def store(n, p):
        return pltpu.make_async_copy(pairs[n][2].at[piece(p), :], pairs[n][3].at[piece(p), :], s_sem.at[n, p])

    small_copies = [
        pltpu.make_async_copy(src, dst, i_sem.at[3 + i])
        for i, (src, dst) in enumerate((
            (owners_hbm, owners), (total_hbm, total), (norm_hbm, norm_total),
            (norm_m, norm_master), (norm_f, norm_first), (norm_s, norm_second),
        ))
    ]
    state_copies = [
        pltpu.make_async_copy(src, states.at[i], i_sem.at[i]) for i, src in enumerate((master_hbm, first_hbm, second_hbm))
    ]
    result_copies = [
        pltpu.make_async_copy(results.at[i], dst, r_sem.at[i]) for i, dst in enumerate((new_master, new_first, new_second))
    ]

    def loop(count, body):
        def step(i, _):
            body(i)
            return 0

        lax.fori_loop(0, count, step, 0)

    for copy in small_copies:
        copy.start()
    for copy in state_copies:
        copy.start()
    loop(pieces, lambda p: fetch(0, p).start())
    loop(pieces, lambda p: fetch(1, p).start())

    dp = lax.axis_index("dp")
    small_copies[0].wait()
    rows = block_rows(owners)
    held = 0
    for j in range(owners.shape[0]):
        held = held + jnp.where(owners[j] == dp, 1, 0)

    def spread(r):
        is_wide = slot_is_wide(rows, dp * CAP + r)

        @pl.when(is_wide)
        def _():
            for p in range(3):
                flat[pl.ds(p, W, stride=3), :] = total[r, p * W : (p + 1) * W, :]

        @pl.when(jnp.logical_not(is_wide))
        def _():
            for p in range(4):
                flat[pl.ds(p, R // 4, stride=4), :] = total[r, p * (R // 4) : (p + 1) * (R // 4), :]

    small_copies[1].wait()
    for r in range(CAP):
        spread(r)
        grad[:, r, :] = flat[...]

    def convert(n, p):
        fetch(n, p).wait()
        _, low, full, _ = pairs[n]
        full[piece(p), :] = low[piece(p), :].astype(f32)
        store(n, p).start()

    for copy in state_copies:
        copy.wait()
    step = 32
    slot = lax.broadcasted_iota(jnp.int32, (step, CAP, W), 1)

    def update(i):
        here = pl.ds(pl.multiple_of(i * step, step), step)
        new = adamw_update(states[0, here], states[1, here], states[2, here], grad[here], weight_decay, learn_rate)
        for n in range(3):
            results[n, here] = jnp.where(slot < held, new[n], 0.0)


    def both(p):
        convert(0, p)
        for i in range(R // step // pieces):
            update(p * (R // step // pieces) + i)

    loop(pieces, both)
    for copy in result_copies:
        copy.start()
    for copy in small_copies[2:]:
        copy.wait()
    pair = norm_total[:, pl.ds(pl.multiple_of((dp // 2) * W, W), W)]
    mine = jnp.where(lax.rem(dp, 2) == 1, pltpu.roll(pair, W // 2, 1), pair)[0:4, 0 : norm_master.shape[1]]
    new = adamw_update(norm_master[...], norm_first[...], norm_second[...], mine, 0.0, norm_rate)
    for ref, value in zip((new_norm, new_norm_first, new_norm_second), new):
        ref[...] = value
    loop(pieces, lambda p: convert(1, p))
    for n in range(2):
        loop(pieces, lambda p: store(n, p).wait())
    for copy in result_copies:
        copy.wait()


def finish(total, norm_total, slots, norms, owners, out_all, in_all):
    vm = pl.BlockSpec(memory_space=pltpu.VMEM)
    hbm = pl.BlockSpec(memory_space=pltpu.HBM)
    dma = pltpu.SemaphoreType.DMA
    V = pltpu.VMEM
    pieces = 4
    shape = out_all.shape
    return pl.pallas_call(
        finish_kernel,
        name="finish",
        out_shape=(
            (jax.ShapeDtypeStruct(shape, f32),) * 2 + tuple(jax.ShapeDtypeStruct(a.shape, f32) for a in slots + norms)
        ),
        in_specs=[hbm] * 11,
        out_specs=(hbm,) * 5 + (vm,) * 3,
        scratch_shapes=[
            V(shape, bf16), V(shape, bf16), V(shape, f32), V(shape, f32), V((3, R, CAP, W), f32), V((3, R, CAP, W), f32),
            V((R, W), f32), V((R, CAP, W), f32),
            V(total.shape, f32), V(norm_total.shape, f32), *(V(a.shape, f32) for a in norms),
            pltpu.SMEM(owners.shape, jnp.int32), dma((2, pieces)), dma((2, pieces)), dma((9,)), dma((3,)),
        ],
        compiler_params=pltpu.CompilerParams(vmem_limit_bytes=60 << 20),
    )(total, norm_total, *slots, *norms, owners, out_all, in_all)


def fast_shards(
    tokens, cotangent, timesteps, bands, lengths, owners,
    master_slots, first_slots, second_slots, norm_master, norm_first, norm_second,
):
    def tiles(slots):
        return jnp.transpose(slots.reshape(CAP, R, W), (1, 0, 2))

    def flat(slots):
        return jnp.transpose(slots, (1, 0, 2)).reshape(CAP, R * W)

    steps, bands_row, lens_row = (v.reshape(1, -1) for v in (timesteps, bands, lengths))
    slots = tuple(tiles(s) for s in (master_slots, first_slots, second_slots))
    norms = (norm_master, norm_first, norm_second)
    total, out_all, in_all, norm_total = layer(
        tokens, cotangent, slots[0], norm_master, steps, bands_row, lens_row, lengths, owners
    )
    results = finish(total, norm_total, slots, norms, owners, out_all, in_all)
    return (*results[:2], *(flat(s) for s in results[2:5]), *results[5:])


def solution(mesh):
    fits = dict(mesh.shape) == {"dp": 8, "head": 4}
    placed = (
        P("dp", None),
        P("dp", None),
        P("dp"),
        P("dp"),
        P("dp"),
        P(),
        P("dp", "head"),
        P("dp", "head"),
        P("dp", "head"),
        P(None, "dp"),
        P(None, "dp"),
        P(None, "dp"),
    )
    return jax.shard_map(
        fast_shards if fits else shards,
        mesh=mesh,
        in_specs=placed,
        out_specs=(
            P("dp", None),
            P("dp", None),
            P("dp", "head"),
            P("dp", "head"),
            P("dp", "head"),
            P(None, "dp"),
            P(None, "dp"),
            P(None, "dp"),
        ),
        check_vma=False,
    )
```

```python
import math

import jax
import jax.numpy as jnp
from jax import lax
from jax.experimental import pallas as pl
from jax.experimental.pallas import tpu as pltpu
from jax.sharding import PartitionSpec as P

D = 512
H = 8
HD = 64
FF = 2048
SEQ = 256
TSTEPS = 1000
NBANDS = 8
CAP = 3
STEP = 5


beta_one = 0.5
beta_two = 0.5
learn_rate = 0.04
norm_rate = 0.4
weight_decay = 0.1
adam_eps = 1e-08
norm_eps = 1e-05


def contract_rows(left_side, right_side):
    return lax.dot_general(
        left_side, right_side, (((0,), (0,)), ((), ())), preferred_element_type=jnp.float32
    )


def contract_cols(left_side, right_side):
    return lax.dot_general(
        left_side, right_side, (((1,), (1,)), ((), ())), preferred_element_type=jnp.float32
    )


def gelu_tanh(values):
    return jax.nn.gelu(values, approximate=True)


def norm_forward(values, gain_row, shift_row):
    average = jnp.mean(values, axis=-1, keepdims=True)
    centred = values - average
    inverse = lax.rsqrt(jnp.mean(centred * centred, axis=-1, keepdims=True) + norm_eps)
    scaled = centred * inverse
    return (scaled * gain_row + shift_row, scaled, inverse)


def norm_backward(grad_normed, scaled, inverse, gain_row):
    grad_scaled = grad_normed * gain_row
    centre_term = jnp.mean(grad_scaled, axis=-1, keepdims=True)
    slope_term = jnp.mean(grad_scaled * scaled, axis=-1, keepdims=True)
    return inverse * (grad_scaled - centre_term - scaled * slope_term)


def slot_rows(owners, capacity):
    block_index = jnp.arange(owners.shape[0], dtype=jnp.int32)
    earlier = (owners[None, :] == owners[:, None]) & (block_index[None, :] < block_index[:, None])
    return owners * capacity + jnp.sum(earlier.astype(jnp.int32), axis=1)


def attention_scores(query_heads, key_heads, key_valid):
    scores = jnp.einsum(
        "gqad,gkad->gaqk", query_heads, key_heads, preferred_element_type=jnp.float32
    ) / math.sqrt(HD)
    return jnp.where(key_valid[:, None, None, :], scores, -1e30)


def adamw_update(weight, first_moment, second, gradient, decay_rate, step_rate):
    new_first = beta_one * first_moment + (1.0 - beta_one) * gradient
    new_second = beta_two * second + (1.0 - beta_two) * gradient * gradient
    first_hat = new_first / (1.0 - beta_one**STEP)
    second_hat = new_second / (1.0 - beta_two**STEP)
    new_weight = weight - step_rate * (
        first_hat / (jnp.sqrt(second_hat) + adam_eps) + decay_rate * weight
    )
    return (new_weight, new_first, new_second)


def shards(
    tokens,
    cotangent,
    timesteps,
    bands,
    lengths,
    owners,
    master_slots,
    first_slots,
    second_slots,
    norm_master,
    norm_first,
    norm_second,
):
    head_count = lax.axis_size("head")
    owner_index = lax.axis_index("dp")
    heads_here = H // head_count
    width_here = heads_here * HD
    units_here = FF // head_count
    block_len = master_slots.shape[1]
    norm_cols = norm_master.shape[1]
    row_count = tokens.shape[0]
    item_count = lengths.shape[0]
    block_count = owners.shape[0]
    slot_row = slot_rows(owners, CAP)
    gathered, norm_whole = (
        lax.all_gather(master_slots.astype(jnp.bfloat16), "dp", axis=0, tiled=True),
        lax.all_gather(norm_master.astype(jnp.bfloat16), "dp", axis=1, tiled=True),
    )
    flat_params = gathered[slot_row].reshape(-1)
    qkv_end = 3 * D * width_here
    out_end = qkv_end + width_here * D
    up_end = out_end + D * units_here
    qkv_weight = flat_params[:qkv_end].reshape(D, 3 * width_here)
    out_weight = flat_params[qkv_end:out_end].reshape(width_here, D)
    up_weight = flat_params[out_end:up_end].reshape(D, units_here)
    down_weight = flat_params[up_end:].reshape(units_here, D)
    norm_params = norm_whole.astype(jnp.float32)
    item_weight = jnp.exp(-2.0 * timesteps.astype(jnp.float32) / TSTEPS)
    item_length = lengths.astype(jnp.float32)
    band_table = (bands[:, None] == jnp.arange(NBANDS, dtype=jnp.int32)[None, :]).astype(
        jnp.float32
    )
    weight_sums, count_sums = lax.psum(
        (
            jnp.sum(band_table * (item_weight * item_length)[:, None], axis=0),
            jnp.sum(band_table * item_length[:, None], axis=0),
        ),
        "dp",
    )
    item_scale = (
        item_weight
        * jnp.sum(band_table * count_sums[None, :], axis=1)
        / jnp.sum(band_table * weight_sums[None, :], axis=1)
    )
    key_valid = jnp.arange(SEQ, dtype=jnp.int32)[None, :] < lengths[:, None]
    token_scale = jnp.where(key_valid, item_scale[:, None], 0.0).reshape(row_count)
    normed_one, scaled_one, inverse_one = norm_forward(tokens, norm_params[0], norm_params[1])
    normed_one_low = normed_one.astype(jnp.bfloat16)
    projected_low = jnp.dot(normed_one_low, qkv_weight, preferred_element_type=jnp.float32).astype(
        jnp.bfloat16
    )
    head_shape = (item_count, SEQ, heads_here, HD)
    query_heads = projected_low[:, :width_here].reshape(head_shape)
    key_heads = projected_low[:, width_here : 2 * width_here].reshape(head_shape)
    value_heads = projected_low[:, 2 * width_here :].reshape(head_shape)
    scores = attention_scores(query_heads, key_heads, key_valid)
    row_max = jnp.max(scores, axis=-1, keepdims=True)
    exp_scores = jnp.exp(scores - row_max)
    row_total = jnp.sum(exp_scores, axis=-1, keepdims=True)
    log_total = row_max + jnp.log(row_total)
    prob_low = (exp_scores / row_total).astype(jnp.bfloat16)
    attended_low = (
        jnp.einsum("gaqk,gkad->gqad", prob_low, value_heads, preferred_element_type=jnp.float32)
        .astype(jnp.bfloat16)
        .reshape(row_count, width_here)
    )
    attn_sum = lax.psum(
        jnp.dot(attended_low, out_weight, preferred_element_type=jnp.float32).astype(jnp.bfloat16),
        "head",
    ).astype(jnp.float32)
    mixed_state = tokens + attn_sum
    normed_two, scaled_two, inverse_two = norm_forward(mixed_state, norm_params[2], norm_params[3])
    normed_two_low = normed_two.astype(jnp.bfloat16)
    hidden = jnp.dot(normed_two_low, up_weight, preferred_element_type=jnp.float32)
    activated, gelu_pull = jax.vjp(gelu_tanh, hidden)
    activated_low = activated.astype(jnp.bfloat16)
    ffn_sum = lax.psum(
        jnp.dot(activated_low, down_weight, preferred_element_type=jnp.float32).astype(
            jnp.bfloat16
        ),
        "head",
    ).astype(jnp.float32)
    block_output = mixed_state + ffn_sum
    grad_state = cotangent * token_scale[:, None]
    grad_low_two = grad_state.astype(jnp.bfloat16)
    grad_down = contract_rows(activated_low, grad_low_two)
    grad_activated = contract_cols(grad_low_two, down_weight)
    grad_hidden_low = gelu_pull(grad_activated)[0].astype(jnp.bfloat16)
    grad_up = contract_rows(normed_two_low, grad_hidden_low)
    grad_normed_two = lax.psum(
        contract_cols(grad_hidden_low, up_weight).astype(jnp.bfloat16), "head"
    ).astype(jnp.float32)
    grad_mixed = grad_state + norm_backward(
        grad_normed_two, scaled_two, inverse_two, norm_params[2]
    )
    grad_low_one = grad_mixed.astype(jnp.bfloat16)
    grad_out_proj = contract_rows(attended_low, grad_low_one)
    grad_attended_low = (
        contract_cols(grad_low_one, out_weight).astype(jnp.bfloat16).reshape(head_shape)
    )
    scores_again = attention_scores(query_heads, key_heads, key_valid)
    probabilities = jnp.exp(scores_again - log_total)
    prob_again_low = probabilities.astype(jnp.bfloat16)
    grad_values = jnp.einsum(
        "gaqk,gqad->gkad", prob_again_low, grad_attended_low, preferred_element_type=jnp.float32
    )
    grad_probs = jnp.einsum(
        "gqad,gkad->gaqk", grad_attended_low, value_heads, preferred_element_type=jnp.float32
    )
    grad_scores_low = (
        probabilities * (grad_probs - jnp.sum(grad_probs * probabilities, axis=-1, keepdims=True))
    ).astype(jnp.bfloat16)
    grad_queries = jnp.einsum(
        "gaqk,gkad->gqad", grad_scores_low, key_heads, preferred_element_type=jnp.float32
    ) / math.sqrt(HD)
    grad_keys = jnp.einsum(
        "gaqk,gqad->gkad", grad_scores_low, query_heads, preferred_element_type=jnp.float32
    ) / math.sqrt(HD)
    grad_projected_low = jnp.concatenate(
        [
            grad_queries.reshape(row_count, width_here),
            grad_keys.reshape(row_count, width_here),
            grad_values.reshape(row_count, width_here),
        ],
        axis=1,
    ).astype(jnp.bfloat16)
    grad_qkv = contract_rows(normed_one_low, grad_projected_low)
    grad_normed_one = lax.psum(
        contract_cols(grad_projected_low, qkv_weight).astype(jnp.bfloat16), "head"
    ).astype(jnp.float32)
    input_grad = grad_mixed + norm_backward(
        grad_normed_one, scaled_one, inverse_one, norm_params[0]
    )
    norm_grads = jnp.stack(
        [
            jnp.sum(grad_normed_one * scaled_one, axis=0),
            jnp.sum(grad_normed_one, axis=0),
            jnp.sum(grad_normed_two * scaled_two, axis=0),
            jnp.sum(grad_normed_two, axis=0),
        ]
    )
    grad_blocks = jnp.concatenate(
        [
            grad_qkv.reshape(-1),
            grad_out_proj.reshape(-1),
            grad_up.reshape(-1),
            grad_down.reshape(-1),
        ]
    ).reshape(block_count, block_len)
    summed, norm_summed = (
        lax.psum(grad_blocks.astype(jnp.bfloat16), "dp").astype(jnp.float32),
        lax.psum(norm_grads.astype(jnp.bfloat16), "dp").astype(jnp.float32),
    )
    landing = jnp.where(owners == owner_index, slot_row - owner_index * CAP, CAP)
    owned_grad = jnp.zeros((CAP, block_len), jnp.float32).at[landing].set(summed, mode="drop")
    norm_owned = lax.dynamic_slice_in_dim(norm_summed, owner_index * norm_cols, norm_cols, 1)
    held_count = jnp.sum((owners == owner_index).astype(jnp.int32))
    used_slot = (jnp.arange(CAP, dtype=jnp.int32) < held_count)[:, None]
    new_master, new_first, new_second = adamw_update(
        master_slots, first_slots, second_slots, owned_grad, weight_decay, learn_rate
    )
    new_master = jnp.where(used_slot, new_master, 0.0)
    new_first = jnp.where(used_slot, new_first, 0.0)
    new_second = jnp.where(used_slot, new_second, 0.0)
    new_norms, new_norm_first, new_norm_second = adamw_update(
        norm_master, norm_first, norm_second, norm_owned, 0.0, norm_rate
    )
    return (
        block_output,
        input_grad,
        new_master,
        new_first,
        new_second,
        new_norms,
        new_norm_first,
        new_norm_second,
    )


W = 128
R = 384
QB = 4
CB = 12
MESH = pl.DeviceIdType.MESH
bf16 = jnp.bfloat16
f32 = jnp.float32


def place(sizes):
    dp = lax.axis_index("dp")
    head = lax.axis_index("head")
    return dp // sizes.y, lax.rem(dp, sizes.y), head // sizes.c, lax.rem(head, sizes.c)


class Sizes:
    z, y, x, c = 4, 2, 2, 2


def device(z, y, x, c):
    return (z * Sizes.y + y, x * Sizes.c + c)


def block_rows(owners):
    ids = [owners[j] for j in range(owners.shape[0])]
    rows = []
    for j, mine in enumerate(ids):
        row = mine * CAP
        for other in ids[:j]:
            row = row + jnp.where(other == mine, 1, 0)
        rows.append(row)
    return rows


def slot_is_wide(rows, slot_row):
    flag = rows[0] == slot_row
    for row in rows[1:QB]:
        flag = jnp.logical_or(flag, row == slot_row)
    return flag


def dot(left, right):
    return jnp.dot(left, right, preferred_element_type=f32)


def dot_cols(left, right):
    return lax.dot_general(left, right, (((1,), (1,)), ((), ())), preferred_element_type=f32)


def dot_rows(left, right):
    return lax.dot_general(left, right, (((0,), (0,)), ((), ())), preferred_element_type=f32)


def normalise(values):
    centred = values - jnp.mean(values, axis=-1, keepdims=True)
    inverse = lax.rsqrt(jnp.mean(centred * centred, axis=-1, keepdims=True) + norm_eps)
    return centred * inverse, inverse


def panels(ref, h, first, size):
    return jnp.concatenate([ref[h, p, first : first + size, :] for p in range(ref.shape[1])], axis=1)


def cat_pieces(first, size):
    pieces = []
    row = first
    while row < first + size:
        block, inside = divmod(row, R // 4)
        count = min(R // 4 - inside, first + size - row)
        pieces.append((QB + block, inside, row - first, count))
        row += count
    return pieces


RA, RB = 224, 304
GA, GB = 176, 336
TILE = 128


def layer_kernel(
    tok_hbm, cot_hbm, master_hbm, norms_hbm, steps_hbm, bands_hbm, lens_row_hbm, lens_hbm, owners_hbm,
    total, out_all, in_all, norm_total,
    wv, master, flat, mine, meta, norms_v, steps, bands, lens_row, lens, owners, block_at,
    tok, cot, low1, xhat1, inv1, qkv, probs, sums, att, acc, low2, xhat2, inv2, e2, actives, d_qkvs, da, e1,
    out_low, in_low,
    grads, from_core, rxa, sa, rya, sb, ryb, sbx, rxb, fz, rz, sc, rc, ryc, rxc, norm_part, norm_sum, n_core, n_x, n_y, n_z,
    i_sem, z_s, z_r, ya_s, ya_r, xa_s, xa_r, xb_s, xb_r, yb_s, yb_r, core_s, core_r, m_s, m_r,
    c_s, c_r, zc_s, zc_r, cc_s, cc_r, sc_s, sc_r, cy_s, cy_r, cx_s, cx_r,
    cs, cr, as_, ar, say_s, say_r, sby_s, sby_r, sbx_s, sbx_r, fz_s, fz_r, n_s, n_r, o_s, o_r, o_l,
):
    z, y, x, c = place(Sizes)
    nz = Sizes.z
    dp, head = z * 2 + y, x * 2 + c
    dp_peers = [device(lax.rem(z + k, nz), (y + j) % 2, x, c) for k in range(nz) for j in range(2) if k or j]
    x_peer, y_peer, core_peer = device(z, y, 1 - x, c), device(z, 1 - y, x, c), device(z, y, x, 1 - c)
    peers = dp_peers + [x_peer, core_peer]
    barrier = pltpu.get_barrier_semaphore()
    for peer in peers:
        pl.semaphore_signal(barrier, inc=1, device_id=peer, device_id_type=MESH)

    tokens_here = tok.shape[1]
    items_here = tokens_here // SEQ
    tiles = tokens_here // TILE

    def whose(p):
        return lax.rem(x + p, 2) * 2 + c

    def tokens_of(ref, who):
        return ref.at[pl.ds(pl.multiple_of(who * tokens_here, tokens_here), tokens_here), :]

    fetches = [
        pltpu.make_async_copy(src, dst, i_sem.at[n])
        for n, (src, dst) in enumerate((
            (owners_hbm, owners), (master_hbm, master), (steps_hbm, steps), (bands_hbm, bands),
            (lens_row_hbm, lens_row), (norms_hbm, norms_v), (lens_hbm, lens),
            (tokens_of(tok_hbm, whose(0)), tok.at[0]), (tokens_of(cot_hbm, whose(0)), cot.at[0]),
            (tokens_of(tok_hbm, whose(1)), tok.at[1]), (tokens_of(cot_hbm, whose(1)), cot.at[1]),
        ))
    ]
    for fetch in fetches:
        fetch.start()

    def loop(first, last, body):
        def step(i, _):
            body(i)
            return 0

        lax.fori_loop(first, last, step, 0)

    def remote(src, dst, send, recv, peer):
        return pltpu.make_async_remote_copy(
            src_ref=src, dst_ref=dst, send_sem=send, recv_sem=recv, device_id=peer, device_id_type=MESH
        )

    def same(ref, send, recv, peer):
        return remote(ref, ref, send, recv, peer)

    shard, far = x * 2 + c, (1 - x) * 2 + c
    fetches[0].wait()
    rows = block_rows(owners)
    fetches[1].wait()
    for r in range(CAP):
        flat[...] = master[:, r, :]
        wide = jnp.concatenate([flat[pl.ds(p, W, stride=3), :] for p in range(3)], axis=0)
        narrow = jnp.concatenate([flat[pl.ds(p, R // 4, stride=4), :] for p in range(4)], axis=0)
        wv[shard, dp * CAP + r] = jnp.where(slot_is_wide(rows, dp * CAP + r), wide, narrow).astype(bf16)

    for n in (2, 3, 4, 5):
        fetches[n].wait()
    items = steps.shape[1]
    item_weight = jnp.exp(-2.0 * steps[...].astype(f32) / TSTEPS)
    item_length = lens_row[...].astype(f32)
    table = bands[...] == lax.broadcasted_iota(jnp.int32, (NBANDS, items), 0)
    ones = table.astype(f32)
    mine[...] = jnp.zeros_like(mine)
    mine[0:4, 0 : W // 2] = norms_v[...]
    mine[:, W // 2 : W // 2 + 1] = jnp.sum(ones * (item_weight * item_length), axis=1, keepdims=True)
    mine[:, W // 2 + 1 : W // 2 + 2] = jnp.sum(ones * item_length, axis=1, keepdims=True)
    meta[dp] = mine[...]

    pl.semaphore_wait(barrier, len(peers))

    part_a, part_b, part_ab, part_c = pl.ds(0, GA), pl.ds(GA, GB - GA), pl.ds(0, GB), pl.ds(GB, R - GB)

    def slab(sh, zz, yy, part=slice(None)):
        return wv.at[sh, pl.ds((zz * 2 + yy) * CAP, CAP), part, :]

    def order(k):
        late, low = k // 2, z // 2
        return (1 - late) * (z + k * (1 - 2 * lax.rem(z, 2))) + late * (k + low * (3 - 2 * k))

    up, down, inner = z < nz - 1, z > 0, lax.rem(z, nz - 1) != 0
    own_up = same(slab(shard, z, y, part_ab), z_s.at[0], z_r.at[z], device(z + 1, y, x, c))
    own_down = same(slab(shard, z, y, part_ab), z_s.at[nz], z_r.at[z], device(z - 1, y, x, c))
    pl.when(up)(own_up.start)
    pl.when(down)(own_down.start)

    def meta_copy(k):
        return remote(mine, meta.at[dp], m_s.at[k], m_r.at[k], dp_peers[k])

    for k in range(len(dp_peers)):
        meta_copy(k).start()

    def along_z(k):
        zz = order(k)
        late = k // 2
        goal = (1 - late) * (3 - z) + late * 3 * (z - 1)
        return same(slab(shard, zz, y, part_ab), z_s.at[k], z_r.at[zz], device(goal, y, x, c))

    def both(j, zz):
        return wv.at[lax.rem(x + j, 2) * 2 + c, pl.ds(zz * 2 * CAP, 2 * CAP), part_c, :]

    def last_z(j, n):
        return same(both(j, z), zc_s.at[j, n], zc_r.at[j, n], device(lax.rem(z + n, nz), y, x, c))

    def last_here(j, n):
        zz = lax.rem(z + nz - n, nz)
        return same(both(j, zz), zc_s.at[j, n], zc_r.at[j, n], x_peer)

    def last_core(j, n):
        return same(both(j, lax.rem(z + nz - n, nz)), cc_s.at[j, n], cc_r.at[j, n], core_peer)

    own_c = slab(shard, z, y, part_c)
    c_copies = (
        same(own_c, c_s.at[0], c_r.at[0], y_peer),
        same(own_c, c_s.at[1], c_r.at[1], x_peer),
        same(slab(shard, z, 1 - y, part_c), c_s.at[2], c_r.at[2], x_peer),
    )

    def first_copies(k):
        zz = order(k)
        one, two = slab(shard, zz, y, part_a), slab(shard, zz, y, part_b)
        return (
            same(one, ya_s.at[k], ya_r.at[k], y_peer),
            same(two, xb_s.at[k], xb_r.at[k], x_peer),
            same(two, yb_s.at[k, 0], yb_r.at[k, 0], y_peer),
            same(one, xa_s.at[k, 0], xa_r.at[k, 0], x_peer),
            same(slab(shard, zz, y, part_ab), core_s.at[k, 0], core_r.at[k, 0], core_peer),
        )

    def second_copies(k):
        zz = order(k)
        return (
            same(slab(shard, zz, 1 - y, part_a), xa_s.at[k, 1], xa_r.at[k, 1], x_peer),
            same(slab(far, zz, y, part_b), yb_s.at[k, 1], yb_r.at[k, 1], y_peer),
            same(slab(shard, zz, 1 - y, part_ab), core_s.at[k, 1], core_r.at[k, 1], core_peer),
        )

    def third_copies(k):
        zz = order(k)
        return (
            same(slab(far, zz, y, part_ab), core_s.at[k, 2], core_r.at[k, 2], core_peer),
            same(slab(far, zz, 1 - y, part_ab), core_s.at[k, 3], core_r.at[k, 3], core_peer),
        )

    def gather0(k):
        @pl.when(k > 0)
        def _():
            along_z(k).wait_recv()
            pl.when(inner)(along_z(k).start)

        for copy in first_copies(k):
            copy.start()

    def gather1(k):
        zz = order(k)
        over_x, over_y, core = second_copies(k)
        same(slab(shard, zz, 1 - y, part_a), ya_s.at[k], ya_r.at[k], y_peer).wait_recv()
        over_x.start()
        same(slab(far, zz, y, part_b), xb_s.at[k], xb_r.at[k], x_peer).wait_recv()
        over_y.start()
        same(slab(shard, zz, 1 - y, part_b), yb_s.at[k, 0], yb_r.at[k, 0], y_peer).wait_recv()
        core.start()

    def gather2(k):
        zz = order(k)
        near, apart = third_copies(k)
        same(slab(far, zz, y, part_a), xa_s.at[k, 0], xa_r.at[k, 0], x_peer).wait_recv()
        near.start()
        same(slab(far, zz, 1 - y, part_a), xa_s.at[k, 1], xa_r.at[k, 1], x_peer).wait_recv()
        same(slab(far, zz, 1 - y, part_b), yb_s.at[k, 1], yb_r.at[k, 1], y_peer).wait_recv()
        apart.start()

    c_copies[0].start()
    c_copies[1].start()
    gather0(0)

    def gather_last(n):
        for j in range(2):
            last_here(j, n).wait_recv()
            last_core(j, n).start()

    def find_block(row):
        block = 0
        for j, block_row in enumerate(rows):
            block = block + jnp.where(block_row == row, j, 0)
        block_at[row] = block

    loop(0, nz * 2 * CAP, find_block)
    for k in range(len(dp_peers)):
        meta_copy(k).wait_recv()
    lane = lax.broadcasted_iota(jnp.int32, (8, W), 1)
    chunks = []
    for pair in range(meta.shape[0] // 2):
        chunks.append(jnp.where(lane < W // 2, meta[2 * pair], pltpu.roll(meta[2 * pair + 1], W // 2, 1)))
    norms = jnp.concatenate(chunks, axis=1).astype(bf16).astype(f32)
    gain1, shift1, gain2, shift2 = (norms[i : i + 1, :] for i in range(4))
    band_sums = meta[0]
    for d in range(1, meta.shape[0]):
        band_sums = band_sums + meta[d]
    weight_of = jnp.sum(jnp.where(table, band_sums[:, W // 2 : W // 2 + 1], 0.0), axis=0, keepdims=True)
    count_of = jnp.sum(jnp.where(table, band_sums[:, W // 2 + 1 : W // 2 + 2], 0.0), axis=0, keepdims=True)
    scales = item_weight * count_of / weight_of
    item_lane = lax.broadcasted_iota(jnp.int32, (1, items), 1)
    position = lax.broadcasted_iota(jnp.int32, (TILE, 1), 0)
    for n in range(6, 11):
        fetches[n].wait()

    def tile(t):
        return pl.ds(pl.multiple_of(t * TILE, TILE), TILE)

    def first_norm(i):
        p, t = i // tiles, lax.rem(i, tiles)
        here = tile(t)
        scaled, inverse = normalise(tok[p, here, :])
        xhat1[p, here, :] = scaled
        inv1[p, here, :] = inverse
        low1[p, here, :] = (scaled * gain1 + shift1).astype(bf16)
        item = whose(p) * items_here + t // (SEQ // TILE)
        scale = jnp.sum(jnp.where(item_lane == item, scales, 0.0), axis=1, keepdims=True)
        inside = position + lax.rem(t, SEQ // TILE) * TILE < lens[item]
        scaled_cot = cot[p, here, :] * jnp.where(inside, scale, 0.0)
        cot[p, here, :] = scaled_cot
        e2[p, here, :] = scaled_cot.astype(bf16)

    c_copies[0].wait_recv()
    c_copies[2].start()
    loop(0, 2 * tiles, first_norm)
    c_copies[1].wait_recv()
    c_copies[2].wait_recv()
    for j in range(2):
        last_core(j, 0).start()

    def gather(step):
        pl.when(step < nz)(lambda: gather0(step))

        @pl.when(step == nz - 1)
        def _():
            for j in range(2):
                for n in range(1, nz):
                    last_z(j, n).start()

        pl.when(step <= nz)(lambda: gather1(step - 1))
        pl.when(step >= 2)(lambda: gather2(step - 2))

    loop(1, nz + 2, gather)
    loop(1, nz, gather_last)

    def all_here(k):
        zz = order(k)
        for kind, (xx, yy) in enumerate(((x, y), (x, 1 - y), (1 - x, y), (1 - x, 1 - y))):
            same(slab(xx * 2 + 1 - c, zz, yy, part_ab), core_s.at[k, kind], core_r.at[k, kind], core_peer).wait_recv()
        for j in range(2):
            last_core(j, k).wait_recv()

    loop(0, nz, all_here)

    head_lane = lax.broadcasted_iota(jnp.int32, (1, W), 1)
    head_masks = [head_lane < HD, head_lane >= HD]
    key_pos = lax.broadcasted_iota(jnp.int32, (1, SEQ), 1)
    item_rows = [slice(i * SEQ, (i + 1) * SEQ) for i in range(items_here)]

    def only(values, a):
        return jnp.where(head_masks[a], values, jnp.zeros_like(values))

    def stack(values):
        return jnp.concatenate([only(values, 0), only(values, 1)], axis=0)

    def wide_matrix(h):
        return jnp.concatenate(
            [
                jnp.concatenate([wv[h, rows[j], p * W : (p + 1) * W, :] for j in range(QB)], axis=0)
                for p in range(3)
            ],
            axis=1,
        )

    def narrow_matrix(h, first, size):
        pieces = cat_pieces(first, size)
        return jnp.concatenate(
            [
                jnp.concatenate(
                    [wv[h, rows[b], pl.ds(p * (R // 4) + inside, count), :] for b, inside, _, count in pieces], axis=0
                )
                for p in range(4)
            ],
            axis=1,
        )

    deep, low = (QB + 2, CB - 2), (0, QB + 2)
    x_part, y_part, z_part = pl.ds(0, RA), pl.ds(RA, RB - RA), pl.ds(RB, R - RB)

    def core_push(j, n):
        part = pl.ds(*(deep, low)[n])
        return remote(grads.at[j, part], from_core.at[j, part], cs.at[n, j], cr.at[n, j], core_peer)

    def x_push(n):
        part = pl.ds(*(deep, low)[n])
        return remote(grads.at[2, part, x_part, :], rxa.at[part], as_.at[n], ar.at[n], x_peer)

    def hand_over(i, n):
        first, count = (deep, low)[n]
        pl.when(i < 2)(lambda: core_push(i, n).start())

        @pl.when(i >= 2)
        def _():
            core_push(i - 2, n).wait_recv()

            def add(block):
                grads[i, block] = grads[i, block] + from_core[i - 2, block]

            loop(first, first + count, add)
            pl.when(i == 2)(lambda: x_push(n).start())

    pair_z, cross_z = z + 1 - 2 * lax.rem(z, 2), lax.rem(z + 2, nz)

    def chunk(k):
        return lax.rem(pair_z + lax.rem(k, 2) * (z - pair_z) + 2 * (1 - k // 2), nz)

    def block_of(k, yy, r):
        return block_at[(chunk(k) * 2 + yy) * CAP + r]

    def over_y_first(k):
        return remote(sb.at[k], ryb.at[k], sby_s.at[k], sby_r.at[k], y_peer)

    def over_x_last(k):
        return remote(sbx.at[k], rxb.at[k], sbx_s.at[k], sbx_r.at[k], x_peer)

    def over_y_last(k):
        return remote(sa.at[k], rya.at[k], say_s.at[k], say_r.at[k], y_peer)

    def over_z(k, r):
        goal = pair_z + lax.rem(k, 2) * (cross_z - pair_z)
        return remote(fz.at[k, r], rz.at[k, r], fz_s.at[k, r], fz_r.at[k, r], device(goal, y, x, c))

    def z_first(k):
        goal = pair_z + lax.rem(k, 2) * (cross_z - pair_z)
        return remote(sc.at[k], rc.at[k], sc_s.at[k], sc_r.at[k], device(goal, y, x, c))

    def z_then_y():
        return remote(sc.at[nz - 1, :, 1 - y], ryc, cy_s, cy_r, y_peer)

    def z_then_x():
        return remote(sc.at[nz - 1, 0, y], rxc, cx_s, cx_r, x_peer)

    def send_c(k):
        for r in range(2 * CAP):
            block = block_of(k, r // CAP, r % CAP)
            for j in range(2):
                sc[k, j, r // CAP, r % CAP] = grads[2 + j, block, z_part, :]
        pl.when(lax.rem(k, 2) == 0)(lambda: z_first(k).start())

    def cross_c():
        z_first(0).wait_recv()
        for j in range(2):
            sc[1, j] = sc[1, j] + rc[0, j]
        z_first(1).start()

    def own_c():
        z_first(1).wait_recv()
        z_first(2).wait_recv()
        for j in range(2):
            sc[nz - 1, j] = sc[nz - 1, j] + (rc[1, j].astype(f32) + rc[2, j].astype(f32)).astype(bf16)
        z_then_y().start()

    def y_c():
        z_then_y().wait_recv()
        for j in range(2):
            sc[nz - 1, j, y] = sc[nz - 1, j, y] + ryc[j]
        z_then_x().start()

    def norm_copies():
        z_peers = [device(lax.rem(z + k, nz), y, x, c) for k in range(1, nz)]
        return [
            remote(norm_part, n_core, n_s.at[0], n_r.at[0], core_peer),
            remote(norm_sum.at[0], n_x, n_s.at[1], n_r.at[1], x_peer),
            remote(norm_sum.at[1], n_y, n_s.at[2], n_r.at[2], y_peer),
        ] + [remote(norm_sum.at[2], n_z.at[k], n_s.at[3 + k], n_r.at[3 + k], p) for k, p in enumerate(z_peers)]

    def send_b(k):
        for r in range(CAP):
            block = block_of(k, 1 - y, r)
            for j in range(2):
                sb[k, j, r] = grads[2 + j, block, y_part, :]
        over_y_first(k).start()

    def add_x(j):
        grads[3, j, x_part, :] = grads[3, j, x_part, :] + rxa[j]

    def send_a(k):
        for r in range(CAP):
            sa[k, r] = grads[3, block_of(k, 1 - y, r), x_part, :]
        over_y_last(k).start()

    def reduce1(k):
        over_y_first(k).wait_recv()
        for r in range(CAP):
            sbx[k, r] = grads[2, block_of(k, y, r), y_part, :] + ryb[k, 0, r]
        over_x_last(k).start()

    def reduce2(k):
        over_y_last(k).wait_recv()
        over_x_last(k).wait_recv()
        for r in range(CAP):
            block = block_of(k, y, r)
            fz[k, r, x_part, :] = grads[3, block, x_part, :] + rya[k, r]
            part = grads[3, block, y_part, :].astype(f32) + ryb[k, 1, r].astype(f32)
            fz[k, r, y_part, :] = (part + rxb[k, r].astype(f32)).astype(bf16)
            pl.when(lax.rem(k, 2) == 0)(over_z(k, r).start)

    def cross():
        for r in range(CAP):
            over_z(0, r).wait_recv()
            fz[1, r] = fz[1, r] + rz[0, r]
            over_z(1, r).start()

    key_row = lax.broadcasted_iota(jnp.int32, (2 * SEQ, W), 0)
    head_ones = jnp.where((key_row < SEQ) == head_masks[0], 1.0, 0.0).astype(bf16)

    def attention(p, h):
        projected = dot(low1[p], wide_matrix(h))
        qkv[h, 0] = (projected[:, :W].astype(bf16).astype(f32) * (1.0 / math.sqrt(HD))).astype(bf16)
        qkv[h, 1] = projected[:, W : 2 * W].astype(bf16)
        qkv[h, 2] = projected[:, 2 * W :].astype(bf16)
        for i, here in enumerate(item_rows):
            query, key, value = qkv[h, 0, here, :], qkv[h, 1, here, :], qkv[h, 2, here, :]
            valid = key_pos < lens[whose(p) * items_here + i]
            both = []
            for a in range(2):
                scores = jnp.where(valid, dot_cols(only(query, a), key), -1e30)
                exps = jnp.exp(scores - jnp.max(scores, axis=-1, keepdims=True)).astype(bf16)
                probs[h, i, a] = exps
                both.append(exps)
            mixed = dot(jnp.concatenate(both, axis=1), jnp.concatenate([stack(value), head_ones], axis=1))
            inverse = 1.0 / mixed[:, W:]
            sums[h, here, :] = inverse
            att[h, here, :] = (mixed[:, :W] * inverse).astype(bf16)
        acc[...] += dot(att[h], narrow_matrix(h, 0, W))

    def put(i, first, result):
        for block, inside, row, count in cat_pieces(first, result.shape[0]):
            for p in range(4):
                here = pl.ds(p * (R // 4) + inside, count)
                grads[i, block, here, :] = result[row : row + count, p * W : (p + 1) * W].astype(bf16)

    def shard_of(p, i):
        return lax.rem(1 + x + p + i, 2) * 2 + lax.rem(c + 1 + i // 2, 2)

    def feed_forward(p, i):
        h = shard_of(p, i)
        up_matrix, down_matrix = narrow_matrix(h, W, D), narrow_matrix(h, W + D, D)
        hidden = dot(low2[...], up_matrix)
        root = math.sqrt(2.0 / math.pi)
        square = hidden * hidden
        bend = jnp.tanh(root * hidden * (1.0 + 0.044715 * square))
        half = 0.5 * (1.0 + bend)
        active = (hidden * half).astype(bf16)
        slope = half + 0.5 * hidden * (1.0 - bend * bend) * (root + (3.0 * 0.044715 * root) * square)
        if p == 0:
            actives[i] = active
        else:
            acc[...] += dot(active, down_matrix)
        back = (dot_cols(e2[p], down_matrix) * slope).astype(bf16)
        da[...] += dot_cols(back, up_matrix)
        if p == 0:
            put(i, W + D, dot_rows(active, e2[p]))
            put(i, W, dot_rows(low2[...], back))
            hand_over(i, 0)

    def attention_back(p, i):
        h = shard_of(p, i)
        d_all = dot_cols(e1[...], narrow_matrix(h, 0, W)) * sums[h]
        shared_all = (d_all * att[h].astype(f32)).astype(bf16)
        d_all = d_all.astype(bf16)
        parts = []
        for m, here in enumerate(item_rows):
            query, key, value = qkv[h, 0, here, :], qkv[h, 1, here, :], qkv[h, 2, here, :]
            d_here, shared = d_all[here, :], shared_all[here, :]
            against = jnp.concatenate([value, jnp.full((SEQ, W), -1.0, bf16)], axis=1)
            d_scores = []
            for a in range(2):
                change = dot_cols(jnp.concatenate([only(d_here, a), only(shared, a)], axis=1), against)
                d_scores.append((probs[h, m, a].astype(f32) * change).astype(bf16))
            d_query = dot(jnp.concatenate(d_scores, axis=1), stack(key)) * (1.0 / math.sqrt(HD))
            d_key = dot_rows(jnp.concatenate(d_scores, axis=0), stack(query))
            d_value = dot_rows(jnp.concatenate([probs[h, m, 0], probs[h, m, 1]], axis=0), stack(d_here))
            parts.append(jnp.concatenate([d_query, d_key, d_value], axis=1).astype(bf16))
        d_qkv = jnp.concatenate(parts, axis=0)
        if p == 0:
            d_qkvs[i] = d_qkv
            put(i, 0, dot_rows(att[h], e1[...]))
            d_weight = dot_rows(low1[p], d_qkv).astype(bf16)
            for j in range(QB):
                for m in range(3):
                    grads[i, j, m * W : (m + 1) * W, :] = d_weight[j * W : (j + 1) * W, m * W : (m + 1) * W]
            hand_over(i, 1)
        else:
            da[...] += dot_cols(d_qkv, wide_matrix(h))

    def late_output(i):
        acc[...] += dot(actives[i], narrow_matrix(shard_of(0, i), W + D, D))

    def late_input(i):
        da[...] += dot_cols(d_qkvs[i], wide_matrix(shard_of(0, i)))

    def norm_backward(grad, scaled, inverse, gain):
        grad_scaled = grad * gain
        centre = jnp.mean(grad_scaled, axis=-1, keepdims=True)
        slope = jnp.mean(grad_scaled * scaled, axis=-1, keepdims=True)
        return inverse * (grad_scaled - centre - scaled * slope)

    def add_norm(p, row, grad, scaled):
        if p == 0:
            norm_part[row : row + 1, :] += jnp.sum(grad * scaled, axis=0, keepdims=True)
            norm_part[row + 1 : row + 2, :] += jnp.sum(grad, axis=0, keepdims=True)

    norm_part[...] = jnp.zeros_like(norm_part)

    def out_copies(p, n):
        src, dst = ((out_low, out_all), (in_low, in_all))[n]
        there = tokens_of(dst, whose(p))
        return (
            pltpu.make_async_copy(src.at[p], there, o_l.at[p, n]),
            remote(src.at[p], there, o_s.at[p, n], o_r.at[p, n], core_peer),
        )

    def block_result(p):
        out_low[p] = acc[...].astype(bf16)
        for copy in out_copies(p, 0):
            copy.start()

    def input_result(p):
        def first_norm_back(t):
            here = tile(t)
            grad, scaled = da[here, :], xhat1[p, here, :]
            add_norm(p, 0, grad, scaled)
            in_low[p, here, :] = (cot[p, here, :] + norm_backward(grad, scaled, inv1[p, here, :], gain1)).astype(bf16)

        loop(0, tiles, first_norm_back)
        for copy in out_copies(p, 1):
            copy.start()

    def layer_pass(p):
        acc[...] = jnp.zeros_like(acc)
        loop(0, 4, lambda h: attention(p, h))

        def second_norm(t):
            here = tile(t)
            state = acc[here, :] + tok[p, here, :]
            acc[here, :] = state
            scaled, inverse = normalise(state)
            xhat2[here, :] = scaled
            inv2[here, :] = inverse
            low2[here, :] = (scaled * gain2 + shift2).astype(bf16)
            da[here, :] = jnp.zeros((TILE, D), f32)

        loop(0, tiles, second_norm)
        if p == 1:
            for n in range(2):
                x_push(n).wait_recv()
            loop(0, QB + CB, add_x)
            loop(0, nz, send_a)
            loop(0, nz, reduce1)
        loop(0, 4, lambda i: feed_forward(p, i))
        if p == 1:
            block_result(1)
            own_c()
            reduce2(0)
            norm_copies()[0].wait_recv()
            norm_sum[0] = norm_part[...] + n_core[...]
            norm_copies()[1].start()

        def second_norm_back(t):
            here = tile(t)
            grad, scaled = da[here, :], xhat2[here, :]
            add_norm(p, 2, grad, scaled)
            change = cot[p, here, :] + norm_backward(grad, scaled, inv2[here, :], gain2)
            cot[p, here, :] = change
            e1[here, :] = change.astype(bf16)
            da[here, :] = jnp.zeros((TILE, D), f32)

        loop(0, tiles, second_norm_back)
        if p == 1:
            norm_copies()[1].wait_recv()
            norm_sum[1] = norm_sum[0] + n_x[...]
            norm_copies()[2].start()
            reduce2(1)

        def attention_step(i):
            attention_back(p, i)
            if p == 1:
                @pl.when(i == 1)
                def _():
                    cross()
                    reduce2(2)
                    y_c()

        loop(0, 4, attention_step)

    layer_pass(0)
    loop(0, nz, send_c)
    loop(0, nz, send_b)
    loop(0, 4, late_output)
    block_result(0)
    loop(0, 4, late_input)
    input_result(0)
    cross_c()
    norm_copies()[0].start()
    layer_pass(1)
    input_result(1)

    norm_copies()[2].wait_recv()
    norm_sum[2] = norm_sum[1] + n_y[...]
    for copy in norm_copies()[3:]:
        copy.start()
    reduce2(nz - 1)

    for k in range(nz - 1):
        norm_copies()[3 + k].wait_recv()
    z_then_x().wait_recv()
    for r in range(CAP):
        over_z(2, r).wait_recv()
        over_z(1, r).wait_recv()
    norm_total[...] = norm_sum[2] + ((n_z[0] + n_z[1]) + n_z[2])

    def last(r):
        others = rz[1, r].astype(f32) + rz[2, r].astype(f32)
        total[r, pl.ds(0, RB), :] = fz[nz - 1, r].astype(f32) + others
        total[r, z_part, :] = sc[nz - 1, 1, y, r].astype(f32) + rxc[r].astype(f32)

    loop(0, CAP, last)

    for p in range(2):
        for n in range(2):
            local, over_core = out_copies(p, n)
            local.wait()
            over_core.wait()
    for copy in norm_copies():
        copy.wait_send()
    for k in range(len(dp_peers)):
        meta_copy(k).wait_send()
    pl.when(up)(own_up.wait_send)
    pl.when(down)(own_down.wait_send)
    for copy in c_copies:
        copy.wait_send()

    def sent(k):
        for copy in first_copies(k) + second_copies(k) + third_copies(k):
            copy.wait_send()
        pl.when(jnp.logical_and(k > 0, inner))(along_z(k).wait_send)
        for j in range(2):
            last_core(j, k).wait_send()
            pl.when(k > 0)(last_z(j, k).wait_send)
        for copy in (over_y_first(k), over_x_last(k), over_y_last(k)):
            copy.wait_send()
        pl.when(k < nz - 1)(z_first(k).wait_send)
        for r in range(CAP):
            pl.when(k < nz - 1)(over_z(k, r).wait_send)

    loop(0, nz, sent)
    z_then_y().wait_send()
    z_then_x().wait_send()
    for n in range(2):
        x_push(n).wait_send()
        for j in range(2):
            core_push(j, n).wait_send()


def layer(tokens, cotangent, master, norms, steps, bands, lens_row, lens, owners):
    nz = Sizes.z
    here = tokens.shape[0] // lax.axis_size("head")
    items_here = here // SEQ
    items = lens.shape[0]
    vm = pl.BlockSpec(memory_space=pltpu.VMEM)
    hbm = pl.BlockSpec(memory_space=pltpu.HBM)
    dma = pltpu.SemaphoreType.DMA
    V, S = pltpu.VMEM, pltpu.SMEM
    square = (here, D)
    blocks = QB + CB
    rb = RB - RA
    low, full, two_low, two = V(square, bf16), V(square, f32), V((2, *square), bf16), V((2, *square), f32)
    scratch = [
        V((4, nz * 2 * CAP, R, W), bf16), V((R, CAP, W), f32), V((R, W), f32),
        V((8, W), f32), V((nz * 2, 8, W), f32), V(norms.shape, f32),
        V((1, items), jnp.int32), V((1, items), jnp.int32), V((1, items), jnp.int32),
        S((items,), jnp.int32), S(owners.shape, jnp.int32), S((nz * 2 * CAP,), jnp.int32),
        two, two, two_low, two, V((2, here, 1), f32), V((4, 3, here, W), bf16),
        V((4, items_here, 2, SEQ, SEQ), bf16), V((4, here, W), f32), V((4, here, W), bf16),
        full, low, full, V((here, 1), f32), two_low,
        V((4, here, D), bf16), V((4, here, 3 * W), bf16), full, low, two_low, two_low,
        V((4, blocks, R, W), bf16), V((2, blocks, R, W), bf16),
        V((blocks, RA, W), bf16), V((nz, CAP, RA, W), bf16), V((nz, CAP, RA, W), bf16),
        V((nz, 2, CAP, rb, W), bf16), V((nz, 2, CAP, rb, W), bf16), V((nz, CAP, rb, W), bf16),
        V((nz, CAP, rb, W), bf16), V((nz, CAP, RB, W), bf16), V((nz - 1, CAP, RB, W), bf16),
        V((nz, 2, 2, CAP, R - RB, W), bf16), V((nz - 1, 2, 2, CAP, R - RB, W), bf16),
        V((2, CAP, R - RB, W), bf16), V((CAP, R - RB, W), bf16),
        V((8, D), f32), V((3, 8, D), f32), V((8, D), f32), V((8, D), f32), V((8, D), f32), V((nz - 1, 8, D), f32),
        dma((11,)), dma((nz + 1,)), dma((nz,)), dma((nz,)), dma((nz,)), dma((nz, 2)), dma((nz, 2)), dma((nz,)), dma((nz,)),
        dma((nz, 2)), dma((nz, 2)), dma((nz, 4)), dma((nz, 4)), dma((8,)), dma((8,)),
        dma((3,)), dma((3,)), dma((2, nz)), dma((2, nz)), dma((2, nz)), dma((2, nz)),
        dma((nz,)), dma((nz,)), dma, dma, dma, dma,
        dma((2, 2)), dma((2, 2)), dma((2,)), dma((2,)), dma((nz,)), dma((nz,)), dma((nz,)), dma((nz,)),
        dma((nz,)), dma((nz,)), dma((nz, CAP)), dma((nz, CAP)), dma((8,)), dma((8,)), dma((2, 2)), dma((2, 2)), dma((2, 2)),
    ]
    return pl.pallas_call(
        layer_kernel,
        name="layer",
        out_shape=(
            jax.ShapeDtypeStruct((CAP, R, W), f32),
            jax.ShapeDtypeStruct(tokens.shape, bf16),
            jax.ShapeDtypeStruct(tokens.shape, bf16),
            jax.ShapeDtypeStruct((8, D), f32),
        ),
        in_specs=[hbm] * 9,
        out_specs=(vm, hbm, hbm, vm),
        scratch_shapes=scratch,
        compiler_params=pltpu.CompilerParams(collective_id=0, has_side_effects=True, vmem_limit_bytes=56 << 20),
    )(tokens, cotangent, master, norms, steps, bands, lens_row, lens, owners)


def finish_kernel(
    total_hbm, norm_hbm, master_hbm, first_hbm, second_hbm, norm_m, norm_f, norm_s, owners_hbm, out_all, in_all,
    block_output, input_grad, new_master, new_first, new_second, new_norm, new_norm_first, new_norm_second,
    out_low, in_low, out_full, in_full, states, results, flat, grad, total, norm_total, norm_master, norm_first, norm_second, owners, l_sem, s_sem, i_sem, r_sem,
):
    pieces = l_sem.shape[1]
    size = out_low.shape[0] // pieces
    pairs = ((out_all, out_low, out_full, block_output), (in_all, in_low, in_full, input_grad))

    def piece(p):
        return pl.ds(pl.multiple_of(p * size, size), size)

    def fetch(n, p):
        return pltpu.make_async_copy(pairs[n][0].at[piece(p), :], pairs[n][1].at[piece(p), :], l_sem.at[n, p])

    def store(n, p):
        return pltpu.make_async_copy(pairs[n][2].at[piece(p), :], pairs[n][3].at[piece(p), :], s_sem.at[n, p])

    small_copies = [
        pltpu.make_async_copy(src, dst, i_sem.at[3 + i])
        for i, (src, dst) in enumerate((
            (owners_hbm, owners), (total_hbm, total), (norm_hbm, norm_total),
            (norm_m, norm_master), (norm_f, norm_first), (norm_s, norm_second),
        ))
    ]
    state_copies = [
        pltpu.make_async_copy(src, states.at[i], i_sem.at[i]) for i, src in enumerate((master_hbm, first_hbm, second_hbm))
    ]
    result_copies = [
        pltpu.make_async_copy(results.at[i], dst, r_sem.at[i]) for i, dst in enumerate((new_master, new_first, new_second))
    ]

    def loop(count, body):
        def step(i, _):
            body(i)
            return 0

        lax.fori_loop(0, count, step, 0)

    for copy in small_copies:
        copy.start()
    for copy in state_copies:
        copy.start()
    loop(pieces, lambda p: fetch(0, p).start())
    loop(pieces, lambda p: fetch(1, p).start())

    dp = lax.axis_index("dp")
    small_copies[0].wait()
    rows = block_rows(owners)
    held = 0
    for j in range(owners.shape[0]):
        held = held + jnp.where(owners[j] == dp, 1, 0)

    def spread(r):
        is_wide = slot_is_wide(rows, dp * CAP + r)

        @pl.when(is_wide)
        def _():
            for p in range(3):
                flat[pl.ds(p, W, stride=3), :] = total[r, p * W : (p + 1) * W, :]

        @pl.when(jnp.logical_not(is_wide))
        def _():
            for p in range(4):
                flat[pl.ds(p, R // 4, stride=4), :] = total[r, p * (R // 4) : (p + 1) * (R // 4), :]

    small_copies[1].wait()
    for r in range(CAP):
        spread(r)
        grad[:, r, :] = flat[...]

    def convert(n, p):
        fetch(n, p).wait()
        _, low, full, _ = pairs[n]
        full[piece(p), :] = low[piece(p), :].astype(f32)
        store(n, p).start()

    for copy in state_copies:
        copy.wait()
    step = 32
    slot = lax.broadcasted_iota(jnp.int32, (step, CAP, W), 1)

    def update(i):
        here = pl.ds(pl.multiple_of(i * step, step), step)
        new = adamw_update(states[0, here], states[1, here], states[2, here], grad[here], weight_decay, learn_rate)
        for n in range(3):
            results[n, here] = jnp.where(slot < held, new[n], 0.0)


    def both(p):
        convert(0, p)
        for i in range(R // step // pieces):
            update(p * (R // step // pieces) + i)

    loop(pieces, both)
    for copy in result_copies:
        copy.start()
    for copy in small_copies[2:]:
        copy.wait()
    pair = norm_total[:, pl.ds(pl.multiple_of((dp // 2) * W, W), W)]
    mine = jnp.where(lax.rem(dp, 2) == 1, pltpu.roll(pair, W // 2, 1), pair)[0:4, 0 : norm_master.shape[1]]
    new = adamw_update(norm_master[...], norm_first[...], norm_second[...], mine, 0.0, norm_rate)
    for ref, value in zip((new_norm, new_norm_first, new_norm_second), new):
        ref[...] = value
    loop(pieces, lambda p: convert(1, p))
    for n in range(2):
        loop(pieces, lambda p: store(n, p).wait())
    for copy in result_copies:
        copy.wait()


def finish(total, norm_total, slots, norms, owners, out_all, in_all):
    vm = pl.BlockSpec(memory_space=pltpu.VMEM)
    hbm = pl.BlockSpec(memory_space=pltpu.HBM)
    dma = pltpu.SemaphoreType.DMA
    V = pltpu.VMEM
    pieces = 4
    shape = out_all.shape
    return pl.pallas_call(
        finish_kernel,
        name="finish",
        out_shape=(
            (jax.ShapeDtypeStruct(shape, f32),) * 2 + tuple(jax.ShapeDtypeStruct(a.shape, f32) for a in slots + norms)
        ),
        in_specs=[hbm] * 11,
        out_specs=(hbm,) * 5 + (vm,) * 3,
        scratch_shapes=[
            V(shape, bf16), V(shape, bf16), V(shape, f32), V(shape, f32), V((3, R, CAP, W), f32), V((3, R, CAP, W), f32),
            V((R, W), f32), V((R, CAP, W), f32),
            V(total.shape, f32), V(norm_total.shape, f32), *(V(a.shape, f32) for a in norms),
            pltpu.SMEM(owners.shape, jnp.int32), dma((2, pieces)), dma((2, pieces)), dma((9,)), dma((3,)),
        ],
        compiler_params=pltpu.CompilerParams(vmem_limit_bytes=60 << 20),
    )(total, norm_total, *slots, *norms, owners, out_all, in_all)


def fast_shards(
    tokens, cotangent, timesteps, bands, lengths, owners,
    master_slots, first_slots, second_slots, norm_master, norm_first, norm_second,
):
    def tiles(slots):
        return jnp.transpose(slots.reshape(CAP, R, W), (1, 0, 2))

    def flat(slots):
        return jnp.transpose(slots, (1, 0, 2)).reshape(CAP, R * W)

    steps, bands_row, lens_row = (v.reshape(1, -1) for v in (timesteps, bands, lengths))
    slots = tuple(tiles(s) for s in (master_slots, first_slots, second_slots))
    norms = (norm_master, norm_first, norm_second)
    total, out_all, in_all, norm_total = layer(
        tokens, cotangent, slots[0], norm_master, steps, bands_row, lens_row, lengths, owners
    )
    results = finish(total, norm_total, slots, norms, owners, out_all, in_all)
    return (*results[:2], *(flat(s) for s in results[2:5]), *results[5:])


def solution(mesh):
    fits = dict(mesh.shape) == {"dp": 8, "head": 4}
    placed = (
        P("dp", None),
        P("dp", None),
        P("dp"),
        P("dp"),
        P("dp"),
        P(),
        P("dp", "head"),
        P("dp", "head"),
        P("dp", "head"),
        P(None, "dp"),
        P(None, "dp"),
        P(None, "dp"),
    )
    return jax.shard_map(
        fast_shards if fits else shards,
        mesh=mesh,
        in_specs=placed,
        out_specs=(
            P("dp", None),
            P("dp", None),
            P("dp", "head"),
            P("dp", "head"),
            P("dp", "head"),
            P(None, "dp"),
            P(None, "dp"),
            P(None, "dp"),
        ),
        check_vma=False,
    )
```

```python
import math

import jax
import jax.numpy as jnp
from jax import lax
from jax.experimental import pallas as pl
from jax.experimental.pallas import tpu as pltpu
from jax.sharding import PartitionSpec as P

D = 512
H = 8
HD = 64
FF = 2048
SEQ = 256
TSTEPS = 1000
NBANDS = 8
CAP = 3
STEP = 5


beta_one = 0.5
beta_two = 0.5
learn_rate = 0.04
norm_rate = 0.4
weight_decay = 0.1
adam_eps = 1e-08
norm_eps = 1e-05


def contract_rows(left_side, right_side):
    return lax.dot_general(
        left_side, right_side, (((0,), (0,)), ((), ())), preferred_element_type=jnp.float32
    )


def contract_cols(left_side, right_side):
    return lax.dot_general(
        left_side, right_side, (((1,), (1,)), ((), ())), preferred_element_type=jnp.float32
    )


def gelu_tanh(values):
    return jax.nn.gelu(values, approximate=True)


def norm_forward(values, gain_row, shift_row):
    average = jnp.mean(values, axis=-1, keepdims=True)
    centred = values - average
    inverse = lax.rsqrt(jnp.mean(centred * centred, axis=-1, keepdims=True) + norm_eps)
    scaled = centred * inverse
    return (scaled * gain_row + shift_row, scaled, inverse)


def norm_backward(grad_normed, scaled, inverse, gain_row):
    grad_scaled = grad_normed * gain_row
    centre_term = jnp.mean(grad_scaled, axis=-1, keepdims=True)
    slope_term = jnp.mean(grad_scaled * scaled, axis=-1, keepdims=True)
    return inverse * (grad_scaled - centre_term - scaled * slope_term)


def slot_rows(owners, capacity):
    block_index = jnp.arange(owners.shape[0], dtype=jnp.int32)
    earlier = (owners[None, :] == owners[:, None]) & (block_index[None, :] < block_index[:, None])
    return owners * capacity + jnp.sum(earlier.astype(jnp.int32), axis=1)


def attention_scores(query_heads, key_heads, key_valid):
    scores = jnp.einsum(
        "gqad,gkad->gaqk", query_heads, key_heads, preferred_element_type=jnp.float32
    ) / math.sqrt(HD)
    return jnp.where(key_valid[:, None, None, :], scores, -1e30)


def adamw_update(weight, first_moment, second, gradient, decay_rate, step_rate):
    new_first = beta_one * first_moment + (1.0 - beta_one) * gradient
    new_second = beta_two * second + (1.0 - beta_two) * gradient * gradient
    first_hat = new_first / (1.0 - beta_one**STEP)
    second_hat = new_second / (1.0 - beta_two**STEP)
    new_weight = weight - step_rate * (
        first_hat / (jnp.sqrt(second_hat) + adam_eps) + decay_rate * weight
    )
    return (new_weight, new_first, new_second)


def shards(
    tokens,
    cotangent,
    timesteps,
    bands,
    lengths,
    owners,
    master_slots,
    first_slots,
    second_slots,
    norm_master,
    norm_first,
    norm_second,
):
    head_count = lax.axis_size("head")
    owner_index = lax.axis_index("dp")
    heads_here = H // head_count
    width_here = heads_here * HD
    units_here = FF // head_count
    block_len = master_slots.shape[1]
    norm_cols = norm_master.shape[1]
    row_count = tokens.shape[0]
    item_count = lengths.shape[0]
    block_count = owners.shape[0]
    slot_row = slot_rows(owners, CAP)
    gathered, norm_whole = (
        lax.all_gather(master_slots.astype(jnp.bfloat16), "dp", axis=0, tiled=True),
        lax.all_gather(norm_master.astype(jnp.bfloat16), "dp", axis=1, tiled=True),
    )
    flat_params = gathered[slot_row].reshape(-1)
    qkv_end = 3 * D * width_here
    out_end = qkv_end + width_here * D
    up_end = out_end + D * units_here
    qkv_weight = flat_params[:qkv_end].reshape(D, 3 * width_here)
    out_weight = flat_params[qkv_end:out_end].reshape(width_here, D)
    up_weight = flat_params[out_end:up_end].reshape(D, units_here)
    down_weight = flat_params[up_end:].reshape(units_here, D)
    norm_params = norm_whole.astype(jnp.float32)
    item_weight = jnp.exp(-2.0 * timesteps.astype(jnp.float32) / TSTEPS)
    item_length = lengths.astype(jnp.float32)
    band_table = (bands[:, None] == jnp.arange(NBANDS, dtype=jnp.int32)[None, :]).astype(
        jnp.float32
    )
    weight_sums, count_sums = lax.psum(
        (
            jnp.sum(band_table * (item_weight * item_length)[:, None], axis=0),
            jnp.sum(band_table * item_length[:, None], axis=0),
        ),
        "dp",
    )
    item_scale = (
        item_weight
        * jnp.sum(band_table * count_sums[None, :], axis=1)
        / jnp.sum(band_table * weight_sums[None, :], axis=1)
    )
    key_valid = jnp.arange(SEQ, dtype=jnp.int32)[None, :] < lengths[:, None]
    token_scale = jnp.where(key_valid, item_scale[:, None], 0.0).reshape(row_count)
    normed_one, scaled_one, inverse_one = norm_forward(tokens, norm_params[0], norm_params[1])
    normed_one_low = normed_one.astype(jnp.bfloat16)
    projected_low = jnp.dot(normed_one_low, qkv_weight, preferred_element_type=jnp.float32).astype(
        jnp.bfloat16
    )
    head_shape = (item_count, SEQ, heads_here, HD)
    query_heads = projected_low[:, :width_here].reshape(head_shape)
    key_heads = projected_low[:, width_here : 2 * width_here].reshape(head_shape)
    value_heads = projected_low[:, 2 * width_here :].reshape(head_shape)
    scores = attention_scores(query_heads, key_heads, key_valid)
    row_max = jnp.max(scores, axis=-1, keepdims=True)
    exp_scores = jnp.exp(scores - row_max)
    row_total = jnp.sum(exp_scores, axis=-1, keepdims=True)
    log_total = row_max + jnp.log(row_total)
    prob_low = (exp_scores / row_total).astype(jnp.bfloat16)
    attended_low = (
        jnp.einsum("gaqk,gkad->gqad", prob_low, value_heads, preferred_element_type=jnp.float32)
        .astype(jnp.bfloat16)
        .reshape(row_count, width_here)
    )
    attn_sum = lax.psum(
        jnp.dot(attended_low, out_weight, preferred_element_type=jnp.float32).astype(jnp.bfloat16),
        "head",
    ).astype(jnp.float32)
    mixed_state = tokens + attn_sum
    normed_two, scaled_two, inverse_two = norm_forward(mixed_state, norm_params[2], norm_params[3])
    normed_two_low = normed_two.astype(jnp.bfloat16)
    hidden = jnp.dot(normed_two_low, up_weight, preferred_element_type=jnp.float32)
    activated, gelu_pull = jax.vjp(gelu_tanh, hidden)
    activated_low = activated.astype(jnp.bfloat16)
    ffn_sum = lax.psum(
        jnp.dot(activated_low, down_weight, preferred_element_type=jnp.float32).astype(
            jnp.bfloat16
        ),
        "head",
    ).astype(jnp.float32)
    block_output = mixed_state + ffn_sum
    grad_state = cotangent * token_scale[:, None]
    grad_low_two = grad_state.astype(jnp.bfloat16)
    grad_down = contract_rows(activated_low, grad_low_two)
    grad_activated = contract_cols(grad_low_two, down_weight)
    grad_hidden_low = gelu_pull(grad_activated)[0].astype(jnp.bfloat16)
    grad_up = contract_rows(normed_two_low, grad_hidden_low)
    grad_normed_two = lax.psum(
        contract_cols(grad_hidden_low, up_weight).astype(jnp.bfloat16), "head"
    ).astype(jnp.float32)
    grad_mixed = grad_state + norm_backward(
        grad_normed_two, scaled_two, inverse_two, norm_params[2]
    )
    grad_low_one = grad_mixed.astype(jnp.bfloat16)
    grad_out_proj = contract_rows(attended_low, grad_low_one)
    grad_attended_low = (
        contract_cols(grad_low_one, out_weight).astype(jnp.bfloat16).reshape(head_shape)
    )
    scores_again = attention_scores(query_heads, key_heads, key_valid)
    probabilities = jnp.exp(scores_again - log_total)
    prob_again_low = probabilities.astype(jnp.bfloat16)
    grad_values = jnp.einsum(
        "gaqk,gqad->gkad", prob_again_low, grad_attended_low, preferred_element_type=jnp.float32
    )
    grad_probs = jnp.einsum(
        "gqad,gkad->gaqk", grad_attended_low, value_heads, preferred_element_type=jnp.float32
    )
    grad_scores_low = (
        probabilities * (grad_probs - jnp.sum(grad_probs * probabilities, axis=-1, keepdims=True))
    ).astype(jnp.bfloat16)
    grad_queries = jnp.einsum(
        "gaqk,gkad->gqad", grad_scores_low, key_heads, preferred_element_type=jnp.float32
    ) / math.sqrt(HD)
    grad_keys = jnp.einsum(
        "gaqk,gqad->gkad", grad_scores_low, query_heads, preferred_element_type=jnp.float32
    ) / math.sqrt(HD)
    grad_projected_low = jnp.concatenate(
        [
            grad_queries.reshape(row_count, width_here),
            grad_keys.reshape(row_count, width_here),
            grad_values.reshape(row_count, width_here),
        ],
        axis=1,
    ).astype(jnp.bfloat16)
    grad_qkv = contract_rows(normed_one_low, grad_projected_low)
    grad_normed_one = lax.psum(
        contract_cols(grad_projected_low, qkv_weight).astype(jnp.bfloat16), "head"
    ).astype(jnp.float32)
    input_grad = grad_mixed + norm_backward(
        grad_normed_one, scaled_one, inverse_one, norm_params[0]
    )
    norm_grads = jnp.stack(
        [
            jnp.sum(grad_normed_one * scaled_one, axis=0),
            jnp.sum(grad_normed_one, axis=0),
            jnp.sum(grad_normed_two * scaled_two, axis=0),
            jnp.sum(grad_normed_two, axis=0),
        ]
    )
    grad_blocks = jnp.concatenate(
        [
            grad_qkv.reshape(-1),
            grad_out_proj.reshape(-1),
            grad_up.reshape(-1),
            grad_down.reshape(-1),
        ]
    ).reshape(block_count, block_len)
    summed, norm_summed = (
        lax.psum(grad_blocks.astype(jnp.bfloat16), "dp").astype(jnp.float32),
        lax.psum(norm_grads.astype(jnp.bfloat16), "dp").astype(jnp.float32),
    )
    landing = jnp.where(owners == owner_index, slot_row - owner_index * CAP, CAP)
    owned_grad = jnp.zeros((CAP, block_len), jnp.float32).at[landing].set(summed, mode="drop")
    norm_owned = lax.dynamic_slice_in_dim(norm_summed, owner_index * norm_cols, norm_cols, 1)
    held_count = jnp.sum((owners == owner_index).astype(jnp.int32))
    used_slot = (jnp.arange(CAP, dtype=jnp.int32) < held_count)[:, None]
    new_master, new_first, new_second = adamw_update(
        master_slots, first_slots, second_slots, owned_grad, weight_decay, learn_rate
    )
    new_master = jnp.where(used_slot, new_master, 0.0)
    new_first = jnp.where(used_slot, new_first, 0.0)
    new_second = jnp.where(used_slot, new_second, 0.0)
    new_norms, new_norm_first, new_norm_second = adamw_update(
        norm_master, norm_first, norm_second, norm_owned, 0.0, norm_rate
    )
    return (
        block_output,
        input_grad,
        new_master,
        new_first,
        new_second,
        new_norms,
        new_norm_first,
        new_norm_second,
    )


W = 128
R = 384
QB = 4
CB = 12
MESH = pl.DeviceIdType.MESH
bf16 = jnp.bfloat16
f32 = jnp.float32


def place(sizes):
    dp = lax.axis_index("dp")
    head = lax.axis_index("head")
    return dp // sizes.y, lax.rem(dp, sizes.y), head // sizes.c, lax.rem(head, sizes.c)


class Sizes:
    z, y, x, c = 4, 2, 2, 2


def device(z, y, x, c):
    return (z * Sizes.y + y, x * Sizes.c + c)


def block_rows(owners):
    ids = [owners[j] for j in range(owners.shape[0])]
    rows = []
    for j, mine in enumerate(ids):
        row = mine * CAP
        for other in ids[:j]:
            row = row + jnp.where(other == mine, 1, 0)
        rows.append(row)
    return rows


def slot_is_wide(rows, slot_row):
    flag = rows[0] == slot_row
    for row in rows[1:QB]:
        flag = jnp.logical_or(flag, row == slot_row)
    return flag


def dot(left, right):
    return jnp.dot(left, right, preferred_element_type=f32)


def dot_cols(left, right):
    return lax.dot_general(left, right, (((1,), (1,)), ((), ())), preferred_element_type=f32)


def dot_rows(left, right):
    return lax.dot_general(left, right, (((0,), (0,)), ((), ())), preferred_element_type=f32)


def normalise(values):
    centred = values - jnp.mean(values, axis=-1, keepdims=True)
    inverse = lax.rsqrt(jnp.mean(centred * centred, axis=-1, keepdims=True) + norm_eps)
    return centred * inverse, inverse


def panels(ref, h, first, size):
    return jnp.concatenate([ref[h, p, first : first + size, :] for p in range(ref.shape[1])], axis=1)


def cat_pieces(first, size):
    pieces = []
    row = first
    while row < first + size:
        block, inside = divmod(row, R // 4)
        count = min(R // 4 - inside, first + size - row)
        pieces.append((QB + block, inside, row - first, count))
        row += count
    return pieces


RA, RB = 224, 304
GA, GB = 176, 336
TILE = 256


def layer_kernel(
    tok_hbm, cot_hbm, master_hbm, norms_hbm, steps_hbm, bands_hbm, lens_row_hbm, lens_hbm, owners_hbm,
    total, out_all, in_all, norm_total,
    wv, master, flat, mine, meta, norms_v, steps, bands, lens_row, lens, owners, block_at,
    tok, cot, low1, xhat1, inv1, qkv, probs, sums, att, acc, low2, xhat2, inv2, e2, actives, d_qkvs, da, e1,
    out_low, in_low,
    grads, from_core, rxa, sa, rya, sb, ryb, sbx, rxb, fz, rz, sc, rc, ryc, rxc, norm_part, norm_sum, n_core, n_x, n_y, n_z,
    i_sem, z_s, z_r, ya_s, ya_r, xa_s, xa_r, xb_s, xb_r, yb_s, yb_r, core_s, core_r, m_s, m_r,
    c_s, c_r, zc_s, zc_r, cc_s, cc_r, sc_s, sc_r, cy_s, cy_r, cx_s, cx_r,
    cs, cr, as_, ar, say_s, say_r, sby_s, sby_r, sbx_s, sbx_r, fz_s, fz_r, n_s, n_r, o_s, o_r, o_l,
):
    z, y, x, c = place(Sizes)
    nz = Sizes.z
    dp, head = z * 2 + y, x * 2 + c
    dp_peers = [device(lax.rem(z + k, nz), (y + j) % 2, x, c) for k in range(nz) for j in range(2) if k or j]
    x_peer, y_peer, core_peer = device(z, y, 1 - x, c), device(z, 1 - y, x, c), device(z, y, x, 1 - c)
    peers = dp_peers + [x_peer, core_peer]
    barrier = pltpu.get_barrier_semaphore()
    for peer in peers:
        pl.semaphore_signal(barrier, inc=1, device_id=peer, device_id_type=MESH)

    tokens_here = tok.shape[1]
    items_here = tokens_here // SEQ
    tiles = tokens_here // TILE

    def whose(p):
        return lax.rem(x + p, 2) * 2 + c

    def tokens_of(ref, who):
        return ref.at[pl.ds(pl.multiple_of(who * tokens_here, tokens_here), tokens_here), :]

    fetches = [
        pltpu.make_async_copy(src, dst, i_sem.at[n])
        for n, (src, dst) in enumerate((
            (owners_hbm, owners), (master_hbm, master), (steps_hbm, steps), (bands_hbm, bands),
            (lens_row_hbm, lens_row), (norms_hbm, norms_v), (lens_hbm, lens),
            (tokens_of(tok_hbm, whose(0)), tok.at[0]), (tokens_of(cot_hbm, whose(0)), cot.at[0]),
            (tokens_of(tok_hbm, whose(1)), tok.at[1]), (tokens_of(cot_hbm, whose(1)), cot.at[1]),
        ))
    ]
    for fetch in fetches:
        fetch.start()

    def loop(first, last, body):
        def step(i, _):
            body(i)
            return 0

        lax.fori_loop(first, last, step, 0)

    def remote(src, dst, send, recv, peer):
        return pltpu.make_async_remote_copy(
            src_ref=src, dst_ref=dst, send_sem=send, recv_sem=recv, device_id=peer, device_id_type=MESH
        )

    def same(ref, send, recv, peer):
        return remote(ref, ref, send, recv, peer)

    shard, far = x * 2 + c, (1 - x) * 2 + c
    fetches[0].wait()
    rows = block_rows(owners)
    fetches[1].wait()
    for r in range(CAP):
        flat[...] = master[:, r, :]
        wide = jnp.concatenate([flat[pl.ds(p, W, stride=3), :] for p in range(3)], axis=0)
        narrow = jnp.concatenate([flat[pl.ds(p, R // 4, stride=4), :] for p in range(4)], axis=0)
        wv[shard, dp * CAP + r] = jnp.where(slot_is_wide(rows, dp * CAP + r), wide, narrow).astype(bf16)

    for n in (2, 3, 4, 5):
        fetches[n].wait()
    items = steps.shape[1]
    item_weight = jnp.exp(-2.0 * steps[...].astype(f32) / TSTEPS)
    item_length = lens_row[...].astype(f32)
    table = bands[...] == lax.broadcasted_iota(jnp.int32, (NBANDS, items), 0)
    ones = table.astype(f32)
    mine[...] = jnp.zeros_like(mine)
    mine[0:4, 0 : W // 2] = norms_v[...]
    mine[:, W // 2 : W // 2 + 1] = jnp.sum(ones * (item_weight * item_length), axis=1, keepdims=True)
    mine[:, W // 2 + 1 : W // 2 + 2] = jnp.sum(ones * item_length, axis=1, keepdims=True)
    meta[dp] = mine[...]

    pl.semaphore_wait(barrier, len(peers))

    part_a, part_b, part_ab, part_c = pl.ds(0, GA), pl.ds(GA, GB - GA), pl.ds(0, GB), pl.ds(GB, R - GB)

    def slab(sh, zz, yy, part=slice(None)):
        return wv.at[sh, pl.ds((zz * 2 + yy) * CAP, CAP), part, :]

    def order(k):
        late, low = k // 2, z // 2
        return (1 - late) * (z + k * (1 - 2 * lax.rem(z, 2))) + late * (k + low * (3 - 2 * k))

    up, down, inner = z < nz - 1, z > 0, lax.rem(z, nz - 1) != 0
    own_up = same(slab(shard, z, y, part_ab), z_s.at[0], z_r.at[z], device(z + 1, y, x, c))
    own_down = same(slab(shard, z, y, part_ab), z_s.at[nz], z_r.at[z], device(z - 1, y, x, c))
    pl.when(up)(own_up.start)
    pl.when(down)(own_down.start)

    def meta_copy(k):
        return remote(mine, meta.at[dp], m_s.at[k], m_r.at[k], dp_peers[k])

    for k in range(len(dp_peers)):
        meta_copy(k).start()

    def along_z(k):
        zz = order(k)
        late = k // 2
        goal = (1 - late) * (3 - z) + late * 3 * (z - 1)
        return same(slab(shard, zz, y, part_ab), z_s.at[k], z_r.at[zz], device(goal, y, x, c))

    def both(j, zz):
        return wv.at[lax.rem(x + j, 2) * 2 + c, pl.ds(zz * 2 * CAP, 2 * CAP), part_c, :]

    def last_z(j, n):
        return same(both(j, z), zc_s.at[j, n], zc_r.at[j, n], device(lax.rem(z + n, nz), y, x, c))

    def last_here(j, n):
        zz = lax.rem(z + nz - n, nz)
        return same(both(j, zz), zc_s.at[j, n], zc_r.at[j, n], x_peer)

    def last_core(j, n):
        return same(both(j, lax.rem(z + nz - n, nz)), cc_s.at[j, n], cc_r.at[j, n], core_peer)

    own_c = slab(shard, z, y, part_c)
    c_copies = (
        same(own_c, c_s.at[0], c_r.at[0], y_peer),
        same(own_c, c_s.at[1], c_r.at[1], x_peer),
        same(slab(shard, z, 1 - y, part_c), c_s.at[2], c_r.at[2], x_peer),
    )

    def first_copies(k):
        zz = order(k)
        one, two = slab(shard, zz, y, part_a), slab(shard, zz, y, part_b)
        return (
            same(one, ya_s.at[k], ya_r.at[k], y_peer),
            same(two, xb_s.at[k], xb_r.at[k], x_peer),
            same(two, yb_s.at[k, 0], yb_r.at[k, 0], y_peer),
            same(one, xa_s.at[k, 0], xa_r.at[k, 0], x_peer),
            same(slab(shard, zz, y, part_ab), core_s.at[k, 0], core_r.at[k, 0], core_peer),
        )

    def second_copies(k):
        zz = order(k)
        return (
            same(slab(shard, zz, 1 - y, part_a), xa_s.at[k, 1], xa_r.at[k, 1], x_peer),
            same(slab(far, zz, y, part_b), yb_s.at[k, 1], yb_r.at[k, 1], y_peer),
            same(slab(shard, zz, 1 - y, part_ab), core_s.at[k, 1], core_r.at[k, 1], core_peer),
        )

    def third_copies(k):
        zz = order(k)
        return (
            same(slab(far, zz, y, part_ab), core_s.at[k, 2], core_r.at[k, 2], core_peer),
            same(slab(far, zz, 1 - y, part_ab), core_s.at[k, 3], core_r.at[k, 3], core_peer),
        )

    def gather0(k):
        @pl.when(k > 0)
        def _():
            along_z(k).wait_recv()
            pl.when(inner)(along_z(k).start)

        for copy in first_copies(k):
            copy.start()

    def gather1(k):
        zz = order(k)
        over_x, over_y, core = second_copies(k)
        same(slab(shard, zz, 1 - y, part_a), ya_s.at[k], ya_r.at[k], y_peer).wait_recv()
        over_x.start()
        same(slab(far, zz, y, part_b), xb_s.at[k], xb_r.at[k], x_peer).wait_recv()
        over_y.start()
        same(slab(shard, zz, 1 - y, part_b), yb_s.at[k, 0], yb_r.at[k, 0], y_peer).wait_recv()
        core.start()

    def gather2(k):
        zz = order(k)
        near, apart = third_copies(k)
        same(slab(far, zz, y, part_a), xa_s.at[k, 0], xa_r.at[k, 0], x_peer).wait_recv()
        near.start()
        same(slab(far, zz, 1 - y, part_a), xa_s.at[k, 1], xa_r.at[k, 1], x_peer).wait_recv()
        same(slab(far, zz, 1 - y, part_b), yb_s.at[k, 1], yb_r.at[k, 1], y_peer).wait_recv()
        apart.start()

    c_copies[0].start()
    c_copies[1].start()
    gather0(0)

    def gather_last(n):
        for j in range(2):
            last_here(j, n).wait_recv()
            last_core(j, n).start()

    def find_block(row):
        block = 0
        for j, block_row in enumerate(rows):
            block = block + jnp.where(block_row == row, j, 0)
        block_at[row] = block

    loop(0, nz * 2 * CAP, find_block)
    for k in range(len(dp_peers)):
        meta_copy(k).wait_recv()
    lane = lax.broadcasted_iota(jnp.int32, (8, W), 1)
    chunks = []
    for pair in range(meta.shape[0] // 2):
        chunks.append(jnp.where(lane < W // 2, meta[2 * pair], pltpu.roll(meta[2 * pair + 1], W // 2, 1)))
    norms = jnp.concatenate(chunks, axis=1).astype(bf16).astype(f32)
    gain1, shift1, gain2, shift2 = (norms[i : i + 1, :] for i in range(4))
    band_sums = meta[0]
    for d in range(1, meta.shape[0]):
        band_sums = band_sums + meta[d]
    weight_of = jnp.sum(jnp.where(table, band_sums[:, W // 2 : W // 2 + 1], 0.0), axis=0, keepdims=True)
    count_of = jnp.sum(jnp.where(table, band_sums[:, W // 2 + 1 : W // 2 + 2], 0.0), axis=0, keepdims=True)
    scales = item_weight * count_of / weight_of
    item_lane = lax.broadcasted_iota(jnp.int32, (1, items), 1)
    position = lax.broadcasted_iota(jnp.int32, (TILE, 1), 0)
    for n in range(6, 11):
        fetches[n].wait()

    def tile(t):
        return pl.ds(pl.multiple_of(t * TILE, TILE), TILE)

    def first_norm(i):
        p, t = i // tiles, lax.rem(i, tiles)
        here = tile(t)
        scaled, inverse = normalise(tok[p, here, :])
        xhat1[p, here, :] = scaled
        inv1[p, here, :] = inverse
        low1[p, here, :] = (scaled * gain1 + shift1).astype(bf16)
        item = whose(p) * items_here + t // (SEQ // TILE)
        scale = jnp.sum(jnp.where(item_lane == item, scales, 0.0), axis=1, keepdims=True)
        inside = position + lax.rem(t, SEQ // TILE) * TILE < lens[item]
        scaled_cot = cot[p, here, :] * jnp.where(inside, scale, 0.0)
        cot[p, here, :] = scaled_cot
        e2[p, here, :] = scaled_cot.astype(bf16)

    c_copies[0].wait_recv()
    c_copies[2].start()
    loop(0, 2 * tiles, first_norm)
    c_copies[1].wait_recv()
    c_copies[2].wait_recv()
    for j in range(2):
        last_core(j, 0).start()

    def gather(step):
        pl.when(step < nz)(lambda: gather0(step))

        @pl.when(step == nz - 1)
        def _():
            for j in range(2):
                for n in range(1, nz):
                    last_z(j, n).start()

        pl.when(step <= nz)(lambda: gather1(step - 1))
        pl.when(step >= 2)(lambda: gather2(step - 2))

    loop(1, nz + 2, gather)
    loop(1, nz, gather_last)

    def all_here(k):
        zz = order(k)
        for kind, (xx, yy) in enumerate(((x, y), (x, 1 - y), (1 - x, y), (1 - x, 1 - y))):
            same(slab(xx * 2 + 1 - c, zz, yy, part_ab), core_s.at[k, kind], core_r.at[k, kind], core_peer).wait_recv()
        for j in range(2):
            last_core(j, k).wait_recv()

    loop(0, nz, all_here)

    head_lane = lax.broadcasted_iota(jnp.int32, (1, W), 1)
    head_masks = [head_lane < HD, head_lane >= HD]
    key_pos = lax.broadcasted_iota(jnp.int32, (1, SEQ), 1)
    item_rows = [slice(i * SEQ, (i + 1) * SEQ) for i in range(items_here)]

    def only(values, a):
        return jnp.where(head_masks[a], values, jnp.zeros_like(values))

    def stack(values):
        return jnp.concatenate([only(values, 0), only(values, 1)], axis=0)

    def wide_matrix(h):
        return jnp.concatenate(
            [
                jnp.concatenate([wv[h, rows[j], p * W : (p + 1) * W, :] for j in range(QB)], axis=0)
                for p in range(3)
            ],
            axis=1,
        )

    def narrow_matrix(h, first, size):
        pieces = cat_pieces(first, size)
        return jnp.concatenate(
            [
                jnp.concatenate(
                    [wv[h, rows[b], pl.ds(p * (R // 4) + inside, count), :] for b, inside, _, count in pieces], axis=0
                )
                for p in range(4)
            ],
            axis=1,
        )

    deep, low = (QB + 2, CB - 2), (0, QB + 2)
    x_part, y_part, z_part = pl.ds(0, RA), pl.ds(RA, RB - RA), pl.ds(RB, R - RB)

    def core_push(j, n):
        part = pl.ds(*(deep, low)[n])
        return remote(grads.at[j, part], from_core.at[j, part], cs.at[n, j], cr.at[n, j], core_peer)

    def x_push(n):
        part = pl.ds(*(deep, low)[n])
        return remote(grads.at[2, part, x_part, :], rxa.at[part], as_.at[n], ar.at[n], x_peer)

    def hand_over(i, n):
        first, count = (deep, low)[n]
        pl.when(i < 2)(lambda: core_push(i, n).start())

        @pl.when(i >= 2)
        def _():
            core_push(i - 2, n).wait_recv()

            def add(block):
                grads[i, block] = grads[i, block] + from_core[i - 2, block]

            loop(first, first + count, add)
            pl.when(i == 2)(lambda: x_push(n).start())

    pair_z, cross_z = z + 1 - 2 * lax.rem(z, 2), lax.rem(z + 2, nz)

    def chunk(k):
        return lax.rem(pair_z + lax.rem(k, 2) * (z - pair_z) + 2 * (1 - k // 2), nz)

    def block_of(k, yy, r):
        return block_at[(chunk(k) * 2 + yy) * CAP + r]

    def over_y_first(k):
        return remote(sb.at[k], ryb.at[k], sby_s.at[k], sby_r.at[k], y_peer)

    def over_x_last(k):
        return remote(sbx.at[k], rxb.at[k], sbx_s.at[k], sbx_r.at[k], x_peer)

    def over_y_last(k):
        return remote(sa.at[k], rya.at[k], say_s.at[k], say_r.at[k], y_peer)

    def over_z(k, r):
        goal = pair_z + lax.rem(k, 2) * (cross_z - pair_z)
        return remote(fz.at[k, r], rz.at[k, r], fz_s.at[k, r], fz_r.at[k, r], device(goal, y, x, c))

    def z_first(k):
        goal = pair_z + lax.rem(k, 2) * (cross_z - pair_z)
        return remote(sc.at[k], rc.at[k], sc_s.at[k], sc_r.at[k], device(goal, y, x, c))

    def z_then_y():
        return remote(sc.at[nz - 1, :, 1 - y], ryc, cy_s, cy_r, y_peer)

    def z_then_x():
        return remote(sc.at[nz - 1, 0, y], rxc, cx_s, cx_r, x_peer)

    def send_c(k):
        for r in range(2 * CAP):
            block = block_of(k, r // CAP, r % CAP)
            for j in range(2):
                sc[k, j, r // CAP, r % CAP] = grads[2 + j, block, z_part, :]
        pl.when(lax.rem(k, 2) == 0)(lambda: z_first(k).start())

    def cross_c():
        z_first(0).wait_recv()
        for j in range(2):
            sc[1, j] = sc[1, j] + rc[0, j]
        z_first(1).start()

    def own_c():
        z_first(1).wait_recv()
        z_first(2).wait_recv()
        for j in range(2):
            sc[nz - 1, j] = sc[nz - 1, j] + (rc[1, j].astype(f32) + rc[2, j].astype(f32)).astype(bf16)
        z_then_y().start()

    def y_c():
        z_then_y().wait_recv()
        for j in range(2):
            sc[nz - 1, j, y] = sc[nz - 1, j, y] + ryc[j]
        z_then_x().start()

    def norm_copies():
        z_peers = [device(lax.rem(z + k, nz), y, x, c) for k in range(1, nz)]
        return [
            remote(norm_part, n_core, n_s.at[0], n_r.at[0], core_peer),
            remote(norm_sum.at[0], n_x, n_s.at[1], n_r.at[1], x_peer),
            remote(norm_sum.at[1], n_y, n_s.at[2], n_r.at[2], y_peer),
        ] + [remote(norm_sum.at[2], n_z.at[k], n_s.at[3 + k], n_r.at[3 + k], p) for k, p in enumerate(z_peers)]

    def send_b(k):
        for r in range(CAP):
            block = block_of(k, 1 - y, r)
            for j in range(2):
                sb[k, j, r] = grads[2 + j, block, y_part, :]
        over_y_first(k).start()

    def add_x(j):
        grads[3, j, x_part, :] = grads[3, j, x_part, :] + rxa[j]

    def send_a(k):
        for r in range(CAP):
            sa[k, r] = grads[3, block_of(k, 1 - y, r), x_part, :]
        over_y_last(k).start()

    def reduce1(k):
        over_y_first(k).wait_recv()
        for r in range(CAP):
            sbx[k, r] = grads[2, block_of(k, y, r), y_part, :] + ryb[k, 0, r]
        over_x_last(k).start()

    def reduce2(k):
        over_y_last(k).wait_recv()
        over_x_last(k).wait_recv()
        for r in range(CAP):
            block = block_of(k, y, r)
            fz[k, r, x_part, :] = grads[3, block, x_part, :] + rya[k, r]
            part = grads[3, block, y_part, :].astype(f32) + ryb[k, 1, r].astype(f32)
            fz[k, r, y_part, :] = (part + rxb[k, r].astype(f32)).astype(bf16)
            pl.when(lax.rem(k, 2) == 0)(over_z(k, r).start)

    def cross():
        for r in range(CAP):
            over_z(0, r).wait_recv()
            fz[1, r] = fz[1, r] + rz[0, r]
            over_z(1, r).start()

    key_row = lax.broadcasted_iota(jnp.int32, (2 * SEQ, W), 0)
    head_ones = jnp.where((key_row < SEQ) == head_masks[0], 1.0, 0.0).astype(bf16)

    def attention(p, h):
        projected = dot(low1[p], wide_matrix(h))
        qkv[h, 0] = (projected[:, :W].astype(bf16).astype(f32) * (1.0 / math.sqrt(HD))).astype(bf16)
        qkv[h, 1] = projected[:, W : 2 * W].astype(bf16)
        qkv[h, 2] = projected[:, 2 * W :].astype(bf16)
        for i, here in enumerate(item_rows):
            query, key, value = qkv[h, 0, here, :], qkv[h, 1, here, :], qkv[h, 2, here, :]
            valid = key_pos < lens[whose(p) * items_here + i]
            both = []
            for a in range(2):
                scores = jnp.where(valid, dot_cols(only(query, a), key), -1e30)
                exps = jnp.exp(scores - jnp.max(scores, axis=-1, keepdims=True)).astype(bf16)
                probs[h, i, a] = exps
                both.append(exps)
            mixed = dot(jnp.concatenate(both, axis=1), jnp.concatenate([stack(value), head_ones], axis=1))
            inverse = 1.0 / mixed[:, W:]
            sums[h, here, :] = inverse
            att[h, here, :] = (mixed[:, :W] * inverse).astype(bf16)
        acc[...] += dot(att[h], narrow_matrix(h, 0, W))

    def put(i, first, result):
        for block, inside, row, count in cat_pieces(first, result.shape[0]):
            for p in range(4):
                here = pl.ds(p * (R // 4) + inside, count)
                grads[i, block, here, :] = result[row : row + count, p * W : (p + 1) * W].astype(bf16)

    def shard_of(p, i):
        return lax.rem(1 + x + p + i, 2) * 2 + lax.rem(c + 1 + i // 2, 2)

    def feed_forward(p, i):
        h = shard_of(p, i)
        up_matrix, down_matrix = narrow_matrix(h, W, D), narrow_matrix(h, W + D, D)
        hidden = dot(low2[...], up_matrix)
        root = math.sqrt(2.0 / math.pi)
        square = hidden * hidden
        bend = jnp.tanh(root * hidden * (1.0 + 0.044715 * square))
        half = 0.5 * (1.0 + bend)
        active = (hidden * half).astype(bf16)
        slope = half + 0.5 * hidden * (1.0 - bend * bend) * (root + (3.0 * 0.044715 * root) * square)
        if p == 0:
            actives[i] = active
        else:
            acc[...] += dot(active, down_matrix)
        back = (dot_cols(e2[p], down_matrix) * slope).astype(bf16)
        da[...] += dot_cols(back, up_matrix)
        if p == 0:
            put(i, W + D, dot_rows(active, e2[p]))
            put(i, W, dot_rows(low2[...], back))
            hand_over(i, 0)

    def attention_back(p, i):
        h = shard_of(p, i)
        d_all = dot_cols(e1[...], narrow_matrix(h, 0, W)) * sums[h]
        shared_all = (d_all * att[h].astype(f32)).astype(bf16)
        d_all = d_all.astype(bf16)
        parts = []
        for m, here in enumerate(item_rows):
            query, key, value = qkv[h, 0, here, :], qkv[h, 1, here, :], qkv[h, 2, here, :]
            d_here, shared = d_all[here, :], shared_all[here, :]
            against = jnp.concatenate([value, jnp.full((SEQ, W), -1.0, bf16)], axis=1)
            d_scores = []
            for a in range(2):
                change = dot_cols(jnp.concatenate([only(d_here, a), only(shared, a)], axis=1), against)
                d_scores.append((probs[h, m, a].astype(f32) * change).astype(bf16))
            d_query = dot(jnp.concatenate(d_scores, axis=1), stack(key)) * (1.0 / math.sqrt(HD))
            d_key = dot_rows(jnp.concatenate(d_scores, axis=0), stack(query))
            d_value = dot_rows(jnp.concatenate([probs[h, m, 0], probs[h, m, 1]], axis=0), stack(d_here))
            parts.append(jnp.concatenate([d_query, d_key, d_value], axis=1).astype(bf16))
        d_qkv = jnp.concatenate(parts, axis=0)
        if p == 0:
            d_qkvs[i] = d_qkv
            put(i, 0, dot_rows(att[h], e1[...]))
            d_weight = dot_rows(low1[p], d_qkv).astype(bf16)
            for j in range(QB):
                for m in range(3):
                    grads[i, j, m * W : (m + 1) * W, :] = d_weight[j * W : (j + 1) * W, m * W : (m + 1) * W]
            hand_over(i, 1)
        else:
            da[...] += dot_cols(d_qkv, wide_matrix(h))

    def late_output(i):
        acc[...] += dot(actives[i], narrow_matrix(shard_of(0, i), W + D, D))

    def late_input(i):
        da[...] += dot_cols(d_qkvs[i], wide_matrix(shard_of(0, i)))

    def norm_backward(grad, scaled, inverse, gain):
        grad_scaled = grad * gain
        centre = jnp.mean(grad_scaled, axis=-1, keepdims=True)
        slope = jnp.mean(grad_scaled * scaled, axis=-1, keepdims=True)
        return inverse * (grad_scaled - centre - scaled * slope)

    def add_norm(p, row, grad, scaled):
        if p == 0:
            norm_part[row : row + 1, :] += jnp.sum(grad * scaled, axis=0, keepdims=True)
            norm_part[row + 1 : row + 2, :] += jnp.sum(grad, axis=0, keepdims=True)

    norm_part[...] = jnp.zeros_like(norm_part)

    def out_copies(p, n):
        src, dst = ((out_low, out_all), (in_low, in_all))[n]
        there = tokens_of(dst, whose(p))
        return (
            pltpu.make_async_copy(src.at[p], there, o_l.at[p, n]),
            remote(src.at[p], there, o_s.at[p, n], o_r.at[p, n], core_peer),
        )

    def block_result(p):
        out_low[p] = acc[...].astype(bf16)
        for copy in out_copies(p, 0):
            copy.start()

    def input_result(p):
        def first_norm_back(t):
            here = tile(t)
            grad, scaled = da[here, :], xhat1[p, here, :]
            add_norm(p, 0, grad, scaled)
            in_low[p, here, :] = (cot[p, here, :] + norm_backward(grad, scaled, inv1[p, here, :], gain1)).astype(bf16)

        loop(0, tiles, first_norm_back)
        for copy in out_copies(p, 1):
            copy.start()

    def layer_pass(p):
        acc[...] = jnp.zeros_like(acc)
        loop(0, 4, lambda h: attention(p, h))

        def second_norm(t):
            here = tile(t)
            state = acc[here, :] + tok[p, here, :]
            acc[here, :] = state
            scaled, inverse = normalise(state)
            xhat2[here, :] = scaled
            inv2[here, :] = inverse
            low2[here, :] = (scaled * gain2 + shift2).astype(bf16)
            da[here, :] = jnp.zeros((TILE, D), f32)

        loop(0, tiles, second_norm)
        if p == 1:
            for n in range(2):
                x_push(n).wait_recv()
            loop(0, QB + CB, add_x)
            loop(0, nz, send_a)
            loop(0, nz, reduce1)
        loop(0, 4, lambda i: feed_forward(p, i))
        if p == 1:
            block_result(1)
            own_c()
            reduce2(0)
            norm_copies()[0].wait_recv()
            norm_sum[0] = norm_part[...] + n_core[...]
            norm_copies()[1].start()

        def second_norm_back(t):
            here = tile(t)
            grad, scaled = da[here, :], xhat2[here, :]
            add_norm(p, 2, grad, scaled)
            change = cot[p, here, :] + norm_backward(grad, scaled, inv2[here, :], gain2)
            cot[p, here, :] = change
            e1[here, :] = change.astype(bf16)
            da[here, :] = jnp.zeros((TILE, D), f32)

        loop(0, tiles, second_norm_back)
        if p == 1:
            norm_copies()[1].wait_recv()
            norm_sum[1] = norm_sum[0] + n_x[...]
            norm_copies()[2].start()
            reduce2(1)
            cross()

        def attention_step(i):
            attention_back(p, i)
            if p == 1:
                @pl.when(i == 1)
                def _():
                    reduce2(2)
                    y_c()

        loop(0, 4, attention_step)

    layer_pass(0)
    loop(0, nz, send_c)
    loop(0, nz, send_b)
    loop(0, 4, late_output)
    block_result(0)
    loop(0, 4, late_input)
    input_result(0)
    cross_c()
    norm_copies()[0].start()
    layer_pass(1)
    input_result(1)

    norm_copies()[2].wait_recv()
    norm_sum[2] = norm_sum[1] + n_y[...]
    for copy in norm_copies()[3:]:
        copy.start()
    reduce2(nz - 1)

    for k in range(nz - 1):
        norm_copies()[3 + k].wait_recv()
    z_then_x().wait_recv()
    for r in range(CAP):
        over_z(2, r).wait_recv()
        over_z(1, r).wait_recv()
    norm_total[...] = norm_sum[2] + ((n_z[0] + n_z[1]) + n_z[2])

    def last(r):
        others = rz[1, r].astype(f32) + rz[2, r].astype(f32)
        total[r, pl.ds(0, RB), :] = fz[nz - 1, r].astype(f32) + others
        total[r, z_part, :] = sc[nz - 1, 1, y, r].astype(f32) + rxc[r].astype(f32)

    loop(0, CAP, last)

    for p in range(2):
        for n in range(2):
            local, over_core = out_copies(p, n)
            local.wait()
            over_core.wait()
    for copy in norm_copies():
        copy.wait_send()
    for k in range(len(dp_peers)):
        meta_copy(k).wait_send()
    pl.when(up)(own_up.wait_send)
    pl.when(down)(own_down.wait_send)
    for copy in c_copies:
        copy.wait_send()

    def sent(k):
        for copy in first_copies(k) + second_copies(k) + third_copies(k):
            copy.wait_send()
        pl.when(jnp.logical_and(k > 0, inner))(along_z(k).wait_send)
        for j in range(2):
            last_core(j, k).wait_send()
            pl.when(k > 0)(last_z(j, k).wait_send)
        for copy in (over_y_first(k), over_x_last(k), over_y_last(k)):
            copy.wait_send()
        pl.when(k < nz - 1)(z_first(k).wait_send)
        for r in range(CAP):
            pl.when(k < nz - 1)(over_z(k, r).wait_send)

    loop(0, nz, sent)
    z_then_y().wait_send()
    z_then_x().wait_send()
    for n in range(2):
        x_push(n).wait_send()
        for j in range(2):
            core_push(j, n).wait_send()


def layer(tokens, cotangent, master, norms, steps, bands, lens_row, lens, owners):
    nz = Sizes.z
    here = tokens.shape[0] // lax.axis_size("head")
    items_here = here // SEQ
    items = lens.shape[0]
    vm = pl.BlockSpec(memory_space=pltpu.VMEM)
    hbm = pl.BlockSpec(memory_space=pltpu.HBM)
    dma = pltpu.SemaphoreType.DMA
    V, S = pltpu.VMEM, pltpu.SMEM
    square = (here, D)
    blocks = QB + CB
    rb = RB - RA
    low, full, two_low, two = V(square, bf16), V(square, f32), V((2, *square), bf16), V((2, *square), f32)
    scratch = [
        V((4, nz * 2 * CAP, R, W), bf16), V((R, CAP, W), f32), V((R, W), f32),
        V((8, W), f32), V((nz * 2, 8, W), f32), V(norms.shape, f32),
        V((1, items), jnp.int32), V((1, items), jnp.int32), V((1, items), jnp.int32),
        S((items,), jnp.int32), S(owners.shape, jnp.int32), S((nz * 2 * CAP,), jnp.int32),
        two, two, two_low, two, V((2, here, 1), f32), V((4, 3, here, W), bf16),
        V((4, items_here, 2, SEQ, SEQ), bf16), V((4, here, W), f32), V((4, here, W), bf16),
        full, low, full, V((here, 1), f32), two_low,
        V((4, here, D), bf16), V((4, here, 3 * W), bf16), full, low, two_low, two_low,
        V((4, blocks, R, W), bf16), V((2, blocks, R, W), bf16),
        V((blocks, RA, W), bf16), V((nz, CAP, RA, W), bf16), V((nz, CAP, RA, W), bf16),
        V((nz, 2, CAP, rb, W), bf16), V((nz, 2, CAP, rb, W), bf16), V((nz, CAP, rb, W), bf16),
        V((nz, CAP, rb, W), bf16), V((nz, CAP, RB, W), bf16), V((nz - 1, CAP, RB, W), bf16),
        V((nz, 2, 2, CAP, R - RB, W), bf16), V((nz - 1, 2, 2, CAP, R - RB, W), bf16),
        V((2, CAP, R - RB, W), bf16), V((CAP, R - RB, W), bf16),
        V((8, D), f32), V((3, 8, D), f32), V((8, D), f32), V((8, D), f32), V((8, D), f32), V((nz - 1, 8, D), f32),
        dma((11,)), dma((nz + 1,)), dma((nz,)), dma((nz,)), dma((nz,)), dma((nz, 2)), dma((nz, 2)), dma((nz,)), dma((nz,)),
        dma((nz, 2)), dma((nz, 2)), dma((nz, 4)), dma((nz, 4)), dma((8,)), dma((8,)),
        dma((3,)), dma((3,)), dma((2, nz)), dma((2, nz)), dma((2, nz)), dma((2, nz)),
        dma((nz,)), dma((nz,)), dma, dma, dma, dma,
        dma((2, 2)), dma((2, 2)), dma((2,)), dma((2,)), dma((nz,)), dma((nz,)), dma((nz,)), dma((nz,)),
        dma((nz,)), dma((nz,)), dma((nz, CAP)), dma((nz, CAP)), dma((8,)), dma((8,)), dma((2, 2)), dma((2, 2)), dma((2, 2)),
    ]
    return pl.pallas_call(
        layer_kernel,
        name="layer",
        out_shape=(
            jax.ShapeDtypeStruct((CAP, R, W), f32),
            jax.ShapeDtypeStruct(tokens.shape, bf16),
            jax.ShapeDtypeStruct(tokens.shape, bf16),
            jax.ShapeDtypeStruct((8, D), f32),
        ),
        in_specs=[hbm] * 9,
        out_specs=(vm, hbm, hbm, vm),
        scratch_shapes=scratch,
        compiler_params=pltpu.CompilerParams(collective_id=0, has_side_effects=True, vmem_limit_bytes=56 << 20),
    )(tokens, cotangent, master, norms, steps, bands, lens_row, lens, owners)


def finish_kernel(
    total_hbm, norm_hbm, master_hbm, first_hbm, second_hbm, norm_m, norm_f, norm_s, owners_hbm, out_all, in_all,
    block_output, input_grad, new_master, new_first, new_second, new_norm, new_norm_first, new_norm_second,
    out_low, in_low, out_full, in_full, states, results, flat, grad, total, norm_total, norm_master, norm_first, norm_second, owners, l_sem, s_sem, i_sem, r_sem,
):
    pieces = l_sem.shape[1]
    size = out_low.shape[0] // pieces
    pairs = ((out_all, out_low, out_full, block_output), (in_all, in_low, in_full, input_grad))

    def piece(p):
        return pl.ds(pl.multiple_of(p * size, size), size)

    def fetch(n, p):
        return pltpu.make_async_copy(pairs[n][0].at[piece(p), :], pairs[n][1].at[piece(p), :], l_sem.at[n, p])

    def store(n, p):
        return pltpu.make_async_copy(pairs[n][2].at[piece(p), :], pairs[n][3].at[piece(p), :], s_sem.at[n, p])

    small_copies = [
        pltpu.make_async_copy(src, dst, i_sem.at[3 + i])
        for i, (src, dst) in enumerate((
            (owners_hbm, owners), (total_hbm, total), (norm_hbm, norm_total),
            (norm_m, norm_master), (norm_f, norm_first), (norm_s, norm_second),
        ))
    ]
    state_copies = [
        pltpu.make_async_copy(src, states.at[i], i_sem.at[i]) for i, src in enumerate((master_hbm, first_hbm, second_hbm))
    ]
    result_copies = [
        pltpu.make_async_copy(results.at[i], dst, r_sem.at[i]) for i, dst in enumerate((new_master, new_first, new_second))
    ]

    def loop(count, body):
        def step(i, _):
            body(i)
            return 0

        lax.fori_loop(0, count, step, 0)

    for copy in small_copies:
        copy.start()
    for copy in state_copies:
        copy.start()
    loop(pieces, lambda p: fetch(0, p).start())
    loop(pieces, lambda p: fetch(1, p).start())

    dp = lax.axis_index("dp")
    small_copies[0].wait()
    rows = block_rows(owners)
    held = 0
    for j in range(owners.shape[0]):
        held = held + jnp.where(owners[j] == dp, 1, 0)

    def spread(r):
        is_wide = slot_is_wide(rows, dp * CAP + r)

        @pl.when(is_wide)
        def _():
            for p in range(3):
                flat[pl.ds(p, W, stride=3), :] = total[r, p * W : (p + 1) * W, :]

        @pl.when(jnp.logical_not(is_wide))
        def _():
            for p in range(4):
                flat[pl.ds(p, R // 4, stride=4), :] = total[r, p * (R // 4) : (p + 1) * (R // 4), :]

    small_copies[1].wait()
    for r in range(CAP):
        spread(r)
        grad[:, r, :] = flat[...]

    def convert(n, p):
        fetch(n, p).wait()
        _, low, full, _ = pairs[n]
        full[piece(p), :] = low[piece(p), :].astype(f32)
        store(n, p).start()

    for copy in state_copies:
        copy.wait()
    step = 32
    slot = lax.broadcasted_iota(jnp.int32, (step, CAP, W), 1)

    def update(i):
        here = pl.ds(pl.multiple_of(i * step, step), step)
        new = adamw_update(states[0, here], states[1, here], states[2, here], grad[here], weight_decay, learn_rate)
        for n in range(3):
            results[n, here] = jnp.where(slot < held, new[n], 0.0)


    def both(p):
        convert(0, p)
        for i in range(R // step // pieces):
            update(p * (R // step // pieces) + i)

    loop(pieces, both)
    for copy in result_copies:
        copy.start()
    for copy in small_copies[2:]:
        copy.wait()
    pair = norm_total[:, pl.ds(pl.multiple_of((dp // 2) * W, W), W)]
    mine = jnp.where(lax.rem(dp, 2) == 1, pltpu.roll(pair, W // 2, 1), pair)[0:4, 0 : norm_master.shape[1]]
    new = adamw_update(norm_master[...], norm_first[...], norm_second[...], mine, 0.0, norm_rate)
    for ref, value in zip((new_norm, new_norm_first, new_norm_second), new):
        ref[...] = value
    loop(pieces, lambda p: convert(1, p))
    for n in range(2):
        loop(pieces, lambda p: store(n, p).wait())
    for copy in result_copies:
        copy.wait()


def finish(total, norm_total, slots, norms, owners, out_all, in_all):
    vm = pl.BlockSpec(memory_space=pltpu.VMEM)
    hbm = pl.BlockSpec(memory_space=pltpu.HBM)
    dma = pltpu.SemaphoreType.DMA
    V = pltpu.VMEM
    pieces = 4
    shape = out_all.shape
    return pl.pallas_call(
        finish_kernel,
        name="finish",
        out_shape=(
            (jax.ShapeDtypeStruct(shape, f32),) * 2 + tuple(jax.ShapeDtypeStruct(a.shape, f32) for a in slots + norms)
        ),
        in_specs=[hbm] * 11,
        out_specs=(hbm,) * 5 + (vm,) * 3,
        scratch_shapes=[
            V(shape, bf16), V(shape, bf16), V(shape, f32), V(shape, f32), V((3, R, CAP, W), f32), V((3, R, CAP, W), f32),
            V((R, W), f32), V((R, CAP, W), f32),
            V(total.shape, f32), V(norm_total.shape, f32), *(V(a.shape, f32) for a in norms),
            pltpu.SMEM(owners.shape, jnp.int32), dma((2, pieces)), dma((2, pieces)), dma((9,)), dma((3,)),
        ],
        compiler_params=pltpu.CompilerParams(vmem_limit_bytes=60 << 20),
    )(total, norm_total, *slots, *norms, owners, out_all, in_all)


def fast_shards(
    tokens, cotangent, timesteps, bands, lengths, owners,
    master_slots, first_slots, second_slots, norm_master, norm_first, norm_second,
):
    def tiles(slots):
        return jnp.transpose(slots.reshape(CAP, R, W), (1, 0, 2))

    def flat(slots):
        return jnp.transpose(slots, (1, 0, 2)).reshape(CAP, R * W)

    steps, bands_row, lens_row = (v.reshape(1, -1) for v in (timesteps, bands, lengths))
    slots = tuple(tiles(s) for s in (master_slots, first_slots, second_slots))
    norms = (norm_master, norm_first, norm_second)
    total, out_all, in_all, norm_total = layer(
        tokens, cotangent, slots[0], norm_master, steps, bands_row, lens_row, lengths, owners
    )
    results = finish(total, norm_total, slots, norms, owners, out_all, in_all)
    return (*results[:2], *(flat(s) for s in results[2:5]), *results[5:])


def solution(mesh):
    fits = dict(mesh.shape) == {"dp": 8, "head": 4}
    placed = (
        P("dp", None),
        P("dp", None),
        P("dp"),
        P("dp"),
        P("dp"),
        P(),
        P("dp", "head"),
        P("dp", "head"),
        P("dp", "head"),
        P(None, "dp"),
        P(None, "dp"),
        P(None, "dp"),
    )
    return jax.shard_map(
        fast_shards if fits else shards,
        mesh=mesh,
        in_specs=placed,
        out_specs=(
            P("dp", None),
            P("dp", None),
            P("dp", "head"),
            P("dp", "head"),
            P("dp", "head"),
            P(None, "dp"),
            P(None, "dp"),
            P(None, "dp"),
        ),
        check_vma=False,
    )
```
